32 devices in a mesh: ha: 8 (over y, x, core), wa: 4 (over z).
Axes of the slice: x: 2, y: 2, z: 4, core: 2. Of those that a mesh axis runs over, the one named last changes fastest.
Arguments:
- tokens: bfloat16 [128, 64, 256], P('ha', 'wa'), may hold values from -6 to 6
- gain_attn: float32 [256], replicated, may hold values from 0.25 to 1.75
- qkv_fine: bfloat16 [256, 768], replicated, may hold values from -0.375 to 0.375
- scale_fine: float32 [4], replicated, may hold values from 2 to 24
- out_fine: bfloat16 [256, 256], replicated, may hold values from -0.375 to 0.375
- gain_ffn: float32 [256], replicated, may hold values from 0.25 to 1.75
- ffn_in: bfloat16 [256, 1536], replicated, may hold values from -0.375 to 0.375
- ffn_out: bfloat16 [768, 256], replicated, may hold values from -0.21875 to 0.21875
- up_proj: bfloat16 [256, 1024], replicated, may hold values from -0.375 to 0.375
- gain_coarse: float32 [1024], replicated, may hold values from 0.25 to 1.75
- qkv_coarse: bfloat16 [1024, 3072], replicated, may hold values from -0.1875 to 0.1875
- scale_coarse: float32 [16], replicated, may hold values from 2 to 24
- out_coarse: bfloat16 [1024, 1024], replicated, may hold values from -0.1875 to 0.1875
Outputs:
- fine_out: bfloat16 [128, 64, 256], P('ha', 'wa')
- coarse_out: bfloat16 [8, 4, 1024], P('ha', 'wa')
The draws below stay inside these ranges and needn't reach their ends.
All inputs are finite; a program needn't handle non-finite values.
Results may differ from the reference program's by a relative error of at most 0.03.
Values may be sent and summed in bfloat16 or wider, within the bound.
No kernel may reach another device: no remote copies, remote signals or barrier semaphores. Data moves between devices by JAX's collectives and lax.ppermute only.
A program may use at most 128 MiB of HBM per device.

```python
import math
import jax
import jax.numpy as jnp
from jax import lax

C = 256
CC = 1024
HD = 64
FFH = 768
RADIUS = 3
POOL = 16
HEADS = 4
HEADS_C = 16
H0 = 128
W0 = 64


def block_levels(stream_key, shape, shards, least, largest):
    level, own = 1.0, jax.random.fold_in(stream_key, 6)
    for dim, parts in shards:
        draws = jnp.exp(jax.random.uniform(jax.random.fold_in(own, dim), (parts,), jnp.float32, least / len(shards), largest / len(shards)))
        level = level * jnp.repeat(draws, shape[dim] // parts).reshape([-1 if axis == dim else 1 for axis in range(len(shape))])
    return level


def centred(stream_key, shape, scale, most, pieces=(), kind=jnp.bfloat16):
    array = jax.random.normal(stream_key, shape, jnp.float32) * scale
    if len(pieces) > 0:
        array = block_levels(stream_key, shape, pieces, -0.22, 0.18) * array
    return jnp.clip(array, min=-most, max=most).astype(kind)


def setup_inputs(seed: int = 0) -> dict:
    arg_keys = jax.random.split(jax.random.key(seed), 14)
    tokens = centred(arg_keys[0], (H0, W0, C), 1.0, 6.0, ((0, 8), (1, 4)))
    gain_attn = jnp.clip(1.0 + 0.15 * jax.random.normal(arg_keys[1], (C,), jnp.float32), 0.25, 1.75)
    qkv_fine = centred(arg_keys[2], (C, 3 * C), C ** -0.5, 0.375)
    scale_fine = jnp.clip(jnp.exp(jax.random.uniform(arg_keys[3], (HEADS,), jnp.float32, math.log(2.0), math.log(24.0))), 2.0, 24.0)
    out_fine = centred(arg_keys[4], (C, C), C ** -0.5, 0.375)
    gain_ffn = jnp.clip(1.0 + 0.15 * jax.random.normal(arg_keys[5], (C,), jnp.float32), 0.25, 1.75)
    ffn_in = centred(arg_keys[6], (C, 2 * FFH), C ** -0.5, 0.375)
    ffn_out = centred(arg_keys[7], (FFH, C), FFH ** -0.5, 0.21875)
    up_proj = centred(arg_keys[8], (C, CC), C ** -0.5, 0.375)
    gain_coarse = jnp.clip(1.0 + 0.15 * jax.random.normal(arg_keys[9], (CC,), jnp.float32), 0.25, 1.75)
    qkv_coarse = centred(arg_keys[10], (CC, 3 * CC), CC ** -0.5, 0.1875)
    scale_coarse = jnp.clip(jnp.exp(jax.random.uniform(arg_keys[11], (HEADS_C,), jnp.float32, math.log(2.0), math.log(24.0))), 2.0, 24.0)
    out_coarse = centred(arg_keys[12], (CC, CC), CC ** -0.5, 0.1875)
    return dict(tokens=tokens, gain_attn=gain_attn, qkv_fine=qkv_fine, scale_fine=scale_fine, out_fine=out_fine, gain_ffn=gain_ffn, ffn_in=ffn_in, ffn_out=ffn_out, up_proj=up_proj, gain_coarse=gain_coarse, qkv_coarse=qkv_coarse, scale_coarse=scale_coarse, out_coarse=out_coarse)


def rms_scale(values, gain):
    values = values.astype(jnp.float32)
    return values * lax.rsqrt(lax.optimization_barrier(jnp.mean(values * values, -1, keepdims=True)) + 1e-06) * gain

def head_norm(values, heads):
    shaped = values.reshape(values.shape[:-1] + (heads, HD))
    return shaped * lax.rsqrt(lax.optimization_barrier(jnp.mean(shaped * shaped, -1, keepdims=True)) + 1e-06)

def reference(tokens, gain_attn, qkv_fine, scale_fine, out_fine, gain_ffn, ffn_in, ffn_out, up_proj, gain_coarse, qkv_coarse, scale_coarse, out_coarse):
    height, width_grid = (tokens.shape[0], tokens.shape[1])
    heads = C // HD
    count = height * width_grid
    normed = rms_scale(tokens, gain_attn).astype(jnp.bfloat16).reshape(count, C)
    proj = jnp.dot(normed, qkv_fine, preferred_element_type=jnp.float32).reshape(height, width_grid, 3 * C)
    query = head_norm(proj[..., :C], heads).astype(jnp.bfloat16).astype(jnp.float32)
    key = head_norm(proj[..., C:2 * C], heads).astype(jnp.bfloat16).astype(jnp.float32)
    value = proj[..., 2 * C:].reshape(height, width_grid, heads, HD).astype(jnp.bfloat16).astype(jnp.float32)
    pad_spec = ((RADIUS, RADIUS), (RADIUS, RADIUS), (0, 0), (0, 0))
    key_pad = jnp.pad(key, pad_spec)
    value_pad = jnp.pad(value, pad_spec)
    valid = jnp.pad(jnp.ones((height, width_grid), jnp.float32), RADIUS)
    span = 2 * RADIUS + 1
    score_list = []
    for shift_a in range(span):
        for shift_b in range(span):
            ks = key_pad[shift_a:shift_a + height, shift_b:shift_b + width_grid]
            inside = valid[shift_a:shift_a + height, shift_b:shift_b + width_grid]
            raw = jnp.einsum('xyhd,xyhd->xyh', query, ks) * scale_fine / HD
            score_list.append(jnp.where(inside[..., None] > 0.5, raw, -1e+30))
    scores = jnp.stack(score_list)
    top = lax.optimization_barrier(jnp.max(scores, 0, keepdims=True))
    expo = jnp.exp(scores - top)
    weights = (expo / lax.optimization_barrier(jnp.sum(expo, 0, keepdims=True))).astype(jnp.bfloat16).astype(jnp.float32)
    attn = jnp.zeros((height, width_grid, heads, HD), jnp.float32)
    index = 0
    for shift_a in range(span):
        for shift_b in range(span):
            vs = value_pad[shift_a:shift_a + height, shift_b:shift_b + width_grid]
            attn = attn + weights[index][..., None] * vs
            index = index + 1
    attn = attn.astype(jnp.bfloat16).reshape(count, C)
    h1 = (tokens.reshape(count, C).astype(jnp.float32) + jnp.dot(attn, out_fine, preferred_element_type=jnp.float32)).astype(jnp.bfloat16)
    n2 = rms_scale(h1, gain_ffn).astype(jnp.bfloat16)
    mixed = jnp.dot(n2, ffn_in, preferred_element_type=jnp.float32)
    gated = (jax.nn.gelu(mixed[:, :FFH], approximate=True) * mixed[:, FFH:]).astype(jnp.bfloat16)
    fine_out = (h1.astype(jnp.float32) + jnp.dot(gated, ffn_out, preferred_element_type=jnp.float32)).astype(jnp.bfloat16)
    fine_out = fine_out.reshape(height, width_grid, C)
    rows_c, cols_c = (height // POOL, width_grid // POOL)
    pooled = fine_out.astype(jnp.float32).reshape(rows_c, POOL, cols_c, POOL, C).mean(axis=(1, 3))
    pooled = pooled.astype(jnp.bfloat16).reshape(rows_c * cols_c, C)
    coarse = jnp.dot(pooled, up_proj, preferred_element_type=jnp.float32).astype(jnp.bfloat16)
    heads_c = CC // HD
    ncoarse = rms_scale(coarse, gain_coarse).astype(jnp.bfloat16)
    pc = jnp.dot(ncoarse, qkv_coarse, preferred_element_type=jnp.float32)
    cq = head_norm(pc[:, :CC], heads_c).astype(jnp.bfloat16).astype(jnp.float32)
    ck = head_norm(pc[:, CC:2 * CC], heads_c).astype(jnp.bfloat16).astype(jnp.float32)
    cv = pc[:, 2 * CC:].reshape(-1, heads_c, HD).astype(jnp.bfloat16).astype(jnp.float32)
    cscores = jnp.einsum('qhd,khd->hqk', cq, ck) * (scale_coarse / HD)[:, None, None]
    ctop = lax.optimization_barrier(jnp.max(cscores, -1, keepdims=True))
    cexp = jnp.exp(cscores - ctop)
    cweights = (cexp / lax.optimization_barrier(jnp.sum(cexp, -1, keepdims=True))).astype(jnp.bfloat16).astype(jnp.float32)
    cattn = jnp.einsum('hqk,khd->qhd', cweights, cv).astype(jnp.bfloat16).reshape(-1, CC)
    coarse_out = (coarse.astype(jnp.float32) + jnp.dot(cattn, out_coarse, preferred_element_type=jnp.float32)).astype(jnp.bfloat16)
    return (fine_out, coarse_out.reshape(rows_c, cols_c, CC))
```

```python
import functools

import jax
import jax.numpy as jnp
from jax import lax
from jax.experimental import pallas as pl
from jax.experimental.pallas import tpu as pltpu
from jax.sharding import PartitionSpec as P

HD = 64
RADIUS = 3
LOG2E = 1.4426950408889634
BIG = 2.0**30
BF = jnp.bfloat16
F32 = jnp.float32
MIB = 1 << 20


def rounded_up(value, step):
    return -(-value // step) * step


def dot(a, b):
    return jnp.dot(a, b, preferred_element_type=F32)


def dot_nt(a, b):
    return lax.dot_general(a, b, (((1,), (1,)), ((), ())), preferred_element_type=F32)


def dot_split(values, ones):
    high = values.astype(BF)
    low = (values - high.astype(F32)).astype(BF)
    return dot(high, ones) + dot(low, ones)


def same_head(rows, cols):
    shape = (rows, cols)
    left = lax.broadcasted_iota(jnp.int32, shape, 0) // HD
    right = lax.broadcasted_iota(jnp.int32, shape, 1) // HD
    return (left == right).astype(F32).astype(BF)


def head_norm(values, ones):
    return values * lax.rsqrt(dot_split(values * values, ones) * (1.0 / HD) + 1e-06)


def rms_norm(values, gain):
    mean = jnp.mean(values * values, -1, keepdims=True)
    return values * lax.rsqrt(mean + 1e-06) * gain


def edge_kernel(rows, cols, tok_ref, up_ref, down_ref, left_ref, right_ref):
    height = rows + 2 * RADIUS
    strip = RADIUS * cols
    padded = left_ref.shape[0]
    block = jnp.concatenate([up_ref[...], tok_ref[...], down_ref[...]], 0)
    out = lax.broadcasted_iota(jnp.int32, (padded, block.shape[0]), 0)
    src = lax.broadcasted_iota(jnp.int32, (padded, block.shape[0]), 1)
    row = (out * 21846) >> 16
    first = row * cols + (out - 3 * row)
    inside = out < height * RADIUS
    pick = jnp.where(inside & (src == first), 1.0, 0.0).astype(BF)
    left_ref[...] = dot(pick, block).astype(BF)
    pick = jnp.where(inside & (src == first + (cols - RADIUS)), 1.0, 0.0).astype(BF)
    right_ref[...] = dot(pick, block).astype(BF)


def fine_kernel(
    rows, cols, heads, axes,
    tok_ref, up_ref, down_ref, left_ref, right_ref, gain_attn_ref, qkv_ref, scale_ref,
    out_ref, gain_ffn_ref, ffn_in_ref, ffn_out_ref,
    fine_ref, pooled_ref,
):
    count = rows * cols
    strip = RADIUS * cols
    side = left_ref.shape[0]
    width = heads * HD
    total = count + 2 * strip + 2 * side
    row_axis, col_axis = axes
    row0 = lax.axis_index(row_axis) * rows
    col0 = lax.axis_index(col_axis) * cols
    grid_rows = lax.axis_size(row_axis) * rows
    grid_cols = lax.axis_size(col_axis) * cols

    gain = gain_attn_ref[...]
    tok = tok_ref[...].astype(F32)
    halo = jnp.concatenate([up_ref[...], down_ref[...], left_ref[...], right_ref[...]], 0)
    normed = rms_norm(tok, gain).astype(BF)
    normed_halo = rms_norm(halo.astype(F32), gain).astype(BF)
    ones = same_head(width, width)
    query = head_norm(dot(normed, qkv_ref[:, :width]), ones).astype(BF)
    every = jnp.concatenate([normed, normed_halo], 0)
    key = head_norm(dot(every, qkv_ref[:, width : 2 * width]), ones).astype(BF)
    value = dot(every, qkv_ref[:, 2 * width :]).astype(BF)

    lanes = 2 * HD
    spot = lax.broadcasted_iota(jnp.int32, (total, 1), 0)
    past_own = spot - count
    past_up = past_own - strip
    past_down = past_up - strip
    past_left = past_down - side
    side_at = jnp.where(past_left >= 0, past_left, past_down)
    side_row = (side_at * 21846) >> 16
    side_col = side_at - 3 * side_row - RADIUS
    strip_at = jnp.where(past_up >= 0, past_up, past_own)
    in_own = past_own < 0
    in_strip = past_down < 0
    krow = jnp.where(
        in_own,
        spot // cols,
        jnp.where(
            in_strip,
            strip_at // cols + jnp.where(past_up >= 0, rows, -RADIUS),
            side_row - RADIUS,
        ),
    )
    kcol = jnp.where(
        in_own,
        spot % cols,
        jnp.where(in_strip, strip_at % cols, side_col + jnp.where(past_left >= 0, cols + RADIUS, 0)),
    )
    real = in_strip | (side_at < (rows + 2 * RADIUS) * RADIUS)
    real = real & (krow + row0 >= 0) & (krow + row0 < grid_rows)
    real = real & (kcol + col0 >= 0) & (kcol + col0 < grid_cols)
    krow = jnp.where(real, krow, -1000)

    lane = lax.broadcasted_iota(jnp.int32, (1, lanes), 1)
    place = lane % HD
    is_row = place < rows
    is_col = (place >= rows) & (place < rows + cols)
    far_row = jnp.abs(krow - place) > RADIUS
    far_col = jnp.abs(kcol - (place - rows)) > RADIUS
    key_mask = jnp.where((is_row & far_row) | (is_col & far_col), -BIG, 0.0).astype(BF)
    qspot = lax.broadcasted_iota(jnp.int32, (count, 1), 0)
    hot = (is_row & (qspot // cols == place)) | (is_col & (qspot % cols == place - rows))
    query_mask = jnp.where(hot, 1.0, 0.0).astype(BF)

    low_half = lane < HD
    one = jnp.ones((1, lanes), BF)
    parts = []
    for pair in range(heads // 2):
        span = slice(pair * lanes, (pair + 1) * lanes)
        sums = []
        for half in range(2):
            mine = low_half if half == 0 else ~low_half
            q = jnp.where(mine, query[:, span], query_mask)
            k = jnp.where(mine, key[:, span], key_mask)
            v = jnp.where(mine, value[:, span], one)
            factor = scale_ref[2 * pair + half] * (LOG2E / HD)
            weights = jnp.exp2(dot_nt(q, k) * factor).astype(BF)
            sums.append(dot(weights, v))
        top = jnp.where(low_half, sums[0], sums[1])
        bottom = pltpu.roll(jnp.where(low_half, sums[1], sums[0]), HD, 1)
        parts.append((top / bottom).astype(BF))
    attn = jnp.concatenate(parts, 1)

    h1 = (tok + dot(attn, out_ref[...])).astype(BF)
    h1_wide = h1.astype(F32)
    n2 = rms_norm(h1_wide, gain_ffn_ref[...]).astype(BF)
    hidden = ffn_out_ref.shape[0]
    gate = dot(n2, ffn_in_ref[:, :hidden])
    up = dot(n2, ffn_in_ref[:, hidden:])
    gated = (jax.nn.gelu(gate, approximate=True) * up).astype(BF)
    fine = (h1_wide + dot(gated, ffn_out_ref[...])).astype(BF)
    fine_ref[...] = fine
    pooled_ref[...] = jnp.mean(fine.astype(F32), 0, keepdims=True).astype(BF)


def coarse_kernel(
    heads, axes,
    pooled_ref, up_ref, gain_ref, qkv_ref, scale_ref, out_ref,
    coarse_out_ref,
    query_ref, coarse_ref,
):
    width = heads * HD
    row_axis, col_axis = axes
    mine = lax.axis_index(row_axis) * lax.axis_size(col_axis) + lax.axis_index(col_axis)
    coarse = dot(pooled_ref[...], up_ref[...]).astype(BF).astype(F32)
    coarse_ref[...] = coarse
    normed = rms_norm(coarse, gain_ref[...]).astype(BF)
    group = 4 * HD
    ones = same_head(group, group)
    keys = []
    for at in range(0, width, group):
        span = slice(at, at + group)
        query_ref[:, span] = head_norm(dot(normed, qkv_ref[:, span]), ones).astype(BF).astype(F32)
        keys.append(head_norm(dot(normed, qkv_ref[:, width + at : width + at + group]), ones))
    key = jnp.concatenate(keys, 1).astype(BF).astype(F32)
    value = dot(normed, qkv_ref[:, 2 * width :]).astype(BF).astype(F32)
    query = query_ref[pl.ds(mine, 1), :]
    lanes = 2 * HD
    scale = jnp.zeros((1, lanes), F32)
    lane = lax.broadcasted_iota(jnp.int32, (1, lanes), 1)
    for head in range(heads):
        scale = jnp.where(lane == head, scale_ref[head], scale)
    shape = (width, lanes)
    fold = lax.broadcasted_iota(jnp.int32, shape, 0) // HD == lax.broadcasted_iota(jnp.int32, shape, 1)
    fold = fold.astype(F32).astype(BF)
    scores = dot_split(key * query, fold) * (scale * (1.0 / HD))
    expo = jnp.exp(scores - jnp.max(scores, 0, keepdims=True))
    weights = (expo / jnp.sum(expo, 0, keepdims=True)).astype(BF)
    spread = dot_nt(weights, fold)
    cattn = jnp.sum(spread * value, 0, keepdims=True).astype(BF)
    coarse_out_ref[...] = (coarse_ref[pl.ds(mine, 1), :] + dot(cattn, out_ref[...])).astype(BF)


def vmem():
    return pl.BlockSpec(memory_space=pltpu.VMEM)


def smem():
    return pl.BlockSpec(memory_space=pltpu.SMEM)


def in_vmem(array):
    return pltpu.with_memory_space_constraint(array, pltpu.VMEM)


def shards(
    tokens, gain_attn, qkv_fine, scale_fine, out_fine, gain_ffn, ffn_in, ffn_out,
    up_proj, gain_coarse, qkv_coarse, scale_coarse, out_coarse,
):
    rows, cols, width = tokens.shape
    count = rows * cols
    strip = RADIUS * cols
    side = rounded_up((rows + 2 * RADIUS) * RADIUS, 16)
    heads = width // HD
    width_c = out_coarse.shape[0]
    heads_c = width_c // HD
    devices = lax.axis_size("ha") * lax.axis_size("wa")
    axes = ("ha", "wa")

    def shifted(array, axis, forward):
        size = lax.axis_size(axis)
        pairs = [(i, i + 1) if forward else (i + 1, i) for i in range(size - 1)]
        return lax.ppermute(array, axis, pairs)

    flat = tokens.reshape(count, width)
    up = shifted(flat[count - strip :], "ha", True)
    down = shifted(flat[:strip], "ha", False)
    left_edge, right_edge = pl.pallas_call(
        functools.partial(edge_kernel, rows, cols),
        out_shape=[jax.ShapeDtypeStruct((side, width), BF)] * 2,
        in_specs=[vmem()] * 3,
        out_specs=[vmem()] * 2,
        name="edges",
    )(flat, up, down)
    left = shifted(right_edge, "wa", True)
    right = shifted(left_edge, "wa", False)

    fine, pooled = pl.pallas_call(
        functools.partial(fine_kernel, rows, cols, heads, axes),
        out_shape=[
            jax.ShapeDtypeStruct((count, width), BF),
            jax.ShapeDtypeStruct((1, width), BF),
        ],
        in_specs=[vmem()] * 7 + [smem()] + [vmem()] * 4,
        out_specs=[vmem()] * 2,
        compiler_params=pltpu.CompilerParams(vmem_limit_bytes=24 * MIB),
        name="fine",
    )(
        flat, up, down, left, right, gain_attn.reshape(1, -1), in_vmem(qkv_fine), scale_fine,
        in_vmem(out_fine), gain_ffn.reshape(1, -1), in_vmem(ffn_in), in_vmem(ffn_out),
    )

    every = lax.all_gather(pooled, axes, axis=0, tiled=True)
    coarse_out = pl.pallas_call(
        functools.partial(coarse_kernel, heads_c, axes),
        out_shape=jax.ShapeDtypeStruct((1, width_c), BF),
        in_specs=[vmem()] * 4 + [smem()] + [vmem()],
        out_specs=vmem(),
        scratch_shapes=[pltpu.VMEM((devices, width_c), F32)] * 2,
        compiler_params=pltpu.CompilerParams(vmem_limit_bytes=24 * MIB),
        name="coarse",
    )(
        every, in_vmem(up_proj), gain_coarse.reshape(1, -1), in_vmem(qkv_coarse), scale_coarse,
        in_vmem(out_coarse),
    )
    return fine.reshape(rows, cols, width), coarse_out.reshape(1, 1, width_c)


def solution(mesh):
    return jax.shard_map(
        shards,
        mesh=mesh,
        in_specs=(P("ha", "wa", None), P(), P(), P(), P(), P(), P(), P(), P(), P(), P(), P(), P()),
        out_specs=(P("ha", "wa", None), P("ha", "wa", None)),
        check_vma=False,
    )
```

```python
import functools

import jax
import jax.numpy as jnp
from jax import lax
from jax.experimental import pallas as pl
from jax.experimental.pallas import tpu as pltpu
from jax.sharding import PartitionSpec as P

HD = 64
RADIUS = 3
LOG2E = 1.4426950408889634
BIG = 2.0**30
BF = jnp.bfloat16
F32 = jnp.float32
MIB = 1 << 20


def rounded_up(value, step):
    return -(-value // step) * step


def dot(a, b):
    return jnp.dot(a, b, preferred_element_type=F32)


def dot_nt(a, b):
    return lax.dot_general(a, b, (((1,), (1,)), ((), ())), preferred_element_type=F32)


def dot_split(values, ones):
    high = values.astype(BF)
    low = (values - high.astype(F32)).astype(BF)
    return dot(high, ones) + dot(low, ones)


def same_head(rows, cols):
    shape = (rows, cols)
    left = lax.broadcasted_iota(jnp.int32, shape, 0) // HD
    right = lax.broadcasted_iota(jnp.int32, shape, 1) // HD
    return (left == right).astype(F32).astype(BF)


def head_norm(values, ones):
    return values * lax.rsqrt(dot_split(values * values, ones) * (1.0 / HD) + 1e-06)


def rms_norm(values, gain):
    mean = jnp.mean(values * values, -1, keepdims=True)
    return values * lax.rsqrt(mean + 1e-06) * gain


def edge_kernel(rows, cols, tok_ref, up_ref, down_ref, left_ref, right_ref):
    height = rows + 2 * RADIUS
    padded = left_ref.shape[0]
    block = jnp.concatenate([up_ref[...], tok_ref[...], down_ref[...]], 0)
    out = lax.broadcasted_iota(jnp.int32, (padded, block.shape[0]), 0)
    src = lax.broadcasted_iota(jnp.int32, (padded, block.shape[0]), 1)
    row = (out * 21846) >> 16
    first = row * cols + (out - 3 * row)
    inside = out < height * RADIUS
    pick = jnp.where(inside & (src == first), 1.0, 0.0).astype(BF)
    left_ref[...] = dot(pick, block).astype(BF)
    pick = jnp.where(inside & (src == first + (cols - RADIUS)), 1.0, 0.0).astype(BF)
    right_ref[...] = dot(pick, block).astype(BF)


def half_lanes():
    return lax.broadcasted_iota(jnp.int32, (1, 2 * HD), 1) < HD


def mask_columns(rows, cols):
    place = lax.broadcasted_iota(jnp.int32, (1, 2 * HD), 1) % HD
    return place, place < rows, (place >= rows) & (place < rows + cols)


def query_columns(rows, cols):
    place, is_row, is_col = mask_columns(rows, cols)
    spot = lax.broadcasted_iota(jnp.int32, (rows * cols, 1), 0)
    hot = (is_row & (spot // cols == place)) | (is_col & (spot % cols == place - rows))
    return jnp.where(hot, 1.0, 0.0).astype(BF)


def key_columns(rows, cols, krow, kcol):
    place, is_row, is_col = mask_columns(rows, cols)
    far_row = jnp.abs(krow - place) > RADIUS
    far_col = jnp.abs(kcol - (place - rows)) > RADIUS
    return jnp.where((is_row & far_row) | (is_col & far_col), -BIG, 0.0).astype(BF)


def attend(head, query, key, value, query_mask, key_mask, factor):
    lanes = 2 * HD
    low = half_lanes()
    mine = low if head % 2 == 0 else ~low
    span = slice(head // 2 * lanes, (head // 2 + 1) * lanes)
    q = jnp.where(mine, query[:, span], query_mask)
    k = jnp.where(mine, key[:, span], key_mask)
    v = jnp.where(mine, value[:, span], jnp.ones((1, lanes), BF))
    weights = jnp.exp2(dot_nt(q, k) * (factor * (LOG2E / HD))).astype(BF)
    return dot(weights, v)


def own_kernel(rows, cols, heads, *refs):
    count = (len(refs) - 8) // 2
    moved, (tok_in, scale_in) = refs[:count], refs[count : count + 2]
    outs = refs[count + 2 : 2 * count + 2]
    tok_ref, scale_out, query_ref, acc_ref, scale_ref, sems = refs[2 * count + 2 :]
    gain_ref, qkv_ref = outs[0], outs[1]
    copies = [pltpu.make_async_copy(tok_in, tok_ref, sems.at[0])]
    copies += [pltpu.make_async_copy(scale_in, scale_ref, sems.at[1])]
    copies += [pltpu.make_async_copy(scale_in, scale_out, sems.at[2])]
    copies += [
        pltpu.make_async_copy(src, dst, sems.at[3 + i]) for i, (src, dst) in enumerate(zip(moved, outs))
    ]
    for copy in copies:
        copy.start()
    width = heads * HD
    ones = same_head(width, width)
    query_mask = query_columns(rows, cols)
    spot = lax.broadcasted_iota(jnp.int32, (rows * cols, 1), 0)
    key_mask = key_columns(rows, cols, spot // cols, spot % cols)
    for copy in copies[:5]:
        copy.wait()
    normed = rms_norm(tok_ref[...].astype(F32), gain_ref[...]).astype(BF)
    query = head_norm(dot(normed, qkv_ref[:, :width]), ones).astype(BF)
    key = head_norm(dot(normed, qkv_ref[:, width : 2 * width]), ones).astype(BF)
    value = dot(normed, qkv_ref[:, 2 * width :]).astype(BF)
    query_ref[...] = query
    for head in range(heads):
        acc_ref[head] = attend(head, query, key, value, query_mask, key_mask, scale_ref[0, head])
    for copy in copies[5:]:
        copy.wait()


def fine_kernel(
    rows, cols, heads, axes,
    tok_ref, up_ref, down_ref, left_ref, right_ref, query_ref, acc_ref, gain_attn_ref, qkv_ref, scale_ref,
    out_ref, gain_ffn_ref, ffn_in_ref, ffn_out_ref,
    fine_ref, pooled_ref,
):
    strip = RADIUS * cols
    side = left_ref.shape[0]
    width = heads * HD
    total = 2 * strip + 2 * side
    row_axis, col_axis = axes
    row0 = lax.axis_index(row_axis) * rows
    col0 = lax.axis_index(col_axis) * cols
    grid_rows = lax.axis_size(row_axis) * rows
    grid_cols = lax.axis_size(col_axis) * cols

    halo = jnp.concatenate([up_ref[...], down_ref[...], left_ref[...], right_ref[...]], 0)
    normed = rms_norm(halo.astype(F32), gain_attn_ref[...]).astype(BF)
    ones = same_head(width, width)
    key = head_norm(dot(normed, qkv_ref[:, width : 2 * width]), ones).astype(BF)
    value = dot(normed, qkv_ref[:, 2 * width :]).astype(BF)

    spot = lax.broadcasted_iota(jnp.int32, (total, 1), 0)
    past_up = spot - strip
    past_down = past_up - strip
    past_left = past_down - side
    side_at = jnp.where(past_left >= 0, past_left, past_down)
    side_row = (side_at * 21846) >> 16
    side_col = side_at - 3 * side_row - RADIUS
    strip_at = jnp.where(past_up >= 0, past_up, spot)
    in_strip = past_down < 0
    krow = jnp.where(
        in_strip,
        strip_at // cols + jnp.where(past_up >= 0, rows, -RADIUS),
        side_row - RADIUS,
    )
    kcol = jnp.where(in_strip, strip_at % cols, side_col + jnp.where(past_left >= 0, cols + RADIUS, 0))
    real = in_strip | (side_at < (rows + 2 * RADIUS) * RADIUS)
    real = real & (krow + row0 >= 0) & (krow + row0 < grid_rows)
    real = real & (kcol + col0 >= 0) & (kcol + col0 < grid_cols)
    key_mask = key_columns(rows, cols, jnp.where(real, krow, -1000), kcol)
    query_mask = query_columns(rows, cols)

    query = query_ref[...]
    low = half_lanes()
    parts = []
    for pair in range(heads // 2):
        sums = []
        for head in (2 * pair, 2 * pair + 1):
            factor = scale_ref[0:1, head : head + 1]
            sums.append(acc_ref[head] + attend(head, query, key, value, query_mask, key_mask, factor))
        top = jnp.where(low, sums[0], sums[1])
        bottom = pltpu.roll(jnp.where(low, sums[1], sums[0]), HD, 1)
        parts.append((top / bottom).astype(BF))
    attn = jnp.concatenate(parts, 1)

    h1 = (tok_ref[...].astype(F32) + dot(attn, out_ref[...])).astype(BF)
    h1_wide = h1.astype(F32)
    n2 = rms_norm(h1_wide, gain_ffn_ref[...]).astype(BF)
    hidden = ffn_out_ref.shape[0]
    gate = dot(n2, ffn_in_ref[:, :hidden])
    up = dot(n2, ffn_in_ref[:, hidden:])
    gated = (jax.nn.gelu(gate, approximate=True) * up).astype(BF)
    fine = (h1_wide + dot(gated, ffn_out_ref[...])).astype(BF)
    fine_ref[...] = fine
    pooled = jnp.mean(fine.astype(F32), 0, keepdims=True).astype(BF).astype(F32)
    for part in range(pooled_ref.shape[1]):
        pooled_ref[:, part, :] = jnp.broadcast_to(
            pooled[:, part * 128 : (part + 1) * 128], (pooled_ref.shape[0], 128)
        )


def coarse_kernel(
    heads, axes,
    pooled_ref, up_ref, gain_ref, qkv_ref, scale_ref, out_ref,
    coarse_out_ref,
    query_ref, coarse_ref,
):
    width = heads * HD
    row_axis, col_axis = axes
    mine = lax.axis_index(row_axis) * lax.axis_size(col_axis) + lax.axis_index(col_axis)
    pooled = jnp.concatenate([pooled_ref[:, part, :] for part in range(pooled_ref.shape[1])], 1)
    coarse = dot(pooled.astype(BF), up_ref[...]).astype(BF).astype(F32)
    coarse_ref[...] = coarse
    normed = rms_norm(coarse, gain_ref[...]).astype(BF)
    group = 4 * HD
    ones = same_head(group, group)
    keys = []
    for at in range(0, width, group):
        span = slice(at, at + group)
        query_ref[:, span] = head_norm(dot(normed, qkv_ref[:, span]), ones).astype(BF).astype(F32)
        keys.append(head_norm(dot(normed, qkv_ref[:, width + at : width + at + group]), ones))
    key = jnp.concatenate(keys, 1).astype(BF).astype(F32)
    value = dot(normed, qkv_ref[:, 2 * width :]).astype(BF).astype(F32)
    query = query_ref[pl.ds(mine, 1), :]
    lanes = scale_ref.shape[1]
    shape = (width, lanes)
    fold = lax.broadcasted_iota(jnp.int32, shape, 0) // HD == lax.broadcasted_iota(jnp.int32, shape, 1)
    fold = fold.astype(F32).astype(BF)
    scores = dot_split(key * query, fold) * (scale_ref[...] * (1.0 / HD))
    expo = jnp.exp(scores - jnp.max(scores, 0, keepdims=True))
    weights = (expo / jnp.sum(expo, 0, keepdims=True)).astype(BF)
    spread = dot_nt(weights, fold)
    cattn = jnp.sum(spread * value, 0, keepdims=True).astype(BF)
    coarse_out_ref[...] = (coarse_ref[pl.ds(mine, 1), :] + dot(cattn, out_ref[...])).astype(BF)


def vmem(count):
    return [pl.BlockSpec(memory_space=pltpu.VMEM)] * count


def in_vmem(arrays):
    return [pltpu.with_memory_space_constraint(array, pltpu.VMEM) for array in arrays]


def in_hbm(arrays):
    return [pltpu.with_memory_space_constraint(array, pltpu.HBM) for array in arrays]


def shards(
    tokens, gain_attn, qkv_fine, scale_fine, out_fine, gain_ffn, ffn_in, ffn_out,
    up_proj, gain_coarse, qkv_coarse, scale_coarse, out_coarse,
):
    rows, cols, width = tokens.shape
    count = rows * cols
    strip = RADIUS * cols
    side = rounded_up((rows + 2 * RADIUS) * RADIUS, 16)
    heads = width // HD
    width_c = out_coarse.shape[0]
    heads_c = width_c // HD
    devices = lax.axis_size("ha") * lax.axis_size("wa")
    axes = ("ha", "wa")
    params = pltpu.CompilerParams(vmem_limit_bytes=16 * MIB)

    def shifted(array, axis, forward):
        size = lax.axis_size(axis)
        pairs = [(i, i + 1) if forward else (i + 1, i) for i in range(size - 1)]
        return lax.ppermute(array, axis, pairs)

    flat = tokens.reshape(count, width)
    up = shifted(flat[count - strip :], "ha", True)
    down = shifted(flat[:strip], "ha", False)

    moved = [
        gain_attn.reshape(1, -1), qkv_fine, out_fine, gain_ffn.reshape(1, -1), ffn_in, ffn_out,
        gain_coarse.reshape(1, -1), scale_coarse.reshape(1, -1), up_proj, qkv_coarse, out_coarse,
    ]
    weight_bytes = sum(array.size * array.dtype.itemsize for array in moved)
    results = pl.pallas_call(
        functools.partial(own_kernel, rows, cols, heads),
        out_shape=[pltpu.VMEM(array.shape, array.dtype) for array in moved]
        + [
            pltpu.VMEM((count, width), BF),
            pltpu.VMEM((1, heads), F32),
            pltpu.VMEM((count, width), BF),
            pltpu.VMEM((heads, count, 2 * HD), F32),
        ],
        in_specs=[pl.BlockSpec(memory_space=pl.ANY)] * (len(moved) + 2),
        out_specs=vmem(len(moved) + 4),
        scratch_shapes=[pltpu.SMEM((1, heads), F32), pltpu.SemaphoreType.DMA((len(moved) + 3,))],
        compiler_params=params,
        cost_estimate=pl.CostEstimate(
            flops=2 * count * width * (3 * width + 2 * count), bytes_accessed=weight_bytes, transcendentals=0
        ),
        name="own",
    )(*in_hbm(moved + [flat, scale_fine.reshape(1, -1)]))
    gain_attn_v, qkv_v, out_v, gain_ffn_v, ffn_in_v, ffn_out_v = results[:6]
    gain_c_v, scale_c_v, up_v, qkv_c_v, out_c_v, tok_v, scale_v, query, acc = results[6:]

    left_edge, right_edge = pl.pallas_call(
        functools.partial(edge_kernel, rows, cols),
        out_shape=[pltpu.VMEM((side, width), BF)] * 2,
        in_specs=vmem(3),
        out_specs=vmem(2),
        compiler_params=params,
        name="edges",
    )(*in_vmem([tok_v, up, down]))
    left = shifted(right_edge, "wa", True)
    right = shifted(left_edge, "wa", False)

    fine, pooled = pl.pallas_call(
        functools.partial(fine_kernel, rows, cols, heads, axes),
        out_shape=[
            jax.ShapeDtypeStruct((count, width), BF),
            pltpu.VMEM((devices, width // 128, 128), F32),
        ],
        in_specs=vmem(14),
        out_specs=vmem(2),
        compiler_params=params,
        name="fine",
    )(
        *in_vmem(
            [tok_v, up, down, left, right, query, acc, gain_attn_v, qkv_v, scale_v]
            + [out_v, gain_ffn_v, ffn_in_v, ffn_out_v]
        )
    )

    every = lax.all_to_all(pooled, axes, split_axis=0, concat_axis=0, tiled=True)
    coarse_out = pl.pallas_call(
        functools.partial(coarse_kernel, heads_c, axes),
        out_shape=jax.ShapeDtypeStruct((1, width_c), BF),
        in_specs=vmem(6),
        out_specs=vmem(1)[0],
        scratch_shapes=[pltpu.VMEM((devices, width_c), F32)] * 2,
        compiler_params=params,
        name="coarse",
    )(*in_vmem([every, up_v, gain_c_v, qkv_c_v, scale_c_v, out_c_v]))
    return fine.reshape(rows, cols, width), coarse_out.reshape(1, 1, width_c)


def solution(mesh):
    return jax.shard_map(
        shards,
        mesh=mesh,
        in_specs=(P("ha", "wa", None), P(), P(), P(), P(), P(), P(), P(), P(), P(), P(), P(), P()),
        out_specs=(P("ha", "wa", None), P("ha", "wa", None)),
        check_vma=False,
    )
```

```python
import functools

import jax
import jax.numpy as jnp
from jax import lax
from jax.experimental import pallas as pl
from jax.experimental.pallas import tpu as pltpu
from jax.sharding import PartitionSpec as P

HD = 64
RADIUS = 3
LOG2E = 1.4426950408889634
BIG = 2.0**30
BF = jnp.bfloat16
F32 = jnp.float32
MIB = 1 << 20


def rounded_up(value, step):
    return -(-value // step) * step


def dot(a, b):
    return jnp.dot(a, b, preferred_element_type=F32)


def dot_nt(a, b):
    return lax.dot_general(a, b, (((1,), (1,)), ((), ())), preferred_element_type=F32)


def dot_split(values, ones):
    high = values.astype(BF)
    low = (values - high.astype(F32)).astype(BF)
    return dot(high, ones) + dot(low, ones)


def same_head(rows, cols):
    shape = (rows, cols)
    left = lax.broadcasted_iota(jnp.int32, shape, 0) // HD
    right = lax.broadcasted_iota(jnp.int32, shape, 1) // HD
    return (left == right).astype(F32).astype(BF)


def head_norm(values, ones):
    return values * lax.rsqrt(dot_split(values * values, ones) * (1.0 / HD) + 1e-06)


def rms_norm(values, gain):
    mean = jnp.mean(values * values, -1, keepdims=True)
    return values * lax.rsqrt(mean + 1e-06) * gain


def copy_all(pairs, sems):
    copies = [pltpu.make_async_copy(src, dst, sems.at[i]) for i, (src, dst) in enumerate(pairs)]
    for copy in copies:
        copy.start()
    for copy in copies:
        copy.wait()


def strip_kernel(rows, cols, axis, *refs):
    count, strip = rows * cols, RADIUS * cols
    moved, sems = (len(refs) - 3) // 2, refs[-1]
    ins, outs = refs[:moved], refs[moved : 2 * moved]
    across_ref, within_ref = refs[2 * moved : 2 * moved + 2]
    odd = lax.axis_index(axis) % 2
    last = count - strip
    first = pl.multiple_of(odd * last, 16)
    second = pl.multiple_of((1 - odd) * last, 16)
    pairs = [(ins[0].at[pl.ds(first, strip), :], across_ref), (ins[0].at[pl.ds(second, strip), :], within_ref)]
    copy_all(pairs + list(zip(ins, outs)), sems)


def edge_kernel(rows, cols, axes, tok_ref, across_ref, within_ref, after_ref, across_out, within_out):
    height = rows + 2 * RADIUS
    strip = RADIUS * cols
    padded = across_out.shape[0]
    odd, odd_col = lax.axis_index(axes[0]) % 2, lax.axis_index(axes[1]) % 2
    block = jnp.concatenate([tok_ref[...], across_ref[...], within_ref[...]], 0)
    out = lax.broadcasted_iota(jnp.int32, (padded, 1), 0)
    src = lax.broadcasted_iota(jnp.int32, (padded, block.shape[0]), 1)
    row = ((out * 21846) >> 16) - RADIUS
    col = out - 3 * (row + RADIUS)
    above = rows * cols + strip * odd + RADIUS * cols
    below = rows * cols + strip * (1 - odd) - rows * cols
    first = row * cols + col + jnp.where(row < 0, above, jnp.where(row >= rows, below, 0))
    first = jnp.where(out < height * RADIUS, first, -2 * cols)
    far = cols - RADIUS
    pick = jnp.where(src == first + far * odd_col, 1.0, 0.0).astype(BF)
    across_out[...] = dot(pick, block).astype(BF)
    pick = jnp.where(src == first + far * (1 - odd_col), 1.0, 0.0).astype(BF)
    within_out[...] = dot(pick, block).astype(BF)


def load_kernel(*refs):
    count = (len(refs) - 2) // 2
    copy_all(list(zip(refs[:count], refs[count + 1 : 2 * count + 1])), refs[-1])


def half_lanes():
    return lax.broadcasted_iota(jnp.int32, (1, 2 * HD), 1) < HD


def mask_columns(rows, cols):
    place = lax.broadcasted_iota(jnp.int32, (1, 2 * HD), 1) % HD
    return place, place < rows, (place >= rows) & (place < rows + cols)


def query_columns(rows, cols):
    place, is_row, is_col = mask_columns(rows, cols)
    spot = lax.broadcasted_iota(jnp.int32, (rows * cols, 1), 0)
    hot = (is_row & (spot // cols == place)) | (is_col & (spot % cols == place - rows))
    return jnp.where(hot, 1.0, 0.0).astype(BF)


def key_columns(rows, cols, krow, kcol):
    place, is_row, is_col = mask_columns(rows, cols)
    far_row = jnp.abs(krow - place) > RADIUS
    far_col = jnp.abs(kcol - (place - rows)) > RADIUS
    return jnp.where((is_row & far_row) | (is_col & far_col), -BIG, 0.0).astype(BF)


def attend(head, query, key, value, query_mask, key_mask, factor):
    lanes = 2 * HD
    low = half_lanes()
    mine = low if head % 2 == 0 else ~low
    span = slice(head // 2 * lanes, (head // 2 + 1) * lanes)
    q = jnp.where(mine, query[:, span], query_mask)
    k = jnp.where(mine, key[:, span], key_mask)
    v = jnp.where(mine, value[:, span], jnp.ones((1, lanes), BF))
    weights = jnp.exp2(dot_nt(q, k) * (factor * (LOG2E / HD))).astype(BF)
    return dot(weights, v)


def own_kernel(rows, cols, heads, tok_ref, gain_ref, qkv_ref, scale_ref, query_ref, acc_ref):
    width = heads * HD
    ones = same_head(width, width)
    query_mask = query_columns(rows, cols)
    spot = lax.broadcasted_iota(jnp.int32, (rows * cols, 1), 0)
    key_mask = key_columns(rows, cols, spot // cols, spot % cols)
    normed = rms_norm(tok_ref[...].astype(F32), gain_ref[...]).astype(BF)
    query = head_norm(dot(normed, qkv_ref[:, :width]), ones).astype(BF)
    key = head_norm(dot(normed, qkv_ref[:, width : 2 * width]), ones).astype(BF)
    value = dot(normed, qkv_ref[:, 2 * width :]).astype(BF)
    query_ref[...] = query
    for head in range(heads):
        factor = scale_ref[0:1, head : head + 1]
        acc_ref[head] = attend(head, query, key, value, query_mask, key_mask, factor)


def fine_kernel(
    rows, cols, heads, axes,
    tok_ref, halo_refs, query_ref, acc_ref, gain_attn_ref, qkv_ref, scale_ref,
    out_ref, gain_ffn_ref, ffn_in_ref, ffn_out_ref,
    fine_ref, pooled_ref,
):
    strip = RADIUS * cols
    side = halo_refs[-1].shape[0]
    width = heads * HD
    total = 2 * strip + 2 * side
    row_axis, col_axis = axes
    row0 = lax.axis_index(row_axis) * rows
    col0 = lax.axis_index(col_axis) * cols
    grid_rows = lax.axis_size(row_axis) * rows
    grid_cols = lax.axis_size(col_axis) * cols

    halo = jnp.concatenate([ref[...] for ref in halo_refs], 0)
    normed = rms_norm(halo.astype(F32), gain_attn_ref[...]).astype(BF)
    ones = same_head(width, width)
    key = head_norm(dot(normed, qkv_ref[:, width : 2 * width]), ones).astype(BF)
    value = dot(normed, qkv_ref[:, 2 * width :]).astype(BF)

    odd, odd_col = lax.axis_index(row_axis) % 2, lax.axis_index(col_axis) % 2
    row_at = (odd * (rows + RADIUS) - RADIUS, (1 - odd) * (rows + RADIUS) - RADIUS)
    col_at = (odd_col * (cols + RADIUS) - RADIUS, (1 - odd_col) * (cols + RADIUS) - RADIUS)
    spot = lax.broadcasted_iota(jnp.int32, (total, 1), 0)
    past_first = spot - strip
    past_strips = past_first - strip
    past_third = past_strips - side
    strip_at = jnp.where(past_first >= 0, past_first, spot)
    side_at = jnp.where(past_third >= 0, past_third, past_strips)
    side_row = (side_at * 21846) >> 16
    in_strip = past_strips < 0
    krow = jnp.where(
        in_strip,
        strip_at // cols + jnp.where(past_first >= 0, row_at[1], row_at[0]),
        side_row - RADIUS,
    )
    kcol = jnp.where(
        in_strip,
        strip_at % cols,
        side_at - 3 * side_row + jnp.where(past_third >= 0, col_at[1], col_at[0]),
    )
    real = in_strip | (side_at < (rows + 2 * RADIUS) * RADIUS)
    real = real & (krow + row0 >= 0) & (krow + row0 < grid_rows)
    real = real & (kcol + col0 >= 0) & (kcol + col0 < grid_cols)
    key_mask = key_columns(rows, cols, jnp.where(real, krow, -1000), kcol)
    query_mask = query_columns(rows, cols)

    query = query_ref[...]
    low = half_lanes()
    parts = []
    for pair in range(heads // 2):
        sums = []
        for head in (2 * pair, 2 * pair + 1):
            factor = scale_ref[0:1, head : head + 1]
            sums.append(acc_ref[head] + attend(head, query, key, value, query_mask, key_mask, factor))
        top = jnp.where(low, sums[0], sums[1])
        bottom = pltpu.roll(jnp.where(low, sums[1], sums[0]), HD, 1)
        parts.append((top / bottom).astype(BF))
    attn = jnp.concatenate(parts, 1)

    h1 = (tok_ref[...].astype(F32) + dot(attn, out_ref[...])).astype(BF)
    h1_wide = h1.astype(F32)
    n2 = rms_norm(h1_wide, gain_ffn_ref[...]).astype(BF)
    hidden = ffn_out_ref.shape[0]
    gate = dot(n2, ffn_in_ref[:, :hidden])
    up = dot(n2, ffn_in_ref[:, hidden:])
    gated = (jax.nn.gelu(gate, approximate=True) * up).astype(BF)
    fine = (h1_wide + dot(gated, ffn_out_ref[...])).astype(BF)
    fine_ref[...] = fine
    pooled = jnp.mean(fine.astype(F32), 0, keepdims=True).astype(BF).astype(F32)
    for part in range(pooled_ref.shape[1]):
        pooled_ref[:, part, :] = jnp.broadcast_to(
            pooled[:, part * 128 : (part + 1) * 128], (pooled_ref.shape[0], 128)
        )


def coarse_kernel(
    heads, axes,
    pooled_ref, up_ref, gain_ref, qkv_ref, scale_ref, out_ref,
    coarse_out_ref,
    query_ref, coarse_ref,
):
    width = heads * HD
    row_axis, col_axis = axes
    mine = lax.axis_index(row_axis) * lax.axis_size(col_axis) + lax.axis_index(col_axis)
    pooled = jnp.concatenate([pooled_ref[:, part, :] for part in range(pooled_ref.shape[1])], 1)
    coarse = dot(pooled.astype(BF), up_ref[...]).astype(BF).astype(F32)
    coarse_ref[...] = coarse
    normed = rms_norm(coarse, gain_ref[...]).astype(BF)
    group = 4 * HD
    ones = same_head(group, group)
    keys = []
    for at in range(0, width, group):
        span = slice(at, at + group)
        query_ref[:, span] = head_norm(dot(normed, qkv_ref[:, span]), ones).astype(BF).astype(F32)
        keys.append(head_norm(dot(normed, qkv_ref[:, width + at : width + at + group]), ones))
    key = jnp.concatenate(keys, 1).astype(BF).astype(F32)
    value = dot(normed, qkv_ref[:, 2 * width :]).astype(BF).astype(F32)
    query = query_ref[pl.ds(mine, 1), :]
    lanes = scale_ref.shape[1]
    shape = (width, lanes)
    fold = lax.broadcasted_iota(jnp.int32, shape, 0) // HD == lax.broadcasted_iota(jnp.int32, shape, 1)
    fold = fold.astype(F32).astype(BF)
    scores = dot_split(key * query, fold) * (scale_ref[...] * (1.0 / HD))
    expo = jnp.exp(scores - jnp.max(scores, 0, keepdims=True))
    weights = (expo / jnp.sum(expo, 0, keepdims=True)).astype(BF)
    spread = dot_nt(weights, fold)
    cattn = jnp.sum(spread * value, 0, keepdims=True).astype(BF)
    coarse_out_ref[...] = (coarse_ref[pl.ds(mine, 1), :] + dot(cattn, out_ref[...])).astype(BF)


def vmem(count):
    return [pl.BlockSpec(memory_space=pltpu.VMEM)] * count


def anywhere(count):
    return [pl.BlockSpec(memory_space=pl.ANY)] * count


def in_vmem(arrays):
    return [pltpu.with_memory_space_constraint(array, pltpu.VMEM) for array in arrays]


def in_hbm(arrays):
    return [pltpu.with_memory_space_constraint(array, pltpu.HBM) for array in arrays]


def shards(
    tokens, gain_attn, qkv_fine, scale_fine, out_fine, gain_ffn, ffn_in, ffn_out,
    up_proj, gain_coarse, qkv_coarse, scale_coarse, out_coarse,
):
    rows, cols, width = tokens.shape
    count = rows * cols
    strip = RADIUS * cols
    side = rounded_up((rows + 2 * RADIUS) * RADIUS, 16)
    heads = width // HD
    width_c = out_coarse.shape[0]
    heads_c = width_c // HD
    devices = lax.axis_size("ha") * lax.axis_size("wa")
    axes = ("ha", "wa")
    params = pltpu.CompilerParams(vmem_limit_bytes=16 * MIB)

    def swapped(array, axis, first):
        pairs = [(i, i + 1) for i in range(first, lax.axis_size(axis) - 1, 2)]
        return lax.ppermute(array, axis, pairs + [(j, i) for i, j in pairs])

    flat = tokens.reshape(count, width)
    early = [flat, gain_attn.reshape(1, -1), qkv_fine, scale_fine.reshape(1, -1)]
    *early_v, across, within = pl.pallas_call(
        functools.partial(strip_kernel, rows, cols, "ha"),
        out_shape=[pltpu.VMEM(array.shape, array.dtype) for array in early]
        + [pltpu.VMEM((strip, width), BF)] * 2,
        in_specs=anywhere(len(early)),
        out_specs=vmem(len(early) + 2),
        scratch_shapes=[pltpu.SemaphoreType.DMA((len(early) + 2,))],
        compiler_params=params,
        name="strips",
    )(*in_hbm(early))
    tok_v, gain_attn_v, qkv_v, scale_v = early_v
    across = swapped(across, "ha", 1)
    within = swapped(within, "ha", 0)

    query, acc = pl.pallas_call(
        functools.partial(own_kernel, rows, cols, heads),
        out_shape=[pltpu.VMEM((count, width), BF), pltpu.VMEM((heads, count, 2 * HD), F32)],
        in_specs=vmem(4),
        out_specs=vmem(2),
        compiler_params=params,
        cost_estimate=pl.CostEstimate(
            flops=2 * count * width * (3 * width + 2 * count), bytes_accessed=2 * MIB, transcendentals=0
        ),
        name="own",
    )(*in_vmem(early_v))

    across_edge, within_edge = pl.pallas_call(
        functools.partial(edge_kernel, rows, cols, axes),
        out_shape=[pltpu.VMEM((side, width), BF)] * 2,
        in_specs=vmem(4),
        out_specs=vmem(2),
        compiler_params=params,
        name="edges",
    )(*in_vmem([tok_v, across, within, query]))
    across_side = swapped(across_edge, "wa", 1)
    within_side = swapped(within_edge, "wa", 0)

    late = [
        out_fine, gain_ffn.reshape(1, -1), ffn_in, ffn_out,
        gain_coarse.reshape(1, -1), scale_coarse.reshape(1, -1), up_proj, qkv_coarse, out_coarse,
    ]
    late_v = pl.pallas_call(
        load_kernel,
        out_shape=[pltpu.VMEM(array.shape, array.dtype) for array in late],
        in_specs=anywhere(len(late)) + vmem(1),
        out_specs=vmem(len(late)),
        scratch_shapes=[pltpu.SemaphoreType.DMA((len(late),))],
        compiler_params=params,
        cost_estimate=pl.CostEstimate(flops=0, bytes_accessed=12 * MIB, transcendentals=0),
        name="load",
    )(*in_hbm(late), *in_vmem([within_edge]))
    out_v, gain_ffn_v, ffn_in_v, ffn_out_v, gain_c_v, scale_c_v, up_v, qkv_c_v, out_c_v = late_v

    def fine_body(tok_ref, *refs):
        fine_kernel(rows, cols, heads, axes, tok_ref, refs[:4], *refs[4:])

    fine, pooled = pl.pallas_call(
        fine_body,
        out_shape=[
            jax.ShapeDtypeStruct((count, width), BF),
            pltpu.VMEM((devices, width // 128, 128), F32),
        ],
        in_specs=vmem(14),
        out_specs=vmem(2),
        compiler_params=params,
        name="fine",
    )(
        *in_vmem(
            [tok_v, across, within, across_side, within_side, query, acc, gain_attn_v, qkv_v, scale_v]
            + [out_v, gain_ffn_v, ffn_in_v, ffn_out_v]
        )
    )

    every = lax.all_to_all(pooled, axes, split_axis=0, concat_axis=0, tiled=True)
    coarse_out = pl.pallas_call(
        functools.partial(coarse_kernel, heads_c, axes),
        out_shape=jax.ShapeDtypeStruct((1, width_c), BF),
        in_specs=vmem(6),
        out_specs=vmem(1)[0],
        scratch_shapes=[pltpu.VMEM((devices, width_c), F32)] * 2,
        compiler_params=params,
        name="coarse",
    )(*in_vmem([every, up_v, gain_c_v, qkv_c_v, scale_c_v, out_c_v]))
    return fine.reshape(rows, cols, width), coarse_out.reshape(1, 1, width_c)


def solution(mesh):
    return jax.shard_map(
        shards,
        mesh=mesh,
        in_specs=(P("ha", "wa", None), P(), P(), P(), P(), P(), P(), P(), P(), P(), P(), P(), P()),
        out_specs=(P("ha", "wa", None), P("ha", "wa", None)),
        check_vma=False,
    )
```

```python
import functools

import jax
import jax.numpy as jnp
from jax import lax
from jax.experimental import pallas as pl
from jax.experimental.pallas import tpu as pltpu
from jax.sharding import PartitionSpec as P

HD = 64
RADIUS = 3
LOG2E = 1.4426950408889634
BIG = 2.0**30
BF = jnp.bfloat16
F32 = jnp.float32
MIB = 1 << 20


def rounded_up(value, step):
    return -(-value // step) * step


def dot(a, b):
    return jnp.dot(a, b, preferred_element_type=F32)


def dot_nt(a, b):
    return lax.dot_general(a, b, (((1,), (1,)), ((), ())), preferred_element_type=F32)


def dot_split(values, ones):
    high = values.astype(BF)
    low = (values - high.astype(F32)).astype(BF)
    return dot(high, ones) + dot(low, ones)


def same_head(rows, cols):
    shape = (rows, cols)
    left = lax.broadcasted_iota(jnp.int32, shape, 0) // HD
    right = lax.broadcasted_iota(jnp.int32, shape, 1) // HD
    return (left == right).astype(F32).astype(BF)


def head_norm(values, ones):
    return values * lax.rsqrt(dot_split(values * values, ones) * (1.0 / HD) + 1e-06)


def rms_norm(values, gain):
    mean = jnp.mean(values * values, -1, keepdims=True)
    return values * lax.rsqrt(mean + 1e-06) * gain


def copy_all(pairs, sems):
    copies = [pltpu.make_async_copy(src, dst, sems.at[i]) for i, (src, dst) in enumerate(pairs)]
    for copy in copies:
        copy.start()
    for copy in copies:
        copy.wait()


def strip_kernel(rows, cols, axis, *refs):
    count, strip = rows * cols, RADIUS * cols
    moved, sems = (len(refs) - 3) // 2, refs[-1]
    ins, outs = refs[:moved], refs[moved : 2 * moved]
    across_ref, within_ref = refs[2 * moved : 2 * moved + 2]
    odd = lax.axis_index(axis) % 2
    last = count - strip
    first = pl.multiple_of(odd * last, 16)
    second = pl.multiple_of((1 - odd) * last, 16)
    pairs = [(ins[0].at[pl.ds(first, strip), :], across_ref), (ins[0].at[pl.ds(second, strip), :], within_ref)]
    copy_all(pairs + list(zip(ins, outs)), sems)


def edge_kernel(rows, cols, axes, tok_ref, across_ref, within_ref, after_ref, across_out, within_out):
    height = rows + 2 * RADIUS
    strip = RADIUS * cols
    padded = across_out.shape[0]
    odd, odd_col = lax.axis_index(axes[0]) % 2, lax.axis_index(axes[1]) % 2
    block = jnp.concatenate([tok_ref[...], across_ref[...], within_ref[...]], 0)
    out = lax.broadcasted_iota(jnp.int32, (padded, 1), 0)
    src = lax.broadcasted_iota(jnp.int32, (padded, block.shape[0]), 1)
    row = ((out * 21846) >> 16) - RADIUS
    col = out - 3 * (row + RADIUS)
    above = rows * cols + strip * odd + RADIUS * cols
    below = rows * cols + strip * (1 - odd) - rows * cols
    first = row * cols + col + jnp.where(row < 0, above, jnp.where(row >= rows, below, 0))
    first = jnp.where(out < height * RADIUS, first, -2 * cols)
    far = cols - RADIUS
    pick = jnp.where(src == first + far * odd_col, 1.0, 0.0).astype(BF)
    across_out[...] = dot(pick, block).astype(BF)
    pick = jnp.where(src == first + far * (1 - odd_col), 1.0, 0.0).astype(BF)
    within_out[...] = dot(pick, block).astype(BF)


def merge_kernel(after_ref, up_ref, gain_ref, scale_ref, qkv_hbm, merged_ref, scale_out, weight_ref, sems):
    blocks = sems.shape[0]
    size = merged_ref.shape[1] // blocks
    spans = [pl.ds(i * size, size) for i in range(blocks)]
    copies = [
        pltpu.make_async_copy(qkv_hbm.at[:, span], weight_ref.at[:, span], sems.at[i])
        for i, span in enumerate(spans)
    ]
    for copy in copies:
        copy.start()
    lane = lax.broadcasted_iota(jnp.int32, scale_out.shape, 1) // HD
    scale = jnp.zeros(scale_out.shape, F32)
    for head in range(scale_ref.shape[1]):
        scale = jnp.where(lane == head, scale_ref[0:1, head : head + 1], scale)
    scale_out[...] = scale * (1.0 / HD)
    scaled = (up_ref[...].astype(F32) * gain_ref[...]).astype(BF)
    for copy, span in zip(copies, spans):
        copy.wait()
        merged_ref[:, span] = dot(scaled, weight_ref[:, span]).astype(BF)


def half_lanes():
    return lax.broadcasted_iota(jnp.int32, (1, 2 * HD), 1) < HD


def mask_columns(rows, cols):
    place = lax.broadcasted_iota(jnp.int32, (1, 2 * HD), 1) % HD
    return place, place < rows, (place >= rows) & (place < rows + cols)


def query_columns(rows, cols):
    place, is_row, is_col = mask_columns(rows, cols)
    spot = lax.broadcasted_iota(jnp.int32, (rows * cols, 1), 0)
    hot = (is_row & (spot // cols == place)) | (is_col & (spot % cols == place - rows))
    return jnp.where(hot, 1.0, 0.0).astype(BF)


def key_columns(rows, cols, krow, kcol):
    place, is_row, is_col = mask_columns(rows, cols)
    far_row = jnp.abs(krow - place) > RADIUS
    far_col = jnp.abs(kcol - (place - rows)) > RADIUS
    return jnp.where((is_row & far_row) | (is_col & far_col), -BIG, 0.0).astype(BF)


def attend(head, query, key, value, query_mask, key_mask, factor):
    lanes = 2 * HD
    low = half_lanes()
    mine = low if head % 2 == 0 else ~low
    span = slice(head // 2 * lanes, (head // 2 + 1) * lanes)
    q = jnp.where(mine, query[:, span], query_mask)
    k = jnp.where(mine, key[:, span], key_mask)
    v = jnp.where(mine, value[:, span], jnp.ones((1, lanes), BF))
    weights = jnp.exp2(dot_nt(q, k) * (factor * (LOG2E / HD))).astype(BF)
    return dot(weights, v)


def own_kernel(rows, cols, heads, tok_ref, *refs):
    count = (len(refs) - 3) // 2
    outs, (query_ref, acc_ref, sems) = refs[count : 2 * count], refs[2 * count :]
    qkv_ref, gain_ref, scale_ref = outs[:3]
    copies = [
        pltpu.make_async_copy(src, dst, sems.at[i]) for i, (src, dst) in enumerate(zip(refs[:count], outs))
    ]
    for copy in copies:
        copy.start()
    width = heads * HD
    ones = same_head(width, width)
    query_mask = query_columns(rows, cols)
    spot = lax.broadcasted_iota(jnp.int32, (rows * cols, 1), 0)
    key_mask = key_columns(rows, cols, spot // cols, spot % cols)
    for copy in copies[:3]:
        copy.wait()
    normed = rms_norm(tok_ref[...].astype(F32), gain_ref[...]).astype(BF)
    query = head_norm(dot(normed, qkv_ref[:, :width]), ones).astype(BF)
    key = head_norm(dot(normed, qkv_ref[:, width : 2 * width]), ones).astype(BF)
    value = dot(normed, qkv_ref[:, 2 * width :]).astype(BF)
    query_ref[...] = query
    for head in range(heads):
        factor = scale_ref[0:1, head : head + 1]
        acc_ref[head] = attend(head, query, key, value, query_mask, key_mask, factor)
    for copy in copies[3:]:
        copy.wait()


def fine_kernel(
    rows, cols, heads, axes,
    tok_ref, halo_refs, query_ref, acc_ref, gain_attn_ref, qkv_ref, scale_ref,
    out_ref, gain_ffn_ref, ffn_in_ref, ffn_out_ref,
    fine_ref, pooled_ref,
):
    strip = RADIUS * cols
    side = halo_refs[-1].shape[0]
    width = heads * HD
    total = 2 * strip + 2 * side
    row_axis, col_axis = axes
    row0 = lax.axis_index(row_axis) * rows
    col0 = lax.axis_index(col_axis) * cols
    grid_rows = lax.axis_size(row_axis) * rows
    grid_cols = lax.axis_size(col_axis) * cols

    halo = jnp.concatenate([ref[...] for ref in halo_refs], 0)
    normed = rms_norm(halo.astype(F32), gain_attn_ref[...]).astype(BF)
    ones = same_head(width, width)
    key = head_norm(dot(normed, qkv_ref[:, width : 2 * width]), ones).astype(BF)
    value = dot(normed, qkv_ref[:, 2 * width :]).astype(BF)

    odd, odd_col = lax.axis_index(row_axis) % 2, lax.axis_index(col_axis) % 2
    row_at = (odd * (rows + RADIUS) - RADIUS, (1 - odd) * (rows + RADIUS) - RADIUS)
    col_at = (odd_col * (cols + RADIUS) - RADIUS, (1 - odd_col) * (cols + RADIUS) - RADIUS)
    spot = lax.broadcasted_iota(jnp.int32, (total, 1), 0)
    past_first = spot - strip
    past_strips = past_first - strip
    past_third = past_strips - side
    strip_at = jnp.where(past_first >= 0, past_first, spot)
    side_at = jnp.where(past_third >= 0, past_third, past_strips)
    side_row = (side_at * 21846) >> 16
    in_strip = past_strips < 0
    krow = jnp.where(
        in_strip,
        strip_at // cols + jnp.where(past_first >= 0, row_at[1], row_at[0]),
        side_row - RADIUS,
    )
    kcol = jnp.where(
        in_strip,
        strip_at % cols,
        side_at - 3 * side_row + jnp.where(past_third >= 0, col_at[1], col_at[0]),
    )
    real = in_strip | (side_at < (rows + 2 * RADIUS) * RADIUS)
    real = real & (krow + row0 >= 0) & (krow + row0 < grid_rows)
    real = real & (kcol + col0 >= 0) & (kcol + col0 < grid_cols)
    key_mask = key_columns(rows, cols, jnp.where(real, krow, -1000), kcol)
    query_mask = query_columns(rows, cols)

    query = query_ref[...]
    low = half_lanes()
    parts = []
    for pair in range(heads // 2):
        sums = []
        for head in (2 * pair, 2 * pair + 1):
            factor = scale_ref[0:1, head : head + 1]
            sums.append(acc_ref[head] + attend(head, query, key, value, query_mask, key_mask, factor))
        top = jnp.where(low, sums[0], sums[1])
        bottom = pltpu.roll(jnp.where(low, sums[1], sums[0]), HD, 1)
        parts.append((top / bottom).astype(BF))
    attn = jnp.concatenate(parts, 1)

    h1 = (tok_ref[...].astype(F32) + dot(attn, out_ref[...])).astype(BF)
    h1_wide = h1.astype(F32)
    n2 = rms_norm(h1_wide, gain_ffn_ref[...]).astype(BF)
    hidden = ffn_out_ref.shape[0]
    gate = dot(n2, ffn_in_ref[:, :hidden])
    up = dot(n2, ffn_in_ref[:, hidden:])
    gated = (jax.nn.gelu(gate, approximate=True) * up).astype(BF)
    fine = (h1_wide + dot(gated, ffn_out_ref[...])).astype(BF)
    fine_ref[...] = fine
    pooled = jnp.mean(fine.astype(F32), 0, keepdims=True).astype(BF).astype(F32)
    for part in range(pooled_ref.shape[1]):
        pooled_ref[:, part, :] = jnp.broadcast_to(
            pooled[:, part * 128 : (part + 1) * 128], (pooled_ref.shape[0], 128)
        )


def coarse_kernel(
    axes, pooled_ref, up_ref, merged_ref, scale_ref, out_ref, coarse_out_ref, query_ref, coarse_ref
):
    width = out_ref.shape[0]
    row_axis, col_axis = axes
    mine = lax.axis_index(row_axis) * lax.axis_size(col_axis) + lax.axis_index(col_axis)
    pooled = jnp.concatenate([pooled_ref[:, part, :] for part in range(pooled_ref.shape[1])], 1).astype(BF)
    coarse = dot(pooled, up_ref[...]).astype(BF).astype(F32)
    coarse_ref[...] = coarse
    rms = lax.rsqrt(jnp.mean(coarse * coarse, -1, keepdims=True) + 1e-06)
    query_ref[...] = dot(pooled, merged_ref[:, :width]) * rms
    key = dot(pooled, merged_ref[:, width : 2 * width]) * rms
    value = dot(pooled, merged_ref[:, 2 * width :]) * rms
    query = query_ref[pl.ds(mine, 1), :]
    group = 4 * HD
    spans = [slice(at, at + group) for at in range(0, width, group)]
    tall = jnp.concatenate([key[:, span] for span in spans], 0)
    queries = [query[:, span] for span in spans]
    cross = jnp.concatenate([key[:, span] * q for span, q in zip(spans, queries)], 0)
    ones = same_head(group, group)
    query_norm = lax.rsqrt(dot_split(jnp.concatenate([q * q for q in queries], 0), ones) * (1.0 / HD) + 1e-06)
    key_norm = lax.rsqrt(dot_split(tall * tall, ones) * (1.0 / HD) + 1e-06)
    scores = dot_split(cross, ones) * key_norm
    count = key.shape[0]
    parts = []
    for at, span in enumerate(spans):
        factor = query_norm[at : at + 1] * scale_ref[:, span]
        expo = jnp.exp(scores[at * count : (at + 1) * count] * factor)
        total = jnp.sum(expo, 0, keepdims=True)
        parts.append(jnp.sum(expo * value[:, span], 0, keepdims=True) / total)
    cattn = jnp.concatenate(parts, 1).astype(BF)
    coarse_out_ref[...] = (coarse_ref[pl.ds(mine, 1), :] + dot(cattn, out_ref[...])).astype(BF)


def vmem(count):
    return [pl.BlockSpec(memory_space=pltpu.VMEM)] * count


def anywhere(count):
    return [pl.BlockSpec(memory_space=pl.ANY)] * count


def in_vmem(arrays):
    return [pltpu.with_memory_space_constraint(array, pltpu.VMEM) for array in arrays]


def in_hbm(arrays):
    return [pltpu.with_memory_space_constraint(array, pltpu.HBM) for array in arrays]


def shards(
    tokens, gain_attn, qkv_fine, scale_fine, out_fine, gain_ffn, ffn_in, ffn_out,
    up_proj, gain_coarse, qkv_coarse, scale_coarse, out_coarse,
):
    rows, cols, width = tokens.shape
    count = rows * cols
    strip = RADIUS * cols
    side = rounded_up((rows + 2 * RADIUS) * RADIUS, 16)
    heads = width // HD
    width_c = out_coarse.shape[0]
    devices = lax.axis_size("ha") * lax.axis_size("wa")
    axes = ("ha", "wa")
    params = pltpu.CompilerParams(vmem_limit_bytes=16 * MIB)

    def swapped(array, axis, first):
        pairs = [(i, i + 1) for i in range(first, lax.axis_size(axis) - 1, 2)]
        return lax.ppermute(array, axis, pairs + [(j, i) for i, j in pairs])

    flat = tokens.reshape(count, width)
    tok_v, across, within = pl.pallas_call(
        functools.partial(strip_kernel, rows, cols, "ha"),
        out_shape=[pltpu.VMEM((count, width), BF)] + [pltpu.VMEM((strip, width), BF)] * 2,
        in_specs=anywhere(1),
        out_specs=vmem(3),
        scratch_shapes=[pltpu.SemaphoreType.DMA((3,))],
        compiler_params=params,
        name="strips",
    )(*in_hbm([flat]))
    across = swapped(across, "ha", 1)
    within = swapped(within, "ha", 0)

    weights = [
        qkv_fine, gain_attn.reshape(1, -1), scale_fine.reshape(1, -1),
        out_fine, gain_ffn.reshape(1, -1), ffn_in, ffn_out,
        up_proj, gain_coarse.reshape(1, -1), scale_coarse.reshape(1, -1), out_coarse,
    ]
    *weights, query, acc = pl.pallas_call(
        functools.partial(own_kernel, rows, cols, heads),
        out_shape=[pltpu.VMEM(array.shape, array.dtype) for array in weights]
        + [pltpu.VMEM((count, width), BF), pltpu.VMEM((heads, count, 2 * HD), F32)],
        in_specs=vmem(1) + anywhere(len(weights)),
        out_specs=vmem(len(weights) + 2),
        scratch_shapes=[pltpu.SemaphoreType.DMA((len(weights),))],
        compiler_params=params,
        cost_estimate=pl.CostEstimate(
            flops=2 * count * width * (3 * width + 2 * count), bytes_accessed=8 * MIB, transcendentals=0
        ),
        name="own",
    )(*in_vmem([tok_v]), *in_hbm(weights))
    qkv_v, gain_attn_v, scale_v, out_v, gain_ffn_v, ffn_in_v, ffn_out_v = weights[:7]
    up_v, gain_c_v, scale_c_v, out_c_v = weights[7:]

    across_edge, within_edge = pl.pallas_call(
        functools.partial(edge_kernel, rows, cols, axes),
        out_shape=[pltpu.VMEM((side, width), BF)] * 2,
        in_specs=vmem(4),
        out_specs=vmem(2),
        compiler_params=params,
        name="edges",
    )(*in_vmem([tok_v, across, within, query]))
    across_side = swapped(across_edge, "wa", 1)
    within_side = swapped(within_edge, "wa", 0)

    merged, scale_lanes = pl.pallas_call(
        merge_kernel,
        out_shape=[pltpu.VMEM((width, 3 * width_c), BF), pltpu.VMEM((1, width_c), F32)],
        in_specs=vmem(4) + anywhere(1),
        out_specs=vmem(2),
        scratch_shapes=[pltpu.VMEM(qkv_coarse.shape, BF), pltpu.SemaphoreType.DMA((6,))],
        compiler_params=params,
        cost_estimate=pl.CostEstimate(
            flops=6 * width * width_c * width_c, bytes_accessed=8 * MIB, transcendentals=0
        ),
        name="merge",
    )(*in_vmem([within_edge, up_v, gain_c_v, scale_c_v]), *in_hbm([qkv_coarse]))

    def fine_body(tok_ref, *refs):
        fine_kernel(rows, cols, heads, axes, tok_ref, refs[:4], *refs[4:])

    fine, pooled = pl.pallas_call(
        fine_body,
        out_shape=[
            jax.ShapeDtypeStruct((count, width), BF),
            pltpu.VMEM((devices, width // 128, 128), F32),
        ],
        in_specs=vmem(14),
        out_specs=vmem(2),
        compiler_params=params,
        name="fine",
    )(
        *in_vmem(
            [tok_v, across, within, across_side, within_side, query, acc, gain_attn_v, qkv_v, scale_v]
            + [out_v, gain_ffn_v, ffn_in_v, ffn_out_v]
        )
    )

    every = lax.all_to_all(pooled, axes, split_axis=0, concat_axis=0, tiled=True)
    coarse_out = pl.pallas_call(
        functools.partial(coarse_kernel, axes),
        out_shape=jax.ShapeDtypeStruct((1, width_c), BF),
        in_specs=vmem(5),
        out_specs=vmem(1)[0],
        scratch_shapes=[pltpu.VMEM((devices, width_c), F32)] * 2,
        compiler_params=params,
        name="coarse",
    )(*in_vmem([every, up_v, merged, scale_lanes, out_c_v]))
    return fine.reshape(rows, cols, width), coarse_out.reshape(1, 1, width_c)


def solution(mesh):
    return jax.shard_map(
        shards,
        mesh=mesh,
        in_specs=(P("ha", "wa", None), P(), P(), P(), P(), P(), P(), P(), P(), P(), P(), P(), P()),
        out_specs=(P("ha", "wa", None), P("ha", "wa", None)),
        check_vma=False,
    )
```

```python
import functools

import jax
import jax.numpy as jnp
from jax import lax
from jax.experimental import pallas as pl
from jax.experimental.pallas import tpu as pltpu
from jax.sharding import PartitionSpec as P

HD = 64
RADIUS = 3
LOG2E = 1.4426950408889634
BIG = 2.0**30
BF = jnp.bfloat16
F32 = jnp.float32
MIB = 1 << 20


def rounded_up(value, step):
    return -(-value // step) * step


def dot(a, b):
    return jnp.dot(a, b, preferred_element_type=F32)


def dot_nt(a, b):
    return lax.dot_general(a, b, (((1,), (1,)), ((), ())), preferred_element_type=F32)


def dot_split(values, ones):
    high = values.astype(BF)
    low = (values - high.astype(F32)).astype(BF)
    return dot(high, ones) + dot(low, ones)


def same_head(rows, cols):
    shape = (rows, cols)
    left = lax.broadcasted_iota(jnp.int32, shape, 0) // HD
    right = lax.broadcasted_iota(jnp.int32, shape, 1) // HD
    return (left == right).astype(F32).astype(BF)


def head_norm(values, ones):
    return values * lax.rsqrt(dot_split(values * values, ones) * (1.0 / HD) + 1e-06)


def rms_norm(values, gain):
    mean = jnp.mean(values * values, -1, keepdims=True)
    return values * lax.rsqrt(mean + 1e-06) * gain


def copies_of(pairs, sems):
    return [pltpu.make_async_copy(src, dst, sems.at[i]) for i, (src, dst) in enumerate(pairs)]


def start_all(copies):
    for copy in copies:
        copy.start()


def wait_all(copies):
    for copy in copies:
        copy.wait()


def strip_kernel(rows, cols, axis, tok_hbm, across_ref, within_ref, sems):
    count, strip = rows * cols, RADIUS * cols
    odd = lax.axis_index(axis) % 2
    last = count - strip
    first = pl.multiple_of(odd * last, 16)
    second = pl.multiple_of((1 - odd) * last, 16)
    copies = copies_of(
        [
            (tok_hbm.at[pl.ds(first, strip), :], across_ref),
            (tok_hbm.at[pl.ds(second, strip), :], within_ref),
        ],
        sems,
    )
    start_all(copies)
    wait_all(copies)


def edge_kernel(rows, cols, axes, tok_ref, across_ref, within_ref, after_ref, across_out, within_out):
    height = rows + 2 * RADIUS
    strip = RADIUS * cols
    padded = across_out.shape[0]
    odd, odd_col = lax.axis_index(axes[0]) % 2, lax.axis_index(axes[1]) % 2
    block = jnp.concatenate([tok_ref[...], across_ref[...], within_ref[...]], 0)
    out = lax.broadcasted_iota(jnp.int32, (padded, 1), 0)
    src = lax.broadcasted_iota(jnp.int32, (padded, block.shape[0]), 1)
    row = ((out * 21846) >> 16) - RADIUS
    col = out - 3 * (row + RADIUS)
    above = rows * cols + strip * odd + RADIUS * cols
    below = rows * cols + strip * (1 - odd) - rows * cols
    first = row * cols + col + jnp.where(row < 0, above, jnp.where(row >= rows, below, 0))
    first = jnp.where(out < height * RADIUS, first, -2 * cols)
    far = cols - RADIUS
    pick = jnp.where(src == first + far * odd_col, 1.0, 0.0).astype(BF)
    across_out[...] = dot(pick, block).astype(BF)
    pick = jnp.where(src == first + far * (1 - odd_col), 1.0, 0.0).astype(BF)
    within_out[...] = dot(pick, block).astype(BF)


def column_copies(src, dst, start, blocks, sems):
    size = dst.shape[1] // blocks
    spans = [pl.ds(i * size, size) for i in range(blocks)]
    pairs = [(src.at[:, pl.ds(start + i * size, size)], dst.at[:, span]) for i, span in enumerate(spans)]
    return copies_of(pairs, sems), spans


def merge_columns(copies, spans, scaled, weight_ref, merged_ref):
    for copy, span in zip(copies, spans):
        copy.wait()
        merged_ref[:, span] = dot(scaled, weight_ref[:, span]).astype(BF)


def merge_kernel(after_ref, scaled_ref, qkv_hbm, merged_ref, weight_ref, sems):
    copies, spans = column_copies(qkv_hbm, weight_ref, weight_ref.shape[0], sems.shape[0], sems)
    start_all(copies)
    merge_columns(copies, spans, scaled_ref[...], weight_ref, merged_ref)


def half_lanes():
    return lax.broadcasted_iota(jnp.int32, (1, 2 * HD), 1) < HD


def mask_columns(rows, cols):
    place = lax.broadcasted_iota(jnp.int32, (1, 2 * HD), 1) % HD
    return place, place < rows, (place >= rows) & (place < rows + cols)


def query_columns(rows, cols):
    place, is_row, is_col = mask_columns(rows, cols)
    spot = lax.broadcasted_iota(jnp.int32, (rows * cols, 1), 0)
    hot = (is_row & (spot // cols == place)) | (is_col & (spot % cols == place - rows))
    return jnp.where(hot, 1.0, 0.0).astype(BF)


def key_columns(rows, cols, krow, kcol):
    place, is_row, is_col = mask_columns(rows, cols)
    far_row = jnp.abs(krow - place) > RADIUS
    far_col = jnp.abs(kcol - (place - rows)) > RADIUS
    return jnp.where((is_row & far_row) | (is_col & far_col), -BIG, 0.0).astype(BF)


def attend(head, query, key, value, query_mask, key_mask, factor):
    lanes = 2 * HD
    low = half_lanes()
    mine = low if head % 2 == 0 else ~low
    span = slice(head // 2 * lanes, (head // 2 + 1) * lanes)
    q = jnp.where(mine, query[:, span], query_mask)
    k = jnp.where(mine, key[:, span], key_mask)
    v = jnp.where(mine, value[:, span], jnp.ones((1, lanes), BF))
    weights = jnp.exp2(dot_nt(q, k) * (factor * (LOG2E / HD))).astype(BF)
    return dot(weights, v)


def own_kernel(rows, cols, heads, *refs):
    count = (len(refs) - 9) // 2
    ins, qkv_c_hbm, outs = refs[:count], refs[count], refs[count + 1 : 2 * count + 1]
    query_ref, acc_ref, scaled_ref, merged_ref, lanes_ref, weight_ref, sems, block_sems = refs[2 * count + 1 :]
    tok_ref, qkv_ref, gain_ref, scale_ref, up_ref, gain_c_ref, scale_c_ref = outs[:7]
    copies = copies_of(list(zip(ins, outs)), sems)
    blocks, spans = column_copies(qkv_c_hbm, weight_ref, 0, block_sems.shape[0], block_sems)
    start_all(copies[:7])
    start_all(blocks)
    start_all(copies[7:])
    width = heads * HD
    ones = same_head(width, width)
    query_mask = query_columns(rows, cols)
    spot = lax.broadcasted_iota(jnp.int32, (rows * cols, 1), 0)
    key_mask = key_columns(rows, cols, spot // cols, spot % cols)
    wait_all(copies[:4])
    normed = rms_norm(tok_ref[...].astype(F32), gain_ref[...]).astype(BF)
    query = head_norm(dot(normed, qkv_ref[:, :width]), ones).astype(BF)
    key = head_norm(dot(normed, qkv_ref[:, width : 2 * width]), ones).astype(BF)
    value = dot(normed, qkv_ref[:, 2 * width :]).astype(BF)
    query_ref[...] = query
    for head in range(heads):
        factor = scale_ref[0:1, head : head + 1]
        acc_ref[head] = attend(head, query, key, value, query_mask, key_mask, factor)
    wait_all(copies[4:7])
    lane = lax.broadcasted_iota(jnp.int32, lanes_ref.shape, 1) // HD
    lanes = jnp.zeros(lanes_ref.shape, F32)
    for head in range(scale_c_ref.shape[1]):
        lanes = jnp.where(lane == head, scale_c_ref[0:1, head : head + 1], lanes)
    lanes_ref[...] = lanes * (1.0 / HD)
    scaled = (up_ref[...].astype(F32) * gain_c_ref[...]).astype(BF)
    scaled_ref[...] = scaled
    merge_columns(blocks, spans, scaled, weight_ref, merged_ref)
    wait_all(copies[7:])


def fine_kernel(
    rows, cols, heads, axes,
    tok_ref, halo_refs, query_ref, acc_ref, gain_attn_ref, qkv_ref, scale_ref,
    out_ref, gain_ffn_ref, ffn_in_ref, ffn_out_ref, after_ref, out_c_hbm,
    fine_ref, pooled_ref, out_c_ref, sems,
):
    copies = copies_of([(out_c_hbm, out_c_ref)], sems)
    start_all(copies)
    strip = RADIUS * cols
    side = halo_refs[-1].shape[0]
    width = heads * HD
    total = 2 * strip + 2 * side
    row_axis, col_axis = axes
    row0 = lax.axis_index(row_axis) * rows
    col0 = lax.axis_index(col_axis) * cols
    grid_rows = lax.axis_size(row_axis) * rows
    grid_cols = lax.axis_size(col_axis) * cols

    halo = jnp.concatenate([ref[...] for ref in halo_refs], 0)
    normed = rms_norm(halo.astype(F32), gain_attn_ref[...]).astype(BF)
    ones = same_head(width, width)
    key = head_norm(dot(normed, qkv_ref[:, width : 2 * width]), ones).astype(BF)
    value = dot(normed, qkv_ref[:, 2 * width :]).astype(BF)

    odd, odd_col = lax.axis_index(row_axis) % 2, lax.axis_index(col_axis) % 2
    row_at = (odd * (rows + RADIUS) - RADIUS, (1 - odd) * (rows + RADIUS) - RADIUS)
    col_at = (odd_col * (cols + RADIUS) - RADIUS, (1 - odd_col) * (cols + RADIUS) - RADIUS)
    spot = lax.broadcasted_iota(jnp.int32, (total, 1), 0)
    past_first = spot - strip
    past_strips = past_first - strip
    past_third = past_strips - side
    strip_at = jnp.where(past_first >= 0, past_first, spot)
    side_at = jnp.where(past_third >= 0, past_third, past_strips)
    side_row = (side_at * 21846) >> 16
    in_strip = past_strips < 0
    krow = jnp.where(
        in_strip,
        strip_at // cols + jnp.where(past_first >= 0, row_at[1], row_at[0]),
        side_row - RADIUS,
    )
    kcol = jnp.where(
        in_strip,
        strip_at % cols,
        side_at - 3 * side_row + jnp.where(past_third >= 0, col_at[1], col_at[0]),
    )
    real = in_strip | (side_at < (rows + 2 * RADIUS) * RADIUS)
    real = real & (krow + row0 >= 0) & (krow + row0 < grid_rows)
    real = real & (kcol + col0 >= 0) & (kcol + col0 < grid_cols)
    key_mask = key_columns(rows, cols, jnp.where(real, krow, -1000), kcol)
    query_mask = query_columns(rows, cols)

    query = query_ref[...]
    low = half_lanes()
    parts = []
    for pair in range(heads // 2):
        sums = []
        for head in (2 * pair, 2 * pair + 1):
            factor = scale_ref[0:1, head : head + 1]
            sums.append(acc_ref[head] + attend(head, query, key, value, query_mask, key_mask, factor))
        top = jnp.where(low, sums[0], sums[1])
        bottom = pltpu.roll(jnp.where(low, sums[1], sums[0]), HD, 1)
        parts.append((top / bottom).astype(BF))
    attn = jnp.concatenate(parts, 1)

    h1 = (tok_ref[...].astype(F32) + dot(attn, out_ref[...])).astype(BF)
    h1_wide = h1.astype(F32)
    n2 = rms_norm(h1_wide, gain_ffn_ref[...]).astype(BF)
    hidden = ffn_out_ref.shape[0]
    gate = dot(n2, ffn_in_ref[:, :hidden])
    up = dot(n2, ffn_in_ref[:, hidden:])
    gated = (jax.nn.gelu(gate, approximate=True) * up).astype(BF)
    fine = (h1_wide + dot(gated, ffn_out_ref[...])).astype(BF)
    fine_ref[...] = fine
    pooled = jnp.mean(fine.astype(F32), 0, keepdims=True).astype(BF).astype(F32)
    for part in range(pooled_ref.shape[1]):
        pooled_ref[:, part, :] = jnp.broadcast_to(
            pooled[:, part * 128 : (part + 1) * 128], (pooled_ref.shape[0], 128)
        )
    wait_all(copies)


def coarse_kernel(
    axes, pooled_ref, up_ref, merged_query_ref, merged_ref, scale_ref, out_ref, fine_ref,
    coarse_out_ref, fine_hbm,
    query_ref, coarse_ref, sems,
):
    copies = copies_of([(fine_ref, fine_hbm)], sems)
    start_all(copies)
    width = out_ref.shape[0]
    row_axis, col_axis = axes
    mine = lax.axis_index(row_axis) * lax.axis_size(col_axis) + lax.axis_index(col_axis)
    pooled = jnp.concatenate([pooled_ref[:, part, :] for part in range(pooled_ref.shape[1])], 1).astype(BF)
    coarse = dot(pooled, up_ref[...]).astype(BF).astype(F32)
    coarse_ref[...] = coarse
    rms = lax.rsqrt(jnp.mean(coarse * coarse, -1, keepdims=True) + 1e-06)
    query_ref[...] = dot(pooled, merged_query_ref[...]) * rms
    key = dot(pooled, merged_ref[:, :width]) * rms
    value = dot(pooled, merged_ref[:, width:]) * rms
    query = query_ref[pl.ds(mine, 1), :]
    group = 4 * HD
    spans = [slice(at, at + group) for at in range(0, width, group)]
    tall = jnp.concatenate([key[:, span] for span in spans], 0)
    queries = [query[:, span] for span in spans]
    cross = jnp.concatenate([key[:, span] * q for span, q in zip(spans, queries)], 0)
    ones = same_head(group, group)
    query_norm = lax.rsqrt(dot_split(jnp.concatenate([q * q for q in queries], 0), ones) * (1.0 / HD) + 1e-06)
    key_norm = lax.rsqrt(dot_split(tall * tall, ones) * (1.0 / HD) + 1e-06)
    scores = dot_split(cross, ones) * key_norm
    count = key.shape[0]
    parts = []
    for at, span in enumerate(spans):
        factor = query_norm[at : at + 1] * scale_ref[:, span]
        expo = jnp.exp(scores[at * count : (at + 1) * count] * factor)
        total = jnp.sum(expo, 0, keepdims=True)
        parts.append(jnp.sum(expo * value[:, span], 0, keepdims=True) / total)
    cattn = jnp.concatenate(parts, 1).astype(BF)
    coarse_out_ref[...] = (coarse_ref[pl.ds(mine, 1), :] + dot(cattn, out_ref[...])).astype(BF)
    wait_all(copies)


def vmem(count):
    return [pl.BlockSpec(memory_space=pltpu.VMEM)] * count


def anywhere(count):
    return [pl.BlockSpec(memory_space=pl.ANY)] * count


def in_vmem(arrays):
    return [pltpu.with_memory_space_constraint(array, pltpu.VMEM) for array in arrays]


def in_hbm(arrays):
    return [pltpu.with_memory_space_constraint(array, pltpu.HBM) for array in arrays]


def shards(
    tokens, gain_attn, qkv_fine, scale_fine, out_fine, gain_ffn, ffn_in, ffn_out,
    up_proj, gain_coarse, qkv_coarse, scale_coarse, out_coarse,
):
    rows, cols, width = tokens.shape
    count = rows * cols
    strip = RADIUS * cols
    side = rounded_up((rows + 2 * RADIUS) * RADIUS, 16)
    heads = width // HD
    width_c = out_coarse.shape[0]
    devices = lax.axis_size("ha") * lax.axis_size("wa")
    axes = ("ha", "wa")
    params = pltpu.CompilerParams(vmem_limit_bytes=16 * MIB)

    def swapped(array, axis, first):
        pairs = [(i, i + 1) for i in range(first, lax.axis_size(axis) - 1, 2)]
        return lax.ppermute(array, axis, pairs + [(j, i) for i, j in pairs])

    flat = tokens.reshape(count, width)
    across, within = pl.pallas_call(
        functools.partial(strip_kernel, rows, cols, "ha"),
        out_shape=[pltpu.VMEM((strip, width), BF)] * 2,
        in_specs=anywhere(1),
        out_specs=vmem(2),
        scratch_shapes=[pltpu.SemaphoreType.DMA((2,))],
        compiler_params=params,
        name="strips",
    )(*in_hbm([flat]))
    across = swapped(across, "ha", 1)
    within = swapped(within, "ha", 0)

    weights = [
        flat, qkv_fine, gain_attn.reshape(1, -1), scale_fine.reshape(1, -1),
        up_proj, gain_coarse.reshape(1, -1), scale_coarse.reshape(1, -1),
        out_fine, gain_ffn.reshape(1, -1), ffn_in, ffn_out,
    ]
    *weights, query, acc, scaled, merged_query, scale_lanes = pl.pallas_call(
        functools.partial(own_kernel, rows, cols, heads),
        out_shape=[pltpu.VMEM(array.shape, array.dtype) for array in weights]
        + [
            pltpu.VMEM((count, width), BF),
            pltpu.VMEM((heads, count, 2 * HD), F32),
            pltpu.VMEM((width, width_c), BF),
            pltpu.VMEM((width, width_c), BF),
            pltpu.VMEM((1, width_c), F32),
        ],
        in_specs=anywhere(len(weights) + 1),
        out_specs=vmem(len(weights) + 5),
        scratch_shapes=[
            pltpu.VMEM((width_c, width_c), BF),
            pltpu.SemaphoreType.DMA((len(weights),)),
            pltpu.SemaphoreType.DMA((2,)),
        ],
        compiler_params=params,
        cost_estimate=pl.CostEstimate(
            flops=2 * count * width * (3 * width + 2 * count) + 2 * width * width_c * width_c,
            bytes_accessed=8 * MIB,
            transcendentals=0,
        ),
        name="own",
    )(*in_hbm(weights + [qkv_coarse]))
    tok_v, qkv_v, gain_attn_v, scale_v, up_v = weights[:5]
    out_v, gain_ffn_v, ffn_in_v, ffn_out_v = weights[7:]

    across_edge, within_edge = pl.pallas_call(
        functools.partial(edge_kernel, rows, cols, axes),
        out_shape=[pltpu.VMEM((side, width), BF)] * 2,
        in_specs=vmem(4),
        out_specs=vmem(2),
        compiler_params=params,
        name="edges",
    )(*in_vmem([tok_v, across, within, query]))
    across_side = swapped(across_edge, "wa", 1)
    within_side = swapped(within_edge, "wa", 0)

    merged = pl.pallas_call(
        merge_kernel,
        out_shape=pltpu.VMEM((width, 2 * width_c), BF),
        in_specs=vmem(2) + anywhere(1),
        out_specs=vmem(1)[0],
        scratch_shapes=[pltpu.VMEM((width_c, 2 * width_c), BF), pltpu.SemaphoreType.DMA((4,))],
        compiler_params=params,
        cost_estimate=pl.CostEstimate(
            flops=4 * width * width_c * width_c, bytes_accessed=6 * MIB, transcendentals=0
        ),
        name="merge",
    )(*in_vmem([within_edge, scaled]), *in_hbm([qkv_coarse]))

    def fine_body(tok_ref, *refs):
        fine_kernel(rows, cols, heads, axes, tok_ref, refs[:4], *refs[4:])

    fine, pooled, out_c_v = pl.pallas_call(
        fine_body,
        out_shape=[
            pltpu.VMEM((count, width), BF),
            pltpu.VMEM((devices, width // 128, 128), F32),
            pltpu.VMEM(out_coarse.shape, BF),
        ],
        in_specs=vmem(15) + anywhere(1),
        out_specs=vmem(3),
        scratch_shapes=[pltpu.SemaphoreType.DMA((1,))],
        compiler_params=params,
        name="fine",
    )(
        *in_vmem(
            [tok_v, across, within, across_side, within_side, query, acc, gain_attn_v, qkv_v, scale_v]
            + [out_v, gain_ffn_v, ffn_in_v, ffn_out_v, merged]
        ),
        *in_hbm([out_coarse]),
    )

    every = lax.all_to_all(pooled, axes, split_axis=0, concat_axis=0, tiled=True)
    coarse_out, fine = pl.pallas_call(
        functools.partial(coarse_kernel, axes),
        out_shape=[
            jax.ShapeDtypeStruct((1, width_c), BF),
            jax.ShapeDtypeStruct((count, width), BF),
        ],
        in_specs=vmem(7),
        out_specs=vmem(1) + anywhere(1),
        scratch_shapes=[pltpu.VMEM((devices, width_c), F32)] * 2 + [pltpu.SemaphoreType.DMA((1,))],
        compiler_params=params,
        name="coarse",
    )(*in_vmem([every, up_v, merged_query, merged, scale_lanes, out_c_v, fine]))
    return fine.reshape(rows, cols, width), coarse_out.reshape(1, 1, width_c)


def solution(mesh):
    return jax.shard_map(
        shards,
        mesh=mesh,
        in_specs=(P("ha", "wa", None), P(), P(), P(), P(), P(), P(), P(), P(), P(), P(), P(), P()),
        out_specs=(P("ha", "wa", None), P("ha", "wa", None)),
        check_vma=False,
    )
```

```python
import functools

import jax
import jax.numpy as jnp
from jax import lax
from jax.experimental import pallas as pl
from jax.experimental.pallas import tpu as pltpu
from jax.sharding import PartitionSpec as P

HD = 64
RADIUS = 3
LOG2E = 1.4426950408889634
BIG = 2.0**30
BF = jnp.bfloat16
F32 = jnp.float32
MIB = 1 << 20


def rounded_up(value, step):
    return -(-value // step) * step


def dot(a, b):
    return jnp.dot(a, b, preferred_element_type=F32)


def dot_nt(a, b):
    return lax.dot_general(a, b, (((1,), (1,)), ((), ())), preferred_element_type=F32)


def dot_split(values, ones):
    high = values.astype(BF)
    low = (values - high.astype(F32)).astype(BF)
    return dot(high, ones) + dot(low, ones)


def same_head(rows, cols):
    shape = (rows, cols)
    left = lax.broadcasted_iota(jnp.int32, shape, 0) // HD
    right = lax.broadcasted_iota(jnp.int32, shape, 1) // HD
    return (left == right).astype(F32).astype(BF)


def head_norm(values, ones):
    return values * lax.rsqrt(dot_split(values * values, ones) * (1.0 / HD) + 1e-06)


def rms_norm(values, gain):
    mean = jnp.mean(values * values, -1, keepdims=True)
    return values * lax.rsqrt(mean + 1e-06) * gain


def copies_of(pairs, sems):
    return [pltpu.make_async_copy(src, dst, sems.at[i]) for i, (src, dst) in enumerate(pairs)]


def start_all(copies):
    for copy in copies:
        copy.start()


def wait_all(copies):
    for copy in copies:
        copy.wait()


def strip_kernel(rows, cols, axis, tok_hbm, across_ref, within_ref, sems):
    count, strip = rows * cols, RADIUS * cols
    odd = lax.axis_index(axis) % 2
    last = count - strip
    first = pl.multiple_of(odd * last, 16)
    second = pl.multiple_of((1 - odd) * last, 16)
    copies = copies_of(
        [
            (tok_hbm.at[pl.ds(first, strip), :], across_ref),
            (tok_hbm.at[pl.ds(second, strip), :], within_ref),
        ],
        sems,
    )
    start_all(copies)
    wait_all(copies)


def edge_kernel(rows, cols, axes, tok_ref, across_ref, within_ref, after_ref, across_out, within_out):
    height = rows + 2 * RADIUS
    strip = RADIUS * cols
    padded = across_out.shape[0]
    odd, odd_col = lax.axis_index(axes[0]) % 2, lax.axis_index(axes[1]) % 2
    block = jnp.concatenate([tok_ref[...], across_ref[...], within_ref[...]], 0)
    out = lax.broadcasted_iota(jnp.int32, (padded, 1), 0)
    src = lax.broadcasted_iota(jnp.int32, (padded, block.shape[0]), 1)
    row = ((out * 21846) >> 16) - RADIUS
    col = out - 3 * (row + RADIUS)
    above = rows * cols + strip * odd + RADIUS * cols
    below = rows * cols + strip * (1 - odd) - rows * cols
    first = row * cols + col + jnp.where(row < 0, above, jnp.where(row >= rows, below, 0))
    first = jnp.where(out < height * RADIUS, first, -2 * cols)
    far = cols - RADIUS
    pick = jnp.where(src == first + far * odd_col, 1.0, 0.0).astype(BF)
    across_out[...] = dot(pick, block).astype(BF)
    pick = jnp.where(src == first + far * (1 - odd_col), 1.0, 0.0).astype(BF)
    within_out[...] = dot(pick, block).astype(BF)


def column_copies(src, dst, start, blocks, sems):
    size = dst.shape[1] // blocks
    spans = [pl.ds(i * size, size) for i in range(blocks)]
    pairs = [(src.at[:, pl.ds(start + i * size, size)], dst.at[:, span]) for i, span in enumerate(spans)]
    return copies_of(pairs, sems), spans


def merge_kernel(after_ref, up_ref, gain_ref, qkv_hbm, merged_ref, weight_ref, sems):
    copies, spans = column_copies(qkv_hbm, weight_ref, weight_ref.shape[0], sems.shape[0], sems)
    start_all(copies)
    scaled = (up_ref[...].astype(F32) * gain_ref[...]).astype(BF)
    for copy, span in zip(copies, spans):
        copy.wait()
        merged_ref[:, span] = dot(scaled, weight_ref[:, span]).astype(BF)


def lane_scales(scale_ref, width):
    lane = lax.broadcasted_iota(jnp.int32, (1, width), 1) // HD
    scales = jnp.zeros((1, width), F32)
    for head in range(scale_ref.shape[1]):
        scales = jnp.where(lane == head, scale_ref[0:1, head : head + 1], scales)
    return scales


def query_kernel(pooled_ref, up_ref, gain_ref, scale_ref, qkv_hbm, rows_hbm, weight_ref, rows_ref, sems, out_sems):
    width = weight_ref.shape[0]
    copies, spans = column_copies(qkv_hbm, weight_ref, 0, sems.shape[0], sems)
    start_all(copies)
    count = min(8, pooled_ref.shape[0])
    pooled = jnp.concatenate([pooled_ref[:count, part, :] for part in range(pooled_ref.shape[1])], 1).astype(BF)
    coarse = dot(pooled, up_ref[...]).astype(BF).astype(F32)
    normed = rms_norm(coarse, gain_ref[...]).astype(BF)
    scales = lane_scales(scale_ref, width) * (1.0 / HD)
    group = 4 * HD
    ones = same_head(group, group)
    rows_ref[1:2, :] = coarse[0:1]
    wait_all(copies)
    for at in range(0, width, group):
        span = slice(at, at + group)
        query = head_norm(dot(normed, weight_ref[:, span]), ones)
        rows_ref[0:1, span] = query[0:1] * scales[:, span]
    out = copies_of([(rows_ref, rows_hbm)], out_sems)
    start_all(out)
    wait_all(out)


def half_lanes():
    return lax.broadcasted_iota(jnp.int32, (1, 2 * HD), 1) < HD


def mask_columns(rows, cols):
    place = lax.broadcasted_iota(jnp.int32, (1, 2 * HD), 1) % HD
    return place, place < rows, (place >= rows) & (place < rows + cols)


def query_columns(rows, cols):
    place, is_row, is_col = mask_columns(rows, cols)
    spot = lax.broadcasted_iota(jnp.int32, (rows * cols, 1), 0)
    hot = (is_row & (spot // cols == place)) | (is_col & (spot % cols == place - rows))
    return jnp.where(hot, 1.0, 0.0).astype(BF)


def key_columns(rows, cols, krow, kcol):
    place, is_row, is_col = mask_columns(rows, cols)
    far_row = jnp.abs(krow - place) > RADIUS
    far_col = jnp.abs(kcol - (place - rows)) > RADIUS
    return jnp.where((is_row & far_row) | (is_col & far_col), -BIG, 0.0).astype(BF)


def attend(head, query, key, value, query_mask, key_mask, factor):
    lanes = 2 * HD
    low = half_lanes()
    mine = low if head % 2 == 0 else ~low
    span = slice(head // 2 * lanes, (head // 2 + 1) * lanes)
    q = jnp.where(mine, query[:, span], query_mask)
    k = jnp.where(mine, key[:, span], key_mask)
    v = jnp.where(mine, value[:, span], jnp.ones((1, lanes), BF))
    weights = jnp.exp2(dot_nt(q, k) * (factor * (LOG2E / HD))).astype(BF)
    return dot(weights, v)


def own_kernel(rows, cols, heads, *refs):
    count = (len(refs) - 3) // 2
    outs, (query_ref, acc_ref, sems) = refs[count : 2 * count], refs[2 * count :]
    tok_ref, qkv_ref, gain_ref, scale_ref = outs[:4]
    copies = copies_of(list(zip(refs[:count], outs)), sems)
    start_all(copies)
    width = heads * HD
    ones = same_head(width, width)
    query_mask = query_columns(rows, cols)
    spot = lax.broadcasted_iota(jnp.int32, (rows * cols, 1), 0)
    key_mask = key_columns(rows, cols, spot // cols, spot % cols)
    wait_all(copies[:4])
    normed = rms_norm(tok_ref[...].astype(F32), gain_ref[...]).astype(BF)
    query = head_norm(dot(normed, qkv_ref[:, :width]), ones).astype(BF)
    key = head_norm(dot(normed, qkv_ref[:, width : 2 * width]), ones).astype(BF)
    value = dot(normed, qkv_ref[:, 2 * width :]).astype(BF)
    query_ref[...] = query
    for head in range(heads):
        factor = scale_ref[0:1, head : head + 1]
        acc_ref[head] = attend(head, query, key, value, query_mask, key_mask, factor)
    wait_all(copies[4:])


def fine_kernel(
    rows, cols, heads, axes,
    tok_ref, halo_refs, query_ref, acc_ref, gain_attn_ref, qkv_ref, scale_ref,
    out_ref, gain_ffn_ref, ffn_in_ref, ffn_out_ref, after_ref, out_c_hbm,
    fine_ref, pooled_ref, out_c_ref, sems,
):
    copies = copies_of([(out_c_hbm, out_c_ref)], sems)
    start_all(copies)
    strip = RADIUS * cols
    side = halo_refs[-1].shape[0]
    width = heads * HD
    total = 2 * strip + 2 * side
    row_axis, col_axis = axes
    row0 = lax.axis_index(row_axis) * rows
    col0 = lax.axis_index(col_axis) * cols
    grid_rows = lax.axis_size(row_axis) * rows
    grid_cols = lax.axis_size(col_axis) * cols

    halo = jnp.concatenate([ref[...] for ref in halo_refs], 0)
    normed = rms_norm(halo.astype(F32), gain_attn_ref[...]).astype(BF)
    ones = same_head(width, width)
    key = head_norm(dot(normed, qkv_ref[:, width : 2 * width]), ones).astype(BF)
    value = dot(normed, qkv_ref[:, 2 * width :]).astype(BF)

    odd, odd_col = lax.axis_index(row_axis) % 2, lax.axis_index(col_axis) % 2
    row_at = (odd * (rows + RADIUS) - RADIUS, (1 - odd) * (rows + RADIUS) - RADIUS)
    col_at = (odd_col * (cols + RADIUS) - RADIUS, (1 - odd_col) * (cols + RADIUS) - RADIUS)
    spot = lax.broadcasted_iota(jnp.int32, (total, 1), 0)
    past_first = spot - strip
    past_strips = past_first - strip
    past_third = past_strips - side
    strip_at = jnp.where(past_first >= 0, past_first, spot)
    side_at = jnp.where(past_third >= 0, past_third, past_strips)
    side_row = (side_at * 21846) >> 16
    in_strip = past_strips < 0
    krow = jnp.where(
        in_strip,
        strip_at // cols + jnp.where(past_first >= 0, row_at[1], row_at[0]),
        side_row - RADIUS,
    )
    kcol = jnp.where(
        in_strip,
        strip_at % cols,
        side_at - 3 * side_row + jnp.where(past_third >= 0, col_at[1], col_at[0]),
    )
    real = in_strip | (side_at < (rows + 2 * RADIUS) * RADIUS)
    real = real & (krow + row0 >= 0) & (krow + row0 < grid_rows)
    real = real & (kcol + col0 >= 0) & (kcol + col0 < grid_cols)
    key_mask = key_columns(rows, cols, jnp.where(real, krow, -1000), kcol)
    query_mask = query_columns(rows, cols)

    query = query_ref[...]
    low = half_lanes()
    parts = []
    for pair in range(heads // 2):
        sums = []
        for head in (2 * pair, 2 * pair + 1):
            factor = scale_ref[0:1, head : head + 1]
            sums.append(acc_ref[head] + attend(head, query, key, value, query_mask, key_mask, factor))
        top = jnp.where(low, sums[0], sums[1])
        bottom = pltpu.roll(jnp.where(low, sums[1], sums[0]), HD, 1)
        parts.append((top / bottom).astype(BF))
    attn = jnp.concatenate(parts, 1)

    h1 = (tok_ref[...].astype(F32) + dot(attn, out_ref[...])).astype(BF)
    h1_wide = h1.astype(F32)
    n2 = rms_norm(h1_wide, gain_ffn_ref[...]).astype(BF)
    hidden = ffn_out_ref.shape[0]
    gate = dot(n2, ffn_in_ref[:, :hidden])
    up = dot(n2, ffn_in_ref[:, hidden:])
    gated = (jax.nn.gelu(gate, approximate=True) * up).astype(BF)
    fine = (h1_wide + dot(gated, ffn_out_ref[...])).astype(BF)
    fine_ref[...] = fine
    pooled = jnp.mean(fine.astype(F32), 0, keepdims=True).astype(BF).astype(F32)
    for part in range(pooled_ref.shape[1]):
        pooled_ref[:, part, :] = jnp.broadcast_to(
            pooled[:, part * 128 : (part + 1) * 128], (pooled_ref.shape[0], 128)
        )
    wait_all(copies)


def coarse_kernel(
    pooled_ref, up_ref, merged_ref, out_ref, fine_ref, rows_hbm,
    coarse_out_ref, fine_hbm,
    rows_ref, sems,
):
    copies = copies_of([(rows_hbm, rows_ref), (fine_ref, fine_hbm)], sems)
    start_all(copies)
    width = out_ref.shape[0]
    pooled = jnp.concatenate([pooled_ref[:, part, :] for part in range(pooled_ref.shape[1])], 1).astype(BF)
    coarse = dot(pooled, up_ref[...]).astype(BF).astype(F32)
    rms = lax.rsqrt(jnp.mean(coarse * coarse, -1, keepdims=True) + 1e-06)
    key = dot(pooled, merged_ref[:, :width]) * rms
    value = dot(pooled, merged_ref[:, width:]) * rms
    group = 4 * HD
    spans = [slice(at, at + group) for at in range(0, width, group)]
    tall = jnp.concatenate([key[:, span] for span in spans], 0)
    ones = same_head(group, group)
    copies[0].wait()
    query = rows_ref[0:1, :]
    cross = jnp.concatenate([key[:, span] * query[:, span] for span in spans], 0)
    key_norm = lax.rsqrt(dot_split(tall * tall, ones) * (1.0 / HD) + 1e-06)
    scores = dot_split(cross, ones) * key_norm
    count = key.shape[0]
    parts = []
    for at, span in enumerate(spans):
        expo = jnp.exp(scores[at * count : (at + 1) * count])
        total = jnp.sum(expo, 0, keepdims=True)
        parts.append(jnp.sum(expo * value[:, span], 0, keepdims=True) / total)
    cattn = jnp.concatenate(parts, 1).astype(BF)
    coarse_out_ref[...] = (rows_ref[1:2, :] + dot(cattn, out_ref[...])).astype(BF)
    copies[1].wait()


def vmem(count):
    return [pl.BlockSpec(memory_space=pltpu.VMEM)] * count


def anywhere(count):
    return [pl.BlockSpec(memory_space=pl.ANY)] * count


def in_vmem(arrays):
    return [pltpu.with_memory_space_constraint(array, pltpu.VMEM) for array in arrays]


def in_hbm(arrays):
    return [pltpu.with_memory_space_constraint(array, pltpu.HBM) for array in arrays]


def shards(
    tokens, gain_attn, qkv_fine, scale_fine, out_fine, gain_ffn, ffn_in, ffn_out,
    up_proj, gain_coarse, qkv_coarse, scale_coarse, out_coarse,
):
    rows, cols, width = tokens.shape
    count = rows * cols
    strip = RADIUS * cols
    side = rounded_up((rows + 2 * RADIUS) * RADIUS, 16)
    heads = width // HD
    width_c = out_coarse.shape[0]
    devices = lax.axis_size("ha") * lax.axis_size("wa")
    axes = ("ha", "wa")
    params = pltpu.CompilerParams(vmem_limit_bytes=16 * MIB)

    def swapped(array, axis, first):
        pairs = [(i, i + 1) for i in range(first, lax.axis_size(axis) - 1, 2)]
        return lax.ppermute(array, axis, pairs + [(j, i) for i, j in pairs])

    flat = tokens.reshape(count, width)
    across, within = pl.pallas_call(
        functools.partial(strip_kernel, rows, cols, "ha"),
        out_shape=[pltpu.VMEM((strip, width), BF)] * 2,
        in_specs=anywhere(1),
        out_specs=vmem(2),
        scratch_shapes=[pltpu.SemaphoreType.DMA((2,))],
        compiler_params=params,
        name="strips",
    )(*in_hbm([flat]))
    across = swapped(across, "ha", 1)
    within = swapped(within, "ha", 0)

    weights = [
        flat, qkv_fine, gain_attn.reshape(1, -1), scale_fine.reshape(1, -1),
        up_proj, gain_coarse.reshape(1, -1), scale_coarse.reshape(1, -1),
        out_fine, gain_ffn.reshape(1, -1), ffn_in, ffn_out,
    ]
    *weights, query, acc = pl.pallas_call(
        functools.partial(own_kernel, rows, cols, heads),
        out_shape=[pltpu.VMEM(array.shape, array.dtype) for array in weights]
        + [pltpu.VMEM((count, width), BF), pltpu.VMEM((heads, count, 2 * HD), F32)],
        in_specs=anywhere(len(weights)),
        out_specs=vmem(len(weights) + 2),
        scratch_shapes=[pltpu.SemaphoreType.DMA((len(weights),))],
        compiler_params=params,
        cost_estimate=pl.CostEstimate(
            flops=2 * count * width * (3 * width + 2 * count), bytes_accessed=4 * MIB, transcendentals=0
        ),
        name="own",
    )(*in_hbm(weights))
    tok_v, qkv_v, gain_attn_v, scale_v, up_v, gain_c_v, scale_c_v = weights[:7]
    out_v, gain_ffn_v, ffn_in_v, ffn_out_v = weights[7:]

    across_edge, within_edge = pl.pallas_call(
        functools.partial(edge_kernel, rows, cols, axes),
        out_shape=[pltpu.VMEM((side, width), BF)] * 2,
        in_specs=vmem(4),
        out_specs=vmem(2),
        compiler_params=params,
        name="edges",
    )(*in_vmem([tok_v, across, within, query]))
    across_side = swapped(across_edge, "wa", 1)
    within_side = swapped(within_edge, "wa", 0)

    merged = pl.pallas_call(
        merge_kernel,
        out_shape=pltpu.VMEM((width, 2 * width_c), BF),
        in_specs=vmem(3) + anywhere(1),
        out_specs=vmem(1)[0],
        scratch_shapes=[pltpu.VMEM((width_c, 2 * width_c), BF), pltpu.SemaphoreType.DMA((4,))],
        compiler_params=params,
        cost_estimate=pl.CostEstimate(
            flops=4 * width * width_c * width_c, bytes_accessed=6 * MIB, transcendentals=0
        ),
        name="merge",
    )(*in_vmem([within_edge, up_v, gain_c_v]), *in_hbm([qkv_coarse]))

    def fine_body(tok_ref, *refs):
        fine_kernel(rows, cols, heads, axes, tok_ref, refs[:4], *refs[4:])

    fine, pooled, out_c_v = pl.pallas_call(
        fine_body,
        out_shape=[
            pltpu.VMEM((count, width), BF),
            pltpu.VMEM((devices, width // 128, 128), F32),
            pltpu.VMEM(out_coarse.shape, BF),
        ],
        in_specs=vmem(15) + anywhere(1),
        out_specs=vmem(3),
        scratch_shapes=[pltpu.SemaphoreType.DMA((1,))],
        compiler_params=params,
        name="fine",
    )(
        *in_vmem(
            [tok_v, across, within, across_side, within_side, query, acc, gain_attn_v, qkv_v, scale_v]
            + [out_v, gain_ffn_v, ffn_in_v, ffn_out_v, merged]
        ),
        *in_hbm([out_coarse]),
    )

    every = lax.all_to_all(pooled, axes, split_axis=0, concat_axis=0, tiled=True)
    mine = pl.pallas_call(
        query_kernel,
        out_shape=pltpu.HBM((8, width_c), F32),
        in_specs=vmem(4) + anywhere(1),
        out_specs=anywhere(1)[0],
        scratch_shapes=[
            pltpu.VMEM((width_c, width_c), BF),
            pltpu.VMEM((8, width_c), F32),
            pltpu.SemaphoreType.DMA((1,)),
            pltpu.SemaphoreType.DMA((1,)),
        ],
        compiler_params=params,
        cost_estimate=pl.CostEstimate(
            flops=2 * width * width_c * width_c, bytes_accessed=6 * MIB, transcendentals=0
        ),
        name="query",
    )(*in_vmem([pooled, up_v, gain_c_v, scale_c_v]), *in_hbm([qkv_coarse]))
    coarse_out, fine = pl.pallas_call(
        coarse_kernel,
        out_shape=[
            jax.ShapeDtypeStruct((1, width_c), BF),
            jax.ShapeDtypeStruct((count, width), BF),
        ],
        in_specs=vmem(5) + anywhere(1),
        out_specs=vmem(1) + anywhere(1),
        scratch_shapes=[pltpu.VMEM((8, width_c), F32), pltpu.SemaphoreType.DMA((2,))],
        compiler_params=params,
        name="coarse",
    )(*in_vmem([every, up_v, merged, out_c_v, fine]), *in_hbm([mine]))
    return fine.reshape(rows, cols, width), coarse_out.reshape(1, 1, width_c)


def solution(mesh):
    return jax.shard_map(
        shards,
        mesh=mesh,
        in_specs=(P("ha", "wa", None), P(), P(), P(), P(), P(), P(), P(), P(), P(), P(), P(), P()),
        out_specs=(P("ha", "wa", None), P("ha", "wa", None)),
        check_vma=False,
    )
```

```python
import functools

import jax
import jax.numpy as jnp
from jax import lax
from jax.experimental import pallas as pl
from jax.experimental.pallas import tpu as pltpu
from jax.sharding import PartitionSpec as P

HD = 64
RADIUS = 3
LOG2E = 1.4426950408889634
BIG = 2.0**30
BF = jnp.bfloat16
F32 = jnp.float32
MIB = 1 << 20


def rounded_up(value, step):
    return -(-value // step) * step


def dot(a, b):
    return jnp.dot(a, b, preferred_element_type=F32)


def dot_nt(a, b):
    return lax.dot_general(a, b, (((1,), (1,)), ((), ())), preferred_element_type=F32)


def dot_split(values, ones):
    high = values.astype(BF)
    low = (values - high.astype(F32)).astype(BF)
    return dot(high, ones) + dot(low, ones)


def same_head(rows, cols):
    shape = (rows, cols)
    left = lax.broadcasted_iota(jnp.int32, shape, 0) // HD
    right = lax.broadcasted_iota(jnp.int32, shape, 1) // HD
    return (left == right).astype(F32).astype(BF)


def head_norm(values, ones):
    return values * lax.rsqrt(dot_split(values * values, ones) * (1.0 / HD) + 1e-06)


def rms_norm(values, gain):
    mean = jnp.mean(values * values, -1, keepdims=True)
    return values * lax.rsqrt(mean + 1e-06) * gain


def copies_of(pairs, sems):
    return [pltpu.make_async_copy(src, dst, sems.at[i]) for i, (src, dst) in enumerate(pairs)]


def start_all(copies):
    for copy in copies:
        copy.start()


def wait_all(copies):
    for copy in copies:
        copy.wait()


def strip_kernel(rows, cols, axis, tok_hbm, across_ref, within_ref, sems):
    count, strip = rows * cols, RADIUS * cols
    odd = lax.axis_index(axis) % 2
    last = count - strip
    first = pl.multiple_of(odd * last, 16)
    second = pl.multiple_of((1 - odd) * last, 16)
    copies = copies_of(
        [
            (tok_hbm.at[pl.ds(first, strip), :], across_ref),
            (tok_hbm.at[pl.ds(second, strip), :], within_ref),
        ],
        sems,
    )
    start_all(copies)
    wait_all(copies)


def edge_kernel(rows, cols, axes, tok_ref, across_ref, within_ref, after_ref, across_out, within_out):
    height = rows + 2 * RADIUS
    strip = RADIUS * cols
    padded = across_out.shape[0]
    odd, odd_col = lax.axis_index(axes[0]) % 2, lax.axis_index(axes[1]) % 2
    block = jnp.concatenate([tok_ref[...], across_ref[...], within_ref[...]], 0)
    out = lax.broadcasted_iota(jnp.int32, (padded, 1), 0)
    src = lax.broadcasted_iota(jnp.int32, (padded, block.shape[0]), 1)
    row = ((out * 21846) >> 16) - RADIUS
    col = out - 3 * (row + RADIUS)
    above = rows * cols + strip * odd + RADIUS * cols
    below = rows * cols + strip * (1 - odd) - rows * cols
    first = row * cols + col + jnp.where(row < 0, above, jnp.where(row >= rows, below, 0))
    first = jnp.where(out < height * RADIUS, first, -2 * cols)
    far = cols - RADIUS
    pick = jnp.where(src == first + far * odd_col, 1.0, 0.0).astype(BF)
    across_out[...] = dot(pick, block).astype(BF)
    pick = jnp.where(src == first + far * (1 - odd_col), 1.0, 0.0).astype(BF)
    within_out[...] = dot(pick, block).astype(BF)


def column_copies(src, dst, start, blocks, sems):
    size = dst.shape[1] // blocks
    spans = [pl.ds(i * size, size) for i in range(blocks)]
    pairs = [(src.at[:, pl.ds(start + i * size, size)], dst.at[:, span]) for i, span in enumerate(spans)]
    return copies_of(pairs, sems), spans


def merge_kernel(after_ref, up_ref, gain_ref, qkv_hbm, merged_ref, weight_ref, sems):
    copies, spans = column_copies(qkv_hbm, weight_ref, weight_ref.shape[0], sems.shape[0], sems)
    start_all(copies)
    scaled = (up_ref[...].astype(F32) * gain_ref[...]).astype(BF)
    for copy, span in zip(copies, spans):
        copy.wait()
        merged_ref[:, span] = dot(scaled, weight_ref[:, span]).astype(BF)


def lane_scales(scale_ref, width):
    lane = lax.broadcasted_iota(jnp.int32, (1, width), 1) // HD
    scales = jnp.zeros((1, width), F32)
    for head in range(scale_ref.shape[1]):
        scales = jnp.where(lane == head, scale_ref[0:1, head : head + 1], scales)
    return scales


def half_lanes():
    return lax.broadcasted_iota(jnp.int32, (1, 2 * HD), 1) < HD


def mask_columns(rows, cols):
    place = lax.broadcasted_iota(jnp.int32, (1, 2 * HD), 1) % HD
    return place, place < rows, (place >= rows) & (place < rows + cols)


def query_columns(rows, cols):
    place, is_row, is_col = mask_columns(rows, cols)
    spot = lax.broadcasted_iota(jnp.int32, (rows * cols, 1), 0)
    hot = (is_row & (spot // cols == place)) | (is_col & (spot % cols == place - rows))
    return jnp.where(hot, 1.0, 0.0).astype(BF)


def key_columns(rows, cols, krow, kcol):
    place, is_row, is_col = mask_columns(rows, cols)
    far_row = jnp.abs(krow - place) > RADIUS
    far_col = jnp.abs(kcol - (place - rows)) > RADIUS
    return jnp.where((is_row & far_row) | (is_col & far_col), -BIG, 0.0).astype(BF)


def attend(head, query, key, value, query_mask, key_mask, factor):
    lanes = 2 * HD
    low = half_lanes()
    mine = low if head % 2 == 0 else ~low
    span = slice(head // 2 * lanes, (head // 2 + 1) * lanes)
    q = jnp.where(mine, query[:, span], query_mask)
    k = jnp.where(mine, key[:, span], key_mask)
    v = jnp.where(mine, value[:, span], jnp.ones((1, lanes), BF))
    weights = jnp.exp2(dot_nt(q, k) * (factor * (LOG2E / HD))).astype(BF)
    return dot(weights, v)


def own_kernel(rows, cols, heads, *refs):
    count = (len(refs) - 3) // 2
    outs, (query_ref, acc_ref, sems) = refs[count : 2 * count], refs[2 * count :]
    tok_ref, qkv_ref, gain_ref, scale_ref = outs[:4]
    copies = copies_of(list(zip(refs[:count], outs)), sems)
    start_all(copies[:4])
    width = heads * HD
    ones = same_head(width, width)
    query_mask = query_columns(rows, cols)
    spot = lax.broadcasted_iota(jnp.int32, (rows * cols, 1), 0)
    key_mask = key_columns(rows, cols, spot // cols, spot % cols)
    copies[0].wait()
    start_all(copies[4:])
    wait_all(copies[1:4])
    normed = rms_norm(tok_ref[...].astype(F32), gain_ref[...]).astype(BF)
    query = head_norm(dot(normed, qkv_ref[:, :width]), ones).astype(BF)
    key = head_norm(dot(normed, qkv_ref[:, width : 2 * width]), ones).astype(BF)
    value = dot(normed, qkv_ref[:, 2 * width :]).astype(BF)
    query_ref[...] = query
    for head in range(heads):
        factor = scale_ref[0:1, head : head + 1]
        acc_ref[head] = attend(head, query, key, value, query_mask, key_mask, factor)
    wait_all(copies[4:])


def fine_kernel(
    rows, cols, heads, axes,
    tok_ref, halo_refs, query_ref, acc_ref, gain_attn_ref, qkv_ref, scale_ref,
    out_ref, gain_ffn_ref, ffn_in_ref, after_ref, ffn_out_hbm, qkv_c_hbm,
    fine_ref, pooled_ref, query_c_ref, ffn_out_ref, sems,
):
    columns = qkv_c_hbm.at[:, pl.ds(0, query_c_ref.shape[1])]
    copies = copies_of([(ffn_out_hbm, ffn_out_ref), (columns, query_c_ref)], sems)
    start_all(copies)
    strip = RADIUS * cols
    side = halo_refs[-1].shape[0]
    width = heads * HD
    total = 2 * strip + 2 * side
    row_axis, col_axis = axes
    row0 = lax.axis_index(row_axis) * rows
    col0 = lax.axis_index(col_axis) * cols
    grid_rows = lax.axis_size(row_axis) * rows
    grid_cols = lax.axis_size(col_axis) * cols

    halo = jnp.concatenate([ref[...] for ref in halo_refs], 0)
    normed = rms_norm(halo.astype(F32), gain_attn_ref[...]).astype(BF)
    ones = same_head(width, width)
    key = head_norm(dot(normed, qkv_ref[:, width : 2 * width]), ones).astype(BF)
    value = dot(normed, qkv_ref[:, 2 * width :]).astype(BF)

    odd, odd_col = lax.axis_index(row_axis) % 2, lax.axis_index(col_axis) % 2
    row_at = (odd * (rows + RADIUS) - RADIUS, (1 - odd) * (rows + RADIUS) - RADIUS)
    col_at = (odd_col * (cols + RADIUS) - RADIUS, (1 - odd_col) * (cols + RADIUS) - RADIUS)
    spot = lax.broadcasted_iota(jnp.int32, (total, 1), 0)
    past_first = spot - strip
    past_strips = past_first - strip
    past_third = past_strips - side
    strip_at = jnp.where(past_first >= 0, past_first, spot)
    side_at = jnp.where(past_third >= 0, past_third, past_strips)
    side_row = (side_at * 21846) >> 16
    in_strip = past_strips < 0
    krow = jnp.where(
        in_strip,
        strip_at // cols + jnp.where(past_first >= 0, row_at[1], row_at[0]),
        side_row - RADIUS,
    )
    kcol = jnp.where(
        in_strip,
        strip_at % cols,
        side_at - 3 * side_row + jnp.where(past_third >= 0, col_at[1], col_at[0]),
    )
    real = in_strip | (side_at < (rows + 2 * RADIUS) * RADIUS)
    real = real & (krow + row0 >= 0) & (krow + row0 < grid_rows)
    real = real & (kcol + col0 >= 0) & (kcol + col0 < grid_cols)
    key_mask = key_columns(rows, cols, jnp.where(real, krow, -1000), kcol)
    query_mask = query_columns(rows, cols)

    query = query_ref[...]
    low = half_lanes()
    parts = []
    for pair in range(heads // 2):
        sums = []
        for head in (2 * pair, 2 * pair + 1):
            factor = scale_ref[0:1, head : head + 1]
            sums.append(acc_ref[head] + attend(head, query, key, value, query_mask, key_mask, factor))
        top = jnp.where(low, sums[0], sums[1])
        bottom = pltpu.roll(jnp.where(low, sums[1], sums[0]), HD, 1)
        parts.append((top / bottom).astype(BF))
    attn = jnp.concatenate(parts, 1)

    h1 = (tok_ref[...].astype(F32) + dot(attn, out_ref[...])).astype(BF)
    h1_wide = h1.astype(F32)
    n2 = rms_norm(h1_wide, gain_ffn_ref[...]).astype(BF)
    hidden = ffn_out_ref.shape[0]
    gate = dot(n2, ffn_in_ref[:, :hidden])
    up = dot(n2, ffn_in_ref[:, hidden:])
    gated = (jax.nn.gelu(gate, approximate=True) * up).astype(BF)
    copies[0].wait()
    fine = (h1_wide + dot(gated, ffn_out_ref[...])).astype(BF)
    fine_ref[...] = fine
    pooled = jnp.mean(fine.astype(F32), 0, keepdims=True).astype(BF).astype(F32)
    for part in range(pooled_ref.shape[1]):
        pooled_ref[:, part, :] = jnp.broadcast_to(
            pooled[:, part * 128 : (part + 1) * 128], (pooled_ref.shape[0], 128)
        )
    copies[1].wait()


def coarse_kernel(
    axes, pooled_ref, up_ref, merged_ref, query_c_ref, gain_ref, scale_ref, fine_ref, out_hbm,
    coarse_out_ref, fine_hbm,
    coarse_ref, out_ref, sems,
):
    copies = copies_of([(out_hbm, out_ref), (fine_ref, fine_hbm)], sems)
    start_all(copies)
    width = out_ref.shape[0]
    row_axis, col_axis = axes
    mine = lax.axis_index(row_axis) * lax.axis_size(col_axis) + lax.axis_index(col_axis)
    pooled = jnp.concatenate([pooled_ref[:, part, :] for part in range(pooled_ref.shape[1])], 1).astype(BF)
    coarse = dot(pooled, up_ref[...]).astype(BF).astype(F32)
    coarse_ref[...] = coarse
    own = coarse_ref[pl.ds(mine, 1), :]
    query = dot(rms_norm(own, gain_ref[...]).astype(BF), query_c_ref[...])
    rms = lax.rsqrt(jnp.mean(coarse * coarse, -1, keepdims=True) + 1e-06)
    key = dot(pooled, merged_ref[:, :width]) * rms
    value = dot(pooled, merged_ref[:, width:]) * rms
    group = 4 * HD
    spans = [slice(at, at + group) for at in range(0, width, group)]
    tall = jnp.concatenate([key[:, span] for span in spans], 0)
    ones = same_head(group, group)
    queries = [query[:, span] for span in spans]
    scales = lane_scales(scale_ref, width) * (1.0 / HD)
    cross = jnp.concatenate([key[:, span] * q for span, q in zip(spans, queries)], 0)
    query_norm = lax.rsqrt(dot_split(jnp.concatenate([q * q for q in queries], 0), ones) * (1.0 / HD) + 1e-06)
    key_norm = lax.rsqrt(dot_split(tall * tall, ones) * (1.0 / HD) + 1e-06)
    scores = dot_split(cross, ones) * key_norm
    count = key.shape[0]
    parts = []
    for at, span in enumerate(spans):
        factor = query_norm[at : at + 1] * scales[:, span]
        expo = jnp.exp(scores[at * count : (at + 1) * count] * factor)
        total = jnp.sum(expo, 0, keepdims=True)
        parts.append(jnp.sum(expo * value[:, span], 0, keepdims=True) / total)
    cattn = jnp.concatenate(parts, 1).astype(BF)
    copies[0].wait()
    coarse_out_ref[...] = (own + dot(cattn, out_ref[...])).astype(BF)
    copies[1].wait()


def vmem(count):
    return [pl.BlockSpec(memory_space=pltpu.VMEM)] * count


def anywhere(count):
    return [pl.BlockSpec(memory_space=pl.ANY)] * count


def in_vmem(arrays):
    return [pltpu.with_memory_space_constraint(array, pltpu.VMEM) for array in arrays]


def in_hbm(arrays):
    return [pltpu.with_memory_space_constraint(array, pltpu.HBM) for array in arrays]


def shards(
    tokens, gain_attn, qkv_fine, scale_fine, out_fine, gain_ffn, ffn_in, ffn_out,
    up_proj, gain_coarse, qkv_coarse, scale_coarse, out_coarse,
):
    rows, cols, width = tokens.shape
    count = rows * cols
    strip = RADIUS * cols
    side = rounded_up((rows + 2 * RADIUS) * RADIUS, 16)
    heads = width // HD
    width_c = out_coarse.shape[0]
    devices = lax.axis_size("ha") * lax.axis_size("wa")
    axes = ("ha", "wa")
    params = pltpu.CompilerParams(vmem_limit_bytes=16 * MIB)

    def swapped(array, axis, first):
        pairs = [(i, i + 1) for i in range(first, lax.axis_size(axis) - 1, 2)]
        return lax.ppermute(array, axis, pairs + [(j, i) for i, j in pairs])

    flat = tokens.reshape(count, width)
    across, within = pl.pallas_call(
        functools.partial(strip_kernel, rows, cols, "ha"),
        out_shape=[pltpu.VMEM((strip, width), BF)] * 2,
        in_specs=anywhere(1),
        out_specs=vmem(2),
        scratch_shapes=[pltpu.SemaphoreType.DMA((2,))],
        compiler_params=params,
        name="strips",
    )(*in_hbm([flat]))
    across = swapped(across, "ha", 1)
    within = swapped(within, "ha", 0)

    weights = [
        flat, qkv_fine, gain_attn.reshape(1, -1), scale_fine.reshape(1, -1),
        up_proj, gain_coarse.reshape(1, -1), scale_coarse.reshape(1, -1),
        out_fine, gain_ffn.reshape(1, -1), ffn_in,
    ]
    *weights, query, acc = pl.pallas_call(
        functools.partial(own_kernel, rows, cols, heads),
        out_shape=[pltpu.VMEM(array.shape, array.dtype) for array in weights]
        + [pltpu.VMEM((count, width), BF), pltpu.VMEM((heads, count, 2 * HD), F32)],
        in_specs=anywhere(len(weights)),
        out_specs=vmem(len(weights) + 2),
        scratch_shapes=[pltpu.SemaphoreType.DMA((len(weights),))],
        compiler_params=params,
        cost_estimate=pl.CostEstimate(
            flops=2 * count * width * (3 * width + 2 * count), bytes_accessed=4 * MIB, transcendentals=0
        ),
        name="own",
    )(*in_hbm(weights))
    tok_v, qkv_v, gain_attn_v, scale_v, up_v, gain_c_v, scale_c_v = weights[:7]
    out_v, gain_ffn_v, ffn_in_v = weights[7:]

    across_edge, within_edge = pl.pallas_call(
        functools.partial(edge_kernel, rows, cols, axes),
        out_shape=[pltpu.VMEM((side, width), BF)] * 2,
        in_specs=vmem(4),
        out_specs=vmem(2),
        compiler_params=params,
        name="edges",
    )(*in_vmem([tok_v, across, within, query]))
    across_side = swapped(across_edge, "wa", 1)
    within_side = swapped(within_edge, "wa", 0)

    merged = pl.pallas_call(
        merge_kernel,
        out_shape=pltpu.VMEM((width, 2 * width_c), BF),
        in_specs=vmem(3) + anywhere(1),
        out_specs=vmem(1)[0],
        scratch_shapes=[pltpu.VMEM((width_c, 2 * width_c), BF), pltpu.SemaphoreType.DMA((8,))],
        compiler_params=params,
        cost_estimate=pl.CostEstimate(
            flops=4 * width * width_c * width_c, bytes_accessed=6 * MIB, transcendentals=0
        ),
        name="merge",
    )(*in_vmem([within_edge, up_v, gain_c_v]), *in_hbm([qkv_coarse]))

    def fine_body(tok_ref, *refs):
        fine_kernel(rows, cols, heads, axes, tok_ref, refs[:4], *refs[4:])

    fine, pooled, query_c_v = pl.pallas_call(
        fine_body,
        out_shape=[
            pltpu.VMEM((count, width), BF),
            pltpu.VMEM((devices, width // 128, 128), F32),
            pltpu.VMEM((width_c, width_c), BF),
        ],
        in_specs=vmem(14) + anywhere(2),
        out_specs=vmem(3),
        scratch_shapes=[pltpu.VMEM(ffn_out.shape, BF), pltpu.SemaphoreType.DMA((2,))],
        compiler_params=params,
        name="fine",
    )(
        *in_vmem(
            [tok_v, across, within, across_side, within_side, query, acc, gain_attn_v, qkv_v, scale_v]
            + [out_v, gain_ffn_v, ffn_in_v, merged]
        ),
        *in_hbm([ffn_out, qkv_coarse]),
    )

    every = lax.all_to_all(pooled, axes, split_axis=0, concat_axis=0, tiled=True)
    coarse_out, fine = pl.pallas_call(
        functools.partial(coarse_kernel, axes),
        out_shape=[
            jax.ShapeDtypeStruct((1, width_c), BF),
            jax.ShapeDtypeStruct((count, width), BF),
        ],
        in_specs=vmem(7) + anywhere(1),
        out_specs=vmem(1) + anywhere(1),
        scratch_shapes=[
            pltpu.VMEM((devices, width_c), F32),
            pltpu.VMEM(out_coarse.shape, BF),
            pltpu.SemaphoreType.DMA((2,)),
        ],
        compiler_params=params,
        name="coarse",
    )(*in_vmem([every, up_v, merged, query_c_v, gain_c_v, scale_c_v, fine]), *in_hbm([out_coarse]))
    return fine.reshape(rows, cols, width), coarse_out.reshape(1, 1, width_c)


def solution(mesh):
    return jax.shard_map(
        shards,
        mesh=mesh,
        in_specs=(P("ha", "wa", None), P(), P(), P(), P(), P(), P(), P(), P(), P(), P(), P(), P()),
        out_specs=(P("ha", "wa", None), P("ha", "wa", None)),
        check_vma=False,
    )
```

```python
import functools

import jax
import jax.numpy as jnp
from jax import lax
from jax.experimental import pallas as pl
from jax.experimental.pallas import tpu as pltpu
from jax.sharding import PartitionSpec as P

HD = 64
RADIUS = 3
LOG2E = 1.4426950408889634
BIG = 2.0**30
BF = jnp.bfloat16
F32 = jnp.float32
MIB = 1 << 20


def rounded_up(value, step):
    return -(-value // step) * step


def dot(a, b):
    return jnp.dot(a, b, preferred_element_type=F32)


def dot_nt(a, b):
    return lax.dot_general(a, b, (((1,), (1,)), ((), ())), preferred_element_type=F32)


def dot_split(values, ones):
    high = values.astype(BF)
    low = (values - high.astype(F32)).astype(BF)
    return dot(high, ones) + dot(low, ones)


def same_head(rows, cols):
    shape = (rows, cols)
    left = lax.broadcasted_iota(jnp.int32, shape, 0) // HD
    right = lax.broadcasted_iota(jnp.int32, shape, 1) // HD
    return (left == right).astype(F32).astype(BF)


def head_norm(values, ones):
    return values * lax.rsqrt(dot_split(values * values, ones) * (1.0 / HD) + 1e-06)


def rms_norm(values, gain):
    mean = jnp.mean(values * values, -1, keepdims=True)
    return values * lax.rsqrt(mean + 1e-06) * gain


def copies_of(pairs, sems):
    return [pltpu.make_async_copy(src, dst, sems.at[i]) for i, (src, dst) in enumerate(pairs)]


def start_all(copies):
    for copy in copies:
        copy.start()


def wait_all(copies):
    for copy in copies:
        copy.wait()


def strip_kernel(rows, cols, axis, tok_hbm, across_ref, within_ref, sems):
    count, strip = rows * cols, RADIUS * cols
    odd = lax.axis_index(axis) % 2
    last = count - strip
    first = pl.multiple_of(odd * last, 16)
    second = pl.multiple_of((1 - odd) * last, 16)
    copies = copies_of(
        [
            (tok_hbm.at[pl.ds(first, strip), :], across_ref),
            (tok_hbm.at[pl.ds(second, strip), :], within_ref),
        ],
        sems,
    )
    start_all(copies)
    wait_all(copies)


def edge_kernel(rows, cols, axes, tok_ref, across_ref, within_ref, after_ref, across_out, within_out):
    height = rows + 2 * RADIUS
    strip = RADIUS * cols
    padded = across_out.shape[0]
    odd, odd_col = lax.axis_index(axes[0]) % 2, lax.axis_index(axes[1]) % 2
    block = jnp.concatenate([tok_ref[...], across_ref[...], within_ref[...]], 0)
    out = lax.broadcasted_iota(jnp.int32, (padded, 1), 0)
    src = lax.broadcasted_iota(jnp.int32, (padded, block.shape[0]), 1)
    row = ((out * 21846) >> 16) - RADIUS
    col = out - 3 * (row + RADIUS)
    above = rows * cols + strip * odd + RADIUS * cols
    below = rows * cols + strip * (1 - odd) - rows * cols
    first = row * cols + col + jnp.where(row < 0, above, jnp.where(row >= rows, below, 0))
    first = jnp.where(out < height * RADIUS, first, -2 * cols)
    far = cols - RADIUS
    pick = jnp.where(src == first + far * odd_col, 1.0, 0.0).astype(BF)
    across_out[...] = dot(pick, block).astype(BF)
    pick = jnp.where(src == first + far * (1 - odd_col), 1.0, 0.0).astype(BF)
    within_out[...] = dot(pick, block).astype(BF)


def merge_kernel(after_ref, up_ref, gain_ref, scale_ref, qkv_hbm, merged_ref, scale_out, weight_ref, sems):
    blocks = sems.shape[0]
    size = merged_ref.shape[1] // blocks
    spans = [pl.ds(i * size, size) for i in range(blocks)]
    copies = copies_of([(qkv_hbm.at[:, span], weight_ref.at[:, span]) for span in spans], sems)
    start_all(copies[:2])
    lane = lax.broadcasted_iota(jnp.int32, scale_out.shape, 1) // HD
    scales = jnp.zeros(scale_out.shape, F32)
    for head in range(scale_ref.shape[1]):
        scales = jnp.where(lane == head, scale_ref[0:1, head : head + 1], scales)
    scale_out[...] = scales * (1.0 / HD)
    scaled = (up_ref[...].astype(F32) * gain_ref[...]).astype(BF)
    for i, span in enumerate(spans):
        copies[i].wait()
        start_all(copies[i + 2 : i + 3])
        merged_ref[:, span] = dot(scaled, weight_ref[:, span]).astype(BF)


def half_lanes():
    return lax.broadcasted_iota(jnp.int32, (1, 2 * HD), 1) < HD


def mask_columns(rows, cols):
    place = lax.broadcasted_iota(jnp.int32, (1, 2 * HD), 1) % HD
    return place, place < rows, (place >= rows) & (place < rows + cols)


def query_columns(rows, cols):
    place, is_row, is_col = mask_columns(rows, cols)
    spot = lax.broadcasted_iota(jnp.int32, (rows * cols, 1), 0)
    hot = (is_row & (spot // cols == place)) | (is_col & (spot % cols == place - rows))
    return jnp.where(hot, 1.0, 0.0).astype(BF)


def key_columns(rows, cols, krow, kcol):
    place, is_row, is_col = mask_columns(rows, cols)
    far_row = jnp.abs(krow - place) > RADIUS
    far_col = jnp.abs(kcol - (place - rows)) > RADIUS
    return jnp.where((is_row & far_row) | (is_col & far_col), -BIG, 0.0).astype(BF)


def attend(head, query, key, value, query_mask, key_mask, factor):
    lanes = 2 * HD
    low = half_lanes()
    mine = low if head % 2 == 0 else ~low
    span = slice(head // 2 * lanes, (head // 2 + 1) * lanes)
    q = jnp.where(mine, query[:, span], query_mask)
    k = jnp.where(mine, key[:, span], key_mask)
    v = jnp.where(mine, value[:, span], jnp.ones((1, lanes), BF))
    weights = jnp.exp2(dot_nt(q, k) * (factor * (LOG2E / HD))).astype(BF)
    return dot(weights, v)


def own_kernel(rows, cols, heads, *refs):
    count = (len(refs) - 3) // 2
    outs, (query_ref, acc_ref, sems) = refs[count : 2 * count], refs[2 * count :]
    tok_ref, qkv_ref, gain_ref, scale_ref = outs[:4]
    copies = copies_of(list(zip(refs[:count], outs)), sems)
    start_all(copies)
    width = heads * HD
    ones = same_head(width, width)
    query_mask = query_columns(rows, cols)
    spot = lax.broadcasted_iota(jnp.int32, (rows * cols, 1), 0)
    key_mask = key_columns(rows, cols, spot // cols, spot % cols)
    wait_all(copies[:4])
    normed = rms_norm(tok_ref[...].astype(F32), gain_ref[...]).astype(BF)
    query = head_norm(dot(normed, qkv_ref[:, :width]), ones).astype(BF)
    key = head_norm(dot(normed, qkv_ref[:, width : 2 * width]), ones).astype(BF)
    value = dot(normed, qkv_ref[:, 2 * width :]).astype(BF)
    query_ref[...] = query
    for head in range(heads):
        factor = scale_ref[0:1, head : head + 1]
        acc_ref[head] = attend(head, query, key, value, query_mask, key_mask, factor)
    wait_all(copies[4:])


def fine_kernel(
    rows, cols, heads, axes,
    tok_ref, halo_refs, query_ref, acc_ref, gain_attn_ref, qkv_ref, scale_ref,
    out_ref, gain_ffn_ref, ffn_in_ref, ffn_out_ref, after_ref, out_c_hbm,
    fine_ref, pooled_ref, out_c_ref, sems,
):
    copies = copies_of([(out_c_hbm, out_c_ref)], sems)
    start_all(copies)
    strip = RADIUS * cols
    side = halo_refs[-1].shape[0]
    width = heads * HD
    total = 2 * strip + 2 * side
    row_axis, col_axis = axes
    row0 = lax.axis_index(row_axis) * rows
    col0 = lax.axis_index(col_axis) * cols
    grid_rows = lax.axis_size(row_axis) * rows
    grid_cols = lax.axis_size(col_axis) * cols

    halo = jnp.concatenate([ref[...] for ref in halo_refs], 0)
    normed = rms_norm(halo.astype(F32), gain_attn_ref[...]).astype(BF)
    ones = same_head(width, width)
    key = head_norm(dot(normed, qkv_ref[:, width : 2 * width]), ones).astype(BF)
    value = dot(normed, qkv_ref[:, 2 * width :]).astype(BF)

    odd, odd_col = lax.axis_index(row_axis) % 2, lax.axis_index(col_axis) % 2
    row_at = (odd * (rows + RADIUS) - RADIUS, (1 - odd) * (rows + RADIUS) - RADIUS)
    col_at = (odd_col * (cols + RADIUS) - RADIUS, (1 - odd_col) * (cols + RADIUS) - RADIUS)
    spot = lax.broadcasted_iota(jnp.int32, (total, 1), 0)
    past_first = spot - strip
    past_strips = past_first - strip
    past_third = past_strips - side
    strip_at = jnp.where(past_first >= 0, past_first, spot)
    side_at = jnp.where(past_third >= 0, past_third, past_strips)
    side_row = (side_at * 21846) >> 16
    in_strip = past_strips < 0
    krow = jnp.where(
        in_strip,
        strip_at // cols + jnp.where(past_first >= 0, row_at[1], row_at[0]),
        side_row - RADIUS,
    )
    kcol = jnp.where(
        in_strip,
        strip_at % cols,
        side_at - 3 * side_row + jnp.where(past_third >= 0, col_at[1], col_at[0]),
    )
    real = in_strip | (side_at < (rows + 2 * RADIUS) * RADIUS)
    real = real & (krow + row0 >= 0) & (krow + row0 < grid_rows)
    real = real & (kcol + col0 >= 0) & (kcol + col0 < grid_cols)
    key_mask = key_columns(rows, cols, jnp.where(real, krow, -1000), kcol)
    query_mask = query_columns(rows, cols)

    query = query_ref[...]
    low = half_lanes()
    parts = []
    for pair in range(heads // 2):
        sums = []
        for head in (2 * pair, 2 * pair + 1):
            factor = scale_ref[0:1, head : head + 1]
            sums.append(acc_ref[head] + attend(head, query, key, value, query_mask, key_mask, factor))
        top = jnp.where(low, sums[0], sums[1])
        bottom = pltpu.roll(jnp.where(low, sums[1], sums[0]), HD, 1)
        parts.append((top / bottom).astype(BF))
    attn = jnp.concatenate(parts, 1)

    h1 = (tok_ref[...].astype(F32) + dot(attn, out_ref[...])).astype(BF)
    h1_wide = h1.astype(F32)
    n2 = rms_norm(h1_wide, gain_ffn_ref[...]).astype(BF)
    hidden = ffn_out_ref.shape[0]
    gate = dot(n2, ffn_in_ref[:, :hidden])
    up = dot(n2, ffn_in_ref[:, hidden:])
    gated = (jax.nn.gelu(gate, approximate=True) * up).astype(BF)
    fine = (h1_wide + dot(gated, ffn_out_ref[...])).astype(BF)
    fine_ref[...] = fine
    pooled = jnp.mean(fine.astype(F32), 0, keepdims=True).astype(BF).astype(F32)
    for part in range(pooled_ref.shape[1]):
        pooled_ref[:, part, :] = jnp.broadcast_to(
            pooled[:, part * 128 : (part + 1) * 128], (pooled_ref.shape[0], 128)
        )
    wait_all(copies)


def coarse_kernel(
    axes, pooled_ref, up_ref, merged_ref, scale_ref, out_ref, fine_ref,
    coarse_out_ref, fine_hbm,
    query_ref, coarse_ref, sems,
):
    copies = copies_of([(fine_ref, fine_hbm)], sems)
    start_all(copies)
    width = out_ref.shape[0]
    row_axis, col_axis = axes
    mine = lax.axis_index(row_axis) * lax.axis_size(col_axis) + lax.axis_index(col_axis)
    pooled = jnp.concatenate([pooled_ref[:, part, :] for part in range(pooled_ref.shape[1])], 1).astype(BF)
    coarse = dot(pooled, up_ref[...]).astype(BF).astype(F32)
    coarse_ref[...] = coarse
    rms = lax.rsqrt(jnp.mean(coarse * coarse, -1, keepdims=True) + 1e-06)
    query_ref[...] = dot(pooled, merged_ref[:, :width]) * rms
    key = dot(pooled, merged_ref[:, width : 2 * width]) * rms
    value = dot(pooled, merged_ref[:, 2 * width :]) * rms
    query = query_ref[pl.ds(mine, 1), :]
    group = 4 * HD
    spans = [slice(at, at + group) for at in range(0, width, group)]
    tall = jnp.concatenate([key[:, span] for span in spans], 0)
    queries = [query[:, span] for span in spans]
    cross = jnp.concatenate([key[:, span] * q for span, q in zip(spans, queries)], 0)
    ones = same_head(group, group)
    query_norm = lax.rsqrt(dot_split(jnp.concatenate([q * q for q in queries], 0), ones) * (1.0 / HD) + 1e-06)
    key_norm = lax.rsqrt(dot_split(tall * tall, ones) * (1.0 / HD) + 1e-06)
    scores = dot_split(cross, ones) * key_norm
    count = key.shape[0]
    parts = []
    for at, span in enumerate(spans):
        factor = query_norm[at : at + 1] * scale_ref[:, span]
        expo = jnp.exp(scores[at * count : (at + 1) * count] * factor)
        total = jnp.sum(expo, 0, keepdims=True)
        parts.append(jnp.sum(expo * value[:, span], 0, keepdims=True) / total)
    cattn = jnp.concatenate(parts, 1).astype(BF)
    coarse_out_ref[...] = (coarse_ref[pl.ds(mine, 1), :] + dot(cattn, out_ref[...])).astype(BF)
    wait_all(copies)


def vmem(count):
    return [pl.BlockSpec(memory_space=pltpu.VMEM)] * count


def anywhere(count):
    return [pl.BlockSpec(memory_space=pl.ANY)] * count


def in_vmem(arrays):
    return [pltpu.with_memory_space_constraint(array, pltpu.VMEM) for array in arrays]


def in_hbm(arrays):
    return [pltpu.with_memory_space_constraint(array, pltpu.HBM) for array in arrays]


def shards(
    tokens, gain_attn, qkv_fine, scale_fine, out_fine, gain_ffn, ffn_in, ffn_out,
    up_proj, gain_coarse, qkv_coarse, scale_coarse, out_coarse,
):
    rows, cols, width = tokens.shape
    count = rows * cols
    strip = RADIUS * cols
    side = rounded_up((rows + 2 * RADIUS) * RADIUS, 16)
    heads = width // HD
    width_c = out_coarse.shape[0]
    devices = lax.axis_size("ha") * lax.axis_size("wa")
    axes = ("ha", "wa")
    params = pltpu.CompilerParams(vmem_limit_bytes=16 * MIB)

    def swapped(array, axis, first):
        pairs = [(i, i + 1) for i in range(first, lax.axis_size(axis) - 1, 2)]
        return lax.ppermute(array, axis, pairs + [(j, i) for i, j in pairs])

    flat = tokens.reshape(count, width)
    across, within = pl.pallas_call(
        functools.partial(strip_kernel, rows, cols, "ha"),
        out_shape=[pltpu.VMEM((strip, width), BF)] * 2,
        in_specs=anywhere(1),
        out_specs=vmem(2),
        scratch_shapes=[pltpu.SemaphoreType.DMA((2,))],
        compiler_params=params,
        name="strips",
    )(*in_hbm([flat]))
    across = swapped(across, "ha", 1)
    within = swapped(within, "ha", 0)

    weights = [
        flat, qkv_fine, gain_attn.reshape(1, -1), scale_fine.reshape(1, -1),
        up_proj, gain_coarse.reshape(1, -1), scale_coarse.reshape(1, -1),
        out_fine, gain_ffn.reshape(1, -1), ffn_in, ffn_out,
    ]
    *weights, query, acc = pl.pallas_call(
        functools.partial(own_kernel, rows, cols, heads),
        out_shape=[pltpu.VMEM(array.shape, array.dtype) for array in weights]
        + [pltpu.VMEM((count, width), BF), pltpu.VMEM((heads, count, 2 * HD), F32)],
        in_specs=anywhere(len(weights)),
        out_specs=vmem(len(weights) + 2),
        scratch_shapes=[pltpu.SemaphoreType.DMA((len(weights),))],
        compiler_params=params,
        cost_estimate=pl.CostEstimate(
            flops=2 * count * width * (3 * width + 2 * count), bytes_accessed=4 * MIB, transcendentals=0
        ),
        name="own",
    )(*in_hbm(weights))
    tok_v, qkv_v, gain_attn_v, scale_v, up_v, gain_c_v, scale_c_v = weights[:7]
    out_v, gain_ffn_v, ffn_in_v, ffn_out_v = weights[7:]

    across_edge, within_edge = pl.pallas_call(
        functools.partial(edge_kernel, rows, cols, axes),
        out_shape=[pltpu.VMEM((side, width), BF)] * 2,
        in_specs=vmem(4),
        out_specs=vmem(2),
        compiler_params=params,
        name="edges",
    )(*in_vmem([tok_v, across, within, query]))
    across_side = swapped(across_edge, "wa", 1)
    within_side = swapped(within_edge, "wa", 0)

    merged, scale_lanes = pl.pallas_call(
        merge_kernel,
        out_shape=[pltpu.VMEM((width, 3 * width_c), BF), pltpu.VMEM((1, width_c), F32)],
        in_specs=vmem(4) + anywhere(1),
        out_specs=vmem(2),
        scratch_shapes=[pltpu.VMEM(qkv_coarse.shape, BF), pltpu.SemaphoreType.DMA((3,))],
        compiler_params=params,
        cost_estimate=pl.CostEstimate(
            flops=6 * width * width_c * width_c, bytes_accessed=8 * MIB, transcendentals=0
        ),
        name="merge",
    )(*in_vmem([within_edge, up_v, gain_c_v, scale_c_v]), *in_hbm([qkv_coarse]))

    def fine_body(tok_ref, *refs):
        fine_kernel(rows, cols, heads, axes, tok_ref, refs[:4], *refs[4:])

    fine, pooled, out_c_v = pl.pallas_call(
        fine_body,
        out_shape=[
            pltpu.VMEM((count, width), BF),
            pltpu.VMEM((devices, width // 128, 128), F32),
            pltpu.VMEM(out_coarse.shape, BF),
        ],
        in_specs=vmem(15) + anywhere(1),
        out_specs=vmem(3),
        scratch_shapes=[pltpu.SemaphoreType.DMA((1,))],
        compiler_params=params,
        name="fine",
    )(
        *in_vmem(
            [tok_v, across, within, across_side, within_side, query, acc, gain_attn_v, qkv_v, scale_v]
            + [out_v, gain_ffn_v, ffn_in_v, ffn_out_v, merged]
        ),
        *in_hbm([out_coarse]),
    )

    every = lax.all_to_all(pooled, axes, split_axis=0, concat_axis=0, tiled=True)
    coarse_out, fine = pl.pallas_call(
        functools.partial(coarse_kernel, axes),
        out_shape=[
            jax.ShapeDtypeStruct((1, width_c), BF),
            jax.ShapeDtypeStruct((count, width), BF),
        ],
        in_specs=vmem(6),
        out_specs=vmem(1) + anywhere(1),
        scratch_shapes=[pltpu.VMEM((devices, width_c), F32)] * 2 + [pltpu.SemaphoreType.DMA((1,))],
        compiler_params=params,
        name="coarse",
    )(*in_vmem([every, up_v, merged, scale_lanes, out_c_v, fine]))
    return fine.reshape(rows, cols, width), coarse_out.reshape(1, 1, width_c)


def solution(mesh):
    return jax.shard_map(
        shards,
        mesh=mesh,
        in_specs=(P("ha", "wa", None), P(), P(), P(), P(), P(), P(), P(), P(), P(), P(), P(), P()),
        out_specs=(P("ha", "wa", None), P("ha", "wa", None)),
        check_vma=False,
    )
```

```python
import functools

import jax
import jax.numpy as jnp
from jax import lax
from jax.experimental import pallas as pl
from jax.experimental.pallas import tpu as pltpu
from jax.sharding import PartitionSpec as P

HD = 64
RADIUS = 3
LOG2E = 1.4426950408889634
BIG = 2.0**30
BF = jnp.bfloat16
F32 = jnp.float32
MIB = 1 << 20


def rounded_up(value, step):
    return -(-value // step) * step


def dot(a, b):
    return jnp.dot(a, b, preferred_element_type=F32)


def dot_nt(a, b):
    return lax.dot_general(a, b, (((1,), (1,)), ((), ())), preferred_element_type=F32)


def dot_split(values, ones):
    high = values.astype(BF)
    low = (values - high.astype(F32)).astype(BF)
    return dot(high, ones) + dot(low, ones)


def same_head(rows, cols):
    shape = (rows, cols)
    left = lax.broadcasted_iota(jnp.int32, shape, 0) // HD
    right = lax.broadcasted_iota(jnp.int32, shape, 1) // HD
    return (left == right).astype(F32).astype(BF)


def head_norm(values, ones):
    return values * lax.rsqrt(dot_split(values * values, ones) * (1.0 / HD) + 1e-06)


def rms_norm(values, gain):
    mean = jnp.mean(values * values, -1, keepdims=True)
    return values * lax.rsqrt(mean + 1e-06) * gain


def copies_of(pairs, sems):
    return [pltpu.make_async_copy(src, dst, sems.at[i]) for i, (src, dst) in enumerate(pairs)]


def start_all(copies):
    for copy in copies:
        copy.start()


def wait_all(copies):
    for copy in copies:
        copy.wait()


def strip_kernel(rows, cols, axis, tok_hbm, across_ref, within_ref, sems):
    count, strip = rows * cols, RADIUS * cols
    odd = lax.axis_index(axis) % 2
    last = count - strip
    first = pl.multiple_of(odd * last, 16)
    second = pl.multiple_of((1 - odd) * last, 16)
    copies = copies_of(
        [
            (tok_hbm.at[pl.ds(first, strip), :], across_ref),
            (tok_hbm.at[pl.ds(second, strip), :], within_ref),
        ],
        sems,
    )
    start_all(copies)
    wait_all(copies)


def edge_kernel(rows, cols, axes, tok_ref, across_ref, within_ref, after_ref, across_out, within_out):
    height = rows + 2 * RADIUS
    strip = RADIUS * cols
    padded = across_out.shape[0]
    odd, odd_col = lax.axis_index(axes[0]) % 2, lax.axis_index(axes[1]) % 2
    block = jnp.concatenate([tok_ref[...], across_ref[...], within_ref[...]], 0)
    out = lax.broadcasted_iota(jnp.int32, (padded, 1), 0)
    src = lax.broadcasted_iota(jnp.int32, (padded, block.shape[0]), 1)
    row = ((out * 21846) >> 16) - RADIUS
    col = out - 3 * (row + RADIUS)
    above = rows * cols + strip * odd + RADIUS * cols
    below = rows * cols + strip * (1 - odd) - rows * cols
    first = row * cols + col + jnp.where(row < 0, above, jnp.where(row >= rows, below, 0))
    first = jnp.where(out < height * RADIUS, first, -2 * cols)
    far = cols - RADIUS
    pick = jnp.where(src == first + far * odd_col, 1.0, 0.0).astype(BF)
    across_out[...] = dot(pick, block).astype(BF)
    pick = jnp.where(src == first + far * (1 - odd_col), 1.0, 0.0).astype(BF)
    within_out[...] = dot(pick, block).astype(BF)


def merge_kernel(
    after_ref, up_ref, gain_ref, scale_ref, head_ref, qkv_hbm, merged_ref, scale_out, weight_ref, total_ref, sems
):
    size = head_ref.shape[0]
    blocks = sems.shape[0]
    pairs = [(qkv_hbm.at[pl.ds((i + 1) * size, size), :], weight_ref.at[i]) for i in range(blocks)]
    copies = copies_of(pairs, sems)
    start_all(copies)
    scaled = (up_ref[...].astype(F32) * gain_ref[...]).astype(BF)
    total_ref[...] = dot(scaled[:, :size], head_ref[...])
    lane = lax.broadcasted_iota(jnp.int32, scale_out.shape, 1) // HD
    scales = jnp.zeros(scale_out.shape, F32)
    for head in range(scale_ref.shape[1]):
        scales = jnp.where(lane == head, scale_ref[0:1, head : head + 1], scales)
    scale_out[...] = scales * (1.0 / HD)
    for i, copy in enumerate(copies):
        copy.wait()
        part = dot(scaled[:, (i + 1) * size : (i + 2) * size], weight_ref[i])
        if i < blocks - 1:
            total_ref[...] += part
        else:
            merged_ref[...] = (total_ref[...] + part).astype(BF)


def half_lanes():
    return lax.broadcasted_iota(jnp.int32, (1, 2 * HD), 1) < HD


def mask_columns(rows, cols):
    place = lax.broadcasted_iota(jnp.int32, (1, 2 * HD), 1) % HD
    return place, place < rows, (place >= rows) & (place < rows + cols)


def query_columns(rows, cols):
    place, is_row, is_col = mask_columns(rows, cols)
    spot = lax.broadcasted_iota(jnp.int32, (rows * cols, 1), 0)
    hot = (is_row & (spot // cols == place)) | (is_col & (spot % cols == place - rows))
    return jnp.where(hot, 1.0, 0.0).astype(BF)


def key_columns(rows, cols, krow, kcol):
    place, is_row, is_col = mask_columns(rows, cols)
    far_row = jnp.abs(krow - place) > RADIUS
    far_col = jnp.abs(kcol - (place - rows)) > RADIUS
    return jnp.where((is_row & far_row) | (is_col & far_col), -BIG, 0.0).astype(BF)


def attend(head, query, key, value, query_mask, key_mask, factor):
    lanes = 2 * HD
    low = half_lanes()
    mine = low if head % 2 == 0 else ~low
    span = slice(head // 2 * lanes, (head // 2 + 1) * lanes)
    q = jnp.where(mine, query[:, span], query_mask)
    k = jnp.where(mine, key[:, span], key_mask)
    v = jnp.where(mine, value[:, span], jnp.ones((1, lanes), BF))
    weights = jnp.exp2(dot_nt(q, k) * (factor * (LOG2E / HD))).astype(BF)
    return dot(weights, v)


def own_kernel(rows, cols, heads, *refs):
    count = (len(refs) - 5) // 2
    ins, qkv_c_hbm, outs = refs[:count], refs[count], refs[count + 1 : 2 * count + 1]
    head_ref, query_ref, acc_ref, sems = refs[2 * count + 1 :]
    tok_ref, qkv_ref, gain_ref, scale_ref = outs[:4]
    head = (qkv_c_hbm.at[pl.ds(0, head_ref.shape[0]), :], head_ref)
    copies = copies_of(list(zip(ins, outs)) + [head], sems)
    start_all(copies)
    width = heads * HD
    ones = same_head(width, width)
    query_mask = query_columns(rows, cols)
    spot = lax.broadcasted_iota(jnp.int32, (rows * cols, 1), 0)
    key_mask = key_columns(rows, cols, spot // cols, spot % cols)
    wait_all(copies[:4])
    normed = rms_norm(tok_ref[...].astype(F32), gain_ref[...]).astype(BF)
    query = head_norm(dot(normed, qkv_ref[:, :width]), ones).astype(BF)
    key = head_norm(dot(normed, qkv_ref[:, width : 2 * width]), ones).astype(BF)
    value = dot(normed, qkv_ref[:, 2 * width :]).astype(BF)
    query_ref[...] = query
    for head in range(heads):
        factor = scale_ref[0:1, head : head + 1]
        acc_ref[head] = attend(head, query, key, value, query_mask, key_mask, factor)
    wait_all(copies[4:])


def fine_kernel(
    rows, cols, heads, axes,
    tok_ref, halo_refs, query_ref, acc_ref, gain_attn_ref, qkv_ref, scale_ref,
    out_ref, gain_ffn_ref, ffn_in_ref, ffn_out_ref, after_ref, out_c_hbm,
    fine_ref, pooled_ref, out_c_ref, sems,
):
    copies = copies_of([(out_c_hbm, out_c_ref)], sems)
    start_all(copies)
    strip = RADIUS * cols
    side = halo_refs[-1].shape[0]
    width = heads * HD
    total = 2 * strip + 2 * side
    row_axis, col_axis = axes
    row0 = lax.axis_index(row_axis) * rows
    col0 = lax.axis_index(col_axis) * cols
    grid_rows = lax.axis_size(row_axis) * rows
    grid_cols = lax.axis_size(col_axis) * cols

    halo = jnp.concatenate([ref[...] for ref in halo_refs], 0)
    normed = rms_norm(halo.astype(F32), gain_attn_ref[...]).astype(BF)
    ones = same_head(width, width)
    key = head_norm(dot(normed, qkv_ref[:, width : 2 * width]), ones).astype(BF)
    value = dot(normed, qkv_ref[:, 2 * width :]).astype(BF)

    odd, odd_col = lax.axis_index(row_axis) % 2, lax.axis_index(col_axis) % 2
    row_at = (odd * (rows + RADIUS) - RADIUS, (1 - odd) * (rows + RADIUS) - RADIUS)
    col_at = (odd_col * (cols + RADIUS) - RADIUS, (1 - odd_col) * (cols + RADIUS) - RADIUS)
    spot = lax.broadcasted_iota(jnp.int32, (total, 1), 0)
    past_first = spot - strip
    past_strips = past_first - strip
    past_third = past_strips - side
    strip_at = jnp.where(past_first >= 0, past_first, spot)
    side_at = jnp.where(past_third >= 0, past_third, past_strips)
    side_row = (side_at * 21846) >> 16
    in_strip = past_strips < 0
    krow = jnp.where(
        in_strip,
        strip_at // cols + jnp.where(past_first >= 0, row_at[1], row_at[0]),
        side_row - RADIUS,
    )
    kcol = jnp.where(
        in_strip,
        strip_at % cols,
        side_at - 3 * side_row + jnp.where(past_third >= 0, col_at[1], col_at[0]),
    )
    real = in_strip | (side_at < (rows + 2 * RADIUS) * RADIUS)
    real = real & (krow + row0 >= 0) & (krow + row0 < grid_rows)
    real = real & (kcol + col0 >= 0) & (kcol + col0 < grid_cols)
    key_mask = key_columns(rows, cols, jnp.where(real, krow, -1000), kcol)
    query_mask = query_columns(rows, cols)

    query = query_ref[...]
    low = half_lanes()
    parts = []
    for pair in range(heads // 2):
        sums = []
        for head in (2 * pair, 2 * pair + 1):
            factor = scale_ref[0:1, head : head + 1]
            sums.append(acc_ref[head] + attend(head, query, key, value, query_mask, key_mask, factor))
        top = jnp.where(low, sums[0], sums[1])
        bottom = pltpu.roll(jnp.where(low, sums[1], sums[0]), HD, 1)
        parts.append((top / bottom).astype(BF))
    attn = jnp.concatenate(parts, 1)

    h1 = (tok_ref[...].astype(F32) + dot(attn, out_ref[...])).astype(BF)
    h1_wide = h1.astype(F32)
    n2 = rms_norm(h1_wide, gain_ffn_ref[...]).astype(BF)
    hidden = ffn_out_ref.shape[0]
    gate = dot(n2, ffn_in_ref[:, :hidden])
    up = dot(n2, ffn_in_ref[:, hidden:])
    gated = (jax.nn.gelu(gate, approximate=True) * up).astype(BF)
    fine = (h1_wide + dot(gated, ffn_out_ref[...])).astype(BF)
    fine_ref[...] = fine
    pooled = jnp.mean(fine.astype(F32), 0, keepdims=True).astype(BF).astype(F32)
    for part in range(pooled_ref.shape[1]):
        pooled_ref[:, part, :] = jnp.broadcast_to(
            pooled[:, part * 128 : (part + 1) * 128], (pooled_ref.shape[0], 128)
        )
    wait_all(copies)


def coarse_kernel(
    axes, pooled_ref, up_ref, merged_ref, scale_ref, out_ref, fine_ref,
    coarse_out_ref, fine_hbm,
    query_ref, coarse_ref, sems,
):
    copies = copies_of([(fine_ref, fine_hbm)], sems)
    start_all(copies)
    width = out_ref.shape[0]
    row_axis, col_axis = axes
    mine = lax.axis_index(row_axis) * lax.axis_size(col_axis) + lax.axis_index(col_axis)
    pooled = jnp.concatenate([pooled_ref[:, part, :] for part in range(pooled_ref.shape[1])], 1).astype(BF)
    coarse = dot(pooled, up_ref[...]).astype(BF).astype(F32)
    coarse_ref[...] = coarse
    rms = lax.rsqrt(jnp.mean(coarse * coarse, -1, keepdims=True) + 1e-06)
    query_ref[...] = dot(pooled, merged_ref[:, :width]) * rms
    key = dot(pooled, merged_ref[:, width : 2 * width]) * rms
    value = dot(pooled, merged_ref[:, 2 * width :]) * rms
    query = query_ref[pl.ds(mine, 1), :]
    group = 4 * HD
    spans = [slice(at, at + group) for at in range(0, width, group)]
    tall = jnp.concatenate([key[:, span] for span in spans], 0)
    queries = [query[:, span] for span in spans]
    cross = jnp.concatenate([key[:, span] * q for span, q in zip(spans, queries)], 0)
    ones = same_head(group, group)
    query_norm = lax.rsqrt(dot_split(jnp.concatenate([q * q for q in queries], 0), ones) * (1.0 / HD) + 1e-06)
    key_norm = lax.rsqrt(dot_split(tall * tall, ones) * (1.0 / HD) + 1e-06)
    scores = dot_split(cross, ones) * key_norm
    count = key.shape[0]
    parts = []
    for at, span in enumerate(spans):
        factor = query_norm[at : at + 1] * scale_ref[:, span]
        expo = jnp.exp(scores[at * count : (at + 1) * count] * factor)
        total = jnp.sum(expo, 0, keepdims=True)
        parts.append(jnp.sum(expo * value[:, span], 0, keepdims=True) / total)
    cattn = jnp.concatenate(parts, 1).astype(BF)
    coarse_out_ref[...] = (coarse_ref[pl.ds(mine, 1), :] + dot(cattn, out_ref[...])).astype(BF)
    wait_all(copies)


def vmem(count):
    return [pl.BlockSpec(memory_space=pltpu.VMEM)] * count


def anywhere(count):
    return [pl.BlockSpec(memory_space=pl.ANY)] * count


def in_vmem(arrays):
    return [pltpu.with_memory_space_constraint(array, pltpu.VMEM) for array in arrays]


def in_hbm(arrays):
    return [pltpu.with_memory_space_constraint(array, pltpu.HBM) for array in arrays]


def shards(
    tokens, gain_attn, qkv_fine, scale_fine, out_fine, gain_ffn, ffn_in, ffn_out,
    up_proj, gain_coarse, qkv_coarse, scale_coarse, out_coarse,
):
    rows, cols, width = tokens.shape
    count = rows * cols
    strip = RADIUS * cols
    side = rounded_up((rows + 2 * RADIUS) * RADIUS, 16)
    heads = width // HD
    width_c = out_coarse.shape[0]
    devices = lax.axis_size("ha") * lax.axis_size("wa")
    axes = ("ha", "wa")
    params = pltpu.CompilerParams(vmem_limit_bytes=16 * MIB)

    def swapped(array, axis, first):
        pairs = [(i, i + 1) for i in range(first, lax.axis_size(axis) - 1, 2)]
        return lax.ppermute(array, axis, pairs + [(j, i) for i, j in pairs])

    flat = tokens.reshape(count, width)
    across, within = pl.pallas_call(
        functools.partial(strip_kernel, rows, cols, "ha"),
        out_shape=[pltpu.VMEM((strip, width), BF)] * 2,
        in_specs=anywhere(1),
        out_specs=vmem(2),
        scratch_shapes=[pltpu.SemaphoreType.DMA((2,))],
        compiler_params=params,
        name="strips",
    )(*in_hbm([flat]))
    across = swapped(across, "ha", 1)
    within = swapped(within, "ha", 0)

    block = 256
    weights = [
        flat, qkv_fine, gain_attn.reshape(1, -1), scale_fine.reshape(1, -1),
        up_proj, gain_coarse.reshape(1, -1), scale_coarse.reshape(1, -1),
        out_fine, gain_ffn.reshape(1, -1), ffn_in, ffn_out,
    ]
    *weights, head, query, acc = pl.pallas_call(
        functools.partial(own_kernel, rows, cols, heads),
        out_shape=[pltpu.VMEM(array.shape, array.dtype) for array in weights]
        + [
            pltpu.VMEM((block, 3 * width_c), BF),
            pltpu.VMEM((count, width), BF),
            pltpu.VMEM((heads, count, 2 * HD), F32),
        ],
        in_specs=anywhere(len(weights) + 1),
        out_specs=vmem(len(weights) + 3),
        scratch_shapes=[pltpu.SemaphoreType.DMA((len(weights) + 1,))],
        compiler_params=params,
        cost_estimate=pl.CostEstimate(
            flops=2 * count * width * (3 * width + 2 * count), bytes_accessed=4 * MIB, transcendentals=0
        ),
        name="own",
    )(*in_hbm(weights + [qkv_coarse]))
    tok_v, qkv_v, gain_attn_v, scale_v, up_v, gain_c_v, scale_c_v = weights[:7]
    out_v, gain_ffn_v, ffn_in_v, ffn_out_v = weights[7:]

    across_edge, within_edge = pl.pallas_call(
        functools.partial(edge_kernel, rows, cols, axes),
        out_shape=[pltpu.VMEM((side, width), BF)] * 2,
        in_specs=vmem(4),
        out_specs=vmem(2),
        compiler_params=params,
        name="edges",
    )(*in_vmem([tok_v, across, within, query]))
    across_side = swapped(across_edge, "wa", 1)
    within_side = swapped(within_edge, "wa", 0)

    merged, scale_lanes = pl.pallas_call(
        merge_kernel,
        out_shape=[pltpu.VMEM((width, 3 * width_c), BF), pltpu.VMEM((1, width_c), F32)],
        in_specs=vmem(5) + anywhere(1),
        out_specs=vmem(2),
        scratch_shapes=[
            pltpu.VMEM((width_c // block - 1, block, 3 * width_c), BF),
            pltpu.VMEM((width, 3 * width_c), F32),
            pltpu.SemaphoreType.DMA((width_c // block - 1,)),
        ],
        compiler_params=params,
        cost_estimate=pl.CostEstimate(
            flops=6 * width * width_c * width_c, bytes_accessed=8 * MIB, transcendentals=0
        ),
        name="merge",
    )(*in_vmem([within_edge, up_v, gain_c_v, scale_c_v, head]), *in_hbm([qkv_coarse]))

    def fine_body(tok_ref, *refs):
        fine_kernel(rows, cols, heads, axes, tok_ref, refs[:4], *refs[4:])

    fine, pooled, out_c_v = pl.pallas_call(
        fine_body,
        out_shape=[
            pltpu.VMEM((count, width), BF),
            pltpu.VMEM((devices, width // 128, 128), F32),
            pltpu.VMEM(out_coarse.shape, BF),
        ],
        in_specs=vmem(15) + anywhere(1),
        out_specs=vmem(3),
        scratch_shapes=[pltpu.SemaphoreType.DMA((1,))],
        compiler_params=params,
        name="fine",
    )(
        *in_vmem(
            [tok_v, across, within, across_side, within_side, query, acc, gain_attn_v, qkv_v, scale_v]
            + [out_v, gain_ffn_v, ffn_in_v, ffn_out_v, merged]
        ),
        *in_hbm([out_coarse]),
    )

    every = lax.all_to_all(pooled, axes, split_axis=0, concat_axis=0, tiled=True)
    coarse_out, fine = pl.pallas_call(
        functools.partial(coarse_kernel, axes),
        out_shape=[
            jax.ShapeDtypeStruct((1, width_c), BF),
            jax.ShapeDtypeStruct((count, width), BF),
        ],
        in_specs=vmem(6),
        out_specs=vmem(1) + anywhere(1),
        scratch_shapes=[pltpu.VMEM((devices, width_c), F32)] * 2 + [pltpu.SemaphoreType.DMA((1,))],
        compiler_params=params,
        name="coarse",
    )(*in_vmem([every, up_v, merged, scale_lanes, out_c_v, fine]))
    return fine.reshape(rows, cols, width), coarse_out.reshape(1, 1, width_c)


def solution(mesh):
    return jax.shard_map(
        shards,
        mesh=mesh,
        in_specs=(P("ha", "wa", None), P(), P(), P(), P(), P(), P(), P(), P(), P(), P(), P(), P()),
        out_specs=(P("ha", "wa", None), P("ha", "wa", None)),
        check_vma=False,
    )
```

```python
import functools

import jax
import jax.numpy as jnp
from jax import lax
from jax.experimental import pallas as pl
from jax.experimental.pallas import tpu as pltpu
from jax.sharding import PartitionSpec as P

HD = 64
RADIUS = 3
LOG2E = 1.4426950408889634
BIG = 2.0**30
BF = jnp.bfloat16
F32 = jnp.float32
MIB = 1 << 20


def rounded_up(value, step):
    return -(-value // step) * step


def dot(a, b):
    return jnp.dot(a, b, preferred_element_type=F32)


def dot_nt(a, b):
    return lax.dot_general(a, b, (((1,), (1,)), ((), ())), preferred_element_type=F32)


def dot_split(values, ones):
    high = values.astype(BF)
    low = (values - high.astype(F32)).astype(BF)
    return dot(high, ones) + dot(low, ones)


def same_head(rows, cols):
    shape = (rows, cols)
    left = lax.broadcasted_iota(jnp.int32, shape, 0) // HD
    right = lax.broadcasted_iota(jnp.int32, shape, 1) // HD
    return (left == right).astype(F32).astype(BF)


def head_norm(values, ones):
    return values * lax.rsqrt(dot_split(values * values, ones) * (1.0 / HD) + 1e-06)


def rms_factor(values):
    return lax.rsqrt(jnp.mean(values * values, -1, keepdims=True) + 1e-06)


def rms_norm(values, gain):
    return values * rms_factor(values) * gain


def head_factor(squares, factor):
    return factor * lax.rsqrt(squares * (factor * factor * (1.0 / HD)) + 1e-06)


def copies_of(pairs, sems):
    return [pltpu.make_async_copy(src, dst, sems.at[i]) for i, (src, dst) in enumerate(pairs)]


def start_all(copies):
    for copy in copies:
        copy.start()


def wait_all(copies):
    for copy in copies:
        copy.wait()


def strip_kernel(rows, cols, axis, tok_hbm, across_ref, within_ref, sems):
    count, strip = rows * cols, RADIUS * cols
    odd = lax.axis_index(axis) % 2
    last = count - strip
    first = pl.multiple_of(odd * last, 16)
    second = pl.multiple_of((1 - odd) * last, 16)
    copies = copies_of(
        [
            (tok_hbm.at[pl.ds(first, strip), :], across_ref),
            (tok_hbm.at[pl.ds(second, strip), :], within_ref),
        ],
        sems,
    )
    start_all(copies)
    wait_all(copies)


def edge_kernel(rows, cols, axes, tok_ref, across_ref, within_ref, after_ref, across_out, within_out):
    height = rows + 2 * RADIUS
    strip = RADIUS * cols
    padded = across_out.shape[0]
    odd, odd_col = lax.axis_index(axes[0]) % 2, lax.axis_index(axes[1]) % 2
    block = jnp.concatenate([tok_ref[...], across_ref[...], within_ref[...]], 0)
    out = lax.broadcasted_iota(jnp.int32, (padded, 1), 0)
    src = lax.broadcasted_iota(jnp.int32, (padded, block.shape[0]), 1)
    row = ((out * 21846) >> 16) - RADIUS
    col = out - 3 * (row + RADIUS)
    above = rows * cols + strip * odd + RADIUS * cols
    below = rows * cols + strip * (1 - odd) - rows * cols
    first = row * cols + col + jnp.where(row < 0, above, jnp.where(row >= rows, below, 0))
    first = jnp.where(out < height * RADIUS, first, -2 * cols)
    far = cols - RADIUS
    pick = jnp.where(src == first + far * odd_col, 1.0, 0.0).astype(BF)
    across_out[...] = dot(pick, block).astype(BF)
    pick = jnp.where(src == first + far * (1 - odd_col), 1.0, 0.0).astype(BF)
    within_out[...] = dot(pick, block).astype(BF)


def merge_kernel(
    after_ref, up_ref, gain_ref, scale_ref, head_ref, qkv_hbm, merged_ref, scale_out, weight_ref, total_ref, sems
):
    size = head_ref.shape[0]
    blocks = sems.shape[0]
    pairs = [(qkv_hbm.at[pl.ds((i + 1) * size, size), :], weight_ref.at[i]) for i in range(blocks)]
    copies = copies_of(pairs, sems)
    start_all(copies)
    scaled = (up_ref[...].astype(F32) * gain_ref[...]).astype(BF)
    total_ref[...] = dot(scaled[:, :size], head_ref[...])
    lane = lax.broadcasted_iota(jnp.int32, scale_out.shape, 1) // HD
    scales = jnp.zeros(scale_out.shape, F32)
    for head in range(scale_ref.shape[1]):
        scales = jnp.where(lane == head, scale_ref[0:1, head : head + 1], scales)
    scale_out[...] = scales * (1.0 / HD)
    for i, copy in enumerate(copies):
        copy.wait()
        part = dot(scaled[:, (i + 1) * size : (i + 2) * size], weight_ref[i])
        if i < blocks - 1:
            total_ref[...] += part
        else:
            merged_ref[...] = (total_ref[...] + part).astype(BF)


def half_lanes():
    return lax.broadcasted_iota(jnp.int32, (1, 2 * HD), 1) < HD


def mask_columns(rows, cols):
    place = lax.broadcasted_iota(jnp.int32, (1, 2 * HD), 1) % HD
    return place, place < rows, (place >= rows) & (place < rows + cols)


def query_columns(rows, cols):
    place, is_row, is_col = mask_columns(rows, cols)
    spot = lax.broadcasted_iota(jnp.int32, (rows * cols, 1), 0)
    hot = (is_row & (spot // cols == place)) | (is_col & (spot % cols == place - rows))
    return jnp.where(hot, 1.0, 0.0).astype(BF)


def key_columns(rows, cols, krow, kcol):
    place, is_row, is_col = mask_columns(rows, cols)
    far_row = jnp.abs(krow - place) > RADIUS
    far_col = jnp.abs(kcol - (place - rows)) > RADIUS
    return jnp.where((is_row & far_row) | (is_col & far_col), -BIG, 0.0).astype(BF)


def attend(head, query, key, value, query_mask, key_mask, factor):
    lanes = 2 * HD
    low = half_lanes()
    mine = low if head % 2 == 0 else ~low
    span = slice(head // 2 * lanes, (head // 2 + 1) * lanes)
    q = jnp.where(mine, query[:, span], query_mask)
    k = jnp.where(mine, key[:, span], key_mask)
    v = jnp.where(mine, value[:, span], jnp.ones((1, lanes), BF))
    weights = jnp.exp2(dot_nt(q, k) * (factor * (LOG2E / HD))).astype(BF)
    return dot(weights, v)


def own_kernel(rows, cols, heads, *refs):
    count = (len(refs) - 5) // 2
    ins, qkv_c_hbm, outs = refs[:count], refs[count], refs[count + 1 : 2 * count + 1]
    head_ref, query_ref, acc_ref, sems = refs[2 * count + 1 :]
    tok_ref, qkv_ref, gain_ref, scale_ref = outs[:4]
    head = (qkv_c_hbm.at[pl.ds(0, head_ref.shape[0]), :], head_ref)
    copies = copies_of(list(zip(ins, outs)) + [head], sems)
    start_all(copies)
    width = heads * HD
    ones = same_head(width, width)
    query_mask = query_columns(rows, cols)
    spot = lax.broadcasted_iota(jnp.int32, (rows * cols, 1), 0)
    key_mask = key_columns(rows, cols, spot // cols, spot % cols)
    wait_all(copies[:4])
    normed = rms_norm(tok_ref[...].astype(F32), gain_ref[...]).astype(BF)
    query = head_norm(dot(normed, qkv_ref[:, :width]), ones).astype(BF)
    key = head_norm(dot(normed, qkv_ref[:, width : 2 * width]), ones).astype(BF)
    value = dot(normed, qkv_ref[:, 2 * width :]).astype(BF)
    query_ref[...] = query
    for head in range(heads):
        factor = scale_ref[0:1, head : head + 1]
        acc_ref[head] = attend(head, query, key, value, query_mask, key_mask, factor)
    wait_all(copies[4:])


def fine_kernel(
    rows, cols, heads, axes,
    tok_ref, halo_refs, query_ref, acc_ref, gain_attn_ref, qkv_ref, scale_ref,
    out_ref, gain_ffn_ref, ffn_in_ref, ffn_out_ref, after_ref, out_c_hbm,
    fine_ref, pooled_ref, out_c_ref, sems,
):
    copies = copies_of([(out_c_hbm, out_c_ref)], sems)
    start_all(copies)
    strip = RADIUS * cols
    side = halo_refs[-1].shape[0]
    width = heads * HD
    total = 2 * strip + 2 * side
    row_axis, col_axis = axes
    row0 = lax.axis_index(row_axis) * rows
    col0 = lax.axis_index(col_axis) * cols
    grid_rows = lax.axis_size(row_axis) * rows
    grid_cols = lax.axis_size(col_axis) * cols

    halo = jnp.concatenate([ref[...] for ref in halo_refs], 0)
    halo = halo.astype(F32)
    scaled = (halo * gain_attn_ref[...]).astype(BF)
    halo_rms = rms_factor(halo)
    ones = same_head(width, width)
    key = dot(scaled, qkv_ref[:, width : 2 * width])
    key = (key * head_factor(dot_split(key * key, ones), halo_rms)).astype(BF)
    value = (dot(scaled, qkv_ref[:, 2 * width :]) * halo_rms).astype(BF)

    odd, odd_col = lax.axis_index(row_axis) % 2, lax.axis_index(col_axis) % 2
    row_at = (odd * (rows + RADIUS) - RADIUS, (1 - odd) * (rows + RADIUS) - RADIUS)
    col_at = (odd_col * (cols + RADIUS) - RADIUS, (1 - odd_col) * (cols + RADIUS) - RADIUS)
    spot = lax.broadcasted_iota(jnp.int32, (total, 1), 0)
    past_first = spot - strip
    past_strips = past_first - strip
    past_third = past_strips - side
    strip_at = jnp.where(past_first >= 0, past_first, spot)
    side_at = jnp.where(past_third >= 0, past_third, past_strips)
    side_row = (side_at * 21846) >> 16
    in_strip = past_strips < 0
    krow = jnp.where(
        in_strip,
        strip_at // cols + jnp.where(past_first >= 0, row_at[1], row_at[0]),
        side_row - RADIUS,
    )
    kcol = jnp.where(
        in_strip,
        strip_at % cols,
        side_at - 3 * side_row + jnp.where(past_third >= 0, col_at[1], col_at[0]),
    )
    real = in_strip | (side_at < (rows + 2 * RADIUS) * RADIUS)
    real = real & (krow + row0 >= 0) & (krow + row0 < grid_rows)
    real = real & (kcol + col0 >= 0) & (kcol + col0 < grid_cols)
    key_mask = key_columns(rows, cols, jnp.where(real, krow, -1000), kcol)
    query_mask = query_columns(rows, cols)

    query = query_ref[...]
    low = half_lanes()
    parts = []
    for pair in range(heads // 2):
        sums = []
        for head in (2 * pair, 2 * pair + 1):
            factor = scale_ref[0:1, head : head + 1]
            sums.append(acc_ref[head] + attend(head, query, key, value, query_mask, key_mask, factor))
        top = jnp.where(low, sums[0], sums[1])
        bottom = pltpu.roll(jnp.where(low, sums[1], sums[0]), HD, 1)
        parts.append((top / bottom).astype(BF))
    attn = jnp.concatenate(parts, 1)

    h1 = (tok_ref[...].astype(F32) + dot(attn, out_ref[...])).astype(BF)
    h1_wide = h1.astype(F32)
    scaled = (h1_wide * gain_ffn_ref[...]).astype(BF)
    h1_rms = rms_factor(h1_wide)
    hidden = ffn_out_ref.shape[0]
    gate = dot(scaled, ffn_in_ref[:, :hidden]) * h1_rms
    up = dot(scaled, ffn_in_ref[:, hidden:]) * h1_rms
    gated = (jax.nn.gelu(gate, approximate=True) * up).astype(BF)
    fine = (h1_wide + dot(gated, ffn_out_ref[...])).astype(BF)
    fine_ref[...] = fine
    pooled = jnp.mean(fine.astype(F32), 0, keepdims=True).astype(BF).astype(F32)
    for part in range(pooled_ref.shape[1]):
        pooled_ref[:, part, :] = jnp.broadcast_to(
            pooled[:, part * 128 : (part + 1) * 128], (pooled_ref.shape[0], 128)
        )
    wait_all(copies)


def coarse_kernel(
    axes, pooled_ref, up_ref, merged_ref, scale_ref, out_ref, fine_ref,
    coarse_out_ref, fine_hbm,
    query_ref, coarse_ref, sems,
):
    copies = copies_of([(fine_ref, fine_hbm)], sems)
    start_all(copies)
    width = out_ref.shape[0]
    row_axis, col_axis = axes
    mine = lax.axis_index(row_axis) * lax.axis_size(col_axis) + lax.axis_index(col_axis)
    pooled = jnp.concatenate([pooled_ref[:, part, :] for part in range(pooled_ref.shape[1])], 1).astype(BF)
    coarse = dot(pooled, up_ref[...]).astype(BF).astype(F32)
    coarse_ref[...] = coarse
    query_ref[...] = dot(pooled, merged_ref[:, :width])
    key = dot(pooled, merged_ref[:, width : 2 * width])
    value = dot(pooled, merged_ref[:, 2 * width :])
    own = coarse_ref[pl.ds(mine, 1), :]
    query = query_ref[pl.ds(mine, 1), :]
    rms = rms_factor(coarse)
    group = 4 * HD
    spans = [slice(at, at + group) for at in range(0, width, group)]
    tall = jnp.concatenate([key[:, span] for span in spans], 0)
    queries = [query[:, span] for span in spans]
    cross = jnp.concatenate([key[:, span] * q for span, q in zip(spans, queries)], 0)
    ones = same_head(group, group)
    query_norm = head_factor(dot_split(jnp.concatenate([q * q for q in queries], 0), ones), rms_factor(own))
    key_norm = head_factor(dot_split(tall * tall, ones), jnp.concatenate([rms] * len(spans), 0))
    scores = dot_split(cross, ones) * key_norm
    count = key.shape[0]
    parts = []
    for at, span in enumerate(spans):
        factor = query_norm[at : at + 1] * scale_ref[:, span]
        expo = jnp.exp(scores[at * count : (at + 1) * count] * factor)
        total = jnp.sum(expo, 0, keepdims=True)
        parts.append(jnp.sum(expo * rms * value[:, span], 0, keepdims=True) / total)
    cattn = jnp.concatenate(parts, 1).astype(BF)
    coarse_out_ref[...] = (own + dot(cattn, out_ref[...])).astype(BF)
    wait_all(copies)


def vmem(count):
    return [pl.BlockSpec(memory_space=pltpu.VMEM)] * count


def anywhere(count):
    return [pl.BlockSpec(memory_space=pl.ANY)] * count


def in_vmem(arrays):
    return [pltpu.with_memory_space_constraint(array, pltpu.VMEM) for array in arrays]


def in_hbm(arrays):
    return [pltpu.with_memory_space_constraint(array, pltpu.HBM) for array in arrays]


def shards(
    tokens, gain_attn, qkv_fine, scale_fine, out_fine, gain_ffn, ffn_in, ffn_out,
    up_proj, gain_coarse, qkv_coarse, scale_coarse, out_coarse,
):
    rows, cols, width = tokens.shape
    count = rows * cols
    strip = RADIUS * cols
    side = rounded_up((rows + 2 * RADIUS) * RADIUS, 16)
    heads = width // HD
    width_c = out_coarse.shape[0]
    devices = lax.axis_size("ha") * lax.axis_size("wa")
    axes = ("ha", "wa")
    params = pltpu.CompilerParams(vmem_limit_bytes=16 * MIB)

    def swapped(array, axis, first):
        pairs = [(i, i + 1) for i in range(first, lax.axis_size(axis) - 1, 2)]
        return lax.ppermute(array, axis, pairs + [(j, i) for i, j in pairs])

    flat = tokens.reshape(count, width)
    across, within = pl.pallas_call(
        functools.partial(strip_kernel, rows, cols, "ha"),
        out_shape=[pltpu.VMEM((strip, width), BF)] * 2,
        in_specs=anywhere(1),
        out_specs=vmem(2),
        scratch_shapes=[pltpu.SemaphoreType.DMA((2,))],
        compiler_params=params,
        name="strips",
    )(*in_hbm([flat]))
    across = swapped(across, "ha", 1)
    within = swapped(within, "ha", 0)

    block = 256
    weights = [
        flat, qkv_fine, gain_attn.reshape(1, -1), scale_fine.reshape(1, -1),
        up_proj, gain_coarse.reshape(1, -1), scale_coarse.reshape(1, -1),
        out_fine, gain_ffn.reshape(1, -1), ffn_in, ffn_out,
    ]
    *weights, head, query, acc = pl.pallas_call(
        functools.partial(own_kernel, rows, cols, heads),
        out_shape=[pltpu.VMEM(array.shape, array.dtype) for array in weights]
        + [
            pltpu.VMEM((block, 3 * width_c), BF),
            pltpu.VMEM((count, width), BF),
            pltpu.VMEM((heads, count, 2 * HD), F32),
        ],
        in_specs=anywhere(len(weights) + 1),
        out_specs=vmem(len(weights) + 3),
        scratch_shapes=[pltpu.SemaphoreType.DMA((len(weights) + 1,))],
        compiler_params=params,
        cost_estimate=pl.CostEstimate(
            flops=2 * count * width * (3 * width + 2 * count), bytes_accessed=4 * MIB, transcendentals=0
        ),
        name="own",
    )(*in_hbm(weights + [qkv_coarse]))
    tok_v, qkv_v, gain_attn_v, scale_v, up_v, gain_c_v, scale_c_v = weights[:7]
    out_v, gain_ffn_v, ffn_in_v, ffn_out_v = weights[7:]

    across_edge, within_edge = pl.pallas_call(
        functools.partial(edge_kernel, rows, cols, axes),
        out_shape=[pltpu.VMEM((side, width), BF)] * 2,
        in_specs=vmem(4),
        out_specs=vmem(2),
        compiler_params=params,
        name="edges",
    )(*in_vmem([tok_v, across, within, query]))
    across_side = swapped(across_edge, "wa", 1)
    within_side = swapped(within_edge, "wa", 0)

    merged, scale_lanes = pl.pallas_call(
        merge_kernel,
        out_shape=[pltpu.VMEM((width, 3 * width_c), BF), pltpu.VMEM((1, width_c), F32)],
        in_specs=vmem(5) + anywhere(1),
        out_specs=vmem(2),
        scratch_shapes=[
            pltpu.VMEM((width_c // block - 1, block, 3 * width_c), BF),
            pltpu.VMEM((width, 3 * width_c), F32),
            pltpu.SemaphoreType.DMA((width_c // block - 1,)),
        ],
        compiler_params=params,
        cost_estimate=pl.CostEstimate(
            flops=6 * width * width_c * width_c, bytes_accessed=8 * MIB, transcendentals=0
        ),
        name="merge",
    )(*in_vmem([within_edge, up_v, gain_c_v, scale_c_v, head]), *in_hbm([qkv_coarse]))

    def fine_body(tok_ref, *refs):
        fine_kernel(rows, cols, heads, axes, tok_ref, refs[:4], *refs[4:])

    fine, pooled, out_c_v = pl.pallas_call(
        fine_body,
        out_shape=[
            pltpu.VMEM((count, width), BF),
            pltpu.VMEM((devices, width // 128, 128), F32),
            pltpu.VMEM(out_coarse.shape, BF),
        ],
        in_specs=vmem(15) + anywhere(1),
        out_specs=vmem(3),
        scratch_shapes=[pltpu.SemaphoreType.DMA((1,))],
        compiler_params=params,
        name="fine",
    )(
        *in_vmem(
            [tok_v, across, within, across_side, within_side, query, acc, gain_attn_v, qkv_v, scale_v]
            + [out_v, gain_ffn_v, ffn_in_v, ffn_out_v, merged]
        ),
        *in_hbm([out_coarse]),
    )

    every = lax.all_to_all(pooled, axes, split_axis=0, concat_axis=0, tiled=True)
    coarse_out, fine = pl.pallas_call(
        functools.partial(coarse_kernel, axes),
        out_shape=[
            jax.ShapeDtypeStruct((1, width_c), BF),
            jax.ShapeDtypeStruct((count, width), BF),
        ],
        in_specs=vmem(6),
        out_specs=vmem(1) + anywhere(1),
        scratch_shapes=[pltpu.VMEM((devices, width_c), F32)] * 2 + [pltpu.SemaphoreType.DMA((1,))],
        compiler_params=params,
        name="coarse",
    )(*in_vmem([every, up_v, merged, scale_lanes, out_c_v, fine]))
    return fine.reshape(rows, cols, width), coarse_out.reshape(1, 1, width_c)


def solution(mesh):
    return jax.shard_map(
        shards,
        mesh=mesh,
        in_specs=(P("ha", "wa", None), P(), P(), P(), P(), P(), P(), P(), P(), P(), P(), P(), P()),
        out_specs=(P("ha", "wa", None), P("ha", "wa", None)),
        check_vma=False,
    )
```

```python
import functools

import jax
import jax.numpy as jnp
from jax import lax
from jax.experimental import pallas as pl
from jax.experimental.pallas import tpu as pltpu
from jax.sharding import PartitionSpec as P

HD = 64
RADIUS = 3
LOG2E = 1.4426950408889634
BIG = 2.0**30
BF = jnp.bfloat16
F32 = jnp.float32
MIB = 1 << 20


def rounded_up(value, step):
    return -(-value // step) * step


def over(values, size):
    assert size & (size - 1) == 0
    return values >> (size.bit_length() - 1)


def dot(a, b):
    return jnp.dot(a, b, preferred_element_type=F32)


def dot_nt(a, b):
    return lax.dot_general(a, b, (((1,), (1,)), ((), ())), preferred_element_type=F32)


def dot_split(values, ones):
    high = values.astype(BF)
    low = (values - high.astype(F32)).astype(BF)
    return dot(high, ones) + dot(low, ones)


def same_head(size):
    left = over(lax.broadcasted_iota(jnp.int32, (size, 1), 0), HD)
    right = over(lax.broadcasted_iota(jnp.int32, (1, size), 1), HD)
    return jnp.where(left == right, 1.0, 0.0).astype(BF)


def head_norm(values, ones):
    return values * lax.rsqrt(dot_split(values * values, ones) * (1.0 / HD) + 1e-06)


def rms_factor(values):
    return lax.rsqrt(jnp.mean(values * values, -1, keepdims=True) + 1e-06)


def rms_norm(values, gain):
    return values * rms_factor(values) * gain


def head_factor(squares, factor):
    return factor * lax.rsqrt(squares * (factor * factor * (1.0 / HD)) + 1e-06)


def copies_of(pairs, sems):
    return [pltpu.make_async_copy(src, dst, sems.at[i]) for i, (src, dst) in enumerate(pairs)]


def start_all(copies):
    for copy in copies:
        copy.start()


def wait_all(copies):
    for copy in copies:
        copy.wait()


def strip_kernel(rows, cols, axis, tok_hbm, across_ref, within_ref, sems):
    count, strip = rows * cols, RADIUS * cols
    odd = lax.axis_index(axis) & 1
    last = count - strip
    first = pl.multiple_of(odd * last, 16)
    second = pl.multiple_of((1 - odd) * last, 16)
    copies = copies_of(
        [
            (tok_hbm.at[pl.ds(first, strip), :], across_ref),
            (tok_hbm.at[pl.ds(second, strip), :], within_ref),
        ],
        sems,
    )
    start_all(copies)
    wait_all(copies)


def edge_kernel(rows, cols, axes, tok_ref, across_ref, within_ref, after_ref, across_out, within_out):
    height = rows + 2 * RADIUS
    strip = RADIUS * cols
    padded = across_out.shape[0]
    odd, odd_col = lax.axis_index(axes[0]) & 1, lax.axis_index(axes[1]) & 1
    block = jnp.concatenate([tok_ref[...], across_ref[...], within_ref[...]], 0)
    out = lax.broadcasted_iota(jnp.int32, (padded, 1), 0)
    src = lax.broadcasted_iota(jnp.int32, (padded, block.shape[0]), 1)
    row = ((out * 21846) >> 16) - RADIUS
    col = out - 3 * (row + RADIUS)
    above = rows * cols + strip * odd + RADIUS * cols
    below = rows * cols + strip * (1 - odd) - rows * cols
    first = row * cols + col + jnp.where(row < 0, above, jnp.where(row >= rows, below, 0))
    first = jnp.where(out < height * RADIUS, first, -2 * cols)
    far = cols - RADIUS
    pick = jnp.where(src == first + far * odd_col, 1.0, 0.0).astype(BF)
    across_out[...] = dot(pick, block).astype(BF)
    pick = jnp.where(src == first + far * (1 - odd_col), 1.0, 0.0).astype(BF)
    within_out[...] = dot(pick, block).astype(BF)


def merge_kernel(
    after_ref, up_ref, gain_ref, scale_ref, head_ref, qkv_hbm, merged_ref, scale_out, weight_ref, total_ref, sems
):
    size = head_ref.shape[0]
    blocks = sems.shape[0]
    pairs = [(qkv_hbm.at[pl.ds((i + 1) * size, size), :], weight_ref.at[i]) for i in range(blocks)]
    copies = copies_of(pairs, sems)
    start_all(copies)
    scaled = (up_ref[...].astype(F32) * gain_ref[...]).astype(BF)
    total_ref[...] = dot(scaled[:, :size], head_ref[...])
    lane = over(lax.broadcasted_iota(jnp.int32, scale_out.shape, 1), HD)
    scales = jnp.zeros(scale_out.shape, F32)
    for head in range(scale_ref.shape[1]):
        scales = jnp.where(lane == head, scale_ref[0:1, head : head + 1], scales)
    scale_out[...] = scales * (1.0 / HD)
    for i, copy in enumerate(copies):
        copy.wait()
        part = dot(scaled[:, (i + 1) * size : (i + 2) * size], weight_ref[i])
        if i < blocks - 1:
            total_ref[...] += part
        else:
            merged_ref[...] = (total_ref[...] + part).astype(BF)


def half_lanes():
    return lax.broadcasted_iota(jnp.int32, (1, 2 * HD), 1) < HD


def mask_columns(rows, cols):
    place = lax.broadcasted_iota(jnp.int32, (1, 2 * HD), 1) & (HD - 1)
    return place, place < rows, (place >= rows) & (place < rows + cols)


def query_columns(rows, cols):
    place, is_row, is_col = mask_columns(rows, cols)
    spot = lax.broadcasted_iota(jnp.int32, (rows * cols, 1), 0)
    hot = (is_row & (over(spot, cols) == place)) | (is_col & ((spot & (cols - 1)) == place - rows))
    return jnp.where(hot, 1.0, 0.0).astype(BF)


def key_columns(rows, cols, krow, kcol):
    place, is_row, is_col = mask_columns(rows, cols)
    far_row = jnp.abs(krow - place) > RADIUS
    far_col = jnp.abs(kcol - (place - rows)) > RADIUS
    return jnp.where((is_row & far_row) | (is_col & far_col), -BIG, 0.0).astype(BF)


def halo_columns(rows, cols, side, axes):
    strip = RADIUS * cols
    row_axis, col_axis = axes
    place_row, place_col = lax.axis_index(row_axis), lax.axis_index(col_axis)
    row0, col0 = place_row * rows, place_col * cols
    grid_rows = lax.axis_size(row_axis) * rows
    grid_cols = lax.axis_size(col_axis) * cols
    odd, odd_col = place_row & 1, place_col & 1
    row_at = (odd * (rows + RADIUS) - RADIUS, (1 - odd) * (rows + RADIUS) - RADIUS)
    col_at = (odd_col * (cols + RADIUS) - RADIUS, (1 - odd_col) * (cols + RADIUS) - RADIUS)
    spot = lax.broadcasted_iota(jnp.int32, (2 * strip + 2 * side, 1), 0)
    past_first = spot - strip
    past_strips = past_first - strip
    past_third = past_strips - side
    strip_at = jnp.where(past_first >= 0, past_first, spot)
    side_at = jnp.where(past_third >= 0, past_third, past_strips)
    side_row = (side_at * 21846) >> 16
    in_strip = past_strips < 0
    krow = jnp.where(
        in_strip,
        over(strip_at, cols) + jnp.where(past_first >= 0, row_at[1], row_at[0]),
        side_row - RADIUS,
    )
    kcol = jnp.where(
        in_strip,
        strip_at & (cols - 1),
        side_at - 3 * side_row + jnp.where(past_third >= 0, col_at[1], col_at[0]),
    )
    real = in_strip | (side_at < (rows + 2 * RADIUS) * RADIUS)
    real = real & (krow + row0 >= 0) & (krow + row0 < grid_rows)
    real = real & (kcol + col0 >= 0) & (kcol + col0 < grid_cols)
    return key_columns(rows, cols, jnp.where(real, krow, -1000), kcol)


def half_of(head):
    low = half_lanes()
    lanes = 2 * HD
    return (low if head % 2 == 0 else ~low), slice(head // 2 * lanes, (head // 2 + 1) * lanes)


def attend(head, query, key, value, key_mask, factor):
    mine, span = half_of(head)
    k = jnp.where(mine, key[:, span], key_mask)
    v = jnp.where(mine, value[:, span], jnp.ones((1, 2 * HD), BF))
    weights = jnp.exp2(dot_nt(query, k) * (factor * (LOG2E / HD))).astype(BF)
    return dot(weights, v)


def own_kernel(rows, cols, heads, side, axes, *refs):
    count = (len(refs) - 7) // 2
    ins, qkv_c_hbm, outs = refs[:count], refs[count], refs[count + 1 : 2 * count + 1]
    head_ref, query_ref, acc_ref, ones_ref, mask_ref, sems = refs[2 * count + 1 :]
    tok_ref, qkv_ref, gain_ref, scale_ref = outs[:4]
    head = (qkv_c_hbm.at[pl.ds(0, head_ref.shape[0]), :], head_ref)
    copies = copies_of(list(zip(ins, outs)) + [head], sems)
    start_all(copies)
    width = heads * HD
    ones = same_head(width)
    ones_ref[...] = ones
    mask_ref[...] = halo_columns(rows, cols, side, axes)
    query_mask = query_columns(rows, cols)
    spot = lax.broadcasted_iota(jnp.int32, (rows * cols, 1), 0)
    key_mask = key_columns(rows, cols, over(spot, cols), spot & (cols - 1))
    wait_all(copies[:4])
    normed = rms_norm(tok_ref[...].astype(F32), gain_ref[...]).astype(BF)
    query = head_norm(dot(normed, qkv_ref[:, :width]), ones).astype(BF)
    key = head_norm(dot(normed, qkv_ref[:, width : 2 * width]), ones).astype(BF)
    value = dot(normed, qkv_ref[:, 2 * width :]).astype(BF)
    for head in range(heads):
        factor = scale_ref[0:1, head : head + 1]
        mine, span = half_of(head)
        masked = jnp.where(mine, query[:, span], query_mask)
        query_ref[head] = masked
        acc_ref[head] = attend(head, masked, key, value, key_mask, factor)
    wait_all(copies[4:])


def fine_kernel(
    heads,
    tok_ref, halo_refs, query_ref, acc_ref, ones_ref, mask_ref, gain_attn_ref, qkv_ref, scale_ref,
    out_ref, gain_ffn_ref, ffn_in_ref, ffn_out_ref, after_ref, out_c_hbm,
    fine_ref, pooled_ref, out_c_ref, sems,
):
    copies = copies_of([(out_c_hbm, out_c_ref)], sems)
    start_all(copies)
    width = heads * HD
    halo = jnp.concatenate([ref[...] for ref in halo_refs], 0)
    halo = halo.astype(F32)
    scaled = (halo * gain_attn_ref[...]).astype(BF)
    halo_rms = rms_factor(halo)
    ones = ones_ref[...]
    key = dot(scaled, qkv_ref[:, width : 2 * width])
    key = (key * head_factor(dot_split(key * key, ones), halo_rms)).astype(BF)
    value = (dot(scaled, qkv_ref[:, 2 * width :]) * halo_rms).astype(BF)

    key_mask = mask_ref[...]
    low = half_lanes()
    parts = []
    for pair in range(heads // 2):
        sums = []
        for head in (2 * pair, 2 * pair + 1):
            factor = scale_ref[0:1, head : head + 1]
            sums.append(acc_ref[head] + attend(head, query_ref[head], key, value, key_mask, factor))
        top = jnp.where(low, sums[0], sums[1])
        bottom = pltpu.roll(jnp.where(low, sums[1], sums[0]), HD, 1)
        parts.append((top / bottom).astype(BF))
    attn = jnp.concatenate(parts, 1)

    h1 = (tok_ref[...].astype(F32) + dot(attn, out_ref[...])).astype(BF)
    h1_wide = h1.astype(F32)
    scaled = (h1_wide * gain_ffn_ref[...]).astype(BF)
    h1_rms = rms_factor(h1_wide)
    hidden = ffn_out_ref.shape[0]
    gate = dot(scaled, ffn_in_ref[:, :hidden]) * h1_rms
    up = dot(scaled, ffn_in_ref[:, hidden:]) * h1_rms
    gated = (jax.nn.gelu(gate, approximate=True) * up).astype(BF)
    fine = (h1_wide + dot(gated, ffn_out_ref[...])).astype(BF)
    fine_ref[...] = fine
    pooled = jnp.mean(fine.astype(F32), 0, keepdims=True).astype(BF).astype(F32)
    for part in range(pooled_ref.shape[1]):
        pooled_ref[:, part, :] = jnp.broadcast_to(
            pooled[:, part * 128 : (part + 1) * 128], (pooled_ref.shape[0], 128)
        )
    wait_all(copies)


def coarse_kernel(
    axes, pooled_ref, up_ref, merged_ref, scale_ref, out_ref, fine_ref, ones_ref,
    coarse_out_ref, fine_hbm,
    query_ref, coarse_ref, sems,
):
    copies = copies_of([(fine_ref, fine_hbm)], sems)
    start_all(copies)
    width = out_ref.shape[0]
    row_axis, col_axis = axes
    mine = lax.axis_index(row_axis) * lax.axis_size(col_axis) + lax.axis_index(col_axis)
    pooled = jnp.concatenate([pooled_ref[:, part, :] for part in range(pooled_ref.shape[1])], 1).astype(BF)
    coarse = dot(pooled, up_ref[...]).astype(BF).astype(F32)
    coarse_ref[...] = coarse
    query_ref[...] = dot(pooled, merged_ref[:, :width])
    key = dot(pooled, merged_ref[:, width : 2 * width])
    value = dot(pooled, merged_ref[:, 2 * width :])
    own = coarse_ref[pl.ds(mine, 1), :]
    query = query_ref[pl.ds(mine, 1), :]
    rms = rms_factor(coarse)
    group = 4 * HD
    spans = [slice(at, at + group) for at in range(0, width, group)]
    tall = jnp.concatenate([key[:, span] for span in spans], 0)
    queries = [query[:, span] for span in spans]
    cross = jnp.concatenate([key[:, span] * q for span, q in zip(spans, queries)], 0)
    ones = ones_ref[...]
    query_norm = head_factor(dot_split(jnp.concatenate([q * q for q in queries], 0), ones), rms_factor(own))
    key_norm = head_factor(dot_split(tall * tall, ones), jnp.concatenate([rms] * len(spans), 0))
    scores = dot_split(cross, ones) * key_norm
    count = key.shape[0]
    parts = []
    for at, span in enumerate(spans):
        factor = query_norm[at : at + 1] * scale_ref[:, span]
        expo = jnp.exp(scores[at * count : (at + 1) * count] * factor)
        total = jnp.sum(expo, 0, keepdims=True)
        parts.append(jnp.sum(expo * rms * value[:, span], 0, keepdims=True) / total)
    cattn = jnp.concatenate(parts, 1).astype(BF)
    coarse_out_ref[...] = (own + dot(cattn, out_ref[...])).astype(BF)
    wait_all(copies)


def vmem(count):
    return [pl.BlockSpec(memory_space=pltpu.VMEM)] * count


def anywhere(count):
    return [pl.BlockSpec(memory_space=pl.ANY)] * count


def in_vmem(arrays):
    return [pltpu.with_memory_space_constraint(array, pltpu.VMEM) for array in arrays]


def in_hbm(arrays):
    return [pltpu.with_memory_space_constraint(array, pltpu.HBM) for array in arrays]


def shards(
    tokens, gain_attn, qkv_fine, scale_fine, out_fine, gain_ffn, ffn_in, ffn_out,
    up_proj, gain_coarse, qkv_coarse, scale_coarse, out_coarse,
):
    rows, cols, width = tokens.shape
    count = rows * cols
    strip = RADIUS * cols
    side = rounded_up((rows + 2 * RADIUS) * RADIUS, 16)
    heads = width // HD
    width_c = out_coarse.shape[0]
    devices = lax.axis_size("ha") * lax.axis_size("wa")
    axes = ("ha", "wa")
    params = pltpu.CompilerParams(vmem_limit_bytes=16 * MIB)

    def swapped(array, axis, first):
        pairs = [(i, i + 1) for i in range(first, lax.axis_size(axis) - 1, 2)]
        return lax.ppermute(array, axis, pairs + [(j, i) for i, j in pairs])

    flat = tokens.reshape(count, width)
    across, within = pl.pallas_call(
        functools.partial(strip_kernel, rows, cols, "ha"),
        out_shape=[pltpu.VMEM((strip, width), BF)] * 2,
        in_specs=anywhere(1),
        out_specs=vmem(2),
        scratch_shapes=[pltpu.SemaphoreType.DMA((2,))],
        compiler_params=params,
        name="strips",
    )(*in_hbm([flat]))
    across = swapped(across, "ha", 1)
    within = swapped(within, "ha", 0)

    block = 256
    weights = [
        flat, qkv_fine, gain_attn.reshape(1, -1), scale_fine.reshape(1, -1),
        up_proj, gain_coarse.reshape(1, -1), scale_coarse.reshape(1, -1),
        out_fine, gain_ffn.reshape(1, -1), ffn_in, ffn_out,
    ]
    *weights, head, query, acc, ones, mask = pl.pallas_call(
        functools.partial(own_kernel, rows, cols, heads, side, axes),
        out_shape=[pltpu.VMEM(array.shape, array.dtype) for array in weights]
        + [
            pltpu.VMEM((block, 3 * width_c), BF),
            pltpu.VMEM((heads, count, 2 * HD), BF),
            pltpu.VMEM((heads, count, 2 * HD), F32),
            pltpu.VMEM((4 * HD, 4 * HD), BF),
            pltpu.VMEM((2 * strip + 2 * side, 2 * HD), BF),
        ],
        in_specs=anywhere(len(weights) + 1),
        out_specs=vmem(len(weights) + 5),
        scratch_shapes=[pltpu.SemaphoreType.DMA((len(weights) + 1,))],
        compiler_params=params,
        cost_estimate=pl.CostEstimate(
            flops=2 * count * width * (3 * width + 2 * count), bytes_accessed=4 * MIB, transcendentals=0
        ),
        name="own",
    )(*in_hbm(weights + [qkv_coarse]))
    tok_v, qkv_v, gain_attn_v, scale_v, up_v, gain_c_v, scale_c_v = weights[:7]
    out_v, gain_ffn_v, ffn_in_v, ffn_out_v = weights[7:]

    across_edge, within_edge = pl.pallas_call(
        functools.partial(edge_kernel, rows, cols, axes),
        out_shape=[pltpu.VMEM((side, width), BF)] * 2,
        in_specs=vmem(4),
        out_specs=vmem(2),
        compiler_params=params,
        name="edges",
    )(*in_vmem([tok_v, across, within, query]))
    across_side = swapped(across_edge, "wa", 1)
    within_side = swapped(within_edge, "wa", 0)

    merged, scale_lanes = pl.pallas_call(
        merge_kernel,
        out_shape=[pltpu.VMEM((width, 3 * width_c), BF), pltpu.VMEM((1, width_c), F32)],
        in_specs=vmem(5) + anywhere(1),
        out_specs=vmem(2),
        scratch_shapes=[
            pltpu.VMEM((width_c // block - 1, block, 3 * width_c), BF),
            pltpu.VMEM((width, 3 * width_c), F32),
            pltpu.SemaphoreType.DMA((width_c // block - 1,)),
        ],
        compiler_params=params,
        cost_estimate=pl.CostEstimate(
            flops=6 * width * width_c * width_c, bytes_accessed=8 * MIB, transcendentals=0
        ),
        name="merge",
    )(*in_vmem([within_edge, up_v, gain_c_v, scale_c_v, head]), *in_hbm([qkv_coarse]))

    def fine_body(tok_ref, *refs):
        fine_kernel(heads, tok_ref, refs[:4], *refs[4:])

    fine, pooled, out_c_v = pl.pallas_call(
        fine_body,
        out_shape=[
            pltpu.VMEM((count, width), BF),
            pltpu.VMEM((devices, width // 128, 128), F32),
            pltpu.VMEM(out_coarse.shape, BF),
        ],
        in_specs=vmem(17) + anywhere(1),
        out_specs=vmem(3),
        scratch_shapes=[pltpu.SemaphoreType.DMA((1,))],
        compiler_params=params,
        name="fine",
    )(
        *in_vmem(
            [tok_v, across, within, across_side, within_side, query, acc, ones, mask, gain_attn_v, qkv_v, scale_v]
            + [out_v, gain_ffn_v, ffn_in_v, ffn_out_v, merged]
        ),
        *in_hbm([out_coarse]),
    )

    every = lax.all_to_all(pooled, axes, split_axis=0, concat_axis=0, tiled=True)
    coarse_out, fine = pl.pallas_call(
        functools.partial(coarse_kernel, axes),
        out_shape=[
            jax.ShapeDtypeStruct((1, width_c), BF),
            jax.ShapeDtypeStruct((count, width), BF),
        ],
        in_specs=vmem(7),
        out_specs=vmem(1) + anywhere(1),
        scratch_shapes=[pltpu.VMEM((devices, width_c), F32)] * 2 + [pltpu.SemaphoreType.DMA((1,))],
        compiler_params=params,
        name="coarse",
    )(*in_vmem([every, up_v, merged, scale_lanes, out_c_v, fine, ones]))
    return fine.reshape(rows, cols, width), coarse_out.reshape(1, 1, width_c)


def solution(mesh):
    return jax.shard_map(
        shards,
        mesh=mesh,
        in_specs=(P("ha", "wa", None), P(), P(), P(), P(), P(), P(), P(), P(), P(), P(), P(), P()),
        out_specs=(P("ha", "wa", None), P("ha", "wa", None)),
        check_vma=False,
    )
```

```python
import functools

import jax
import jax.numpy as jnp
from jax import lax
from jax.experimental import pallas as pl
from jax.experimental.pallas import tpu as pltpu
from jax.sharding import PartitionSpec as P

HD = 64
RADIUS = 3
LOG2E = 1.4426950408889634
BIG = 2.0**30
BF = jnp.bfloat16
F32 = jnp.float32
MIB = 1 << 20


def rounded_up(value, step):
    return -(-value // step) * step


def over(values, size):
    assert size & (size - 1) == 0
    return values >> (size.bit_length() - 1)


def dot(a, b):
    return jnp.dot(a, b, preferred_element_type=F32)


def dot_nt(a, b):
    return lax.dot_general(a, b, (((1,), (1,)), ((), ())), preferred_element_type=F32)


def dot_split(values, ones):
    high = values.astype(BF)
    low = (values - high.astype(F32)).astype(BF)
    return dot(high, ones) + dot(low, ones)


def same_head(size):
    left = over(lax.broadcasted_iota(jnp.int32, (size, 1), 0), HD)
    right = over(lax.broadcasted_iota(jnp.int32, (1, size), 1), HD)
    return jnp.where(left == right, 1.0, 0.0).astype(BF)


def head_norm(values, ones):
    return values * lax.rsqrt(dot_split(values * values, ones) * (1.0 / HD) + 1e-06)


def rms_factor(values):
    return lax.rsqrt(jnp.mean(values * values, -1, keepdims=True) + 1e-06)


def rms_norm(values, gain):
    return values * rms_factor(values) * gain


def head_factor(squares, factor):
    return factor * lax.rsqrt(squares * (factor * factor * (1.0 / HD)) + 1e-06)


def copies_of(pairs, sems):
    return [pltpu.make_async_copy(src, dst, sems.at[i]) for i, (src, dst) in enumerate(pairs)]


def start_all(copies):
    for copy in copies:
        copy.start()


def wait_all(copies):
    for copy in copies:
        copy.wait()


def strip_kernel(rows, cols, axis, tok_hbm, across_ref, within_ref, sems):
    count, strip = rows * cols, RADIUS * cols
    odd = lax.axis_index(axis) & 1
    last = count - strip
    first = pl.multiple_of(odd * last, 16)
    second = pl.multiple_of((1 - odd) * last, 16)
    copies = copies_of(
        [
            (tok_hbm.at[pl.ds(first, strip), :], across_ref),
            (tok_hbm.at[pl.ds(second, strip), :], within_ref),
        ],
        sems,
    )
    start_all(copies)
    wait_all(copies)


def edge_kernel(rows, cols, axes, tok_ref, across_ref, within_ref, after_ref, across_out, within_out):
    height = rows + 2 * RADIUS
    strip = RADIUS * cols
    padded = across_out.shape[0]
    odd, odd_col = lax.axis_index(axes[0]) & 1, lax.axis_index(axes[1]) & 1
    block = jnp.concatenate([tok_ref[...], across_ref[...], within_ref[...]], 0)
    out = lax.broadcasted_iota(jnp.int32, (padded, 1), 0)
    src = lax.broadcasted_iota(jnp.int32, (padded, block.shape[0]), 1)
    row = ((out * 21846) >> 16) - RADIUS
    col = out - 3 * (row + RADIUS)
    above = rows * cols + strip * odd + RADIUS * cols
    below = rows * cols + strip * (1 - odd) - rows * cols
    first = row * cols + col + jnp.where(row < 0, above, jnp.where(row >= rows, below, 0))
    first = jnp.where(out < height * RADIUS, first, -2 * cols)
    far = cols - RADIUS
    pick = jnp.where(src == first + far * odd_col, 1.0, 0.0).astype(BF)
    across_out[...] = dot(pick, block).astype(BF)
    pick = jnp.where(src == first + far * (1 - odd_col), 1.0, 0.0).astype(BF)
    within_out[...] = dot(pick, block).astype(BF)


def merge_kernel(
    after_ref, up_ref, gain_ref, scale_ref, head_ref, qkv_hbm, merged_ref, scale_out, weight_ref, total_ref, sems
):
    size = head_ref.shape[0]
    blocks = sems.shape[0]
    pairs = [(qkv_hbm.at[pl.ds((i + 1) * size, size), :], weight_ref.at[i]) for i in range(blocks)]
    copies = copies_of(pairs, sems)
    start_all(copies)
    scaled = (up_ref[...].astype(F32) * gain_ref[...]).astype(BF)
    width = merged_ref.shape[1]
    spans = [slice(at, at + 4 * HD) for at in range(0, width, 4 * HD)]
    for span in spans:
        total_ref[:, span] = dot(scaled[:, :size], head_ref[:, span])
    lane = over(lax.broadcasted_iota(jnp.int32, scale_out.shape, 1), HD)
    scales = jnp.zeros(scale_out.shape, F32)
    for head in range(scale_ref.shape[1]):
        scales = jnp.where(lane == head, scale_ref[0:1, head : head + 1], scales)
    scale_out[...] = scales * (1.0 / HD)
    for i, copy in enumerate(copies):
        copy.wait()
        rows = scaled[:, (i + 1) * size : (i + 2) * size]
        for span in spans:
            total = total_ref[:, span] + dot(rows, weight_ref[i, :, span])
            if i < blocks - 1:
                total_ref[:, span] = total
            else:
                merged_ref[:, span] = total.astype(BF)


def half_lanes():
    return lax.broadcasted_iota(jnp.int32, (1, 2 * HD), 1) < HD


def mask_columns(rows, cols):
    place = lax.broadcasted_iota(jnp.int32, (1, 2 * HD), 1) & (HD - 1)
    return place, place < rows, (place >= rows) & (place < rows + cols)


def query_columns(rows, cols):
    place, is_row, is_col = mask_columns(rows, cols)
    spot = lax.broadcasted_iota(jnp.int32, (rows * cols, 1), 0)
    hot = (is_row & (over(spot, cols) == place)) | (is_col & ((spot & (cols - 1)) == place - rows))
    return jnp.where(hot, 1.0, 0.0).astype(BF)


def key_columns(rows, cols, krow, kcol):
    place, is_row, is_col = mask_columns(rows, cols)
    far_row = jnp.abs(krow - place) > RADIUS
    far_col = jnp.abs(kcol - (place - rows)) > RADIUS
    return jnp.where((is_row & far_row) | (is_col & far_col), -BIG, 0.0).astype(BF)


def halo_columns(rows, cols, side, axes):
    strip = RADIUS * cols
    row_axis, col_axis = axes
    place_row, place_col = lax.axis_index(row_axis), lax.axis_index(col_axis)
    row0, col0 = place_row * rows, place_col * cols
    grid_rows = lax.axis_size(row_axis) * rows
    grid_cols = lax.axis_size(col_axis) * cols
    odd, odd_col = place_row & 1, place_col & 1
    row_at = (odd * (rows + RADIUS) - RADIUS, (1 - odd) * (rows + RADIUS) - RADIUS)
    col_at = (odd_col * (cols + RADIUS) - RADIUS, (1 - odd_col) * (cols + RADIUS) - RADIUS)
    spot = lax.broadcasted_iota(jnp.int32, (2 * strip + 2 * side, 1), 0)
    past_first = spot - strip
    past_strips = past_first - strip
    past_third = past_strips - side
    strip_at = jnp.where(past_first >= 0, past_first, spot)
    side_at = jnp.where(past_third >= 0, past_third, past_strips)
    side_row = (side_at * 21846) >> 16
    in_strip = past_strips < 0
    krow = jnp.where(
        in_strip,
        over(strip_at, cols) + jnp.where(past_first >= 0, row_at[1], row_at[0]),
        side_row - RADIUS,
    )
    kcol = jnp.where(
        in_strip,
        strip_at & (cols - 1),
        side_at - 3 * side_row + jnp.where(past_third >= 0, col_at[1], col_at[0]),
    )
    real = in_strip | (side_at < (rows + 2 * RADIUS) * RADIUS)
    real = real & (krow + row0 >= 0) & (krow + row0 < grid_rows)
    real = real & (kcol + col0 >= 0) & (kcol + col0 < grid_cols)
    return key_columns(rows, cols, jnp.where(real, krow, -1000), kcol)


def half_of(head):
    low = half_lanes()
    lanes = 2 * HD
    return (low if head % 2 == 0 else ~low), slice(head // 2 * lanes, (head // 2 + 1) * lanes)


def attend(head, query, key, value, key_mask, factor):
    mine, span = half_of(head)
    k = jnp.where(mine, key[:, span], key_mask)
    v = jnp.where(mine, value[:, span], jnp.ones((1, 2 * HD), BF))
    weights = jnp.exp2(dot_nt(query, k) * (factor * (LOG2E / HD))).astype(BF)
    return dot(weights, v)


def own_kernel(rows, cols, heads, side, axes, *refs):
    count = (len(refs) - 7) // 2
    ins, qkv_c_hbm, outs = refs[:count], refs[count], refs[count + 1 : 2 * count + 1]
    head_ref, query_ref, acc_ref, ones_ref, mask_ref, sems = refs[2 * count + 1 :]
    tok_ref, qkv_ref, gain_ref, scale_ref = outs[:4]
    head = (qkv_c_hbm.at[pl.ds(0, head_ref.shape[0]), :], head_ref)
    copies = copies_of(list(zip(ins, outs)) + [head], sems)
    start_all(copies)
    width = heads * HD
    ones = same_head(width)
    ones_ref[...] = ones
    mask_ref[...] = halo_columns(rows, cols, side, axes)
    query_mask = query_columns(rows, cols)
    spot = lax.broadcasted_iota(jnp.int32, (rows * cols, 1), 0)
    key_mask = key_columns(rows, cols, over(spot, cols), spot & (cols - 1))
    wait_all(copies[:4])
    normed = rms_norm(tok_ref[...].astype(F32), gain_ref[...]).astype(BF)
    query = head_norm(dot(normed, qkv_ref[:, :width]), ones).astype(BF)
    key = head_norm(dot(normed, qkv_ref[:, width : 2 * width]), ones).astype(BF)
    value = dot(normed, qkv_ref[:, 2 * width :]).astype(BF)
    for head in range(heads):
        factor = scale_ref[0:1, head : head + 1]
        mine, span = half_of(head)
        masked = jnp.where(mine, query[:, span], query_mask)
        query_ref[head] = masked
        acc_ref[head] = attend(head, masked, key, value, key_mask, factor)
    wait_all(copies[4:])


def fine_kernel(
    heads,
    tok_ref, halo_refs, query_ref, acc_ref, ones_ref, mask_ref, gain_attn_ref, qkv_ref, scale_ref,
    out_ref, gain_ffn_ref, ffn_in_ref, ffn_out_ref, after_ref, out_c_hbm,
    fine_ref, pooled_ref, out_c_ref, sems,
):
    copies = copies_of([(out_c_hbm, out_c_ref)], sems)
    start_all(copies)
    width = heads * HD
    halo = jnp.concatenate([ref[...] for ref in halo_refs], 0)
    halo = halo.astype(F32)
    scaled = (halo * gain_attn_ref[...]).astype(BF)
    halo_rms = rms_factor(halo)
    ones = ones_ref[...]
    key = dot(scaled, qkv_ref[:, width : 2 * width])
    key = (key * head_factor(dot_split(key * key, ones), halo_rms)).astype(BF)
    value = (dot(scaled, qkv_ref[:, 2 * width :]) * halo_rms).astype(BF)

    key_mask = mask_ref[...]
    low = half_lanes()
    parts = []
    for pair in range(heads // 2):
        sums = []
        for head in (2 * pair, 2 * pair + 1):
            factor = scale_ref[0:1, head : head + 1]
            sums.append(acc_ref[head] + attend(head, query_ref[head], key, value, key_mask, factor))
        top = jnp.where(low, sums[0], sums[1])
        bottom = pltpu.roll(jnp.where(low, sums[1], sums[0]), HD, 1)
        parts.append((top / bottom).astype(BF))
    attn = jnp.concatenate(parts, 1)

    h1 = (tok_ref[...].astype(F32) + dot(attn, out_ref[...])).astype(BF)
    h1_wide = h1.astype(F32)
    scaled = (h1_wide * gain_ffn_ref[...]).astype(BF)
    h1_rms = rms_factor(h1_wide)
    hidden = ffn_out_ref.shape[0]
    fine = h1_wide
    size = 4 * HD
    for at in range(0, hidden, size):
        gate = dot(scaled, ffn_in_ref[:, at : at + size]) * h1_rms
        up = dot(scaled, ffn_in_ref[:, hidden + at : hidden + at + size]) * h1_rms
        gated = (jax.nn.gelu(gate, approximate=True) * up).astype(BF)
        fine = fine + dot(gated, ffn_out_ref[at : at + size, :])
    fine = fine.astype(BF)
    fine_ref[...] = fine
    pooled = jnp.mean(fine.astype(F32), 0, keepdims=True).astype(BF).astype(F32)
    for part in range(pooled_ref.shape[1]):
        pooled_ref[:, part, :] = jnp.broadcast_to(
            pooled[:, part * 128 : (part + 1) * 128], (pooled_ref.shape[0], 128)
        )
    wait_all(copies)


def coarse_kernel(
    axes, pooled_ref, up_ref, merged_ref, scale_ref, out_ref, fine_ref, ones_ref,
    coarse_out_ref, fine_hbm,
    query_ref, coarse_ref, sems,
):
    copies = copies_of([(fine_ref, fine_hbm)], sems)
    start_all(copies)
    width = out_ref.shape[0]
    row_axis, col_axis = axes
    mine = lax.axis_index(row_axis) * lax.axis_size(col_axis) + lax.axis_index(col_axis)
    pooled = jnp.concatenate([pooled_ref[:, part, :] for part in range(pooled_ref.shape[1])], 1).astype(BF)
    coarse = dot(pooled, up_ref[...]).astype(BF).astype(F32)
    coarse_ref[...] = coarse
    query_ref[...] = dot(pooled, merged_ref[:, :width])
    key = dot(pooled, merged_ref[:, width : 2 * width])
    value = dot(pooled, merged_ref[:, 2 * width :])
    own = coarse_ref[pl.ds(mine, 1), :]
    query = query_ref[pl.ds(mine, 1), :]
    rms = rms_factor(coarse)
    group = 4 * HD
    spans = [slice(at, at + group) for at in range(0, width, group)]
    tall = jnp.concatenate([key[:, span] for span in spans], 0)
    queries = [query[:, span] for span in spans]
    cross = jnp.concatenate([key[:, span] * q for span, q in zip(spans, queries)], 0)
    ones = ones_ref[...]
    query_norm = head_factor(dot_split(jnp.concatenate([q * q for q in queries], 0), ones), rms_factor(own))
    key_norm = head_factor(dot_split(tall * tall, ones), jnp.concatenate([rms] * len(spans), 0))
    scores = dot_split(cross, ones) * key_norm
    count = key.shape[0]
    parts = []
    for at, span in enumerate(spans):
        factor = query_norm[at : at + 1] * scale_ref[:, span]
        expo = jnp.exp(scores[at * count : (at + 1) * count] * factor)
        total = jnp.sum(expo, 0, keepdims=True)
        parts.append(jnp.sum(expo * rms * value[:, span], 0, keepdims=True) / total)
    cattn = jnp.concatenate(parts, 1).astype(BF)
    coarse_out_ref[...] = (own + dot(cattn, out_ref[...])).astype(BF)
    wait_all(copies)


def vmem(count):
    return [pl.BlockSpec(memory_space=pltpu.VMEM)] * count


def anywhere(count):
    return [pl.BlockSpec(memory_space=pl.ANY)] * count


def in_vmem(arrays):
    return [pltpu.with_memory_space_constraint(array, pltpu.VMEM) for array in arrays]


def in_hbm(arrays):
    return [pltpu.with_memory_space_constraint(array, pltpu.HBM) for array in arrays]


def shards(
    tokens, gain_attn, qkv_fine, scale_fine, out_fine, gain_ffn, ffn_in, ffn_out,
    up_proj, gain_coarse, qkv_coarse, scale_coarse, out_coarse,
):
    rows, cols, width = tokens.shape
    count = rows * cols
    strip = RADIUS * cols
    side = rounded_up((rows + 2 * RADIUS) * RADIUS, 16)
    heads = width // HD
    width_c = out_coarse.shape[0]
    devices = lax.axis_size("ha") * lax.axis_size("wa")
    axes = ("ha", "wa")
    params = pltpu.CompilerParams(vmem_limit_bytes=16 * MIB)

    def swapped(array, axis, first):
        pairs = [(i, i + 1) for i in range(first, lax.axis_size(axis) - 1, 2)]
        return lax.ppermute(array, axis, pairs + [(j, i) for i, j in pairs])

    flat = tokens.reshape(count, width)
    across, within = pl.pallas_call(
        functools.partial(strip_kernel, rows, cols, "ha"),
        out_shape=[pltpu.VMEM((strip, width), BF)] * 2,
        in_specs=anywhere(1),
        out_specs=vmem(2),
        scratch_shapes=[pltpu.SemaphoreType.DMA((2,))],
        compiler_params=params,
        name="strips",
    )(*in_hbm([flat]))
    across = swapped(across, "ha", 1)
    within = swapped(within, "ha", 0)

    block = 256
    weights = [
        flat, qkv_fine, gain_attn.reshape(1, -1), scale_fine.reshape(1, -1),
        up_proj, gain_coarse.reshape(1, -1), scale_coarse.reshape(1, -1),
        out_fine, gain_ffn.reshape(1, -1), ffn_in, ffn_out,
    ]
    *weights, head, query, acc, ones, mask = pl.pallas_call(
        functools.partial(own_kernel, rows, cols, heads, side, axes),
        out_shape=[pltpu.VMEM(array.shape, array.dtype) for array in weights]
        + [
            pltpu.VMEM((block, 3 * width_c), BF),
            pltpu.VMEM((heads, count, 2 * HD), BF),
            pltpu.VMEM((heads, count, 2 * HD), F32),
            pltpu.VMEM((4 * HD, 4 * HD), BF),
            pltpu.VMEM((2 * strip + 2 * side, 2 * HD), BF),
        ],
        in_specs=anywhere(len(weights) + 1),
        out_specs=vmem(len(weights) + 5),
        scratch_shapes=[pltpu.SemaphoreType.DMA((len(weights) + 1,))],
        compiler_params=params,
        cost_estimate=pl.CostEstimate(
            flops=2 * count * width * (3 * width + 2 * count), bytes_accessed=4 * MIB, transcendentals=0
        ),
        name="own",
    )(*in_hbm(weights + [qkv_coarse]))
    tok_v, qkv_v, gain_attn_v, scale_v, up_v, gain_c_v, scale_c_v = weights[:7]
    out_v, gain_ffn_v, ffn_in_v, ffn_out_v = weights[7:]

    across_edge, within_edge = pl.pallas_call(
        functools.partial(edge_kernel, rows, cols, axes),
        out_shape=[pltpu.VMEM((side, width), BF)] * 2,
        in_specs=vmem(4),
        out_specs=vmem(2),
        compiler_params=params,
        name="edges",
    )(*in_vmem([tok_v, across, within, query]))
    across_side = swapped(across_edge, "wa", 1)
    within_side = swapped(within_edge, "wa", 0)

    merged, scale_lanes = pl.pallas_call(
        merge_kernel,
        out_shape=[pltpu.VMEM((width, 3 * width_c), BF), pltpu.VMEM((1, width_c), F32)],
        in_specs=vmem(5) + anywhere(1),
        out_specs=vmem(2),
        scratch_shapes=[
            pltpu.VMEM((width_c // block - 1, block, 3 * width_c), BF),
            pltpu.VMEM((width, 3 * width_c), F32),
            pltpu.SemaphoreType.DMA((width_c // block - 1,)),
        ],
        compiler_params=params,
        cost_estimate=pl.CostEstimate(
            flops=6 * width * width_c * width_c, bytes_accessed=8 * MIB, transcendentals=0
        ),
        name="merge",
    )(*in_vmem([within_edge, up_v, gain_c_v, scale_c_v, head]), *in_hbm([qkv_coarse]))

    def fine_body(tok_ref, *refs):
        fine_kernel(heads, tok_ref, refs[:4], *refs[4:])

    fine, pooled, out_c_v = pl.pallas_call(
        fine_body,
        out_shape=[
            pltpu.VMEM((count, width), BF),
            pltpu.VMEM((devices, width // 128, 128), F32),
            pltpu.VMEM(out_coarse.shape, BF),
        ],
        in_specs=vmem(17) + anywhere(1),
        out_specs=vmem(3),
        scratch_shapes=[pltpu.SemaphoreType.DMA((1,))],
        compiler_params=params,
        name="fine",
    )(
        *in_vmem(
            [tok_v, across, within, across_side, within_side, query, acc, ones, mask, gain_attn_v, qkv_v, scale_v]
            + [out_v, gain_ffn_v, ffn_in_v, ffn_out_v, merged]
        ),
        *in_hbm([out_coarse]),
    )

    every = lax.all_to_all(pooled, axes, split_axis=0, concat_axis=0, tiled=True)
    coarse_out, fine = pl.pallas_call(
        functools.partial(coarse_kernel, axes),
        out_shape=[
            jax.ShapeDtypeStruct((1, width_c), BF),
            jax.ShapeDtypeStruct((count, width), BF),
        ],
        in_specs=vmem(7),
        out_specs=vmem(1) + anywhere(1),
        scratch_shapes=[pltpu.VMEM((devices, width_c), F32)] * 2 + [pltpu.SemaphoreType.DMA((1,))],
        compiler_params=params,
        name="coarse",
    )(*in_vmem([every, up_v, merged, scale_lanes, out_c_v, fine, ones]))
    return fine.reshape(rows, cols, width), coarse_out.reshape(1, 1, width_c)


def solution(mesh):
    return jax.shard_map(
        shards,
        mesh=mesh,
        in_specs=(P("ha", "wa", None), P(), P(), P(), P(), P(), P(), P(), P(), P(), P(), P(), P()),
        out_specs=(P("ha", "wa", None), P("ha", "wa", None)),
        check_vma=False,
    )
```

```python
import functools

import jax
import jax.numpy as jnp
from jax import lax
from jax.experimental import pallas as pl
from jax.experimental.pallas import tpu as pltpu
from jax.sharding import PartitionSpec as P

HD = 64
RADIUS = 3
LOG2E = 1.4426950408889634
BIG = 2.0**30
BF = jnp.bfloat16
F32 = jnp.float32
MIB = 1 << 20


def rounded_up(value, step):
    return -(-value // step) * step


def over(values, size):
    assert size & (size - 1) == 0
    return values >> (size.bit_length() - 1)


def dot(a, b):
    return jnp.dot(a, b, preferred_element_type=F32)


def dot_nt(a, b):
    return lax.dot_general(a, b, (((1,), (1,)), ((), ())), preferred_element_type=F32)


def dot_split(values, ones):
    high = values.astype(BF)
    low = (values - high.astype(F32)).astype(BF)
    return dot(high, ones) + dot(low, ones)


def same_head(size):
    left = over(lax.broadcasted_iota(jnp.int32, (size, 1), 0), HD)
    right = over(lax.broadcasted_iota(jnp.int32, (1, size), 1), HD)
    return jnp.where(left == right, 1.0, 0.0).astype(BF)


def head_norm(values, ones):
    return values * lax.rsqrt(dot_split(values * values, ones) * (1.0 / HD) + 1e-06)


def rms_factor(values):
    return lax.rsqrt(jnp.mean(values * values, -1, keepdims=True) + 1e-06)


def rms_norm(values, gain):
    return values * rms_factor(values) * gain


def head_factor(squares, factor):
    return factor * lax.rsqrt(squares * (factor * factor * (1.0 / HD)) + 1e-06)


def copies_of(pairs, sems):
    return [pltpu.make_async_copy(src, dst, sems.at[i]) for i, (src, dst) in enumerate(pairs)]


def start_all(copies):
    for copy in copies:
        copy.start()


def wait_all(copies):
    for copy in copies:
        copy.wait()


def row_copies(src, dst, sems):
    size = dst.shape[0] // sems.shape[0]
    spans = [pl.ds(i * size, size) for i in range(sems.shape[0])]
    return copies_of([(src.at[span, :], dst.at[span, :]) for span in spans], sems)


def strip_kernel(rows, cols, axis, tok_hbm, across_ref, within_ref, sems):
    count, strip = rows * cols, RADIUS * cols
    odd = lax.axis_index(axis) & 1
    last = count - strip
    first = pl.multiple_of(odd * last, 16)
    second = pl.multiple_of((1 - odd) * last, 16)
    copies = copies_of(
        [
            (tok_hbm.at[pl.ds(first, strip), :], across_ref),
            (tok_hbm.at[pl.ds(second, strip), :], within_ref),
        ],
        sems,
    )
    start_all(copies)
    wait_all(copies)


def edge_kernel(rows, cols, axes, tok_ref, across_ref, within_ref, after_ref, across_out, within_out):
    height = rows + 2 * RADIUS
    strip = RADIUS * cols
    padded = across_out.shape[0]
    odd, odd_col = lax.axis_index(axes[0]) & 1, lax.axis_index(axes[1]) & 1
    block = jnp.concatenate([tok_ref[...], across_ref[...], within_ref[...]], 0)
    out = lax.broadcasted_iota(jnp.int32, (padded, 1), 0)
    src = lax.broadcasted_iota(jnp.int32, (padded, block.shape[0]), 1)
    row = ((out * 21846) >> 16) - RADIUS
    col = out - 3 * (row + RADIUS)
    above = rows * cols + strip * odd + RADIUS * cols
    below = rows * cols + strip * (1 - odd) - rows * cols
    first = row * cols + col + jnp.where(row < 0, above, jnp.where(row >= rows, below, 0))
    first = jnp.where(out < height * RADIUS, first, -2 * cols)
    far = cols - RADIUS
    pick = jnp.where(src == first + far * odd_col, 1.0, 0.0).astype(BF)
    across_out[...] = dot(pick, block).astype(BF)
    pick = jnp.where(src == first + far * (1 - odd_col), 1.0, 0.0).astype(BF)
    within_out[...] = dot(pick, block).astype(BF)


def merge_kernel(
    after_ref, up_ref, gain_ref, scale_ref, head_ref, qkv_hbm, merged_ref, scale_out, weight_ref, total_ref, sems
):
    size = head_ref.shape[0]
    blocks = weight_ref.shape[0] // size
    copies = row_copies(qkv_hbm.at[pl.ds(size, blocks * size), :], weight_ref, sems)
    each = len(copies) // blocks
    start_all(copies)
    scaled = (up_ref[...].astype(F32) * gain_ref[...]).astype(BF)
    width = merged_ref.shape[1]
    spans = [slice(at, at + 4 * HD) for at in range(0, width, 4 * HD)]
    for span in spans:
        total_ref[:, span] = dot(scaled[:, :size], head_ref[:, span])
    lane = over(lax.broadcasted_iota(jnp.int32, scale_out.shape, 1), HD)
    scales = jnp.zeros(scale_out.shape, F32)
    for head in range(scale_ref.shape[1]):
        scales = jnp.where(lane == head, scale_ref[0:1, head : head + 1], scales)
    scale_out[...] = scales * (1.0 / HD)
    for i in range(blocks):
        wait_all(copies[i * each : (i + 1) * each])
        rows = scaled[:, (i + 1) * size : (i + 2) * size]
        for span in spans:
            total = total_ref[:, span] + dot(rows, weight_ref[i * size : (i + 1) * size, span])
            if i < blocks - 1:
                total_ref[:, span] = total
            else:
                merged_ref[:, span] = total.astype(BF)


def half_lanes():
    return lax.broadcasted_iota(jnp.int32, (1, 2 * HD), 1) < HD


def mask_columns(rows, cols):
    place = lax.broadcasted_iota(jnp.int32, (1, 2 * HD), 1) & (HD - 1)
    return place, place < rows, (place >= rows) & (place < rows + cols)


def query_columns(rows, cols):
    place, is_row, is_col = mask_columns(rows, cols)
    spot = lax.broadcasted_iota(jnp.int32, (rows * cols, 1), 0)
    hot = (is_row & (over(spot, cols) == place)) | (is_col & ((spot & (cols - 1)) == place - rows))
    return jnp.where(hot, 1.0, 0.0).astype(BF)


def key_columns(rows, cols, krow, kcol):
    place, is_row, is_col = mask_columns(rows, cols)
    far_row = jnp.abs(krow - place) > RADIUS
    far_col = jnp.abs(kcol - (place - rows)) > RADIUS
    return jnp.where((is_row & far_row) | (is_col & far_col), -BIG, 0.0).astype(BF)


def halo_columns(rows, cols, side, axes):
    strip = RADIUS * cols
    row_axis, col_axis = axes
    place_row, place_col = lax.axis_index(row_axis), lax.axis_index(col_axis)
    row0, col0 = place_row * rows, place_col * cols
    grid_rows = lax.axis_size(row_axis) * rows
    grid_cols = lax.axis_size(col_axis) * cols
    odd, odd_col = place_row & 1, place_col & 1
    row_at = (odd * (rows + RADIUS) - RADIUS, (1 - odd) * (rows + RADIUS) - RADIUS)
    col_at = (odd_col * (cols + RADIUS) - RADIUS, (1 - odd_col) * (cols + RADIUS) - RADIUS)
    spot = lax.broadcasted_iota(jnp.int32, (2 * strip + 2 * side, 1), 0)
    past_first = spot - strip
    past_strips = past_first - strip
    past_third = past_strips - side
    strip_at = jnp.where(past_first >= 0, past_first, spot)
    side_at = jnp.where(past_third >= 0, past_third, past_strips)
    side_row = (side_at * 21846) >> 16
    in_strip = past_strips < 0
    krow = jnp.where(
        in_strip,
        over(strip_at, cols) + jnp.where(past_first >= 0, row_at[1], row_at[0]),
        side_row - RADIUS,
    )
    kcol = jnp.where(
        in_strip,
        strip_at & (cols - 1),
        side_at - 3 * side_row + jnp.where(past_third >= 0, col_at[1], col_at[0]),
    )
    real = in_strip | (side_at < (rows + 2 * RADIUS) * RADIUS)
    real = real & (krow + row0 >= 0) & (krow + row0 < grid_rows)
    real = real & (kcol + col0 >= 0) & (kcol + col0 < grid_cols)
    return key_columns(rows, cols, jnp.where(real, krow, -1000), kcol)


def half_of(head):
    low = half_lanes()
    lanes = 2 * HD
    return (low if head % 2 == 0 else ~low), slice(head // 2 * lanes, (head // 2 + 1) * lanes)


def attend(head, query, key, value, key_mask, factor):
    mine, span = half_of(head)
    k = jnp.where(mine, key[:, span], key_mask)
    v = jnp.where(mine, value[:, span], jnp.ones((1, 2 * HD), BF))
    weights = jnp.exp2(dot_nt(query, k) * (factor * (LOG2E / HD))).astype(BF)
    return dot(weights, v)


def own_kernel(rows, cols, heads, side, axes, *refs):
    count = (len(refs) - 7) // 2
    ins, qkv_c_hbm, outs = refs[:count], refs[count], refs[count + 1 : 2 * count + 1]
    head_ref, query_ref, acc_ref, ones_ref, mask_ref, sems = refs[2 * count + 1 :]
    tok_ref, qkv_ref, gain_ref, scale_ref = outs[:4]
    head = (qkv_c_hbm.at[pl.ds(0, head_ref.shape[0]), :], head_ref)
    copies = copies_of(list(zip(ins, outs)) + [head], sems)
    start_all(copies)
    width = heads * HD
    ones = same_head(width)
    ones_ref[...] = ones
    mask_ref[...] = halo_columns(rows, cols, side, axes)
    query_mask = query_columns(rows, cols)
    spot = lax.broadcasted_iota(jnp.int32, (rows * cols, 1), 0)
    key_mask = key_columns(rows, cols, over(spot, cols), spot & (cols - 1))
    wait_all(copies[:4])
    normed = rms_norm(tok_ref[...].astype(F32), gain_ref[...]).astype(BF)
    query = head_norm(dot(normed, qkv_ref[:, :width]), ones).astype(BF)
    key = head_norm(dot(normed, qkv_ref[:, width : 2 * width]), ones).astype(BF)
    value = dot(normed, qkv_ref[:, 2 * width :]).astype(BF)
    for head in range(heads):
        factor = scale_ref[0:1, head : head + 1]
        mine, span = half_of(head)
        masked = jnp.where(mine, query[:, span], query_mask)
        query_ref[head] = masked
        acc_ref[head] = attend(head, masked, key, value, key_mask, factor)
    wait_all(copies[4:])


def fine_kernel(
    heads,
    tok_ref, halo_refs, query_ref, acc_ref, ones_ref, mask_ref, gain_attn_ref, qkv_ref, scale_ref,
    out_ref, gain_ffn_ref, ffn_in_ref, ffn_out_ref, after_ref, out_c_hbm,
    fine_ref, pooled_ref, out_c_ref, sems,
):
    copies = row_copies(out_c_hbm, out_c_ref, sems)
    start_all(copies)
    width = heads * HD
    halo = jnp.concatenate([ref[...] for ref in halo_refs], 0)
    halo = halo.astype(F32)
    scaled = (halo * gain_attn_ref[...]).astype(BF)
    halo_rms = rms_factor(halo)
    ones = ones_ref[...]
    key = dot(scaled, qkv_ref[:, width : 2 * width])
    key = (key * head_factor(dot_split(key * key, ones), halo_rms)).astype(BF)
    value = (dot(scaled, qkv_ref[:, 2 * width :]) * halo_rms).astype(BF)

    key_mask = mask_ref[...]
    low = half_lanes()
    parts = []
    for pair in range(heads // 2):
        sums = []
        for head in (2 * pair, 2 * pair + 1):
            factor = scale_ref[0:1, head : head + 1]
            sums.append(acc_ref[head] + attend(head, query_ref[head], key, value, key_mask, factor))
        top = jnp.where(low, sums[0], sums[1])
        bottom = pltpu.roll(jnp.where(low, sums[1], sums[0]), HD, 1)
        parts.append((top / bottom).astype(BF))
    attn = jnp.concatenate(parts, 1)

    h1 = (tok_ref[...].astype(F32) + dot(attn, out_ref[...])).astype(BF)
    h1_wide = h1.astype(F32)
    scaled = (h1_wide * gain_ffn_ref[...]).astype(BF)
    h1_rms = rms_factor(h1_wide)
    hidden = ffn_out_ref.shape[0]
    gate = dot(scaled, ffn_in_ref[:, :hidden]) * h1_rms
    up = dot(scaled, ffn_in_ref[:, hidden:]) * h1_rms
    gated = (jax.nn.gelu(gate, approximate=True) * up).astype(BF)
    fine = (h1_wide + dot(gated, ffn_out_ref[...])).astype(BF)
    fine_ref[...] = fine
    pooled = jnp.mean(fine.astype(F32), 0, keepdims=True).astype(BF).astype(F32)
    for part in range(pooled_ref.shape[1]):
        pooled_ref[:, part, :] = jnp.broadcast_to(
            pooled[:, part * 128 : (part + 1) * 128], (pooled_ref.shape[0], 128)
        )
    wait_all(copies)


def coarse_kernel(
    axes, pooled_ref, up_ref, merged_ref, scale_ref, out_ref, fine_ref, ones_ref,
    coarse_out_ref, fine_hbm,
    query_ref, coarse_ref, sems,
):
    copies = copies_of([(fine_ref, fine_hbm)], sems)
    start_all(copies)
    width = out_ref.shape[0]
    row_axis, col_axis = axes
    mine = lax.axis_index(row_axis) * lax.axis_size(col_axis) + lax.axis_index(col_axis)
    pooled = jnp.concatenate([pooled_ref[:, part, :] for part in range(pooled_ref.shape[1])], 1).astype(BF)
    coarse = dot(pooled, up_ref[...]).astype(BF).astype(F32)
    coarse_ref[...] = coarse
    query_ref[...] = dot(pooled, merged_ref[:, :width])
    key = dot(pooled, merged_ref[:, width : 2 * width])
    value = dot(pooled, merged_ref[:, 2 * width :])
    own = coarse_ref[pl.ds(mine, 1), :]
    query = query_ref[pl.ds(mine, 1), :]
    rms = rms_factor(coarse)
    group = 4 * HD
    spans = [slice(at, at + group) for at in range(0, width, group)]
    tall = jnp.concatenate([key[:, span] for span in spans], 0)
    queries = [query[:, span] for span in spans]
    cross = jnp.concatenate([key[:, span] * q for span, q in zip(spans, queries)], 0)
    ones = ones_ref[...]
    query_norm = head_factor(dot_split(jnp.concatenate([q * q for q in queries], 0), ones), rms_factor(own))
    key_norm = head_factor(dot_split(tall * tall, ones), jnp.concatenate([rms] * len(spans), 0))
    scores = dot_split(cross, ones) * key_norm
    count = key.shape[0]
    parts = []
    for at, span in enumerate(spans):
        factor = query_norm[at : at + 1] * scale_ref[:, span]
        expo = jnp.exp(scores[at * count : (at + 1) * count] * factor)
        total = jnp.sum(expo, 0, keepdims=True)
        parts.append(jnp.sum(expo * rms * value[:, span], 0, keepdims=True) / total)
    cattn = jnp.concatenate(parts, 1).astype(BF)
    coarse_out_ref[...] = (own + dot(cattn, out_ref[...])).astype(BF)
    wait_all(copies)


def vmem(count):
    return [pl.BlockSpec(memory_space=pltpu.VMEM)] * count


def anywhere(count):
    return [pl.BlockSpec(memory_space=pl.ANY)] * count


def in_vmem(arrays):
    return [pltpu.with_memory_space_constraint(array, pltpu.VMEM) for array in arrays]


def in_hbm(arrays):
    return [pltpu.with_memory_space_constraint(array, pltpu.HBM) for array in arrays]


def shards(
    tokens, gain_attn, qkv_fine, scale_fine, out_fine, gain_ffn, ffn_in, ffn_out,
    up_proj, gain_coarse, qkv_coarse, scale_coarse, out_coarse,
):
    rows, cols, width = tokens.shape
    count = rows * cols
    strip = RADIUS * cols
    side = rounded_up((rows + 2 * RADIUS) * RADIUS, 16)
    heads = width // HD
    width_c = out_coarse.shape[0]
    devices = lax.axis_size("ha") * lax.axis_size("wa")
    axes = ("ha", "wa")
    params = pltpu.CompilerParams(vmem_limit_bytes=16 * MIB)

    def swapped(array, axis, first):
        pairs = [(i, i + 1) for i in range(first, lax.axis_size(axis) - 1, 2)]
        return lax.ppermute(array, axis, pairs + [(j, i) for i, j in pairs])

    flat = tokens.reshape(count, width)
    across, within = pl.pallas_call(
        functools.partial(strip_kernel, rows, cols, "ha"),
        out_shape=[pltpu.VMEM((strip, width), BF)] * 2,
        in_specs=anywhere(1),
        out_specs=vmem(2),
        scratch_shapes=[pltpu.SemaphoreType.DMA((2,))],
        compiler_params=params,
        name="strips",
    )(*in_hbm([flat]))
    across = swapped(across, "ha", 1)
    within = swapped(within, "ha", 0)

    block = 256
    weights = [
        flat, qkv_fine, gain_attn.reshape(1, -1), scale_fine.reshape(1, -1),
        up_proj, gain_coarse.reshape(1, -1), scale_coarse.reshape(1, -1),
        out_fine, gain_ffn.reshape(1, -1), ffn_in, ffn_out,
    ]
    *weights, head, query, acc, ones, mask = pl.pallas_call(
        functools.partial(own_kernel, rows, cols, heads, side, axes),
        out_shape=[pltpu.VMEM(array.shape, array.dtype) for array in weights]
        + [
            pltpu.VMEM((block, 3 * width_c), BF),
            pltpu.VMEM((heads, count, 2 * HD), BF),
            pltpu.VMEM((heads, count, 2 * HD), F32),
            pltpu.VMEM((4 * HD, 4 * HD), BF),
            pltpu.VMEM((2 * strip + 2 * side, 2 * HD), BF),
        ],
        in_specs=anywhere(len(weights) + 1),
        out_specs=vmem(len(weights) + 5),
        scratch_shapes=[pltpu.SemaphoreType.DMA((len(weights) + 1,))],
        compiler_params=params,
        cost_estimate=pl.CostEstimate(
            flops=2 * count * width * (3 * width + 2 * count), bytes_accessed=4 * MIB, transcendentals=0
        ),
        name="own",
    )(*in_hbm(weights + [qkv_coarse]))
    tok_v, qkv_v, gain_attn_v, scale_v, up_v, gain_c_v, scale_c_v = weights[:7]
    out_v, gain_ffn_v, ffn_in_v, ffn_out_v = weights[7:]

    across_edge, within_edge = pl.pallas_call(
        functools.partial(edge_kernel, rows, cols, axes),
        out_shape=[pltpu.VMEM((side, width), BF)] * 2,
        in_specs=vmem(4),
        out_specs=vmem(2),
        compiler_params=params,
        name="edges",
    )(*in_vmem([tok_v, across, within, query]))
    across_side = swapped(across_edge, "wa", 1)
    within_side = swapped(within_edge, "wa", 0)

    merged, scale_lanes = pl.pallas_call(
        merge_kernel,
        out_shape=[pltpu.VMEM((width, 3 * width_c), BF), pltpu.VMEM((1, width_c), F32)],
        in_specs=vmem(5) + anywhere(1),
        out_specs=vmem(2),
        scratch_shapes=[
            pltpu.VMEM((width_c - block, 3 * width_c), BF),
            pltpu.VMEM((width, 3 * width_c), F32),
            pltpu.SemaphoreType.DMA((2 * (width_c // block - 1),)),
        ],
        compiler_params=params,
        cost_estimate=pl.CostEstimate(
            flops=6 * width * width_c * width_c, bytes_accessed=8 * MIB, transcendentals=0
        ),
        name="merge",
    )(*in_vmem([within_edge, up_v, gain_c_v, scale_c_v, head]), *in_hbm([qkv_coarse]))

    def fine_body(tok_ref, *refs):
        fine_kernel(heads, tok_ref, refs[:4], *refs[4:])

    fine, pooled, out_c_v = pl.pallas_call(
        fine_body,
        out_shape=[
            pltpu.VMEM((count, width), BF),
            pltpu.VMEM((devices, width // 128, 128), F32),
            pltpu.VMEM(out_coarse.shape, BF),
        ],
        in_specs=vmem(17) + anywhere(1),
        out_specs=vmem(3),
        scratch_shapes=[pltpu.SemaphoreType.DMA((4,))],
        compiler_params=params,
        name="fine",
    )(
        *in_vmem(
            [tok_v, across, within, across_side, within_side, query, acc, ones, mask, gain_attn_v, qkv_v, scale_v]
            + [out_v, gain_ffn_v, ffn_in_v, ffn_out_v, merged]
        ),
        *in_hbm([out_coarse]),
    )

    every = lax.all_to_all(pooled, axes, split_axis=0, concat_axis=0, tiled=True)
    coarse_out, fine = pl.pallas_call(
        functools.partial(coarse_kernel, axes),
        out_shape=[
            jax.ShapeDtypeStruct((1, width_c), BF),
            jax.ShapeDtypeStruct((count, width), BF),
        ],
        in_specs=vmem(7),
        out_specs=vmem(1) + anywhere(1),
        scratch_shapes=[pltpu.VMEM((devices, width_c), F32)] * 2 + [pltpu.SemaphoreType.DMA((1,))],
        compiler_params=params,
        name="coarse",
    )(*in_vmem([every, up_v, merged, scale_lanes, out_c_v, fine, ones]))
    return fine.reshape(rows, cols, width), coarse_out.reshape(1, 1, width_c)


def solution(mesh):
    return jax.shard_map(
        shards,
        mesh=mesh,
        in_specs=(P("ha", "wa", None), P(), P(), P(), P(), P(), P(), P(), P(), P(), P(), P(), P()),
        out_specs=(P("ha", "wa", None), P("ha", "wa", None)),
        check_vma=False,
    )
```

```python
import functools

import jax
import jax.numpy as jnp
from jax import lax
from jax.experimental import pallas as pl
from jax.experimental.pallas import tpu as pltpu
from jax.sharding import PartitionSpec as P

HD = 64
RADIUS = 3
LOG2E = 1.4426950408889634
BIG = 2.0**30
BF = jnp.bfloat16
F32 = jnp.float32
MIB = 1 << 20


def rounded_up(value, step):
    return -(-value // step) * step


def over(values, size):
    assert size & (size - 1) == 0
    return values >> (size.bit_length() - 1)


def dot(a, b):
    return jnp.dot(a, b, preferred_element_type=F32)


def dot_nt(a, b):
    return lax.dot_general(a, b, (((1,), (1,)), ((), ())), preferred_element_type=F32)


def dot_split(values, ones):
    high = values.astype(BF)
    low = (values - high.astype(F32)).astype(BF)
    return dot(high, ones) + dot(low, ones)


def same_head(size):
    left = over(lax.broadcasted_iota(jnp.int32, (size, 1), 0), HD)
    right = over(lax.broadcasted_iota(jnp.int32, (1, size), 1), HD)
    return jnp.where(left == right, 1.0, 0.0).astype(BF)


def head_norm(values, ones):
    return values * lax.rsqrt(dot_split(values * values, ones) * (1.0 / HD) + 1e-06)


def rms_factor(values):
    return lax.rsqrt(jnp.mean(values * values, -1, keepdims=True) + 1e-06)


def rms_norm(values, gain):
    return values * rms_factor(values) * gain


def head_factor(squares, factor):
    return factor * lax.rsqrt(squares * (factor * factor * (1.0 / HD)) + 1e-06)


def copies_of(pairs, sems):
    return [pltpu.make_async_copy(src, dst, sems.at[i]) for i, (src, dst) in enumerate(pairs)]


def start_all(copies):
    for copy in copies:
        copy.start()


def wait_all(copies):
    for copy in copies:
        copy.wait()


def strip_kernel(rows, cols, axis, tok_hbm, across_ref, within_ref, sems):
    count, strip = rows * cols, RADIUS * cols
    odd = lax.axis_index(axis) & 1
    last = count - strip
    first = pl.multiple_of(odd * last, 16)
    second = pl.multiple_of((1 - odd) * last, 16)
    copies = copies_of(
        [
            (tok_hbm.at[pl.ds(first, strip), :], across_ref),
            (tok_hbm.at[pl.ds(second, strip), :], within_ref),
        ],
        sems,
    )
    start_all(copies)
    wait_all(copies)


def edge_kernel(rows, cols, axes, tok_ref, across_ref, within_ref, after_ref, across_out, within_out):
    height = rows + 2 * RADIUS
    strip = RADIUS * cols
    padded = across_out.shape[0]
    odd, odd_col = lax.axis_index(axes[0]) & 1, lax.axis_index(axes[1]) & 1
    block = jnp.concatenate([tok_ref[...], across_ref[...], within_ref[...]], 0)
    out = lax.broadcasted_iota(jnp.int32, (padded, 1), 0)
    src = lax.broadcasted_iota(jnp.int32, (padded, block.shape[0]), 1)
    row = ((out * 21846) >> 16) - RADIUS
    col = out - 3 * (row + RADIUS)
    above = rows * cols + strip * odd + RADIUS * cols
    below = rows * cols + strip * (1 - odd) - rows * cols
    first = row * cols + col + jnp.where(row < 0, above, jnp.where(row >= rows, below, 0))
    first = jnp.where(out < height * RADIUS, first, -2 * cols)
    far = cols - RADIUS
    pick = jnp.where(src == first + far * odd_col, 1.0, 0.0).astype(BF)
    across_out[...] = dot(pick, block).astype(BF)
    pick = jnp.where(src == first + far * (1 - odd_col), 1.0, 0.0).astype(BF)
    within_out[...] = dot(pick, block).astype(BF)


def merge_kernel(
    after_ref, up_ref, gain_ref, scale_ref, head_ref, qkv_hbm,
    merged_ref, scale_out, weight_ref, scaled_ref, total_ref, sems,
):
    size = head_ref.shape[0]
    blocks = sems.shape[0]

    def span_of(block):
        return pl.ds(pl.multiple_of(block * size, size), size)

    def copy(block):
        return pltpu.make_async_copy(
            qkv_hbm.at[span_of(block + 1), :], weight_ref.at[span_of(block), :], sems.at[block]
        )

    for block in range(blocks):
        copy(block).start()
    lane = over(lax.broadcasted_iota(jnp.int32, scale_out.shape, 1), HD)
    scales = jnp.zeros(scale_out.shape, F32)
    for head in range(scale_ref.shape[1]):
        scales = jnp.where(lane == head, scale_ref[0:1, head : head + 1], scales)
    scale_out[...] = scales * (1.0 / HD)
    scaled_ref[...] = (up_ref[...].astype(F32) * gain_ref[...]).astype(BF)
    total_ref[...] = dot(scaled_ref[:, :size], head_ref[...])

    def step(block, carry):
        copy(block).wait()
        rows = scaled_ref[:, span_of(block + 1)]
        depth = span_of(block)
        for at in range(0, merged_ref.shape[1], size):
            span = slice(at, at + size)
            total = total_ref[:, span] + dot(rows, weight_ref[depth, span])
            total_ref[:, span] = total
            merged_ref[:, span] = total.astype(BF)
        return carry

    lax.fori_loop(0, blocks, step, 0)


def half_lanes():
    return lax.broadcasted_iota(jnp.int32, (1, 2 * HD), 1) < HD


def mask_columns(rows, cols):
    place = lax.broadcasted_iota(jnp.int32, (1, 2 * HD), 1) & (HD - 1)
    return place, place < rows, (place >= rows) & (place < rows + cols)


def query_columns(rows, cols):
    place, is_row, is_col = mask_columns(rows, cols)
    spot = lax.broadcasted_iota(jnp.int32, (rows * cols, 1), 0)
    hot = (is_row & (over(spot, cols) == place)) | (is_col & ((spot & (cols - 1)) == place - rows))
    return jnp.where(hot, 1.0, 0.0).astype(BF)


def key_columns(rows, cols, krow, kcol):
    place, is_row, is_col = mask_columns(rows, cols)
    far_row = jnp.abs(krow - place) > RADIUS
    far_col = jnp.abs(kcol - (place - rows)) > RADIUS
    return jnp.where((is_row & far_row) | (is_col & far_col), -BIG, 0.0).astype(BF)


def halo_columns(rows, cols, side, axes):
    strip = RADIUS * cols
    row_axis, col_axis = axes
    place_row, place_col = lax.axis_index(row_axis), lax.axis_index(col_axis)
    row0, col0 = place_row * rows, place_col * cols
    grid_rows = lax.axis_size(row_axis) * rows
    grid_cols = lax.axis_size(col_axis) * cols
    odd, odd_col = place_row & 1, place_col & 1
    row_at = (odd * (rows + RADIUS) - RADIUS, (1 - odd) * (rows + RADIUS) - RADIUS)
    col_at = (odd_col * (cols + RADIUS) - RADIUS, (1 - odd_col) * (cols + RADIUS) - RADIUS)
    spot = lax.broadcasted_iota(jnp.int32, (2 * strip + 2 * side, 1), 0)
    past_first = spot - strip
    past_strips = past_first - strip
    past_third = past_strips - side
    strip_at = jnp.where(past_first >= 0, past_first, spot)
    side_at = jnp.where(past_third >= 0, past_third, past_strips)
    side_row = (side_at * 21846) >> 16
    in_strip = past_strips < 0
    krow = jnp.where(
        in_strip,
        over(strip_at, cols) + jnp.where(past_first >= 0, row_at[1], row_at[0]),
        side_row - RADIUS,
    )
    kcol = jnp.where(
        in_strip,
        strip_at & (cols - 1),
        side_at - 3 * side_row + jnp.where(past_third >= 0, col_at[1], col_at[0]),
    )
    real = in_strip | (side_at < (rows + 2 * RADIUS) * RADIUS)
    real = real & (krow + row0 >= 0) & (krow + row0 < grid_rows)
    real = real & (kcol + col0 >= 0) & (kcol + col0 < grid_cols)
    return key_columns(rows, cols, jnp.where(real, krow, -1000), kcol)


def half_of(head):
    low = half_lanes()
    lanes = 2 * HD
    return (low if head % 2 == 0 else ~low), slice(head // 2 * lanes, (head // 2 + 1) * lanes)


def attend(head, query, key, value, key_mask, factor):
    mine, span = half_of(head)
    k = jnp.where(mine, key[:, span], key_mask)
    v = jnp.where(mine, value[:, span], jnp.ones((1, 2 * HD), BF))
    weights = jnp.exp2(dot_nt(query, k) * (factor * (LOG2E / HD))).astype(BF)
    return dot(weights, v)


def own_kernel(rows, cols, heads, side, axes, *refs):
    count = (len(refs) - 7) // 2
    ins, qkv_c_hbm, outs = refs[:count], refs[count], refs[count + 1 : 2 * count + 1]
    head_ref, query_ref, acc_ref, ones_ref, mask_ref, sems = refs[2 * count + 1 :]
    tok_ref, qkv_ref, gain_ref, scale_ref = outs[:4]
    head = (qkv_c_hbm.at[pl.ds(0, head_ref.shape[0]), :], head_ref)
    copies = copies_of(list(zip(ins, outs)) + [head], sems)
    start_all(copies)
    width = heads * HD
    ones = same_head(width)
    ones_ref[...] = ones
    mask_ref[...] = halo_columns(rows, cols, side, axes)
    query_mask = query_columns(rows, cols)
    spot = lax.broadcasted_iota(jnp.int32, (rows * cols, 1), 0)
    key_mask = key_columns(rows, cols, over(spot, cols), spot & (cols - 1))
    wait_all(copies[:4])
    normed = rms_norm(tok_ref[...].astype(F32), gain_ref[...]).astype(BF)
    query = head_norm(dot(normed, qkv_ref[:, :width]), ones).astype(BF)
    key = head_norm(dot(normed, qkv_ref[:, width : 2 * width]), ones).astype(BF)
    value = dot(normed, qkv_ref[:, 2 * width :]).astype(BF)
    for head in range(heads):
        factor = scale_ref[0:1, head : head + 1]
        mine, span = half_of(head)
        masked = jnp.where(mine, query[:, span], query_mask)
        query_ref[head] = masked
        acc_ref[head] = attend(head, masked, key, value, key_mask, factor)
    wait_all(copies[4:])


def fine_kernel(
    heads,
    tok_ref, halo_refs, query_ref, acc_ref, ones_ref, mask_ref, gain_attn_ref, qkv_ref, scale_ref,
    out_ref, gain_ffn_ref, ffn_in_ref, ffn_out_ref, after_ref, out_c_hbm,
    fine_ref, pooled_ref, out_c_ref, sems,
):
    copies = copies_of([(out_c_hbm, out_c_ref)], sems)
    start_all(copies)
    width = heads * HD
    halo = jnp.concatenate([ref[...] for ref in halo_refs], 0)
    halo = halo.astype(F32)
    scaled = (halo * gain_attn_ref[...]).astype(BF)
    halo_rms = rms_factor(halo)
    ones = ones_ref[...]
    key = dot(scaled, qkv_ref[:, width : 2 * width])
    key = (key * head_factor(dot_split(key * key, ones), halo_rms)).astype(BF)
    value = (dot(scaled, qkv_ref[:, 2 * width :]) * halo_rms).astype(BF)

    key_mask = mask_ref[...]
    low = half_lanes()
    parts = []
    for pair in range(heads // 2):
        sums = []
        for head in (2 * pair, 2 * pair + 1):
            factor = scale_ref[0:1, head : head + 1]
            sums.append(acc_ref[head] + attend(head, query_ref[head], key, value, key_mask, factor))
        top = jnp.where(low, sums[0], sums[1])
        bottom = pltpu.roll(jnp.where(low, sums[1], sums[0]), HD, 1)
        parts.append((top / bottom).astype(BF))
    attn = jnp.concatenate(parts, 1)

    h1 = (tok_ref[...].astype(F32) + dot(attn, out_ref[...])).astype(BF)
    h1_wide = h1.astype(F32)
    scaled = (h1_wide * gain_ffn_ref[...]).astype(BF)
    h1_rms = rms_factor(h1_wide)
    hidden = ffn_out_ref.shape[0]
    gate = dot(scaled, ffn_in_ref[:, :hidden]) * h1_rms
    up = dot(scaled, ffn_in_ref[:, hidden:]) * h1_rms
    gated = (jax.nn.gelu(gate, approximate=True) * up).astype(BF)
    fine = (h1_wide + dot(gated, ffn_out_ref[...])).astype(BF)
    fine_ref[...] = fine
    pooled = jnp.mean(fine.astype(F32), 0, keepdims=True).astype(BF).astype(F32)
    for part in range(pooled_ref.shape[1]):
        pooled_ref[:, part, :] = jnp.broadcast_to(
            pooled[:, part * 128 : (part + 1) * 128], (pooled_ref.shape[0], 128)
        )
    wait_all(copies)


def coarse_kernel(
    axes, pooled_ref, up_ref, merged_ref, scale_ref, out_ref, fine_ref, ones_ref,
    coarse_out_ref, fine_hbm,
    query_ref, coarse_ref, sems,
):
    copies = copies_of([(fine_ref, fine_hbm)], sems)
    start_all(copies)
    width = out_ref.shape[0]
    row_axis, col_axis = axes
    mine = lax.axis_index(row_axis) * lax.axis_size(col_axis) + lax.axis_index(col_axis)
    pooled = jnp.concatenate([pooled_ref[:, part, :] for part in range(pooled_ref.shape[1])], 1).astype(BF)
    coarse = dot(pooled, up_ref[...]).astype(BF).astype(F32)
    coarse_ref[...] = coarse
    query_ref[...] = dot(pooled, merged_ref[:, :width])
    key = dot(pooled, merged_ref[:, width : 2 * width])
    value = dot(pooled, merged_ref[:, 2 * width :])
    own = coarse_ref[pl.ds(mine, 1), :]
    query = query_ref[pl.ds(mine, 1), :]
    rms = rms_factor(coarse)
    group = 4 * HD
    spans = [slice(at, at + group) for at in range(0, width, group)]
    tall = jnp.concatenate([key[:, span] for span in spans], 0)
    queries = [query[:, span] for span in spans]
    cross = jnp.concatenate([key[:, span] * q for span, q in zip(spans, queries)], 0)
    ones = ones_ref[...]
    query_norm = head_factor(dot_split(jnp.concatenate([q * q for q in queries], 0), ones), rms_factor(own))
    key_norm = head_factor(dot_split(tall * tall, ones), jnp.concatenate([rms] * len(spans), 0))
    scores = dot_split(cross, ones) * key_norm
    count = key.shape[0]
    parts = []
    for at, span in enumerate(spans):
        factor = query_norm[at : at + 1] * scale_ref[:, span]
        expo = jnp.exp(scores[at * count : (at + 1) * count] * factor)
        total = jnp.sum(expo, 0, keepdims=True)
        parts.append(jnp.sum(expo * rms * value[:, span], 0, keepdims=True) / total)
    cattn = jnp.concatenate(parts, 1).astype(BF)
    coarse_out_ref[...] = (own + dot(cattn, out_ref[...])).astype(BF)
    wait_all(copies)


def vmem(count):
    return [pl.BlockSpec(memory_space=pltpu.VMEM)] * count


def anywhere(count):
    return [pl.BlockSpec(memory_space=pl.ANY)] * count


def in_vmem(arrays):
    return [pltpu.with_memory_space_constraint(array, pltpu.VMEM) for array in arrays]


def in_hbm(arrays):
    return [pltpu.with_memory_space_constraint(array, pltpu.HBM) for array in arrays]


def shards(
    tokens, gain_attn, qkv_fine, scale_fine, out_fine, gain_ffn, ffn_in, ffn_out,
    up_proj, gain_coarse, qkv_coarse, scale_coarse, out_coarse,
):
    rows, cols, width = tokens.shape
    count = rows * cols
    strip = RADIUS * cols
    side = rounded_up((rows + 2 * RADIUS) * RADIUS, 16)
    heads = width // HD
    width_c = out_coarse.shape[0]
    devices = lax.axis_size("ha") * lax.axis_size("wa")
    axes = ("ha", "wa")
    params = pltpu.CompilerParams(vmem_limit_bytes=16 * MIB)

    def swapped(array, axis, first):
        pairs = [(i, i + 1) for i in range(first, lax.axis_size(axis) - 1, 2)]
        return lax.ppermute(array, axis, pairs + [(j, i) for i, j in pairs])

    flat = tokens.reshape(count, width)
    across, within = pl.pallas_call(
        functools.partial(strip_kernel, rows, cols, "ha"),
        out_shape=[pltpu.VMEM((strip, width), BF)] * 2,
        in_specs=anywhere(1),
        out_specs=vmem(2),
        scratch_shapes=[pltpu.SemaphoreType.DMA((2,))],
        compiler_params=params,
        name="strips",
    )(*in_hbm([flat]))
    across = swapped(across, "ha", 1)
    within = swapped(within, "ha", 0)

    block = 256
    weights = [
        flat, qkv_fine, gain_attn.reshape(1, -1), scale_fine.reshape(1, -1),
        up_proj, gain_coarse.reshape(1, -1), scale_coarse.reshape(1, -1),
        out_fine, gain_ffn.reshape(1, -1), ffn_in, ffn_out,
    ]
    *weights, head, query, acc, ones, mask = pl.pallas_call(
        functools.partial(own_kernel, rows, cols, heads, side, axes),
        out_shape=[pltpu.VMEM(array.shape, array.dtype) for array in weights]
        + [
            pltpu.VMEM((block, 3 * width_c), BF),
            pltpu.VMEM((heads, count, 2 * HD), BF),
            pltpu.VMEM((heads, count, 2 * HD), F32),
            pltpu.VMEM((4 * HD, 4 * HD), BF),
            pltpu.VMEM((2 * strip + 2 * side, 2 * HD), BF),
        ],
        in_specs=anywhere(len(weights) + 1),
        out_specs=vmem(len(weights) + 5),
        scratch_shapes=[pltpu.SemaphoreType.DMA((len(weights) + 1,))],
        compiler_params=params,
        cost_estimate=pl.CostEstimate(
            flops=2 * count * width * (3 * width + 2 * count), bytes_accessed=4 * MIB, transcendentals=0
        ),
        name="own",
    )(*in_hbm(weights + [qkv_coarse]))
    tok_v, qkv_v, gain_attn_v, scale_v, up_v, gain_c_v, scale_c_v = weights[:7]
    out_v, gain_ffn_v, ffn_in_v, ffn_out_v = weights[7:]

    across_edge, within_edge = pl.pallas_call(
        functools.partial(edge_kernel, rows, cols, axes),
        out_shape=[pltpu.VMEM((side, width), BF)] * 2,
        in_specs=vmem(4),
        out_specs=vmem(2),
        compiler_params=params,
        name="edges",
    )(*in_vmem([tok_v, across, within, query]))
    across_side = swapped(across_edge, "wa", 1)
    within_side = swapped(within_edge, "wa", 0)

    merged, scale_lanes = pl.pallas_call(
        merge_kernel,
        out_shape=[pltpu.VMEM((width, 3 * width_c), BF), pltpu.VMEM((1, width_c), F32)],
        in_specs=vmem(5) + anywhere(1),
        out_specs=vmem(2),
        scratch_shapes=[
            pltpu.VMEM((width_c - block, 3 * width_c), BF),
            pltpu.VMEM(up_proj.shape, BF),
            pltpu.VMEM((width, 3 * width_c), F32),
            pltpu.SemaphoreType.DMA((width_c // block - 1,)),
        ],
        compiler_params=params,
        cost_estimate=pl.CostEstimate(
            flops=6 * width * width_c * width_c, bytes_accessed=8 * MIB, transcendentals=0
        ),
        name="merge",
    )(*in_vmem([within_edge, up_v, gain_c_v, scale_c_v, head]), *in_hbm([qkv_coarse]))

    def fine_body(tok_ref, *refs):
        fine_kernel(heads, tok_ref, refs[:4], *refs[4:])

    fine, pooled, out_c_v = pl.pallas_call(
        fine_body,
        out_shape=[
            pltpu.VMEM((count, width), BF),
            pltpu.VMEM((devices, width // 128, 128), F32),
            pltpu.VMEM(out_coarse.shape, BF),
        ],
        in_specs=vmem(17) + anywhere(1),
        out_specs=vmem(3),
        scratch_shapes=[pltpu.SemaphoreType.DMA((1,))],
        compiler_params=params,
        name="fine",
    )(
        *in_vmem(
            [tok_v, across, within, across_side, within_side, query, acc, ones, mask, gain_attn_v, qkv_v, scale_v]
            + [out_v, gain_ffn_v, ffn_in_v, ffn_out_v, merged]
        ),
        *in_hbm([out_coarse]),
    )

    every = lax.all_to_all(pooled, axes, split_axis=0, concat_axis=0, tiled=True)
    coarse_out, fine = pl.pallas_call(
        functools.partial(coarse_kernel, axes),
        out_shape=[
            jax.ShapeDtypeStruct((1, width_c), BF),
            jax.ShapeDtypeStruct((count, width), BF),
        ],
        in_specs=vmem(7),
        out_specs=vmem(1) + anywhere(1),
        scratch_shapes=[pltpu.VMEM((devices, width_c), F32)] * 2 + [pltpu.SemaphoreType.DMA((1,))],
        compiler_params=params,
        name="coarse",
    )(*in_vmem([every, up_v, merged, scale_lanes, out_c_v, fine, ones]))
    return fine.reshape(rows, cols, width), coarse_out.reshape(1, 1, width_c)


def solution(mesh):
    return jax.shard_map(
        shards,
        mesh=mesh,
        in_specs=(P("ha", "wa", None), P(), P(), P(), P(), P(), P(), P(), P(), P(), P(), P(), P()),
        out_specs=(P("ha", "wa", None), P("ha", "wa", None)),
        check_vma=False,
    )
```

```python
import functools

import jax
import jax.numpy as jnp
from jax import lax
from jax.experimental import pallas as pl
from jax.experimental.pallas import tpu as pltpu
from jax.sharding import PartitionSpec as P

HD = 64
RADIUS = 3
LOG2E = 1.4426950408889634
BIG = 2.0**30
BF = jnp.bfloat16
F32 = jnp.float32
MIB = 1 << 20


def rounded_up(value, step):
    return -(-value // step) * step


def over(values, size):
    assert size & (size - 1) == 0
    return values >> (size.bit_length() - 1)


def dot(a, b):
    return jnp.dot(a, b, preferred_element_type=F32)


def dot_nt(a, b):
    return lax.dot_general(a, b, (((1,), (1,)), ((), ())), preferred_element_type=F32)


def dot_split(values, ones):
    high = values.astype(BF)
    low = (values - high.astype(F32)).astype(BF)
    return dot(high, ones) + dot(low, ones)


def same_head(size):
    left = over(lax.broadcasted_iota(jnp.int32, (size, 1), 0), HD)
    right = over(lax.broadcasted_iota(jnp.int32, (1, size), 1), HD)
    return jnp.where(left == right, 1.0, 0.0).astype(BF)


def head_norm(values, ones):
    return values * lax.rsqrt(dot_split(values * values, ones) * (1.0 / HD) + 1e-06)


def rms_factor(values):
    return lax.rsqrt(jnp.mean(values * values, -1, keepdims=True) + 1e-06)


def rms_norm(values, gain):
    return values * rms_factor(values) * gain


def head_factor(squares, factor):
    return factor * lax.rsqrt(squares * (factor * factor * (1.0 / HD)) + 1e-06)


def copies_of(pairs, sems):
    return [pltpu.make_async_copy(src, dst, sems.at[i]) for i, (src, dst) in enumerate(pairs)]


def start_all(copies):
    for copy in copies:
        copy.start()


def wait_all(copies):
    for copy in copies:
        copy.wait()


def strip_kernel(rows, cols, axis, tok_hbm, across_ref, within_ref, sems):
    count, strip = rows * cols, RADIUS * cols
    odd = lax.axis_index(axis) & 1
    last = count - strip
    first = pl.multiple_of(odd * last, 16)
    second = pl.multiple_of((1 - odd) * last, 16)
    copies = copies_of(
        [
            (tok_hbm.at[pl.ds(first, strip), :], across_ref),
            (tok_hbm.at[pl.ds(second, strip), :], within_ref),
        ],
        sems,
    )
    start_all(copies)
    wait_all(copies)


def edge_kernel(rows, cols, axes, tok_ref, across_ref, within_ref, after_ref, *out_refs):
    height = rows + 2 * RADIUS
    strip = RADIUS * cols
    padded = out_refs[0].shape[0]
    odd, turn = lax.axis_index(axes[0]) & 1, lax.rem(lax.axis_index(axes[1]), len(out_refs))
    block = jnp.concatenate([tok_ref[...], across_ref[...], within_ref[...]], 0)
    out = lax.broadcasted_iota(jnp.int32, (padded, 1), 0)
    src = lax.broadcasted_iota(jnp.int32, (padded, block.shape[0]), 1)
    row = ((out * 21846) >> 16) - RADIUS
    col = out - 3 * (row + RADIUS)
    above = rows * cols + strip * odd + RADIUS * cols
    below = rows * cols + strip * (1 - odd) - rows * cols
    first = row * cols + col + jnp.where(row < 0, above, jnp.where(row >= rows, below, 0))
    first = jnp.where(out < height * RADIUS, first, -2 * cols)
    for number, out_ref in enumerate(out_refs):
        shift = jnp.where(turn == number, cols - RADIUS, 0)
        pick = jnp.where(src == first + shift, 1.0, 0.0).astype(BF)
        out_ref[...] = dot(pick, block).astype(BF)


def merge_kernel(
    after_ref, up_ref, gain_ref, scale_ref, head_ref, qkv_hbm,
    merged_ref, scale_out, weight_ref, scaled_ref, total_ref, sems,
):
    size = head_ref.shape[0]
    blocks = sems.shape[0]

    def span_of(block):
        return pl.ds(pl.multiple_of(block * size, size), size)

    def copy(block):
        return pltpu.make_async_copy(
            qkv_hbm.at[span_of(block + 1), :], weight_ref.at[span_of(block), :], sems.at[block]
        )

    for block in range(blocks):
        copy(block).start()
    lane = over(lax.broadcasted_iota(jnp.int32, scale_out.shape, 1), HD)
    scales = jnp.zeros(scale_out.shape, F32)
    for head in range(scale_ref.shape[1]):
        scales = jnp.where(lane == head, scale_ref[0:1, head : head + 1], scales)
    scale_out[...] = scales * (1.0 / HD)
    scaled_ref[...] = (up_ref[...].astype(F32) * gain_ref[...]).astype(BF)
    total_ref[...] = dot(scaled_ref[:, :size], head_ref[...])

    def step(block, carry):
        copy(block).wait()
        rows = scaled_ref[:, span_of(block + 1)]
        depth = span_of(block)
        for at in range(0, merged_ref.shape[1], size):
            span = slice(at, at + size)
            total = total_ref[:, span] + dot(rows, weight_ref[depth, span])
            total_ref[:, span] = total
            merged_ref[:, span] = total.astype(BF)
        return carry

    lax.fori_loop(0, blocks, step, 0)


def half_lanes():
    return lax.broadcasted_iota(jnp.int32, (1, 2 * HD), 1) < HD


def mask_columns(rows, cols):
    place = lax.broadcasted_iota(jnp.int32, (1, 2 * HD), 1) & (HD - 1)
    return place, place < rows, (place >= rows) & (place < rows + cols)


def query_columns(rows, cols):
    place, is_row, is_col = mask_columns(rows, cols)
    spot = lax.broadcasted_iota(jnp.int32, (rows * cols, 1), 0)
    hot = (is_row & (over(spot, cols) == place)) | (is_col & ((spot & (cols - 1)) == place - rows))
    return jnp.where(hot, 1.0, 0.0).astype(BF)


def key_columns(rows, cols, krow, kcol):
    place, is_row, is_col = mask_columns(rows, cols)
    far_row = jnp.abs(krow - place) > RADIUS
    far_col = jnp.abs(kcol - (place - rows)) > RADIUS
    return jnp.where((is_row & far_row) | (is_col & far_col), -BIG, 0.0).astype(BF)


def halo_columns(rows, cols, side, axes):
    strip = RADIUS * cols
    row_axis, col_axis = axes
    place_row, place_col = lax.axis_index(row_axis), lax.axis_index(col_axis)
    row0, col0 = place_row * rows, place_col * cols
    grid_rows = lax.axis_size(row_axis) * rows
    grid_cols = lax.axis_size(col_axis) * cols
    odd = place_row & 1
    row_at = (odd * (rows + RADIUS) - RADIUS, (1 - odd) * (rows + RADIUS) - RADIUS)
    col_at = (-RADIUS, cols)
    spot = lax.broadcasted_iota(jnp.int32, (2 * strip + 2 * side, 1), 0)
    past_first = spot - strip
    past_strips = past_first - strip
    past_third = past_strips - side
    strip_at = jnp.where(past_first >= 0, past_first, spot)
    side_at = jnp.where(past_third >= 0, past_third, past_strips)
    side_row = (side_at * 21846) >> 16
    in_strip = past_strips < 0
    krow = jnp.where(
        in_strip,
        over(strip_at, cols) + jnp.where(past_first >= 0, row_at[1], row_at[0]),
        side_row - RADIUS,
    )
    kcol = jnp.where(
        in_strip,
        strip_at & (cols - 1),
        side_at - 3 * side_row + jnp.where(past_third >= 0, col_at[1], col_at[0]),
    )
    real = in_strip | (side_at < (rows + 2 * RADIUS) * RADIUS)
    real = real & (krow + row0 >= 0) & (krow + row0 < grid_rows)
    real = real & (kcol + col0 >= 0) & (kcol + col0 < grid_cols)
    return key_columns(rows, cols, jnp.where(real, krow, -1000), kcol)


def half_of(head):
    low = half_lanes()
    lanes = 2 * HD
    return (low if head % 2 == 0 else ~low), slice(head // 2 * lanes, (head // 2 + 1) * lanes)


def attend(head, query, key, value, key_mask, factor):
    mine, span = half_of(head)
    k = jnp.where(mine, key[:, span], key_mask)
    v = jnp.where(mine, value[:, span], jnp.ones((1, 2 * HD), BF))
    weights = jnp.exp2(dot_nt(query, k) * (factor * (LOG2E / HD))).astype(BF)
    return dot(weights, v)


def own_kernel(rows, cols, heads, side, axes, *refs):
    count = (len(refs) - 7) // 2
    ins, qkv_c_hbm, outs = refs[:count], refs[count], refs[count + 1 : 2 * count + 1]
    head_ref, query_ref, acc_ref, ones_ref, mask_ref, sems = refs[2 * count + 1 :]
    tok_ref, qkv_ref, gain_ref, scale_ref = outs[:4]
    head = (qkv_c_hbm.at[pl.ds(0, head_ref.shape[0]), :], head_ref)
    copies = copies_of(list(zip(ins, outs)) + [head], sems)
    start_all(copies)
    width = heads * HD
    ones = same_head(width)
    ones_ref[...] = ones
    mask_ref[...] = halo_columns(rows, cols, side, axes)
    query_mask = query_columns(rows, cols)
    spot = lax.broadcasted_iota(jnp.int32, (rows * cols, 1), 0)
    key_mask = key_columns(rows, cols, over(spot, cols), spot & (cols - 1))
    wait_all(copies[:4])
    normed = rms_norm(tok_ref[...].astype(F32), gain_ref[...]).astype(BF)
    query = head_norm(dot(normed, qkv_ref[:, :width]), ones).astype(BF)
    key = head_norm(dot(normed, qkv_ref[:, width : 2 * width]), ones).astype(BF)
    value = dot(normed, qkv_ref[:, 2 * width :]).astype(BF)
    for head in range(heads):
        factor = scale_ref[0:1, head : head + 1]
        mine, span = half_of(head)
        masked = jnp.where(mine, query[:, span], query_mask)
        query_ref[head] = masked
        acc_ref[head] = attend(head, masked, key, value, key_mask, factor)
    wait_all(copies[4:])


def pick_one(turn, first, second, third):
    return lax.select(turn == 0, first, lax.select(turn == 1, second, third))


def fine_kernel(
    heads, axis,
    tok_ref, strip_refs, side_refs, query_ref, acc_ref, ones_ref, mask_ref, gain_attn_ref, qkv_ref, scale_ref,
    out_ref, gain_ffn_ref, ffn_in_ref, ffn_out_ref, after_ref, out_c_hbm,
    fine_ref, pooled_ref, out_c_ref, sems,
):
    copies = copies_of([(out_c_hbm, out_c_ref)], sems)
    start_all(copies)
    width = heads * HD
    turn = lax.rem(lax.axis_index(axis), 3)
    sides = [ref[...] for ref in side_refs]
    before = pick_one(turn, sides[2], sides[0], sides[1])
    after = pick_one(turn, *sides)
    halo = jnp.concatenate([ref[...] for ref in strip_refs] + [before, after], 0)
    halo = halo.astype(F32)
    scaled = (halo * gain_attn_ref[...]).astype(BF)
    halo_rms = rms_factor(halo)
    ones = ones_ref[...]
    key = dot(scaled, qkv_ref[:, width : 2 * width])
    key = (key * head_factor(dot_split(key * key, ones), halo_rms)).astype(BF)
    value = (dot(scaled, qkv_ref[:, 2 * width :]) * halo_rms).astype(BF)

    key_mask = mask_ref[...]
    low = half_lanes()
    parts = []
    for pair in range(heads // 2):
        sums = []
        for head in (2 * pair, 2 * pair + 1):
            factor = scale_ref[0:1, head : head + 1]
            sums.append(acc_ref[head] + attend(head, query_ref[head], key, value, key_mask, factor))
        top = jnp.where(low, sums[0], sums[1])
        bottom = pltpu.roll(jnp.where(low, sums[1], sums[0]), HD, 1)
        parts.append((top / bottom).astype(BF))
    attn = jnp.concatenate(parts, 1)

    h1 = (tok_ref[...].astype(F32) + dot(attn, out_ref[...])).astype(BF)
    h1_wide = h1.astype(F32)
    scaled = (h1_wide * gain_ffn_ref[...]).astype(BF)
    h1_rms = rms_factor(h1_wide)
    hidden = ffn_out_ref.shape[0]
    gate = dot(scaled, ffn_in_ref[:, :hidden]) * h1_rms
    up = dot(scaled, ffn_in_ref[:, hidden:]) * h1_rms
    gated = (jax.nn.gelu(gate, approximate=True) * up).astype(BF)
    fine = (h1_wide + dot(gated, ffn_out_ref[...])).astype(BF)
    fine_ref[...] = fine
    pooled = jnp.mean(fine.astype(F32), 0, keepdims=True).astype(BF).astype(F32)
    for part in range(pooled_ref.shape[1]):
        pooled_ref[:, part, :] = jnp.broadcast_to(
            pooled[:, part * 128 : (part + 1) * 128], (pooled_ref.shape[0], 128)
        )
    wait_all(copies)


def coarse_kernel(
    axes, pooled_ref, up_ref, merged_ref, scale_ref, out_ref, fine_ref, ones_ref,
    coarse_out_ref, fine_hbm,
    query_ref, coarse_ref, sems,
):
    copies = copies_of([(fine_ref, fine_hbm)], sems)
    start_all(copies)
    width = out_ref.shape[0]
    row_axis, col_axis = axes
    mine = lax.axis_index(row_axis) * lax.axis_size(col_axis) + lax.axis_index(col_axis)
    pooled = jnp.concatenate([pooled_ref[:, part, :] for part in range(pooled_ref.shape[1])], 1).astype(BF)
    coarse = dot(pooled, up_ref[...]).astype(BF).astype(F32)
    coarse_ref[...] = coarse
    query_ref[...] = dot(pooled, merged_ref[:, :width])
    key = dot(pooled, merged_ref[:, width : 2 * width])
    value = dot(pooled, merged_ref[:, 2 * width :])
    own = coarse_ref[pl.ds(mine, 1), :]
    query = query_ref[pl.ds(mine, 1), :]
    rms = rms_factor(coarse)
    group = 4 * HD
    spans = [slice(at, at + group) for at in range(0, width, group)]
    tall = jnp.concatenate([key[:, span] for span in spans], 0)
    queries = [query[:, span] for span in spans]
    cross = jnp.concatenate([key[:, span] * q for span, q in zip(spans, queries)], 0)
    ones = ones_ref[...]
    query_norm = head_factor(dot_split(jnp.concatenate([q * q for q in queries], 0), ones), rms_factor(own))
    key_norm = head_factor(dot_split(tall * tall, ones), jnp.concatenate([rms] * len(spans), 0))
    scores = dot_split(cross, ones) * key_norm
    count = key.shape[0]
    parts = []
    for at, span in enumerate(spans):
        factor = query_norm[at : at + 1] * scale_ref[:, span]
        expo = jnp.exp(scores[at * count : (at + 1) * count] * factor)
        total = jnp.sum(expo, 0, keepdims=True)
        parts.append(jnp.sum(expo * rms * value[:, span], 0, keepdims=True) / total)
    cattn = jnp.concatenate(parts, 1).astype(BF)
    coarse_out_ref[...] = (own + dot(cattn, out_ref[...])).astype(BF)
    wait_all(copies)


def vmem(count):
    return [pl.BlockSpec(memory_space=pltpu.VMEM)] * count


def anywhere(count):
    return [pl.BlockSpec(memory_space=pl.ANY)] * count


def in_vmem(arrays):
    return [pltpu.with_memory_space_constraint(array, pltpu.VMEM) for array in arrays]


def in_hbm(arrays):
    return [pltpu.with_memory_space_constraint(array, pltpu.HBM) for array in arrays]


def shards(
    tokens, gain_attn, qkv_fine, scale_fine, out_fine, gain_ffn, ffn_in, ffn_out,
    up_proj, gain_coarse, qkv_coarse, scale_coarse, out_coarse,
):
    rows, cols, width = tokens.shape
    count = rows * cols
    strip = RADIUS * cols
    side = rounded_up((rows + 2 * RADIUS) * RADIUS, 16)
    heads = width // HD
    width_c = out_coarse.shape[0]
    devices = lax.axis_size("ha") * lax.axis_size("wa")
    axes = ("ha", "wa")
    params = pltpu.CompilerParams(vmem_limit_bytes=16 * MIB)

    def swapped(array, axis, first, step):
        pairs = [(i, i + 1) for i in range(first, lax.axis_size(axis) - 1, step)]
        return lax.ppermute(array, axis, pairs + [(j, i) for i, j in pairs])

    flat = tokens.reshape(count, width)
    across, within = pl.pallas_call(
        functools.partial(strip_kernel, rows, cols, "ha"),
        out_shape=[pltpu.VMEM((strip, width), BF)] * 2,
        in_specs=anywhere(1),
        out_specs=vmem(2),
        scratch_shapes=[pltpu.SemaphoreType.DMA((2,))],
        compiler_params=params,
        name="strips",
    )(*in_hbm([flat]))
    across = swapped(across, "ha", 1, 2)
    within = swapped(within, "ha", 0, 2)

    block = 256
    weights = [
        flat, qkv_fine, gain_attn.reshape(1, -1), scale_fine.reshape(1, -1),
        up_proj, gain_coarse.reshape(1, -1), scale_coarse.reshape(1, -1),
        out_fine, gain_ffn.reshape(1, -1), ffn_in, ffn_out,
    ]
    *weights, head, query, acc, ones, mask = pl.pallas_call(
        functools.partial(own_kernel, rows, cols, heads, side, axes),
        out_shape=[pltpu.VMEM(array.shape, array.dtype) for array in weights]
        + [
            pltpu.VMEM((block, 3 * width_c), BF),
            pltpu.VMEM((heads, count, 2 * HD), BF),
            pltpu.VMEM((heads, count, 2 * HD), F32),
            pltpu.VMEM((4 * HD, 4 * HD), BF),
            pltpu.VMEM((2 * strip + 2 * side, 2 * HD), BF),
        ],
        in_specs=anywhere(len(weights) + 1),
        out_specs=vmem(len(weights) + 5),
        scratch_shapes=[pltpu.SemaphoreType.DMA((len(weights) + 1,))],
        compiler_params=params,
        cost_estimate=pl.CostEstimate(
            flops=2 * count * width * (3 * width + 2 * count), bytes_accessed=4 * MIB, transcendentals=0
        ),
        name="own",
    )(*in_hbm(weights + [qkv_coarse]))
    tok_v, qkv_v, gain_attn_v, scale_v, up_v, gain_c_v, scale_c_v = weights[:7]
    out_v, gain_ffn_v, ffn_in_v, ffn_out_v = weights[7:]

    edges = pl.pallas_call(
        functools.partial(edge_kernel, rows, cols, axes),
        out_shape=[pltpu.VMEM((side, width), BF)] * 3,
        in_specs=vmem(4),
        out_specs=vmem(3),
        compiler_params=params,
        name="edges",
    )(*in_vmem([tok_v, across, within, query]))
    sides = [swapped(edge, "wa", number, 3) for number, edge in enumerate(edges)]

    merged, scale_lanes = pl.pallas_call(
        merge_kernel,
        out_shape=[pltpu.VMEM((width, 3 * width_c), BF), pltpu.VMEM((1, width_c), F32)],
        in_specs=vmem(5) + anywhere(1),
        out_specs=vmem(2),
        scratch_shapes=[
            pltpu.VMEM((width_c - block, 3 * width_c), BF),
            pltpu.VMEM(up_proj.shape, BF),
            pltpu.VMEM((width, 3 * width_c), F32),
            pltpu.SemaphoreType.DMA((width_c // block - 1,)),
        ],
        compiler_params=params,
        cost_estimate=pl.CostEstimate(
            flops=6 * width * width_c * width_c, bytes_accessed=8 * MIB, transcendentals=0
        ),
        name="merge",
    )(*in_vmem([edges[2], up_v, gain_c_v, scale_c_v, head]), *in_hbm([qkv_coarse]))

    def fine_body(tok_ref, *refs):
        fine_kernel(heads, axes[1], tok_ref, refs[:2], refs[2:5], *refs[5:])

    fine, pooled, out_c_v = pl.pallas_call(
        fine_body,
        out_shape=[
            pltpu.VMEM((count, width), BF),
            pltpu.VMEM((devices, width // 128, 128), F32),
            pltpu.VMEM(out_coarse.shape, BF),
        ],
        in_specs=vmem(18) + anywhere(1),
        out_specs=vmem(3),
        scratch_shapes=[pltpu.SemaphoreType.DMA((1,))],
        compiler_params=params,
        name="fine",
    )(
        *in_vmem(
            [tok_v, across, within, *sides, query, acc, ones, mask, gain_attn_v, qkv_v, scale_v]
            + [out_v, gain_ffn_v, ffn_in_v, ffn_out_v, merged]
        ),
        *in_hbm([out_coarse]),
    )

    every = lax.all_to_all(pooled, axes, split_axis=0, concat_axis=0, tiled=True)
    coarse_out, fine = pl.pallas_call(
        functools.partial(coarse_kernel, axes),
        out_shape=[
            jax.ShapeDtypeStruct((1, width_c), BF),
            jax.ShapeDtypeStruct((count, width), BF),
        ],
        in_specs=vmem(7),
        out_specs=vmem(1) + anywhere(1),
        scratch_shapes=[pltpu.VMEM((devices, width_c), F32)] * 2 + [pltpu.SemaphoreType.DMA((1,))],
        compiler_params=params,
        name="coarse",
    )(*in_vmem([every, up_v, merged, scale_lanes, out_c_v, fine, ones]))
    return fine.reshape(rows, cols, width), coarse_out.reshape(1, 1, width_c)


def solution(mesh):
    return jax.shard_map(
        shards,
        mesh=mesh,
        in_specs=(P("ha", "wa", None), P(), P(), P(), P(), P(), P(), P(), P(), P(), P(), P(), P()),
        out_specs=(P("ha", "wa", None), P("ha", "wa", None)),
        check_vma=False,
    )
```

```python
import functools

import jax
import jax.numpy as jnp
from jax import lax
from jax.experimental import pallas as pl
from jax.experimental.pallas import tpu as pltpu
from jax.sharding import PartitionSpec as P

HD = 64
RADIUS = 3
LOG2E = 1.4426950408889634
BIG = 2.0**30
GELU = 0.7978845608028654
BF = jnp.bfloat16
F32 = jnp.float32
MIB = 1 << 20


def rounded_up(value, step):
    return -(-value // step) * step


def over(values, size):
    assert size & (size - 1) == 0
    return values >> (size.bit_length() - 1)


def dot(a, b):
    return jnp.dot(a, b, preferred_element_type=F32)


def dot_nt(a, b):
    return lax.dot_general(a, b, (((1,), (1,)), ((), ())), preferred_element_type=F32)


def dot_split(values, ones):
    high = values.astype(BF)
    low = (values - high.astype(F32)).astype(BF)
    return dot(high, ones) + dot(low, ones)


def same_head(size):
    left = over(lax.broadcasted_iota(jnp.int32, (size, 1), 0), HD)
    right = over(lax.broadcasted_iota(jnp.int32, (1, size), 1), HD)
    return jnp.where(left == right, 1.0, 0.0).astype(BF)


def head_norm(values, ones):
    return values * lax.rsqrt(dot((values * values).astype(BF), ones) * (1.0 / HD) + 1e-06)


def rms_factor(values):
    return lax.rsqrt(jnp.mean(values * values, -1, keepdims=True) + 1e-06)


def rms_norm(values, gain):
    return values * rms_factor(values) * gain


def head_factor(squares, factor):
    return factor * lax.rsqrt(squares * (factor * factor * (1.0 / HD)) + 1e-06)


def copies_of(pairs, sems):
    return [pltpu.make_async_copy(src, dst, sems.at[i]) for i, (src, dst) in enumerate(pairs)]


def start_all(copies):
    for copy in copies:
        copy.start()


def wait_all(copies):
    for copy in copies:
        copy.wait()


def strip_kernel(rows, cols, axis, tok_hbm, across_ref, within_ref, sems):
    count, strip = rows * cols, RADIUS * cols
    odd = lax.axis_index(axis) & 1
    last = count - strip
    first = pl.multiple_of(odd * last, 16)
    second = pl.multiple_of((1 - odd) * last, 16)
    copies = copies_of(
        [
            (tok_hbm.at[pl.ds(first, strip), :], across_ref),
            (tok_hbm.at[pl.ds(second, strip), :], within_ref),
        ],
        sems,
    )
    start_all(copies)
    wait_all(copies)


def edge_kernel(rows, cols, axes, tok_ref, across_ref, within_ref, after_ref, across_out, within_out):
    height = rows + 2 * RADIUS
    strip = RADIUS * cols
    padded = across_out.shape[0]
    odd, odd_col = lax.axis_index(axes[0]) & 1, lax.axis_index(axes[1]) & 1
    block = jnp.concatenate([tok_ref[...], across_ref[...], within_ref[...]], 0)
    out = lax.broadcasted_iota(jnp.int32, (padded, 1), 0)
    src = lax.broadcasted_iota(jnp.int32, (padded, block.shape[0]), 1)
    row = ((out * 21846) >> 16) - RADIUS
    col = out - 3 * (row + RADIUS)
    above = rows * cols + strip * odd + RADIUS * cols
    below = rows * cols + strip * (1 - odd) - rows * cols
    first = row * cols + col + jnp.where(row < 0, above, jnp.where(row >= rows, below, 0))
    first = jnp.where(out < height * RADIUS, first, -2 * cols)
    far = cols - RADIUS
    pick = jnp.where(src == first + far * odd_col, 1.0, 0.0).astype(BF)
    across_out[...] = dot(pick, block).astype(BF)
    pick = jnp.where(src == first + far * (1 - odd_col), 1.0, 0.0).astype(BF)
    within_out[...] = dot(pick, block).astype(BF)


def merge_kernel(
    after_ref, up_ref, gain_ref, scale_ref, head_ref, qkv_hbm,
    merged_ref, scale_out, weight_ref, scaled_ref, total_ref, sems,
):
    size = head_ref.shape[0]
    blocks = sems.shape[0]

    def span_of(block):
        return pl.ds(pl.multiple_of(block * size, size), size)

    def copy(block):
        return pltpu.make_async_copy(
            qkv_hbm.at[span_of(block + 1), :], weight_ref.at[span_of(block), :], sems.at[block]
        )

    for block in range(blocks):
        copy(block).start()
    lane = over(lax.broadcasted_iota(jnp.int32, scale_out.shape, 1), HD)
    scales = jnp.zeros(scale_out.shape, F32)
    for head in range(scale_ref.shape[1]):
        scales = jnp.where(lane == head, scale_ref[0:1, head : head + 1], scales)
    scale_out[...] = scales * (1.0 / HD)
    scaled_ref[...] = (up_ref[...].astype(F32) * gain_ref[...]).astype(BF)
    total_ref[...] = dot(scaled_ref[:, :size], head_ref[...])

    def step(block, carry):
        copy(block).wait()
        rows = scaled_ref[:, span_of(block + 1)]
        depth = span_of(block)
        for at in range(0, merged_ref.shape[1], size):
            span = slice(at, at + size)
            total = total_ref[:, span] + dot(rows, weight_ref[depth, span])
            total_ref[:, span] = total
            merged_ref[:, span] = total.astype(BF)
        return carry

    lax.fori_loop(0, blocks, step, 0)


def half_lanes():
    return lax.broadcasted_iota(jnp.int32, (1, 2 * HD), 1) < HD


def mask_columns(rows, cols):
    place = lax.broadcasted_iota(jnp.int32, (1, 2 * HD), 1) & (HD - 1)
    return place, place < rows, (place >= rows) & (place < rows + cols)


def query_columns(rows, cols):
    place, is_row, is_col = mask_columns(rows, cols)
    spot = lax.broadcasted_iota(jnp.int32, (rows * cols, 1), 0)
    hot = (is_row & (over(spot, cols) == place)) | (is_col & ((spot & (cols - 1)) == place - rows))
    return jnp.where(hot, 1.0, 0.0).astype(BF)


def key_columns(rows, cols, krow, kcol):
    place, is_row, is_col = mask_columns(rows, cols)
    far_row = jnp.abs(krow - place) > RADIUS
    far_col = jnp.abs(kcol - (place - rows)) > RADIUS
    return jnp.where((is_row & far_row) | (is_col & far_col), -BIG, 0.0).astype(BF)


def halo_columns(rows, cols, side, axes):
    strip = RADIUS * cols
    row_axis, col_axis = axes
    place_row, place_col = lax.axis_index(row_axis), lax.axis_index(col_axis)
    row0, col0 = place_row * rows, place_col * cols
    grid_rows = lax.axis_size(row_axis) * rows
    grid_cols = lax.axis_size(col_axis) * cols
    odd, odd_col = place_row & 1, place_col & 1
    row_at = (odd * (rows + RADIUS) - RADIUS, (1 - odd) * (rows + RADIUS) - RADIUS)
    col_at = (odd_col * (cols + RADIUS) - RADIUS, (1 - odd_col) * (cols + RADIUS) - RADIUS)
    spot = lax.broadcasted_iota(jnp.int32, (2 * strip + 2 * side, 1), 0)
    past_first = spot - strip
    past_strips = past_first - strip
    past_third = past_strips - side
    strip_at = jnp.where(past_first >= 0, past_first, spot)
    side_at = jnp.where(past_third >= 0, past_third, past_strips)
    side_row = (side_at * 21846) >> 16
    in_strip = past_strips < 0
    krow = jnp.where(
        in_strip,
        over(strip_at, cols) + jnp.where(past_first >= 0, row_at[1], row_at[0]),
        side_row - RADIUS,
    )
    kcol = jnp.where(
        in_strip,
        strip_at & (cols - 1),
        side_at - 3 * side_row + jnp.where(past_third >= 0, col_at[1], col_at[0]),
    )
    real = in_strip | (side_at < (rows + 2 * RADIUS) * RADIUS)
    real = real & (krow + row0 >= 0) & (krow + row0 < grid_rows)
    real = real & (kcol + col0 >= 0) & (kcol + col0 < grid_cols)
    return key_columns(rows, cols, jnp.where(real, krow, -1000), kcol)


def half_of(head):
    low = half_lanes()
    lanes = 2 * HD
    return (low if head % 2 == 0 else ~low), slice(head // 2 * lanes, (head // 2 + 1) * lanes)


def attend(head, query, key, value, key_mask, factor):
    mine, span = half_of(head)
    k = jnp.where(mine, key[:, span], key_mask)
    v = jnp.where(mine, value[:, span], jnp.ones((1, 2 * HD), BF))
    weights = jnp.exp2(dot_nt(query, k) * (factor * (LOG2E / HD))).astype(BF)
    return dot(weights, v)


def own_kernel(rows, cols, heads, side, axes, *refs):
    count = (len(refs) - 7) // 2
    ins, qkv_c_hbm, outs = refs[:count], refs[count], refs[count + 1 : 2 * count + 1]
    head_ref, query_ref, acc_ref, ones_ref, mask_ref, sems = refs[2 * count + 1 :]
    tok_ref, qkv_ref, gain_ref, scale_ref = outs[:4]
    head = (qkv_c_hbm.at[pl.ds(0, head_ref.shape[0]), :], head_ref)
    copies = copies_of(list(zip(ins, outs)) + [head], sems)
    start_all(copies)
    width = heads * HD
    ones = same_head(width)
    ones_ref[...] = ones
    mask_ref[...] = halo_columns(rows, cols, side, axes)
    query_mask = query_columns(rows, cols)
    spot = lax.broadcasted_iota(jnp.int32, (rows * cols, 1), 0)
    key_mask = key_columns(rows, cols, over(spot, cols), spot & (cols - 1))
    wait_all(copies[:4])
    normed = rms_norm(tok_ref[...].astype(F32), gain_ref[...]).astype(BF)
    query = head_norm(dot(normed, qkv_ref[:, :width]), ones).astype(BF)
    key = head_norm(dot(normed, qkv_ref[:, width : 2 * width]), ones).astype(BF)
    value = dot(normed, qkv_ref[:, 2 * width :]).astype(BF)
    for head in range(heads):
        factor = scale_ref[0:1, head : head + 1]
        mine, span = half_of(head)
        masked = jnp.where(mine, query[:, span], query_mask)
        query_ref[head] = masked
        acc_ref[head] = attend(head, masked, key, value, key_mask, factor)
    wait_all(copies[4:])


def fine_kernel(
    heads,
    tok_ref, halo_refs, query_ref, acc_ref, ones_ref, mask_ref, gain_attn_ref, qkv_ref, scale_ref,
    out_ref, gain_ffn_ref, ffn_in_ref, ffn_out_ref, after_ref, out_c_hbm,
    fine_ref, pooled_ref, out_c_ref, sems,
):
    copies = copies_of([(out_c_hbm, out_c_ref)], sems)
    start_all(copies)
    width = heads * HD
    halo = jnp.concatenate([ref[...] for ref in halo_refs], 0)
    halo = halo.astype(F32)
    scaled = (halo * gain_attn_ref[...]).astype(BF)
    halo_rms = rms_factor(halo)
    ones = ones_ref[...]
    key = dot(scaled, qkv_ref[:, width : 2 * width])
    key = (key * head_factor(dot((key * key).astype(BF), ones), halo_rms)).astype(BF)
    value = (dot(scaled, qkv_ref[:, 2 * width :]) * halo_rms).astype(BF)

    key_mask = mask_ref[...]
    low = half_lanes()
    parts = []
    for pair in range(heads // 2):
        sums = []
        for head in (2 * pair, 2 * pair + 1):
            factor = scale_ref[0:1, head : head + 1]
            sums.append(acc_ref[head] + attend(head, query_ref[head], key, value, key_mask, factor))
        top = jnp.where(low, sums[0], sums[1])
        bottom = pltpu.roll(jnp.where(low, sums[1], sums[0]), HD, 1)
        parts.append((top / bottom).astype(BF))
    attn = jnp.concatenate(parts, 1)

    h1 = (tok_ref[...].astype(F32) + dot(attn, out_ref[...])).astype(BF)
    h1_wide = h1.astype(F32)
    scaled = (h1_wide * gain_ffn_ref[...]).astype(BF)
    h1_rms = rms_factor(h1_wide)
    hidden = ffn_out_ref.shape[0]
    gate = dot(scaled, ffn_in_ref[:, :hidden]) * h1_rms
    up = dot(scaled, ffn_in_ref[:, hidden:]) * (0.5 * h1_rms)
    inner = gate * (GELU + (GELU * 0.044715) * (gate * gate))
    gated = (gate * up * (1.0 + jnp.tanh(inner))).astype(BF)
    fine = (h1_wide + dot(gated, ffn_out_ref[...])).astype(BF)
    fine_ref[...] = fine
    pooled = jnp.mean(fine.astype(F32), 0, keepdims=True).astype(BF).astype(F32)
    for part in range(pooled_ref.shape[1]):
        pooled_ref[:, part, :] = jnp.broadcast_to(
            pooled[:, part * 128 : (part + 1) * 128], (pooled_ref.shape[0], 128)
        )
    wait_all(copies)


def coarse_kernel(
    axes, pooled_ref, up_ref, merged_ref, scale_ref, out_ref, fine_ref, ones_ref,
    coarse_out_ref, fine_hbm,
    query_ref, coarse_ref, sems,
):
    copies = copies_of([(fine_ref, fine_hbm)], sems)
    start_all(copies)
    width = out_ref.shape[0]
    row_axis, col_axis = axes
    mine = lax.axis_index(row_axis) * lax.axis_size(col_axis) + lax.axis_index(col_axis)
    pooled = jnp.concatenate([pooled_ref[:, part, :] for part in range(pooled_ref.shape[1])], 1).astype(BF)
    coarse = dot(pooled, up_ref[...]).astype(BF).astype(F32)
    coarse_ref[...] = coarse
    query_ref[...] = dot(pooled, merged_ref[:, :width])
    key = dot(pooled, merged_ref[:, width : 2 * width])
    value = dot(pooled, merged_ref[:, 2 * width :])
    own = coarse_ref[pl.ds(mine, 1), :]
    query = query_ref[pl.ds(mine, 1), :]
    rms = rms_factor(coarse)
    group = 4 * HD
    spans = [slice(at, at + group) for at in range(0, width, group)]
    tall = jnp.concatenate([key[:, span] for span in spans], 0)
    queries = [query[:, span] for span in spans]
    cross = jnp.concatenate([key[:, span] * q for span, q in zip(spans, queries)], 0)
    ones = ones_ref[...]
    query_norm = head_factor(dot_split(jnp.concatenate([q * q for q in queries], 0), ones), rms_factor(own))
    key_norm = head_factor(dot_split(tall * tall, ones), jnp.concatenate([rms] * len(spans), 0))
    scores = dot_split(cross, ones) * key_norm
    count = key.shape[0]
    parts = []
    for at, span in enumerate(spans):
        factor = query_norm[at : at + 1] * scale_ref[:, span]
        expo = jnp.exp(scores[at * count : (at + 1) * count] * factor)
        total = jnp.sum(expo, 0, keepdims=True)
        parts.append(jnp.sum(expo * rms * value[:, span], 0, keepdims=True) / total)
    cattn = jnp.concatenate(parts, 1).astype(BF)
    coarse_out_ref[...] = (own + dot(cattn, out_ref[...])).astype(BF)
    wait_all(copies)


def vmem(count):
    return [pl.BlockSpec(memory_space=pltpu.VMEM)] * count


def anywhere(count):
    return [pl.BlockSpec(memory_space=pl.ANY)] * count


def in_vmem(arrays):
    return [pltpu.with_memory_space_constraint(array, pltpu.VMEM) for array in arrays]


def in_hbm(arrays):
    return [pltpu.with_memory_space_constraint(array, pltpu.HBM) for array in arrays]


def shards(
    tokens, gain_attn, qkv_fine, scale_fine, out_fine, gain_ffn, ffn_in, ffn_out,
    up_proj, gain_coarse, qkv_coarse, scale_coarse, out_coarse,
):
    rows, cols, width = tokens.shape
    count = rows * cols
    strip = RADIUS * cols
    side = rounded_up((rows + 2 * RADIUS) * RADIUS, 16)
    heads = width // HD
    width_c = out_coarse.shape[0]
    devices = lax.axis_size("ha") * lax.axis_size("wa")
    axes = ("ha", "wa")
    params = pltpu.CompilerParams(vmem_limit_bytes=16 * MIB)

    def swapped(array, axis, first):
        pairs = [(i, i + 1) for i in range(first, lax.axis_size(axis) - 1, 2)]
        return lax.ppermute(array, axis, pairs + [(j, i) for i, j in pairs])

    flat = tokens.reshape(count, width)
    across, within = pl.pallas_call(
        functools.partial(strip_kernel, rows, cols, "ha"),
        out_shape=[pltpu.VMEM((strip, width), BF)] * 2,
        in_specs=anywhere(1),
        out_specs=vmem(2),
        scratch_shapes=[pltpu.SemaphoreType.DMA((2,))],
        compiler_params=params,
        name="strips",
    )(*in_hbm([flat]))
    across = swapped(across, "ha", 1)
    within = swapped(within, "ha", 0)

    block = 256
    weights = [
        flat, qkv_fine, gain_attn.reshape(1, -1), scale_fine.reshape(1, -1),
        up_proj, gain_coarse.reshape(1, -1), scale_coarse.reshape(1, -1),
        out_fine, gain_ffn.reshape(1, -1), ffn_in, ffn_out,
    ]
    *weights, head, query, acc, ones, mask = pl.pallas_call(
        functools.partial(own_kernel, rows, cols, heads, side, axes),
        out_shape=[pltpu.VMEM(array.shape, array.dtype) for array in weights]
        + [
            pltpu.VMEM((block, 3 * width_c), BF),
            pltpu.VMEM((heads, count, 2 * HD), BF),
            pltpu.VMEM((heads, count, 2 * HD), F32),
            pltpu.VMEM((4 * HD, 4 * HD), BF),
            pltpu.VMEM((2 * strip + 2 * side, 2 * HD), BF),
        ],
        in_specs=anywhere(len(weights) + 1),
        out_specs=vmem(len(weights) + 5),
        scratch_shapes=[pltpu.SemaphoreType.DMA((len(weights) + 1,))],
        compiler_params=params,
        cost_estimate=pl.CostEstimate(
            flops=2 * count * width * (3 * width + 2 * count), bytes_accessed=4 * MIB, transcendentals=0
        ),
        name="own",
    )(*in_hbm(weights + [qkv_coarse]))
    tok_v, qkv_v, gain_attn_v, scale_v, up_v, gain_c_v, scale_c_v = weights[:7]
    out_v, gain_ffn_v, ffn_in_v, ffn_out_v = weights[7:]

    across_edge, within_edge = pl.pallas_call(
        functools.partial(edge_kernel, rows, cols, axes),
        out_shape=[pltpu.VMEM((side, width), BF)] * 2,
        in_specs=vmem(4),
        out_specs=vmem(2),
        compiler_params=params,
        name="edges",
    )(*in_vmem([tok_v, across, within, query]))
    across_side = swapped(across_edge, "wa", 1)
    within_side = swapped(within_edge, "wa", 0)

    merged, scale_lanes = pl.pallas_call(
        merge_kernel,
        out_shape=[pltpu.VMEM((width, 3 * width_c), BF), pltpu.VMEM((1, width_c), F32)],
        in_specs=vmem(5) + anywhere(1),
        out_specs=vmem(2),
        scratch_shapes=[
            pltpu.VMEM((width_c - block, 3 * width_c), BF),
            pltpu.VMEM(up_proj.shape, BF),
            pltpu.VMEM((width, 3 * width_c), F32),
            pltpu.SemaphoreType.DMA((width_c // block - 1,)),
        ],
        compiler_params=params,
        cost_estimate=pl.CostEstimate(
            flops=6 * width * width_c * width_c, bytes_accessed=8 * MIB, transcendentals=0
        ),
        name="merge",
    )(*in_vmem([within_edge, up_v, gain_c_v, scale_c_v, head]), *in_hbm([qkv_coarse]))

    def fine_body(tok_ref, *refs):
        fine_kernel(heads, tok_ref, refs[:4], *refs[4:])

    fine, pooled, out_c_v = pl.pallas_call(
        fine_body,
        out_shape=[
            pltpu.VMEM((count, width), BF),
            pltpu.VMEM((devices, width // 128, 128), F32),
            pltpu.VMEM(out_coarse.shape, BF),
        ],
        in_specs=vmem(17) + anywhere(1),
        out_specs=vmem(3),
        scratch_shapes=[pltpu.SemaphoreType.DMA((1,))],
        compiler_params=params,
        name="fine",
    )(
        *in_vmem(
            [tok_v, across, within, across_side, within_side, query, acc, ones, mask, gain_attn_v, qkv_v, scale_v]
            + [out_v, gain_ffn_v, ffn_in_v, ffn_out_v, merged]
        ),
        *in_hbm([out_coarse]),
    )

    every = lax.all_to_all(pooled, axes, split_axis=0, concat_axis=0, tiled=True)
    coarse_out, fine = pl.pallas_call(
        functools.partial(coarse_kernel, axes),
        out_shape=[
            jax.ShapeDtypeStruct((1, width_c), BF),
            jax.ShapeDtypeStruct((count, width), BF),
        ],
        in_specs=vmem(7),
        out_specs=vmem(1) + anywhere(1),
        scratch_shapes=[pltpu.VMEM((devices, width_c), F32)] * 2 + [pltpu.SemaphoreType.DMA((1,))],
        compiler_params=params,
        name="coarse",
    )(*in_vmem([every, up_v, merged, scale_lanes, out_c_v, fine, ones]))
    return fine.reshape(rows, cols, width), coarse_out.reshape(1, 1, width_c)


def solution(mesh):
    return jax.shard_map(
        shards,
        mesh=mesh,
        in_specs=(P("ha", "wa", None), P(), P(), P(), P(), P(), P(), P(), P(), P(), P(), P(), P()),
        out_specs=(P("ha", "wa", None), P("ha", "wa", None)),
        check_vma=False,
    )
```

```python
import functools

import jax
import jax.numpy as jnp
from jax import lax
from jax.experimental import pallas as pl
from jax.experimental.pallas import tpu as pltpu
from jax.sharding import PartitionSpec as P

HD = 64
RADIUS = 3
LOG2E = 1.4426950408889634
BIG = 2.0**30
GELU = 0.7978845608028654
BF = jnp.bfloat16
F32 = jnp.float32
MIB = 1 << 20


def rounded_up(value, step):
    return -(-value // step) * step


def over(values, size):
    assert size & (size - 1) == 0
    return values >> (size.bit_length() - 1)


def dot(a, b):
    return jnp.dot(a, b, preferred_element_type=F32)


def dot_nt(a, b):
    return lax.dot_general(a, b, (((1,), (1,)), ((), ())), preferred_element_type=F32)


def dot_split(values, ones):
    high = values.astype(BF)
    low = (values - high.astype(F32)).astype(BF)
    return dot(high, ones) + dot(low, ones)


def same_head(size):
    left = over(lax.broadcasted_iota(jnp.int32, (size, 1), 0), HD)
    right = over(lax.broadcasted_iota(jnp.int32, (1, size), 1), HD)
    return jnp.where(left == right, 1.0, 0.0).astype(BF)


def head_norm(values, ones):
    return values * lax.rsqrt(dot((values * values).astype(BF), ones) * (1.0 / HD) + 1e-06)


def rms_factor(values):
    return lax.rsqrt(jnp.mean(values * values, -1, keepdims=True) + 1e-06)


def rms_norm(values, gain):
    return values * rms_factor(values) * gain


def head_factor(squares, factor):
    return factor * lax.rsqrt(squares * (factor * factor * (1.0 / HD)) + 1e-06)


def copies_of(pairs, sems):
    return [pltpu.make_async_copy(src, dst, sems.at[i]) for i, (src, dst) in enumerate(pairs)]


def start_all(copies):
    for copy in copies:
        copy.start()


def wait_all(copies):
    for copy in copies:
        copy.wait()


def strip_kernel(rows, cols, axis, tok_hbm, across_ref, within_ref, sems):
    count, strip = rows * cols, RADIUS * cols
    odd = lax.axis_index(axis) & 1
    last = count - strip
    first = pl.multiple_of(odd * last, 16)
    second = pl.multiple_of((1 - odd) * last, 16)
    copies = copies_of(
        [
            (tok_hbm.at[pl.ds(first, strip), :], across_ref),
            (tok_hbm.at[pl.ds(second, strip), :], within_ref),
        ],
        sems,
    )
    start_all(copies)
    wait_all(copies)


def edge_kernel(rows, cols, axes, tok_ref, across_ref, within_ref, after_ref, across_out, within_out):
    height = rows + 2 * RADIUS
    strip = RADIUS * cols
    padded = across_out.shape[0]
    odd, odd_col = lax.axis_index(axes[0]) & 1, lax.axis_index(axes[1]) & 1
    block = jnp.concatenate([tok_ref[...], across_ref[...], within_ref[...]], 0)
    out = lax.broadcasted_iota(jnp.int32, (padded, 1), 0)
    src = lax.broadcasted_iota(jnp.int32, (padded, block.shape[0]), 1)
    row = ((out * 21846) >> 16) - RADIUS
    col = out - 3 * (row + RADIUS)
    above = rows * cols + strip * odd + RADIUS * cols
    below = rows * cols + strip * (1 - odd) - rows * cols
    first = row * cols + col + jnp.where(row < 0, above, jnp.where(row >= rows, below, 0))
    first = jnp.where(out < height * RADIUS, first, -2 * cols)
    far = cols - RADIUS
    pick = jnp.where(src == first + far * odd_col, 1.0, 0.0).astype(BF)
    across_out[...] = dot(pick, block).astype(BF)
    pick = jnp.where(src == first + far * (1 - odd_col), 1.0, 0.0).astype(BF)
    within_out[...] = dot(pick, block).astype(BF)


def merge_kernel(
    after_ref, up_ref, gain_ref, scale_ref, head_ref, qkv_hbm,
    merged_ref, scale_out, weight_ref, scaled_ref, total_ref, sems,
):
    size = head_ref.shape[0]
    blocks = sems.shape[0]

    def span_of(block):
        return pl.ds(pl.multiple_of(block * size, size), size)

    def copy(block):
        return pltpu.make_async_copy(
            qkv_hbm.at[span_of(block + 1), :], weight_ref.at[span_of(block), :], sems.at[block]
        )

    for block in range(blocks):
        copy(block).start()
    lane = over(lax.broadcasted_iota(jnp.int32, scale_out.shape, 1), HD)
    scales = jnp.zeros(scale_out.shape, F32)
    for head in range(scale_ref.shape[1]):
        scales = jnp.where(lane == head, scale_ref[0:1, head : head + 1], scales)
    scale_out[...] = scales * (1.0 / HD)
    scaled_ref[...] = (up_ref[...].astype(F32) * gain_ref[...]).astype(BF)
    wide = 4 * size
    rows = scaled_ref[:, :size]

    def begin(part, carry):
        span = pl.ds(pl.multiple_of(part * wide, wide), wide)
        total_ref[:, span] = dot(rows, head_ref[:, span])
        return carry

    lax.fori_loop(0, merged_ref.shape[1] // wide, begin, 0)

    def step(block, carry):
        copy(block).wait()
        rows = scaled_ref[:, span_of(block + 1)]
        depth = span_of(block)
        for at in range(0, merged_ref.shape[1], size):
            span = slice(at, at + size)
            total = total_ref[:, span] + dot(rows, weight_ref[depth, span])
            total_ref[:, span] = total
            merged_ref[:, span] = total.astype(BF)
        return carry

    lax.fori_loop(0, blocks, step, 0)


def half_lanes():
    return lax.broadcasted_iota(jnp.int32, (1, 2 * HD), 1) < HD


def mask_columns(rows, cols):
    place = lax.broadcasted_iota(jnp.int32, (1, 2 * HD), 1) & (HD - 1)
    return place, place < rows, (place >= rows) & (place < rows + cols)


def query_columns(rows, cols):
    place, is_row, is_col = mask_columns(rows, cols)
    spot = lax.broadcasted_iota(jnp.int32, (rows * cols, 1), 0)
    hot = (is_row & (over(spot, cols) == place)) | (is_col & ((spot & (cols - 1)) == place - rows))
    return jnp.where(hot, 1.0, 0.0).astype(BF)


def key_columns(rows, cols, krow, kcol):
    place, is_row, is_col = mask_columns(rows, cols)
    far_row = jnp.abs(krow - place) > RADIUS
    far_col = jnp.abs(kcol - (place - rows)) > RADIUS
    return jnp.where((is_row & far_row) | (is_col & far_col), -BIG, 0.0).astype(BF)


def halo_columns(rows, cols, side, axes):
    strip = RADIUS * cols
    row_axis, col_axis = axes
    place_row, place_col = lax.axis_index(row_axis), lax.axis_index(col_axis)
    row0, col0 = place_row * rows, place_col * cols
    grid_rows = lax.axis_size(row_axis) * rows
    grid_cols = lax.axis_size(col_axis) * cols
    odd, odd_col = place_row & 1, place_col & 1
    row_at = (odd * (rows + RADIUS) - RADIUS, (1 - odd) * (rows + RADIUS) - RADIUS)
    col_at = (odd_col * (cols + RADIUS) - RADIUS, (1 - odd_col) * (cols + RADIUS) - RADIUS)
    spot = lax.broadcasted_iota(jnp.int32, (2 * strip + 2 * side, 1), 0)
    past_first = spot - strip
    past_strips = past_first - strip
    past_third = past_strips - side
    strip_at = jnp.where(past_first >= 0, past_first, spot)
    side_at = jnp.where(past_third >= 0, past_third, past_strips)
    side_row = (side_at * 21846) >> 16
    in_strip = past_strips < 0
    krow = jnp.where(
        in_strip,
        over(strip_at, cols) + jnp.where(past_first >= 0, row_at[1], row_at[0]),
        side_row - RADIUS,
    )
    kcol = jnp.where(
        in_strip,
        strip_at & (cols - 1),
        side_at - 3 * side_row + jnp.where(past_third >= 0, col_at[1], col_at[0]),
    )
    real = in_strip | (side_at < (rows + 2 * RADIUS) * RADIUS)
    real = real & (krow + row0 >= 0) & (krow + row0 < grid_rows)
    real = real & (kcol + col0 >= 0) & (kcol + col0 < grid_cols)
    return key_columns(rows, cols, jnp.where(real, krow, -1000), kcol)


def half_of(head):
    low = half_lanes()
    lanes = 2 * HD
    return (low if head % 2 == 0 else ~low), slice(head // 2 * lanes, (head // 2 + 1) * lanes)


def attend(head, query, key, value, key_mask, factor):
    mine, span = half_of(head)
    k = jnp.where(mine, key[:, span], key_mask)
    v = jnp.where(mine, value[:, span], jnp.ones((1, 2 * HD), BF))
    weights = jnp.exp2(dot_nt(query, k) * (factor * (LOG2E / HD))).astype(BF)
    return dot(weights, v)


def own_kernel(rows, cols, heads, side, axes, *refs):
    count = (len(refs) - 7) // 2
    ins, qkv_c_hbm, outs = refs[:count], refs[count], refs[count + 1 : 2 * count + 1]
    head_ref, query_ref, acc_ref, ones_ref, mask_ref, sems = refs[2 * count + 1 :]
    tok_ref, qkv_ref, gain_ref, scale_ref = outs[:4]
    head = (qkv_c_hbm.at[pl.ds(0, head_ref.shape[0]), :], head_ref)
    copies = copies_of(list(zip(ins, outs)) + [head], sems)
    start_all(copies)
    width = heads * HD
    ones = same_head(width)
    ones_ref[...] = ones
    mask_ref[...] = halo_columns(rows, cols, side, axes)
    query_mask = query_columns(rows, cols)
    spot = lax.broadcasted_iota(jnp.int32, (rows * cols, 1), 0)
    key_mask = key_columns(rows, cols, over(spot, cols), spot & (cols - 1))
    wait_all(copies[:4])
    normed = rms_norm(tok_ref[...].astype(F32), gain_ref[...]).astype(BF)
    query = head_norm(dot(normed, qkv_ref[:, :width]), ones).astype(BF)
    key = head_norm(dot(normed, qkv_ref[:, width : 2 * width]), ones).astype(BF)
    value = dot(normed, qkv_ref[:, 2 * width :]).astype(BF)
    for head in range(heads):
        factor = scale_ref[0:1, head : head + 1]
        mine, span = half_of(head)
        masked = jnp.where(mine, query[:, span], query_mask)
        query_ref[head] = masked
        acc_ref[head] = attend(head, masked, key, value, key_mask, factor)
    wait_all(copies[4:])


def fine_kernel(
    heads,
    tok_ref, halo_refs, query_ref, acc_ref, ones_ref, mask_ref, gain_attn_ref, qkv_ref, scale_ref,
    out_ref, gain_ffn_ref, ffn_in_ref, ffn_out_ref, after_ref, out_c_hbm,
    fine_ref, pooled_ref, out_c_ref, sems,
):
    copies = copies_of([(out_c_hbm, out_c_ref)], sems)
    start_all(copies)
    width = heads * HD
    halo = jnp.concatenate([ref[...] for ref in halo_refs], 0)
    halo = halo.astype(F32)
    scaled = (halo * gain_attn_ref[...]).astype(BF)
    halo_rms = rms_factor(halo)
    ones = ones_ref[...]
    key = dot(scaled, qkv_ref[:, width : 2 * width])
    key = (key * head_factor(dot((key * key).astype(BF), ones), halo_rms)).astype(BF)
    value = (dot(scaled, qkv_ref[:, 2 * width :]) * halo_rms).astype(BF)

    key_mask = mask_ref[...]
    low = half_lanes()
    parts = []
    for pair in range(heads // 2):
        sums = []
        for head in (2 * pair, 2 * pair + 1):
            factor = scale_ref[0:1, head : head + 1]
            sums.append(acc_ref[head] + attend(head, query_ref[head], key, value, key_mask, factor))
        top = jnp.where(low, sums[0], sums[1])
        bottom = pltpu.roll(jnp.where(low, sums[1], sums[0]), HD, 1)
        parts.append((top / bottom).astype(BF))
    attn = jnp.concatenate(parts, 1)

    h1 = (tok_ref[...].astype(F32) + dot(attn, out_ref[...])).astype(BF)
    h1_wide = h1.astype(F32)
    scaled = (h1_wide * gain_ffn_ref[...]).astype(BF)
    h1_rms = rms_factor(h1_wide)
    hidden = ffn_out_ref.shape[0]
    gate = dot(scaled, ffn_in_ref[:, :hidden]) * h1_rms
    up = dot(scaled, ffn_in_ref[:, hidden:]) * (0.5 * h1_rms)
    inner = gate * (GELU + (GELU * 0.044715) * (gate * gate))
    gated = (gate * up * (1.0 + jnp.tanh(inner))).astype(BF)
    fine = (h1_wide + dot(gated, ffn_out_ref[...])).astype(BF)
    fine_ref[...] = fine
    pooled = jnp.mean(fine.astype(F32), 0, keepdims=True).astype(BF).astype(F32)
    for part in range(pooled_ref.shape[1]):
        pooled_ref[:, part, :] = jnp.broadcast_to(
            pooled[:, part * 128 : (part + 1) * 128], (pooled_ref.shape[0], 128)
        )
    wait_all(copies)


def coarse_kernel(
    axes, pooled_ref, up_ref, merged_ref, scale_ref, out_ref, fine_ref, ones_ref,
    coarse_out_ref, fine_hbm,
    query_ref, coarse_ref, sems,
):
    copies = copies_of([(fine_ref, fine_hbm)], sems)
    start_all(copies)
    width = out_ref.shape[0]
    row_axis, col_axis = axes
    mine = lax.axis_index(row_axis) * lax.axis_size(col_axis) + lax.axis_index(col_axis)
    pooled = jnp.concatenate([pooled_ref[:, part, :] for part in range(pooled_ref.shape[1])], 1).astype(BF)
    coarse = dot(pooled, up_ref[...]).astype(BF).astype(F32)
    coarse_ref[...] = coarse
    query_ref[...] = dot(pooled, merged_ref[:, :width])
    key = dot(pooled, merged_ref[:, width : 2 * width])
    value = dot(pooled, merged_ref[:, 2 * width :])
    own = coarse_ref[pl.ds(mine, 1), :]
    query = query_ref[pl.ds(mine, 1), :]
    rms = rms_factor(coarse)
    group = 4 * HD
    spans = [slice(at, at + group) for at in range(0, width, group)]
    tall = jnp.concatenate([key[:, span] for span in spans], 0)
    queries = [query[:, span] for span in spans]
    cross = jnp.concatenate([key[:, span] * q for span, q in zip(spans, queries)], 0)
    ones = ones_ref[...]
    query_norm = head_factor(dot_split(jnp.concatenate([q * q for q in queries], 0), ones), rms_factor(own))
    key_norm = head_factor(dot_split(tall * tall, ones), jnp.concatenate([rms] * len(spans), 0))
    scores = dot_split(cross, ones) * key_norm
    count = key.shape[0]
    parts = []
    for at, span in enumerate(spans):
        factor = query_norm[at : at + 1] * scale_ref[:, span]
        expo = jnp.exp(scores[at * count : (at + 1) * count] * factor)
        total = jnp.sum(expo, 0, keepdims=True)
        parts.append(jnp.sum(expo * rms * value[:, span], 0, keepdims=True) / total)
    cattn = jnp.concatenate(parts, 1).astype(BF)
    coarse_out_ref[...] = (own + dot(cattn, out_ref[...])).astype(BF)
    wait_all(copies)


def vmem(count):
    return [pl.BlockSpec(memory_space=pltpu.VMEM)] * count


def anywhere(count):
    return [pl.BlockSpec(memory_space=pl.ANY)] * count


def in_vmem(arrays):
    return [pltpu.with_memory_space_constraint(array, pltpu.VMEM) for array in arrays]


def in_hbm(arrays):
    return [pltpu.with_memory_space_constraint(array, pltpu.HBM) for array in arrays]


def shards(
    tokens, gain_attn, qkv_fine, scale_fine, out_fine, gain_ffn, ffn_in, ffn_out,
    up_proj, gain_coarse, qkv_coarse, scale_coarse, out_coarse,
):
    rows, cols, width = tokens.shape
    count = rows * cols
    strip = RADIUS * cols
    side = rounded_up((rows + 2 * RADIUS) * RADIUS, 16)
    heads = width // HD
    width_c = out_coarse.shape[0]
    devices = lax.axis_size("ha") * lax.axis_size("wa")
    axes = ("ha", "wa")
    params = pltpu.CompilerParams(vmem_limit_bytes=16 * MIB)

    def swapped(array, axis, first):
        pairs = [(i, i + 1) for i in range(first, lax.axis_size(axis) - 1, 2)]
        return lax.ppermute(array, axis, pairs + [(j, i) for i, j in pairs])

    flat = tokens.reshape(count, width)
    across, within = pl.pallas_call(
        functools.partial(strip_kernel, rows, cols, "ha"),
        out_shape=[pltpu.VMEM((strip, width), BF)] * 2,
        in_specs=anywhere(1),
        out_specs=vmem(2),
        scratch_shapes=[pltpu.SemaphoreType.DMA((2,))],
        compiler_params=params,
        name="strips",
    )(*in_hbm([flat]))
    across = swapped(across, "ha", 1)
    within = swapped(within, "ha", 0)

    block = 256
    weights = [
        flat, qkv_fine, gain_attn.reshape(1, -1), scale_fine.reshape(1, -1),
        up_proj, gain_coarse.reshape(1, -1), scale_coarse.reshape(1, -1),
        out_fine, gain_ffn.reshape(1, -1), ffn_in, ffn_out,
    ]
    *weights, head, query, acc, ones, mask = pl.pallas_call(
        functools.partial(own_kernel, rows, cols, heads, side, axes),
        out_shape=[pltpu.VMEM(array.shape, array.dtype) for array in weights]
        + [
            pltpu.VMEM((block, 3 * width_c), BF),
            pltpu.VMEM((heads, count, 2 * HD), BF),
            pltpu.VMEM((heads, count, 2 * HD), F32),
            pltpu.VMEM((4 * HD, 4 * HD), BF),
            pltpu.VMEM((2 * strip + 2 * side, 2 * HD), BF),
        ],
        in_specs=anywhere(len(weights) + 1),
        out_specs=vmem(len(weights) + 5),
        scratch_shapes=[pltpu.SemaphoreType.DMA((len(weights) + 1,))],
        compiler_params=params,
        cost_estimate=pl.CostEstimate(
            flops=2 * count * width * (3 * width + 2 * count), bytes_accessed=4 * MIB, transcendentals=0
        ),
        name="own",
    )(*in_hbm(weights + [qkv_coarse]))
    tok_v, qkv_v, gain_attn_v, scale_v, up_v, gain_c_v, scale_c_v = weights[:7]
    out_v, gain_ffn_v, ffn_in_v, ffn_out_v = weights[7:]

    across_edge, within_edge = pl.pallas_call(
        functools.partial(edge_kernel, rows, cols, axes),
        out_shape=[pltpu.VMEM((side, width), BF)] * 2,
        in_specs=vmem(4),
        out_specs=vmem(2),
        compiler_params=params,
        name="edges",
    )(*in_vmem([tok_v, across, within, query]))
    across_side = swapped(across_edge, "wa", 1)
    within_side = swapped(within_edge, "wa", 0)

    merged, scale_lanes = pl.pallas_call(
        merge_kernel,
        out_shape=[pltpu.VMEM((width, 3 * width_c), BF), pltpu.VMEM((1, width_c), F32)],
        in_specs=vmem(5) + anywhere(1),
        out_specs=vmem(2),
        scratch_shapes=[
            pltpu.VMEM((width_c - block, 3 * width_c), BF),
            pltpu.VMEM(up_proj.shape, BF),
            pltpu.VMEM((width, 3 * width_c), F32),
            pltpu.SemaphoreType.DMA((width_c // block - 1,)),
        ],
        compiler_params=params,
        cost_estimate=pl.CostEstimate(
            flops=6 * width * width_c * width_c, bytes_accessed=8 * MIB, transcendentals=0
        ),
        name="merge",
    )(*in_vmem([within_edge, up_v, gain_c_v, scale_c_v, head]), *in_hbm([qkv_coarse]))

    def fine_body(tok_ref, *refs):
        fine_kernel(heads, tok_ref, refs[:4], *refs[4:])

    fine, pooled, out_c_v = pl.pallas_call(
        fine_body,
        out_shape=[
            pltpu.VMEM((count, width), BF),
            pltpu.VMEM((devices, width // 128, 128), F32),
            pltpu.VMEM(out_coarse.shape, BF),
        ],
        in_specs=vmem(17) + anywhere(1),
        out_specs=vmem(3),
        scratch_shapes=[pltpu.SemaphoreType.DMA((1,))],
        compiler_params=params,
        name="fine",
    )(
        *in_vmem(
            [tok_v, across, within, across_side, within_side, query, acc, ones, mask, gain_attn_v, qkv_v, scale_v]
            + [out_v, gain_ffn_v, ffn_in_v, ffn_out_v, merged]
        ),
        *in_hbm([out_coarse]),
    )

    every = lax.all_to_all(pooled, axes, split_axis=0, concat_axis=0, tiled=True)
    coarse_out, fine = pl.pallas_call(
        functools.partial(coarse_kernel, axes),
        out_shape=[
            jax.ShapeDtypeStruct((1, width_c), BF),
            jax.ShapeDtypeStruct((count, width), BF),
        ],
        in_specs=vmem(7),
        out_specs=vmem(1) + anywhere(1),
        scratch_shapes=[pltpu.VMEM((devices, width_c), F32)] * 2 + [pltpu.SemaphoreType.DMA((1,))],
        compiler_params=params,
        name="coarse",
    )(*in_vmem([every, up_v, merged, scale_lanes, out_c_v, fine, ones]))
    return fine.reshape(rows, cols, width), coarse_out.reshape(1, 1, width_c)


def solution(mesh):
    return jax.shard_map(
        shards,
        mesh=mesh,
        in_specs=(P("ha", "wa", None), P(), P(), P(), P(), P(), P(), P(), P(), P(), P(), P(), P()),
        out_specs=(P("ha", "wa", None), P("ha", "wa", None)),
        check_vma=False,
    )
```

```python
import functools

import jax
import jax.numpy as jnp
from jax import lax
from jax.experimental import pallas as pl
from jax.experimental.pallas import tpu as pltpu
from jax.sharding import PartitionSpec as P

HD = 64
RADIUS = 3
LOG2E = 1.4426950408889634
BIG = 2.0**30
GELU = 0.7978845608028654
BF = jnp.bfloat16
F32 = jnp.float32
MIB = 1 << 20


def rounded_up(value, step):
    return -(-value // step) * step


def over(values, size):
    assert size & (size - 1) == 0
    return values >> (size.bit_length() - 1)


def dot(a, b):
    return jnp.dot(a, b, preferred_element_type=F32)


def dot_nt(a, b):
    return lax.dot_general(a, b, (((1,), (1,)), ((), ())), preferred_element_type=F32)


def dot_split(values, ones):
    high = values.astype(BF)
    low = (values - high.astype(F32)).astype(BF)
    return dot(high, ones) + dot(low, ones)


def same_head(size):
    left = over(lax.broadcasted_iota(jnp.int32, (size, 1), 0), HD)
    right = over(lax.broadcasted_iota(jnp.int32, (1, size), 1), HD)
    return jnp.where(left == right, 1.0, 0.0).astype(BF)


def head_norm(values, ones):
    return values * lax.rsqrt(dot((values * values).astype(BF), ones) * (1.0 / HD) + 1e-06)


def rms_factor(values):
    return lax.rsqrt(jnp.mean(values * values, -1, keepdims=True) + 1e-06)


def rms_norm(values, gain):
    return values * rms_factor(values) * gain


def head_factor(squares, factor):
    return factor * lax.rsqrt(squares * (factor * factor * (1.0 / HD)) + 1e-06)


def copies_of(pairs, sems):
    return [pltpu.make_async_copy(src, dst, sems.at[i]) for i, (src, dst) in enumerate(pairs)]


def start_all(copies):
    for copy in copies:
        copy.start()


def wait_all(copies):
    for copy in copies:
        copy.wait()


def after_starts(axis):
    return pl.when(lax.axis_index(axis) >= 0)


def strip_kernel(rows, cols, axis, tok_hbm, across_ref, within_ref, sems):
    count, strip = rows * cols, RADIUS * cols
    odd = lax.axis_index(axis) & 1
    last = count - strip
    first = pl.multiple_of(odd * last, 16)
    second = pl.multiple_of((1 - odd) * last, 16)
    copies = copies_of(
        [
            (tok_hbm.at[pl.ds(first, strip), :], across_ref),
            (tok_hbm.at[pl.ds(second, strip), :], within_ref),
        ],
        sems,
    )
    start_all(copies)
    wait_all(copies)


def edge_kernel(rows, cols, axes, tok_ref, across_ref, within_ref, after_ref, across_out, within_out):
    height = rows + 2 * RADIUS
    strip = RADIUS * cols
    padded = across_out.shape[0]
    odd, odd_col = lax.axis_index(axes[0]) & 1, lax.axis_index(axes[1]) & 1
    block = jnp.concatenate([tok_ref[...], across_ref[...], within_ref[...]], 0)
    out = lax.broadcasted_iota(jnp.int32, (padded, 1), 0)
    src = lax.broadcasted_iota(jnp.int32, (padded, block.shape[0]), 1)
    row = ((out * 21846) >> 16) - RADIUS
    col = out - 3 * (row + RADIUS)
    above = rows * cols + strip * odd + RADIUS * cols
    below = rows * cols + strip * (1 - odd) - rows * cols
    first = row * cols + col + jnp.where(row < 0, above, jnp.where(row >= rows, below, 0))
    first = jnp.where(out < height * RADIUS, first, -2 * cols)
    far = cols - RADIUS
    pick = jnp.where(src == first + far * odd_col, 1.0, 0.0).astype(BF)
    across_out[...] = dot(pick, block).astype(BF)
    pick = jnp.where(src == first + far * (1 - odd_col), 1.0, 0.0).astype(BF)
    within_out[...] = dot(pick, block).astype(BF)


def merge_kernel(
    after_ref, up_ref, gain_ref, scale_ref, head_ref, qkv_hbm,
    merged_ref, scale_out, weight_ref, scaled_ref, total_ref, sems,
):
    size = head_ref.shape[0]
    blocks = sems.shape[0]

    def span_of(block):
        return pl.ds(pl.multiple_of(block * size, size), size)

    def copy(block):
        return pltpu.make_async_copy(
            qkv_hbm.at[span_of(block + 1), :], weight_ref.at[span_of(block), :], sems.at[block]
        )

    for block in range(blocks):
        copy(block).start()
    lane = over(lax.broadcasted_iota(jnp.int32, scale_out.shape, 1), HD)
    scales = jnp.zeros(scale_out.shape, F32)
    for head in range(scale_ref.shape[1]):
        scales = jnp.where(lane == head, scale_ref[0:1, head : head + 1], scales)
    scale_out[...] = scales * (1.0 / HD)
    scaled_ref[...] = (up_ref[...].astype(F32) * gain_ref[...]).astype(BF)
    wide = 4 * size
    rows = scaled_ref[:, :size]

    def begin(part, carry):
        span = pl.ds(pl.multiple_of(part * wide, wide), wide)
        total_ref[:, span] = dot(rows, head_ref[:, span])
        return carry

    lax.fori_loop(0, merged_ref.shape[1] // wide, begin, 0)

    def step(block, carry):
        copy(block).wait()
        rows = scaled_ref[:, span_of(block + 1)]
        depth = span_of(block)
        for at in range(0, merged_ref.shape[1], size):
            span = slice(at, at + size)
            total = total_ref[:, span] + dot(rows, weight_ref[depth, span])
            total_ref[:, span] = total
            merged_ref[:, span] = total.astype(BF)
        return carry

    lax.fori_loop(0, blocks, step, 0)


def half_lanes():
    return lax.broadcasted_iota(jnp.int32, (1, 2 * HD), 1) < HD


def mask_columns(rows, cols):
    place = lax.broadcasted_iota(jnp.int32, (1, 2 * HD), 1) & (HD - 1)
    return place, place < rows, (place >= rows) & (place < rows + cols)


def query_columns(rows, cols):
    place, is_row, is_col = mask_columns(rows, cols)
    spot = lax.broadcasted_iota(jnp.int32, (rows * cols, 1), 0)
    hot = (is_row & (over(spot, cols) == place)) | (is_col & ((spot & (cols - 1)) == place - rows))
    return jnp.where(hot, 1.0, 0.0).astype(BF)


def key_columns(rows, cols, krow, kcol):
    place, is_row, is_col = mask_columns(rows, cols)
    far_row = jnp.abs(krow - place) > RADIUS
    far_col = jnp.abs(kcol - (place - rows)) > RADIUS
    return jnp.where((is_row & far_row) | (is_col & far_col), -BIG, 0.0).astype(BF)


def halo_columns(rows, cols, side, axes):
    strip = RADIUS * cols
    row_axis, col_axis = axes
    place_row, place_col = lax.axis_index(row_axis), lax.axis_index(col_axis)
    row0, col0 = place_row * rows, place_col * cols
    grid_rows = lax.axis_size(row_axis) * rows
    grid_cols = lax.axis_size(col_axis) * cols
    odd, odd_col = place_row & 1, place_col & 1
    row_at = (odd * (rows + RADIUS) - RADIUS, (1 - odd) * (rows + RADIUS) - RADIUS)
    col_at = (odd_col * (cols + RADIUS) - RADIUS, (1 - odd_col) * (cols + RADIUS) - RADIUS)
    spot = lax.broadcasted_iota(jnp.int32, (2 * strip + 2 * side, 1), 0)
    past_first = spot - strip
    past_strips = past_first - strip
    past_third = past_strips - side
    strip_at = jnp.where(past_first >= 0, past_first, spot)
    side_at = jnp.where(past_third >= 0, past_third, past_strips)
    side_row = (side_at * 21846) >> 16
    in_strip = past_strips < 0
    krow = jnp.where(
        in_strip,
        over(strip_at, cols) + jnp.where(past_first >= 0, row_at[1], row_at[0]),
        side_row - RADIUS,
    )
    kcol = jnp.where(
        in_strip,
        strip_at & (cols - 1),
        side_at - 3 * side_row + jnp.where(past_third >= 0, col_at[1], col_at[0]),
    )
    real = in_strip | (side_at < (rows + 2 * RADIUS) * RADIUS)
    real = real & (krow + row0 >= 0) & (krow + row0 < grid_rows)
    real = real & (kcol + col0 >= 0) & (kcol + col0 < grid_cols)
    return key_columns(rows, cols, jnp.where(real, krow, -1000), kcol)


def half_of(head):
    low = half_lanes()
    lanes = 2 * HD
    return (low if head % 2 == 0 else ~low), slice(head // 2 * lanes, (head // 2 + 1) * lanes)


def attend(head, query, key, value, key_mask, factor):
    mine, span = half_of(head)
    k = jnp.where(mine, key[:, span], key_mask)
    v = jnp.where(mine, value[:, span], jnp.ones((1, 2 * HD), BF))
    weights = jnp.exp2(dot_nt(query, k) * (factor * (LOG2E / HD))).astype(BF)
    return dot(weights, v)


def own_kernel(rows, cols, heads, side, axes, *refs):
    count = (len(refs) - 7) // 2
    ins, qkv_c_hbm, outs = refs[:count], refs[count], refs[count + 1 : 2 * count + 1]
    head_ref, query_ref, acc_ref, ones_ref, mask_ref, sems = refs[2 * count + 1 :]
    tok_ref, qkv_ref, gain_ref, scale_ref = outs[:4]
    head = (qkv_c_hbm.at[pl.ds(0, head_ref.shape[0]), :], head_ref)
    copies = copies_of(list(zip(ins, outs)) + [head], sems)
    start_all(copies)

    @after_starts(axes[0])
    def _():
        width = heads * HD
        ones = same_head(width)
        ones_ref[...] = ones
        mask_ref[...] = halo_columns(rows, cols, side, axes)
        query_mask = query_columns(rows, cols)
        spot = lax.broadcasted_iota(jnp.int32, (rows * cols, 1), 0)
        key_mask = key_columns(rows, cols, over(spot, cols), spot & (cols - 1))
        wait_all(copies[:4])
        normed = rms_norm(tok_ref[...].astype(F32), gain_ref[...]).astype(BF)
        query = head_norm(dot(normed, qkv_ref[:, :width]), ones).astype(BF)
        key = head_norm(dot(normed, qkv_ref[:, width : 2 * width]), ones).astype(BF)
        value = dot(normed, qkv_ref[:, 2 * width :]).astype(BF)
        for head in range(heads):
            factor = scale_ref[0:1, head : head + 1]
            mine, span = half_of(head)
            masked = jnp.where(mine, query[:, span], query_mask)
            query_ref[head] = masked
            acc_ref[head] = attend(head, masked, key, value, key_mask, factor)

    wait_all(copies[4:])


def fine_kernel(
    heads, axis,
    tok_ref, halo_refs, query_ref, acc_ref, ones_ref, mask_ref, gain_attn_ref, qkv_ref, scale_ref,
    out_ref, gain_ffn_ref, ffn_in_ref, ffn_out_ref, after_ref, out_c_hbm,
    fine_ref, pooled_ref, out_c_ref, sems,
):
    copies = copies_of([(out_c_hbm, out_c_ref)], sems)
    start_all(copies)

    @after_starts(axis)
    def _():
        width = heads * HD
        halo = jnp.concatenate([ref[...] for ref in halo_refs], 0)
        halo = halo.astype(F32)
        scaled = (halo * gain_attn_ref[...]).astype(BF)
        halo_rms = rms_factor(halo)
        ones = ones_ref[...]
        key = dot(scaled, qkv_ref[:, width : 2 * width])
        key = (key * head_factor(dot((key * key).astype(BF), ones), halo_rms)).astype(BF)
        value = (dot(scaled, qkv_ref[:, 2 * width :]) * halo_rms).astype(BF)

        key_mask = mask_ref[...]
        low = half_lanes()
        parts = []
        for pair in range(heads // 2):
            sums = []
            for head in (2 * pair, 2 * pair + 1):
                factor = scale_ref[0:1, head : head + 1]
                sums.append(acc_ref[head] + attend(head, query_ref[head], key, value, key_mask, factor))
            top = jnp.where(low, sums[0], sums[1])
            bottom = pltpu.roll(jnp.where(low, sums[1], sums[0]), HD, 1)
            parts.append((top / bottom).astype(BF))
        attn = jnp.concatenate(parts, 1)

        h1 = (tok_ref[...].astype(F32) + dot(attn, out_ref[...])).astype(BF)
        h1_wide = h1.astype(F32)
        scaled = (h1_wide * gain_ffn_ref[...]).astype(BF)
        h1_rms = rms_factor(h1_wide)
        hidden = ffn_out_ref.shape[0]
        gate = dot(scaled, ffn_in_ref[:, :hidden]) * h1_rms
        up = dot(scaled, ffn_in_ref[:, hidden:]) * (0.5 * h1_rms)
        inner = gate * (GELU + (GELU * 0.044715) * (gate * gate))
        gated = (gate * up * (1.0 + jnp.tanh(inner))).astype(BF)
        fine = (h1_wide + dot(gated, ffn_out_ref[...])).astype(BF)
        fine_ref[...] = fine
        pooled = jnp.mean(fine.astype(F32), 0, keepdims=True).astype(BF).astype(F32)
        for part in range(pooled_ref.shape[1]):
            pooled_ref[:, part, :] = jnp.broadcast_to(
                pooled[:, part * 128 : (part + 1) * 128], (pooled_ref.shape[0], 128)
            )

    wait_all(copies)


def coarse_kernel(
    axes, pooled_ref, up_ref, merged_ref, scale_ref, out_ref, fine_ref, ones_ref,
    coarse_out_ref, fine_hbm,
    query_ref, coarse_ref, sems,
):
    copies = copies_of([(fine_ref, fine_hbm)], sems)
    start_all(copies)
    width = out_ref.shape[0]
    row_axis, col_axis = axes
    mine = lax.axis_index(row_axis) * lax.axis_size(col_axis) + lax.axis_index(col_axis)
    pooled = jnp.concatenate([pooled_ref[:, part, :] for part in range(pooled_ref.shape[1])], 1).astype(BF)
    coarse = dot(pooled, up_ref[...]).astype(BF).astype(F32)
    coarse_ref[...] = coarse
    query_ref[...] = dot(pooled, merged_ref[:, :width])
    key = dot(pooled, merged_ref[:, width : 2 * width])
    value = dot(pooled, merged_ref[:, 2 * width :])
    own = coarse_ref[pl.ds(mine, 1), :]
    query = query_ref[pl.ds(mine, 1), :]
    rms = rms_factor(coarse)
    group = 4 * HD
    spans = [slice(at, at + group) for at in range(0, width, group)]
    tall = jnp.concatenate([key[:, span] for span in spans], 0)
    queries = [query[:, span] for span in spans]
    cross = jnp.concatenate([key[:, span] * q for span, q in zip(spans, queries)], 0)
    ones = ones_ref[...]
    query_norm = head_factor(dot_split(jnp.concatenate([q * q for q in queries], 0), ones), rms_factor(own))
    key_norm = head_factor(dot_split(tall * tall, ones), jnp.concatenate([rms] * len(spans), 0))
    scores = dot_split(cross, ones) * key_norm
    count = key.shape[0]
    parts = []
    for at, span in enumerate(spans):
        factor = query_norm[at : at + 1] * scale_ref[:, span]
        expo = jnp.exp(scores[at * count : (at + 1) * count] * factor)
        total = jnp.sum(expo, 0, keepdims=True)
        parts.append(jnp.sum(expo * rms * value[:, span], 0, keepdims=True) / total)
    cattn = jnp.concatenate(parts, 1).astype(BF)
    coarse_out_ref[...] = (own + dot(cattn, out_ref[...])).astype(BF)
    wait_all(copies)


def vmem(count):
    return [pl.BlockSpec(memory_space=pltpu.VMEM)] * count


def anywhere(count):
    return [pl.BlockSpec(memory_space=pl.ANY)] * count


def in_vmem(arrays):
    return [pltpu.with_memory_space_constraint(array, pltpu.VMEM) for array in arrays]


def in_hbm(arrays):
    return [pltpu.with_memory_space_constraint(array, pltpu.HBM) for array in arrays]


def shards(
    tokens, gain_attn, qkv_fine, scale_fine, out_fine, gain_ffn, ffn_in, ffn_out,
    up_proj, gain_coarse, qkv_coarse, scale_coarse, out_coarse,
):
    rows, cols, width = tokens.shape
    count = rows * cols
    strip = RADIUS * cols
    side = rounded_up((rows + 2 * RADIUS) * RADIUS, 16)
    heads = width // HD
    width_c = out_coarse.shape[0]
    devices = lax.axis_size("ha") * lax.axis_size("wa")
    axes = ("ha", "wa")
    params = pltpu.CompilerParams(vmem_limit_bytes=16 * MIB)

    def swapped(array, axis, first):
        pairs = [(i, i + 1) for i in range(first, lax.axis_size(axis) - 1, 2)]
        return lax.ppermute(array, axis, pairs + [(j, i) for i, j in pairs])

    flat = tokens.reshape(count, width)
    across, within = pl.pallas_call(
        functools.partial(strip_kernel, rows, cols, "ha"),
        out_shape=[pltpu.VMEM((strip, width), BF)] * 2,
        in_specs=anywhere(1),
        out_specs=vmem(2),
        scratch_shapes=[pltpu.SemaphoreType.DMA((2,))],
        compiler_params=params,
        name="strips",
    )(*in_hbm([flat]))
    across = swapped(across, "ha", 1)
    within = swapped(within, "ha", 0)

    block = 256
    weights = [
        flat, qkv_fine, gain_attn.reshape(1, -1), scale_fine.reshape(1, -1),
        up_proj, gain_coarse.reshape(1, -1), scale_coarse.reshape(1, -1),
        out_fine, gain_ffn.reshape(1, -1), ffn_in, ffn_out,
    ]
    *weights, head, query, acc, ones, mask = pl.pallas_call(
        functools.partial(own_kernel, rows, cols, heads, side, axes),
        out_shape=[pltpu.VMEM(array.shape, array.dtype) for array in weights]
        + [
            pltpu.VMEM((block, 3 * width_c), BF),
            pltpu.VMEM((heads, count, 2 * HD), BF),
            pltpu.VMEM((heads, count, 2 * HD), F32),
            pltpu.VMEM((4 * HD, 4 * HD), BF),
            pltpu.VMEM((2 * strip + 2 * side, 2 * HD), BF),
        ],
        in_specs=anywhere(len(weights) + 1),
        out_specs=vmem(len(weights) + 5),
        scratch_shapes=[pltpu.SemaphoreType.DMA((len(weights) + 1,))],
        compiler_params=params,
        cost_estimate=pl.CostEstimate(
            flops=2 * count * width * (3 * width + 2 * count), bytes_accessed=4 * MIB, transcendentals=0
        ),
        name="own",
    )(*in_hbm(weights + [qkv_coarse]))
    tok_v, qkv_v, gain_attn_v, scale_v, up_v, gain_c_v, scale_c_v = weights[:7]
    out_v, gain_ffn_v, ffn_in_v, ffn_out_v = weights[7:]

    across_edge, within_edge = pl.pallas_call(
        functools.partial(edge_kernel, rows, cols, axes),
        out_shape=[pltpu.VMEM((side, width), BF)] * 2,
        in_specs=vmem(4),
        out_specs=vmem(2),
        compiler_params=params,
        name="edges",
    )(*in_vmem([tok_v, across, within, query]))
    across_side = swapped(across_edge, "wa", 1)
    within_side = swapped(within_edge, "wa", 0)

    merged, scale_lanes = pl.pallas_call(
        merge_kernel,
        out_shape=[pltpu.VMEM((width, 3 * width_c), BF), pltpu.VMEM((1, width_c), F32)],
        in_specs=vmem(5) + anywhere(1),
        out_specs=vmem(2),
        scratch_shapes=[
            pltpu.VMEM((width_c - block, 3 * width_c), BF),
            pltpu.VMEM(up_proj.shape, BF),
            pltpu.VMEM((width, 3 * width_c), F32),
            pltpu.SemaphoreType.DMA((width_c // block - 1,)),
        ],
        compiler_params=params,
        cost_estimate=pl.CostEstimate(
            flops=6 * width * width_c * width_c, bytes_accessed=8 * MIB, transcendentals=0
        ),
        name="merge",
    )(*in_vmem([within_edge, up_v, gain_c_v, scale_c_v, head]), *in_hbm([qkv_coarse]))

    def fine_body(tok_ref, *refs):
        fine_kernel(heads, axes[0], tok_ref, refs[:4], *refs[4:])

    fine, pooled, out_c_v = pl.pallas_call(
        fine_body,
        out_shape=[
            pltpu.VMEM((count, width), BF),
            pltpu.VMEM((devices, width // 128, 128), F32),
            pltpu.VMEM(out_coarse.shape, BF),
        ],
        in_specs=vmem(17) + anywhere(1),
        out_specs=vmem(3),
        scratch_shapes=[pltpu.SemaphoreType.DMA((1,))],
        compiler_params=params,
        name="fine",
    )(
        *in_vmem(
            [tok_v, across, within, across_side, within_side, query, acc, ones, mask, gain_attn_v, qkv_v, scale_v]
            + [out_v, gain_ffn_v, ffn_in_v, ffn_out_v, merged]
        ),
        *in_hbm([out_coarse]),
    )

    every = lax.all_to_all(pooled, axes, split_axis=0, concat_axis=0, tiled=True)
    coarse_out, fine = pl.pallas_call(
        functools.partial(coarse_kernel, axes),
        out_shape=[
            jax.ShapeDtypeStruct((1, width_c), BF),
            jax.ShapeDtypeStruct((count, width), BF),
        ],
        in_specs=vmem(7),
        out_specs=vmem(1) + anywhere(1),
        scratch_shapes=[pltpu.VMEM((devices, width_c), F32)] * 2 + [pltpu.SemaphoreType.DMA((1,))],
        compiler_params=params,
        name="coarse",
    )(*in_vmem([every, up_v, merged, scale_lanes, out_c_v, fine, ones]))
    return fine.reshape(rows, cols, width), coarse_out.reshape(1, 1, width_c)


def solution(mesh):
    return jax.shard_map(
        shards,
        mesh=mesh,
        in_specs=(P("ha", "wa", None), P(), P(), P(), P(), P(), P(), P(), P(), P(), P(), P(), P()),
        out_specs=(P("ha", "wa", None), P("ha", "wa", None)),
        check_vma=False,
    )
```

```python
import functools

import jax
import jax.numpy as jnp
from jax import lax
from jax.experimental import pallas as pl
from jax.experimental.pallas import tpu as pltpu
from jax.sharding import PartitionSpec as P

HD = 64
RADIUS = 3
LOG2E = 1.4426950408889634
BIG = 2.0**30
GELU = 0.7978845608028654
BF = jnp.bfloat16
F32 = jnp.float32
MIB = 1 << 20


def rounded_up(value, step):
    return -(-value // step) * step


def over(values, size):
    assert size & (size - 1) == 0
    return values >> (size.bit_length() - 1)


def dot(a, b):
    return jnp.dot(a, b, preferred_element_type=F32)


def dot_nt(a, b):
    return lax.dot_general(a, b, (((1,), (1,)), ((), ())), preferred_element_type=F32)


def dot_split(values, ones):
    high = values.astype(BF)
    low = (values - high.astype(F32)).astype(BF)
    return dot(high, ones) + dot(low, ones)


def same_head(size):
    left = over(lax.broadcasted_iota(jnp.int32, (size, 1), 0), HD)
    right = over(lax.broadcasted_iota(jnp.int32, (1, size), 1), HD)
    return jnp.where(left == right, 1.0, 0.0).astype(BF)


def head_norm(values, ones):
    return values * lax.rsqrt(dot((values * values).astype(BF), ones) * (1.0 / HD) + 1e-06)


def rms_factor(values):
    return lax.rsqrt(jnp.mean(values * values, -1, keepdims=True) + 1e-06)


def rms_norm(values, gain):
    return values * rms_factor(values) * gain


def head_factor(squares, factor):
    return factor * lax.rsqrt(squares * (factor * factor * (1.0 / HD)) + 1e-06)


def copies_of(pairs, sems):
    return [pltpu.make_async_copy(src, dst, sems.at[i]) for i, (src, dst) in enumerate(pairs)]


def start_all(copies):
    for copy in copies:
        copy.start()


def wait_all(copies):
    for copy in copies:
        copy.wait()


def after_starts(axis):
    return pl.when(lax.axis_index(axis) >= 0)


def strip_kernel(rows, cols, axis, tok_hbm, across_ref, within_ref, sems):
    count, strip = rows * cols, RADIUS * cols
    odd = lax.axis_index(axis) & 1
    last = count - strip
    first = pl.multiple_of(odd * last, 16)
    second = pl.multiple_of((1 - odd) * last, 16)
    copies = copies_of(
        [
            (tok_hbm.at[pl.ds(first, strip), :], across_ref),
            (tok_hbm.at[pl.ds(second, strip), :], within_ref),
        ],
        sems,
    )
    start_all(copies)
    wait_all(copies)


def edge_kernel(rows, cols, axes, tok_ref, across_ref, within_ref, after_ref, across_out, within_out):
    height = rows + 2 * RADIUS
    strip = RADIUS * cols
    padded = across_out.shape[0]
    odd, odd_col = lax.axis_index(axes[0]) & 1, lax.axis_index(axes[1]) & 1
    block = jnp.concatenate([tok_ref[...], across_ref[...], within_ref[...]], 0)
    out = lax.broadcasted_iota(jnp.int32, (padded, 1), 0)
    src = lax.broadcasted_iota(jnp.int32, (padded, block.shape[0]), 1)
    row = ((out * 21846) >> 16) - RADIUS
    col = out - 3 * (row + RADIUS)
    above = rows * cols + strip * odd + RADIUS * cols
    below = rows * cols + strip * (1 - odd) - rows * cols
    first = row * cols + col + jnp.where(row < 0, above, jnp.where(row >= rows, below, 0))
    first = jnp.where(out < height * RADIUS, first, -2 * cols)
    far = cols - RADIUS
    pick = jnp.where(src == first + far * odd_col, 1.0, 0.0).astype(BF)
    across_out[...] = dot(pick, block).astype(BF)
    pick = jnp.where(src == first + far * (1 - odd_col), 1.0, 0.0).astype(BF)
    within_out[...] = dot(pick, block).astype(BF)


def merge_kernel(
    after_ref, up_ref, gain_ref, scale_ref, head_ref, qkv_hbm,
    merged_ref, scale_out, weight_ref, scaled_ref, total_ref, sems,
):
    size = head_ref.shape[0]
    blocks = sems.shape[0]

    def span_of(block):
        return pl.ds(pl.multiple_of(block * size, size), size)

    def copy(block):
        return pltpu.make_async_copy(
            qkv_hbm.at[span_of(block + 1), :], weight_ref.at[span_of(block), :], sems.at[block]
        )

    for block in range(blocks):
        copy(block).start()
    lane = over(lax.broadcasted_iota(jnp.int32, scale_out.shape, 1), HD)
    scales = jnp.zeros(scale_out.shape, F32)
    for head in range(scale_ref.shape[1]):
        scales = jnp.where(lane == head, scale_ref[0:1, head : head + 1], scales)
    scale_out[...] = scales * (1.0 / HD)
    scaled_ref[...] = (up_ref[...].astype(F32) * gain_ref[...]).astype(BF)
    wide = 4 * size
    rows = scaled_ref[:, :size]

    def begin(part, carry):
        span = pl.ds(pl.multiple_of(part * wide, wide), wide)
        total_ref[:, span] = dot(rows, head_ref[:, span])
        return carry

    lax.fori_loop(0, merged_ref.shape[1] // wide, begin, 0)

    def step(block, carry):
        copy(block).wait()
        rows = scaled_ref[:, span_of(block + 1)]
        depth = span_of(block)
        for at in range(0, merged_ref.shape[1], size):
            span = slice(at, at + size)
            total = total_ref[:, span] + dot(rows, weight_ref[depth, span])
            total_ref[:, span] = total
            merged_ref[:, span] = total.astype(BF)
        return carry

    lax.fori_loop(0, blocks, step, 0)


def half_lanes():
    return lax.broadcasted_iota(jnp.int32, (1, 2 * HD), 1) < HD


def mask_columns(rows, cols):
    place = lax.broadcasted_iota(jnp.int32, (1, 2 * HD), 1) & (HD - 1)
    return place, place < rows, (place >= rows) & (place < rows + cols)


def query_columns(rows, cols):
    place, is_row, is_col = mask_columns(rows, cols)
    spot = lax.broadcasted_iota(jnp.int32, (rows * cols, 1), 0)
    hot = (is_row & (over(spot, cols) == place)) | (is_col & ((spot & (cols - 1)) == place - rows))
    return jnp.where(hot, 1.0, 0.0).astype(BF)


def key_columns(rows, cols, krow, kcol):
    place, is_row, is_col = mask_columns(rows, cols)
    far_row = jnp.abs(krow - place) > RADIUS
    far_col = jnp.abs(kcol - (place - rows)) > RADIUS
    return jnp.where((is_row & far_row) | (is_col & far_col), -BIG, 0.0).astype(BF)


def halo_columns(rows, cols, side, axes):
    strip = RADIUS * cols
    row_axis, col_axis = axes
    place_row, place_col = lax.axis_index(row_axis), lax.axis_index(col_axis)
    row0, col0 = place_row * rows, place_col * cols
    grid_rows = lax.axis_size(row_axis) * rows
    grid_cols = lax.axis_size(col_axis) * cols
    odd, odd_col = place_row & 1, place_col & 1
    row_at = (odd * (rows + RADIUS) - RADIUS, (1 - odd) * (rows + RADIUS) - RADIUS)
    col_at = (odd_col * (cols + RADIUS) - RADIUS, (1 - odd_col) * (cols + RADIUS) - RADIUS)
    spot = lax.broadcasted_iota(jnp.int32, (2 * strip + 2 * side, 1), 0)
    past_first = spot - strip
    past_strips = past_first - strip
    past_third = past_strips - side
    strip_at = jnp.where(past_first >= 0, past_first, spot)
    side_at = jnp.where(past_third >= 0, past_third, past_strips)
    side_row = (side_at * 21846) >> 16
    in_strip = past_strips < 0
    krow = jnp.where(
        in_strip,
        over(strip_at, cols) + jnp.where(past_first >= 0, row_at[1], row_at[0]),
        side_row - RADIUS,
    )
    kcol = jnp.where(
        in_strip,
        strip_at & (cols - 1),
        side_at - 3 * side_row + jnp.where(past_third >= 0, col_at[1], col_at[0]),
    )
    real = in_strip | (side_at < (rows + 2 * RADIUS) * RADIUS)
    real = real & (krow + row0 >= 0) & (krow + row0 < grid_rows)
    real = real & (kcol + col0 >= 0) & (kcol + col0 < grid_cols)
    return key_columns(rows, cols, jnp.where(real, krow, -1000), kcol)


def half_of(head):
    low = half_lanes()
    lanes = 2 * HD
    return (low if head % 2 == 0 else ~low), slice(head // 2 * lanes, (head // 2 + 1) * lanes)


def attend(head, query, key, value, key_mask, factor):
    mine, span = half_of(head)
    k = jnp.where(mine, key[:, span], key_mask)
    v = jnp.where(mine, value[:, span], jnp.ones((1, 2 * HD), BF))
    weights = jnp.exp2(dot_nt(query, k) * (factor * (LOG2E / HD))).astype(BF)
    return dot(weights, v)


def own_kernel(rows, cols, heads, side, axes, *refs):
    count = (len(refs) - 7) // 2
    ins, qkv_c_hbm, outs = refs[:count], refs[count], refs[count + 1 : 2 * count + 1]
    head_ref, query_ref, acc_ref, ones_ref, mask_ref, sems = refs[2 * count + 1 :]
    tok_ref, qkv_ref, gain_ref, scale_ref = outs[:4]
    head = (qkv_c_hbm.at[pl.ds(0, head_ref.shape[0]), :], head_ref)
    copies = copies_of(list(zip(ins, outs)) + [head], sems)
    start_all(copies)

    @after_starts(axes[0])
    def _():
        width = heads * HD
        ones = same_head(width)
        ones_ref[...] = ones
        mask_ref[...] = halo_columns(rows, cols, side, axes)
        query_mask = query_columns(rows, cols)
        spot = lax.broadcasted_iota(jnp.int32, (rows * cols, 1), 0)
        key_mask = key_columns(rows, cols, over(spot, cols), spot & (cols - 1))
        wait_all(copies[:4])
        normed = rms_norm(tok_ref[...].astype(F32), gain_ref[...]).astype(BF)
        query = head_norm(dot(normed, qkv_ref[:, :width]), ones).astype(BF)
        key = head_norm(dot(normed, qkv_ref[:, width : 2 * width]), ones).astype(BF)
        value = dot(normed, qkv_ref[:, 2 * width :]).astype(BF)
        for head in range(heads):
            factor = scale_ref[0:1, head : head + 1]
            mine, span = half_of(head)
            masked = jnp.where(mine, query[:, span], query_mask)
            query_ref[head] = masked
            acc_ref[head] = attend(head, masked, key, value, key_mask, factor)

    wait_all(copies[4:])


def fine_kernel(
    heads, axis,
    tok_ref, halo_refs, query_ref, acc_ref, ones_ref, mask_ref, gain_attn_ref, qkv_ref, scale_ref,
    out_ref, gain_ffn_ref, ffn_in_ref, ffn_out_ref, after_ref, out_c_hbm,
    fine_ref, pooled_ref, out_c_ref, sems,
):
    copies = copies_of([(out_c_hbm.at[pl.ds(0, out_c_ref.shape[0]), :], out_c_ref)], sems)
    start_all(copies)

    @after_starts(axis)
    def _():
        width = heads * HD
        halo = jnp.concatenate([ref[...] for ref in halo_refs], 0)
        halo = halo.astype(F32)
        scaled = (halo * gain_attn_ref[...]).astype(BF)
        halo_rms = rms_factor(halo)
        ones = ones_ref[...]
        key = dot(scaled, qkv_ref[:, width : 2 * width])
        key = (key * head_factor(dot((key * key).astype(BF), ones), halo_rms)).astype(BF)
        value = (dot(scaled, qkv_ref[:, 2 * width :]) * halo_rms).astype(BF)

        key_mask = mask_ref[...]
        low = half_lanes()
        parts = []
        for pair in range(heads // 2):
            sums = []
            for head in (2 * pair, 2 * pair + 1):
                factor = scale_ref[0:1, head : head + 1]
                sums.append(acc_ref[head] + attend(head, query_ref[head], key, value, key_mask, factor))
            top = jnp.where(low, sums[0], sums[1])
            bottom = pltpu.roll(jnp.where(low, sums[1], sums[0]), HD, 1)
            parts.append((top / bottom).astype(BF))
        attn = jnp.concatenate(parts, 1)

        h1 = (tok_ref[...].astype(F32) + dot(attn, out_ref[...])).astype(BF)
        h1_wide = h1.astype(F32)
        scaled = (h1_wide * gain_ffn_ref[...]).astype(BF)
        h1_rms = rms_factor(h1_wide)
        hidden = ffn_out_ref.shape[0]
        gate = dot(scaled, ffn_in_ref[:, :hidden]) * h1_rms
        up = dot(scaled, ffn_in_ref[:, hidden:]) * (0.5 * h1_rms)
        inner = gate * (GELU + (GELU * 0.044715) * (gate * gate))
        gated = (gate * up * (1.0 + jnp.tanh(inner))).astype(BF)
        fine = (h1_wide + dot(gated, ffn_out_ref[...])).astype(BF)
        fine_ref[...] = fine
        pooled = jnp.mean(fine.astype(F32), 0, keepdims=True).astype(BF).astype(F32)
        for part in range(pooled_ref.shape[1]):
            pooled_ref[:, part, :] = jnp.broadcast_to(
                pooled[:, part * 128 : (part + 1) * 128], (pooled_ref.shape[0], 128)
            )

    wait_all(copies)


def coarse_kernel(
    axes, pooled_ref, up_ref, merged_ref, scale_ref, out_ref, fine_ref, ones_ref, out_hbm,
    coarse_out_ref, fine_hbm,
    query_ref, coarse_ref, rest_ref, sems,
):
    rest = pl.ds(out_ref.shape[0], rest_ref.shape[0])
    copies = copies_of([(out_hbm.at[rest, :], rest_ref), (fine_ref, fine_hbm)], sems)
    start_all(copies)

    @after_starts(axes[0])
    def _():
        half = out_ref.shape[0]
        width = 2 * half
        row_axis, col_axis = axes
        mine = lax.axis_index(row_axis) * lax.axis_size(col_axis) + lax.axis_index(col_axis)
        pooled = jnp.concatenate([pooled_ref[:, part, :] for part in range(pooled_ref.shape[1])], 1).astype(BF)
        coarse = dot(pooled, up_ref[...]).astype(BF).astype(F32)
        coarse_ref[...] = coarse
        query_ref[...] = dot(pooled, merged_ref[:, :width])
        key = dot(pooled, merged_ref[:, width : 2 * width])
        value = dot(pooled, merged_ref[:, 2 * width :])
        own = coarse_ref[pl.ds(mine, 1), :]
        query = query_ref[pl.ds(mine, 1), :]
        rms = rms_factor(coarse)
        group = 4 * HD
        spans = [slice(at, at + group) for at in range(0, width, group)]
        tall = jnp.concatenate([key[:, span] for span in spans], 0)
        queries = [query[:, span] for span in spans]
        cross = jnp.concatenate([key[:, span] * q for span, q in zip(spans, queries)], 0)
        ones = ones_ref[...]
        query_norm = head_factor(dot_split(jnp.concatenate([q * q for q in queries], 0), ones), rms_factor(own))
        key_norm = head_factor(dot_split(tall * tall, ones), jnp.concatenate([rms] * len(spans), 0))
        scores = dot_split(cross, ones) * key_norm
        count = key.shape[0]
        parts = []
        for at, span in enumerate(spans):
            factor = query_norm[at : at + 1] * scale_ref[:, span]
            expo = jnp.exp(scores[at * count : (at + 1) * count] * factor)
            total = jnp.sum(expo, 0, keepdims=True)
            parts.append(jnp.sum(expo * rms * value[:, span], 0, keepdims=True) / total)
        cattn = jnp.concatenate(parts, 1).astype(BF)
        top = own + dot(cattn[:, :half], out_ref[...])
        copies[0].wait()
        coarse_out_ref[...] = (top + dot(cattn[:, half:], rest_ref[...])).astype(BF)

    copies[1].wait()


def vmem(count):
    return [pl.BlockSpec(memory_space=pltpu.VMEM)] * count


def anywhere(count):
    return [pl.BlockSpec(memory_space=pl.ANY)] * count


def in_vmem(arrays):
    return [pltpu.with_memory_space_constraint(array, pltpu.VMEM) for array in arrays]


def in_hbm(arrays):
    return [pltpu.with_memory_space_constraint(array, pltpu.HBM) for array in arrays]


def shards(
    tokens, gain_attn, qkv_fine, scale_fine, out_fine, gain_ffn, ffn_in, ffn_out,
    up_proj, gain_coarse, qkv_coarse, scale_coarse, out_coarse,
):
    rows, cols, width = tokens.shape
    count = rows * cols
    strip = RADIUS * cols
    side = rounded_up((rows + 2 * RADIUS) * RADIUS, 16)
    heads = width // HD
    width_c = out_coarse.shape[0]
    devices = lax.axis_size("ha") * lax.axis_size("wa")
    axes = ("ha", "wa")
    params = pltpu.CompilerParams(vmem_limit_bytes=16 * MIB)

    def swapped(array, axis, first):
        pairs = [(i, i + 1) for i in range(first, lax.axis_size(axis) - 1, 2)]
        return lax.ppermute(array, axis, pairs + [(j, i) for i, j in pairs])

    flat = tokens.reshape(count, width)
    across, within = pl.pallas_call(
        functools.partial(strip_kernel, rows, cols, "ha"),
        out_shape=[pltpu.VMEM((strip, width), BF)] * 2,
        in_specs=anywhere(1),
        out_specs=vmem(2),
        scratch_shapes=[pltpu.SemaphoreType.DMA((2,))],
        compiler_params=params,
        name="strips",
    )(*in_hbm([flat]))
    across = swapped(across, "ha", 1)
    within = swapped(within, "ha", 0)

    block = 256
    weights = [
        flat, qkv_fine, gain_attn.reshape(1, -1), scale_fine.reshape(1, -1),
        up_proj, gain_coarse.reshape(1, -1), scale_coarse.reshape(1, -1),
        out_fine, gain_ffn.reshape(1, -1), ffn_in, ffn_out,
    ]
    *weights, head, query, acc, ones, mask = pl.pallas_call(
        functools.partial(own_kernel, rows, cols, heads, side, axes),
        out_shape=[pltpu.VMEM(array.shape, array.dtype) for array in weights]
        + [
            pltpu.VMEM((block, 3 * width_c), BF),
            pltpu.VMEM((heads, count, 2 * HD), BF),
            pltpu.VMEM((heads, count, 2 * HD), F32),
            pltpu.VMEM((4 * HD, 4 * HD), BF),
            pltpu.VMEM((2 * strip + 2 * side, 2 * HD), BF),
        ],
        in_specs=anywhere(len(weights) + 1),
        out_specs=vmem(len(weights) + 5),
        scratch_shapes=[pltpu.SemaphoreType.DMA((len(weights) + 1,))],
        compiler_params=params,
        cost_estimate=pl.CostEstimate(
            flops=2 * count * width * (3 * width + 2 * count), bytes_accessed=4 * MIB, transcendentals=0
        ),
        name="own",
    )(*in_hbm(weights + [qkv_coarse]))
    tok_v, qkv_v, gain_attn_v, scale_v, up_v, gain_c_v, scale_c_v = weights[:7]
    out_v, gain_ffn_v, ffn_in_v, ffn_out_v = weights[7:]

    across_edge, within_edge = pl.pallas_call(
        functools.partial(edge_kernel, rows, cols, axes),
        out_shape=[pltpu.VMEM((side, width), BF)] * 2,
        in_specs=vmem(4),
        out_specs=vmem(2),
        compiler_params=params,
        name="edges",
    )(*in_vmem([tok_v, across, within, query]))
    across_side = swapped(across_edge, "wa", 1)
    within_side = swapped(within_edge, "wa", 0)

    merged, scale_lanes = pl.pallas_call(
        merge_kernel,
        out_shape=[pltpu.VMEM((width, 3 * width_c), BF), pltpu.VMEM((1, width_c), F32)],
        in_specs=vmem(5) + anywhere(1),
        out_specs=vmem(2),
        scratch_shapes=[
            pltpu.VMEM((width_c - block, 3 * width_c), BF),
            pltpu.VMEM(up_proj.shape, BF),
            pltpu.VMEM((width, 3 * width_c), F32),
            pltpu.SemaphoreType.DMA((width_c // block - 1,)),
        ],
        compiler_params=params,
        cost_estimate=pl.CostEstimate(
            flops=6 * width * width_c * width_c, bytes_accessed=8 * MIB, transcendentals=0
        ),
        name="merge",
    )(*in_vmem([within_edge, up_v, gain_c_v, scale_c_v, head]), *in_hbm([qkv_coarse]))

    def fine_body(tok_ref, *refs):
        fine_kernel(heads, axes[0], tok_ref, refs[:4], *refs[4:])

    fine, pooled, out_c_v = pl.pallas_call(
        fine_body,
        out_shape=[
            pltpu.VMEM((count, width), BF),
            pltpu.VMEM((devices, width // 128, 128), F32),
            pltpu.VMEM((width_c // 2, width_c), BF),
        ],
        in_specs=vmem(17) + anywhere(1),
        out_specs=vmem(3),
        scratch_shapes=[pltpu.SemaphoreType.DMA((1,))],
        compiler_params=params,
        name="fine",
    )(
        *in_vmem(
            [tok_v, across, within, across_side, within_side, query, acc, ones, mask, gain_attn_v, qkv_v, scale_v]
            + [out_v, gain_ffn_v, ffn_in_v, ffn_out_v, merged]
        ),
        *in_hbm([out_coarse]),
    )

    every = lax.all_to_all(pooled, axes, split_axis=0, concat_axis=0, tiled=True)
    coarse_out, fine = pl.pallas_call(
        functools.partial(coarse_kernel, axes),
        out_shape=[
            jax.ShapeDtypeStruct((1, width_c), BF),
            jax.ShapeDtypeStruct((count, width), BF),
        ],
        in_specs=vmem(7) + anywhere(1),
        out_specs=vmem(1) + anywhere(1),
        scratch_shapes=[pltpu.VMEM((devices, width_c), F32)] * 2
        + [pltpu.VMEM((width_c - width_c // 2, width_c), BF), pltpu.SemaphoreType.DMA((2,))],
        compiler_params=params,
        name="coarse",
    )(*in_vmem([every, up_v, merged, scale_lanes, out_c_v, fine, ones]), *in_hbm([out_coarse]))
    return fine.reshape(rows, cols, width), coarse_out.reshape(1, 1, width_c)


def solution(mesh):
    return jax.shard_map(
        shards,
        mesh=mesh,
        in_specs=(P("ha", "wa", None), P(), P(), P(), P(), P(), P(), P(), P(), P(), P(), P(), P()),
        out_specs=(P("ha", "wa", None), P("ha", "wa", None)),
        check_vma=False,
    )
```

```python
import functools

import jax
import jax.numpy as jnp
from jax import lax
from jax.experimental import pallas as pl
from jax.experimental.pallas import tpu as pltpu
from jax.sharding import PartitionSpec as P

HD = 64
RADIUS = 3
LOG2E = 1.4426950408889634
BIG = 2.0**30
GELU = 0.7978845608028654
BF = jnp.bfloat16
F32 = jnp.float32
MIB = 1 << 20


def rounded_up(value, step):
    return -(-value // step) * step


def over(values, size):
    assert size & (size - 1) == 0
    return values >> (size.bit_length() - 1)


def dot(a, b):
    return jnp.dot(a, b, preferred_element_type=F32)


def dot_nt(a, b):
    return lax.dot_general(a, b, (((1,), (1,)), ((), ())), preferred_element_type=F32)


def dot_split(values, ones):
    high = values.astype(BF)
    low = (values - high.astype(F32)).astype(BF)
    return dot(high, ones) + dot(low, ones)


def same_head(size):
    left = over(lax.broadcasted_iota(jnp.int32, (size, 1), 0), HD)
    right = over(lax.broadcasted_iota(jnp.int32, (1, size), 1), HD)
    return jnp.where(left == right, 1.0, 0.0).astype(BF)


def head_norm(values, ones):
    return values * lax.rsqrt(dot((values * values).astype(BF), ones) * (1.0 / HD) + 1e-06)


def rms_factor(values):
    return lax.rsqrt(jnp.mean(values * values, -1, keepdims=True) + 1e-06)


def rms_norm(values, gain):
    return values * rms_factor(values) * gain


def head_factor(squares, factor):
    return factor * lax.rsqrt(squares * (factor * factor * (1.0 / HD)) + 1e-06)


def copies_of(pairs, sems):
    return [pltpu.make_async_copy(src, dst, sems.at[i]) for i, (src, dst) in enumerate(pairs)]


def start_all(copies):
    for copy in copies:
        copy.start()


def wait_all(copies):
    for copy in copies:
        copy.wait()


def after_starts(axis):
    return pl.when(lax.axis_index(axis) >= 0)


def strip_kernel(rows, cols, axis, tok_hbm, across_ref, within_ref, sems):
    count, strip = rows * cols, RADIUS * cols
    odd = lax.axis_index(axis) & 1
    last = count - strip
    first = pl.multiple_of(odd * last, 16)
    second = pl.multiple_of((1 - odd) * last, 16)
    copies = copies_of(
        [
            (tok_hbm.at[pl.ds(first, strip), :], across_ref),
            (tok_hbm.at[pl.ds(second, strip), :], within_ref),
        ],
        sems,
    )
    start_all(copies)
    wait_all(copies)


def edge_kernel(rows, cols, axes, tok_ref, across_ref, within_ref, after_ref, across_out, within_out):
    height = rows + 2 * RADIUS
    strip = RADIUS * cols
    padded = across_out.shape[0]
    odd, odd_col = lax.axis_index(axes[0]) & 1, lax.axis_index(axes[1]) & 1
    block = jnp.concatenate([tok_ref[...], across_ref[...], within_ref[...]], 0)
    out = lax.broadcasted_iota(jnp.int32, (padded, 1), 0)
    src = lax.broadcasted_iota(jnp.int32, (padded, block.shape[0]), 1)
    row = ((out * 21846) >> 16) - RADIUS
    col = out - 3 * (row + RADIUS)
    above = rows * cols + strip * odd + RADIUS * cols
    below = rows * cols + strip * (1 - odd) - rows * cols
    first = row * cols + col + jnp.where(row < 0, above, jnp.where(row >= rows, below, 0))
    first = jnp.where(out < height * RADIUS, first, -2 * cols)
    far = cols - RADIUS
    pick = jnp.where(src == first + far * odd_col, 1.0, 0.0).astype(BF)
    across_out[...] = dot(pick, block).astype(BF)
    pick = jnp.where(src == first + far * (1 - odd_col), 1.0, 0.0).astype(BF)
    within_out[...] = dot(pick, block).astype(BF)


def merge_kernel(
    after_ref, up_ref, gain_ref, scale_ref, head_ref, qkv_hbm,
    merged_ref, scale_out, weight_ref, scaled_ref, total_ref, sems,
):
    size = head_ref.shape[0]
    blocks = sems.shape[0]

    def span_of(block):
        return pl.ds(pl.multiple_of(block * size, size), size)

    def copy(block):
        return pltpu.make_async_copy(
            qkv_hbm.at[span_of(block + 1), :], weight_ref.at[span_of(block), :], sems.at[block]
        )

    for block in range(blocks):
        copy(block).start()
    lane = over(lax.broadcasted_iota(jnp.int32, scale_out.shape, 1), HD)
    scales = jnp.zeros(scale_out.shape, F32)
    for head in range(scale_ref.shape[1]):
        scales = jnp.where(lane == head, scale_ref[0:1, head : head + 1], scales)
    scale_out[...] = scales * (1.0 / HD)
    scaled_ref[...] = (up_ref[...].astype(F32) * gain_ref[...]).astype(BF)
    wide = 4 * size
    rows = scaled_ref[:, :size]

    def begin(part, carry):
        span = pl.ds(pl.multiple_of(part * wide, wide), wide)
        total_ref[:, span] = dot(rows, head_ref[:, span])
        return carry

    lax.fori_loop(0, merged_ref.shape[1] // wide, begin, 0)

    def step(block, carry):
        copy(block).wait()
        rows = scaled_ref[:, span_of(block + 1)]
        depth = span_of(block)
        for at in range(0, merged_ref.shape[1], size):
            span = slice(at, at + size)
            total = total_ref[:, span] + dot(rows, weight_ref[depth, span])
            total_ref[:, span] = total
            merged_ref[:, span] = total.astype(BF)
        return carry

    lax.fori_loop(0, blocks, step, 0)


def half_lanes():
    return lax.broadcasted_iota(jnp.int32, (1, 2 * HD), 1) < HD


def mask_columns(rows, cols):
    place = lax.broadcasted_iota(jnp.int32, (1, 2 * HD), 1) & (HD - 1)
    return place, place < rows, (place >= rows) & (place < rows + cols)


def query_columns(rows, cols):
    place, is_row, is_col = mask_columns(rows, cols)
    spot = lax.broadcasted_iota(jnp.int32, (rows * cols, 1), 0)
    hot = (is_row & (over(spot, cols) == place)) | (is_col & ((spot & (cols - 1)) == place - rows))
    return jnp.where(hot, 1.0, 0.0).astype(BF)


def key_columns(rows, cols, krow, kcol):
    place, is_row, is_col = mask_columns(rows, cols)
    far_row = jnp.abs(krow - place) > RADIUS
    far_col = jnp.abs(kcol - (place - rows)) > RADIUS
    return jnp.where((is_row & far_row) | (is_col & far_col), -BIG, 0.0).astype(BF)


def halo_columns(rows, cols, side, axes):
    strip = RADIUS * cols
    row_axis, col_axis = axes
    place_row, place_col = lax.axis_index(row_axis), lax.axis_index(col_axis)
    row0, col0 = place_row * rows, place_col * cols
    grid_rows = lax.axis_size(row_axis) * rows
    grid_cols = lax.axis_size(col_axis) * cols
    odd, odd_col = place_row & 1, place_col & 1
    row_at = (odd * (rows + RADIUS) - RADIUS, (1 - odd) * (rows + RADIUS) - RADIUS)
    col_at = (odd_col * (cols + RADIUS) - RADIUS, (1 - odd_col) * (cols + RADIUS) - RADIUS)
    spot = lax.broadcasted_iota(jnp.int32, (2 * strip + 2 * side, 1), 0)
    past_first = spot - strip
    past_strips = past_first - strip
    past_third = past_strips - side
    strip_at = jnp.where(past_first >= 0, past_first, spot)
    side_at = jnp.where(past_third >= 0, past_third, past_strips)
    side_row = (side_at * 21846) >> 16
    in_strip = past_strips < 0
    krow = jnp.where(
        in_strip,
        over(strip_at, cols) + jnp.where(past_first >= 0, row_at[1], row_at[0]),
        side_row - RADIUS,
    )
    kcol = jnp.where(
        in_strip,
        strip_at & (cols - 1),
        side_at - 3 * side_row + jnp.where(past_third >= 0, col_at[1], col_at[0]),
    )
    real = in_strip | (side_at < (rows + 2 * RADIUS) * RADIUS)
    real = real & (krow + row0 >= 0) & (krow + row0 < grid_rows)
    real = real & (kcol + col0 >= 0) & (kcol + col0 < grid_cols)
    return key_columns(rows, cols, jnp.where(real, krow, -1000), kcol)


def half_of(head):
    low = half_lanes()
    lanes = 2 * HD
    return (low if head % 2 == 0 else ~low), slice(head // 2 * lanes, (head // 2 + 1) * lanes)


def attend(head, query, key, value, key_mask, factor):
    mine, span = half_of(head)
    k = jnp.where(mine, key[:, span], key_mask)
    v = jnp.where(mine, value[:, span], jnp.ones((1, 2 * HD), BF))
    weights = jnp.exp2(dot_nt(query, k) * (factor * (LOG2E / HD))).astype(BF)
    return dot(weights, v)


def own_kernel(rows, cols, heads, side, axes, *refs):
    count = (len(refs) - 7) // 2
    ins, qkv_c_hbm, outs = refs[:count], refs[count], refs[count + 1 : 2 * count + 1]
    head_ref, query_ref, acc_ref, ones_ref, mask_ref, sems = refs[2 * count + 1 :]
    tok_ref, qkv_ref, gain_ref, scale_ref = outs[:4]
    head = (qkv_c_hbm.at[pl.ds(0, head_ref.shape[0]), :], head_ref)
    copies = copies_of(list(zip(ins, outs)) + [head], sems)
    start_all(copies)

    @after_starts(axes[0])
    def _():
        width = heads * HD
        ones = same_head(width)
        ones_ref[...] = ones
        mask_ref[...] = halo_columns(rows, cols, side, axes)
        query_mask = query_columns(rows, cols)
        spot = lax.broadcasted_iota(jnp.int32, (rows * cols, 1), 0)
        key_mask = key_columns(rows, cols, over(spot, cols), spot & (cols - 1))
        wait_all(copies[:4])
        normed = rms_norm(tok_ref[...].astype(F32), gain_ref[...]).astype(BF)
        query = head_norm(dot(normed, qkv_ref[:, :width]), ones).astype(BF)
        key = head_norm(dot(normed, qkv_ref[:, width : 2 * width]), ones).astype(BF)
        value = dot(normed, qkv_ref[:, 2 * width :]).astype(BF)
        for head in range(heads):
            factor = scale_ref[0:1, head : head + 1]
            mine, span = half_of(head)
            masked = jnp.where(mine, query[:, span], query_mask)
            query_ref[head] = masked
            acc_ref[head] = attend(head, masked, key, value, key_mask, factor)

    wait_all(copies[4:])


def fine_kernel(
    heads, axes,
    tok_ref, halo_refs, query_ref, acc_ref, ones_ref, mask_ref, gain_attn_ref, qkv_ref, scale_ref,
    out_ref, gain_ffn_ref, ffn_in_ref, ffn_out_ref, after_ref, out_c_hbm,
    fine_ref, pooled_ref, out_c_ref, sems,
):
    copies = copies_of([(out_c_hbm, out_c_ref)], sems)
    start_all(copies)

    @after_starts(axes[0])
    def _():
        width = heads * HD
        halo = jnp.concatenate([ref[...] for ref in halo_refs], 0)
        halo = halo.astype(F32)
        scaled = (halo * gain_attn_ref[...]).astype(BF)
        halo_rms = rms_factor(halo)
        ones = ones_ref[...]
        key = dot(scaled, qkv_ref[:, width : 2 * width])
        key = (key * head_factor(dot((key * key).astype(BF), ones), halo_rms)).astype(BF)
        value = (dot(scaled, qkv_ref[:, 2 * width :]) * halo_rms).astype(BF)

        key_mask = mask_ref[...]
        low = half_lanes()
        parts = []
        for pair in range(heads // 2):
            sums = []
            for head in (2 * pair, 2 * pair + 1):
                factor = scale_ref[0:1, head : head + 1]
                sums.append(acc_ref[head] + attend(head, query_ref[head], key, value, key_mask, factor))
            top = jnp.where(low, sums[0], sums[1])
            bottom = pltpu.roll(jnp.where(low, sums[1], sums[0]), HD, 1)
            parts.append((top / bottom).astype(BF))
        attn = jnp.concatenate(parts, 1)

        h1 = (tok_ref[...].astype(F32) + dot(attn, out_ref[...])).astype(BF)
        h1_wide = h1.astype(F32)
        scaled = (h1_wide * gain_ffn_ref[...]).astype(BF)
        h1_rms = rms_factor(h1_wide)
        hidden = ffn_out_ref.shape[0]
        gate = dot(scaled, ffn_in_ref[:, :hidden]) * h1_rms
        up = dot(scaled, ffn_in_ref[:, hidden:]) * (0.5 * h1_rms)
        inner = gate * (GELU + (GELU * 0.044715) * (gate * gate))
        gated = (gate * up * (1.0 + jnp.tanh(inner))).astype(BF)
        fine = (h1_wide + dot(gated, ffn_out_ref[...])).astype(BF)
        fine_ref[...] = fine
        pooled = jnp.mean(fine.astype(F32), 0, keepdims=True).astype(BF).astype(F32)
        for part in range(pooled_ref.shape[1]):
            mine = lax.axis_index(axes[0]) * lax.axis_size(axes[1]) + lax.axis_index(axes[1])
            row = lax.broadcasted_iota(jnp.int32, (pooled_ref.shape[0], 1), 0)
            pooled_ref[:, part, :] = jnp.where(row == mine, pooled[:, part * 128 : (part + 1) * 128], 0.0)

    wait_all(copies)


def coarse_kernel(
    axes, pooled_ref, up_ref, merged_ref, scale_ref, out_ref, fine_ref, ones_ref,
    coarse_out_ref, fine_hbm,
    query_ref, coarse_ref, sems,
):
    copies = copies_of([(fine_ref, fine_hbm)], sems)
    start_all(copies)
    width = out_ref.shape[0]
    row_axis, col_axis = axes
    mine = lax.axis_index(row_axis) * lax.axis_size(col_axis) + lax.axis_index(col_axis)
    pooled = jnp.concatenate([pooled_ref[:, part, :] for part in range(pooled_ref.shape[1])], 1).astype(BF)
    coarse = dot(pooled, up_ref[...]).astype(BF).astype(F32)
    coarse_ref[...] = coarse
    query_ref[...] = dot(pooled, merged_ref[:, :width])
    key = dot(pooled, merged_ref[:, width : 2 * width])
    value = dot(pooled, merged_ref[:, 2 * width :])
    own = coarse_ref[pl.ds(mine, 1), :]
    query = query_ref[pl.ds(mine, 1), :]
    rms = rms_factor(coarse)
    group = 4 * HD
    spans = [slice(at, at + group) for at in range(0, width, group)]
    tall = jnp.concatenate([key[:, span] for span in spans], 0)
    queries = [query[:, span] for span in spans]
    cross = jnp.concatenate([key[:, span] * q for span, q in zip(spans, queries)], 0)
    ones = ones_ref[...]
    query_norm = head_factor(dot_split(jnp.concatenate([q * q for q in queries], 0), ones), rms_factor(own))
    key_norm = head_factor(dot_split(tall * tall, ones), jnp.concatenate([rms] * len(spans), 0))
    scores = dot_split(cross, ones) * key_norm
    count = key.shape[0]
    parts = []
    for at, span in enumerate(spans):
        factor = query_norm[at : at + 1] * scale_ref[:, span]
        expo = jnp.exp(scores[at * count : (at + 1) * count] * factor)
        total = jnp.sum(expo, 0, keepdims=True)
        parts.append(jnp.sum(expo * rms * value[:, span], 0, keepdims=True) / total)
    cattn = jnp.concatenate(parts, 1).astype(BF)
    coarse_out_ref[...] = (own + dot(cattn, out_ref[...])).astype(BF)
    wait_all(copies)


def vmem(count):
    return [pl.BlockSpec(memory_space=pltpu.VMEM)] * count


def anywhere(count):
    return [pl.BlockSpec(memory_space=pl.ANY)] * count


def in_vmem(arrays):
    return [pltpu.with_memory_space_constraint(array, pltpu.VMEM) for array in arrays]


def in_hbm(arrays):
    return [pltpu.with_memory_space_constraint(array, pltpu.HBM) for array in arrays]


def shards(
    tokens, gain_attn, qkv_fine, scale_fine, out_fine, gain_ffn, ffn_in, ffn_out,
    up_proj, gain_coarse, qkv_coarse, scale_coarse, out_coarse,
):
    rows, cols, width = tokens.shape
    count = rows * cols
    strip = RADIUS * cols
    side = rounded_up((rows + 2 * RADIUS) * RADIUS, 16)
    heads = width // HD
    width_c = out_coarse.shape[0]
    devices = lax.axis_size("ha") * lax.axis_size("wa")
    axes = ("ha", "wa")
    params = pltpu.CompilerParams(vmem_limit_bytes=16 * MIB)

    def swapped(array, axis, first):
        pairs = [(i, i + 1) for i in range(first, lax.axis_size(axis) - 1, 2)]
        return lax.ppermute(array, axis, pairs + [(j, i) for i, j in pairs])

    flat = tokens.reshape(count, width)
    across, within = pl.pallas_call(
        functools.partial(strip_kernel, rows, cols, "ha"),
        out_shape=[pltpu.VMEM((strip, width), BF)] * 2,
        in_specs=anywhere(1),
        out_specs=vmem(2),
        scratch_shapes=[pltpu.SemaphoreType.DMA((2,))],
        compiler_params=params,
        name="strips",
    )(*in_hbm([flat]))
    across = swapped(across, "ha", 1)
    within = swapped(within, "ha", 0)

    block = 256
    weights = [
        flat, qkv_fine, gain_attn.reshape(1, -1), scale_fine.reshape(1, -1),
        up_proj, gain_coarse.reshape(1, -1), scale_coarse.reshape(1, -1),
        out_fine, gain_ffn.reshape(1, -1), ffn_in, ffn_out,
    ]
    *weights, head, query, acc, ones, mask = pl.pallas_call(
        functools.partial(own_kernel, rows, cols, heads, side, axes),
        out_shape=[pltpu.VMEM(array.shape, array.dtype) for array in weights]
        + [
            pltpu.VMEM((block, 3 * width_c), BF),
            pltpu.VMEM((heads, count, 2 * HD), BF),
            pltpu.VMEM((heads, count, 2 * HD), F32),
            pltpu.VMEM((4 * HD, 4 * HD), BF),
            pltpu.VMEM((2 * strip + 2 * side, 2 * HD), BF),
        ],
        in_specs=anywhere(len(weights) + 1),
        out_specs=vmem(len(weights) + 5),
        scratch_shapes=[pltpu.SemaphoreType.DMA((len(weights) + 1,))],
        compiler_params=params,
        cost_estimate=pl.CostEstimate(
            flops=2 * count * width * (3 * width + 2 * count), bytes_accessed=4 * MIB, transcendentals=0
        ),
        name="own",
    )(*in_hbm(weights + [qkv_coarse]))
    tok_v, qkv_v, gain_attn_v, scale_v, up_v, gain_c_v, scale_c_v = weights[:7]
    out_v, gain_ffn_v, ffn_in_v, ffn_out_v = weights[7:]

    across_edge, within_edge = pl.pallas_call(
        functools.partial(edge_kernel, rows, cols, axes),
        out_shape=[pltpu.VMEM((side, width), BF)] * 2,
        in_specs=vmem(4),
        out_specs=vmem(2),
        compiler_params=params,
        name="edges",
    )(*in_vmem([tok_v, across, within, query]))
    across_side = swapped(across_edge, "wa", 1)
    within_side = swapped(within_edge, "wa", 0)

    merged, scale_lanes = pl.pallas_call(
        merge_kernel,
        out_shape=[pltpu.VMEM((width, 3 * width_c), BF), pltpu.VMEM((1, width_c), F32)],
        in_specs=vmem(5) + anywhere(1),
        out_specs=vmem(2),
        scratch_shapes=[
            pltpu.VMEM((width_c - block, 3 * width_c), BF),
            pltpu.VMEM(up_proj.shape, BF),
            pltpu.VMEM((width, 3 * width_c), F32),
            pltpu.SemaphoreType.DMA((width_c // block - 1,)),
        ],
        compiler_params=params,
        cost_estimate=pl.CostEstimate(
            flops=6 * width * width_c * width_c, bytes_accessed=8 * MIB, transcendentals=0
        ),
        name="merge",
    )(*in_vmem([within_edge, up_v, gain_c_v, scale_c_v, head]), *in_hbm([qkv_coarse]))

    def fine_body(tok_ref, *refs):
        fine_kernel(heads, axes, tok_ref, refs[:4], *refs[4:])

    fine, pooled, out_c_v = pl.pallas_call(
        fine_body,
        out_shape=[
            pltpu.VMEM((count, width), BF),
            pltpu.VMEM((devices, width // 128, 128), F32),
            pltpu.VMEM(out_coarse.shape, BF),
        ],
        in_specs=vmem(17) + anywhere(1),
        out_specs=vmem(3),
        scratch_shapes=[pltpu.SemaphoreType.DMA((1,))],
        compiler_params=params,
        name="fine",
    )(
        *in_vmem(
            [tok_v, across, within, across_side, within_side, query, acc, ones, mask, gain_attn_v, qkv_v, scale_v]
            + [out_v, gain_ffn_v, ffn_in_v, ffn_out_v, merged]
        ),
        *in_hbm([out_coarse]),
    )

    every = lax.psum(pooled, axes)
    coarse_out, fine = pl.pallas_call(
        functools.partial(coarse_kernel, axes),
        out_shape=[
            jax.ShapeDtypeStruct((1, width_c), BF),
            jax.ShapeDtypeStruct((count, width), BF),
        ],
        in_specs=vmem(7),
        out_specs=vmem(1) + anywhere(1),
        scratch_shapes=[pltpu.VMEM((devices, width_c), F32)] * 2 + [pltpu.SemaphoreType.DMA((1,))],
        compiler_params=params,
        name="coarse",
    )(*in_vmem([every, up_v, merged, scale_lanes, out_c_v, fine, ones]))
    return fine.reshape(rows, cols, width), coarse_out.reshape(1, 1, width_c)


def solution(mesh):
    return jax.shard_map(
        shards,
        mesh=mesh,
        in_specs=(P("ha", "wa", None), P(), P(), P(), P(), P(), P(), P(), P(), P(), P(), P(), P()),
        out_specs=(P("ha", "wa", None), P("ha", "wa", None)),
        check_vma=False,
    )
```

```python
import functools

import jax
import jax.numpy as jnp
from jax import lax
from jax.experimental import pallas as pl
from jax.experimental.pallas import tpu as pltpu
from jax.sharding import PartitionSpec as P

HD = 64
RADIUS = 3
LOG2E = 1.4426950408889634
BIG = 2.0**30
GELU = 0.7978845608028654
BF = jnp.bfloat16
F32 = jnp.float32
MIB = 1 << 20


def rounded_up(value, step):
    return -(-value // step) * step


def over(values, size):
    assert size & (size - 1) == 0
    return values >> (size.bit_length() - 1)


def dot(a, b):
    return jnp.dot(a, b, preferred_element_type=F32)


def dot_nt(a, b):
    return lax.dot_general(a, b, (((1,), (1,)), ((), ())), preferred_element_type=F32)


def dot_split(values, ones):
    high = values.astype(BF)
    low = (values - high.astype(F32)).astype(BF)
    return dot(high, ones) + dot(low, ones)


def same_head(size):
    left = over(lax.broadcasted_iota(jnp.int32, (size, 1), 0), HD)
    right = over(lax.broadcasted_iota(jnp.int32, (1, size), 1), HD)
    return jnp.where(left == right, 1.0, 0.0).astype(BF)


def head_norm(values, ones):
    return values * lax.rsqrt(dot((values * values).astype(BF), ones) * (1.0 / HD) + 1e-06)


def rms_factor(values):
    return lax.rsqrt(jnp.mean(values * values, -1, keepdims=True) + 1e-06)


def rms_norm(values, gain):
    return values * rms_factor(values) * gain


def head_factor(squares, factor):
    return factor * lax.rsqrt(squares * (factor * factor * (1.0 / HD)) + 1e-06)


def copies_of(pairs, sems):
    return [pltpu.make_async_copy(src, dst, sems.at[i]) for i, (src, dst) in enumerate(pairs)]


def start_all(copies):
    for copy in copies:
        copy.start()


def wait_all(copies):
    for copy in copies:
        copy.wait()


def after_starts(axis):
    return pl.when(lax.axis_index(axis) >= 0)


def strip_kernel(rows, cols, axis, tok_hbm, across_ref, within_ref, sems):
    count, strip = rows * cols, RADIUS * cols
    odd = lax.axis_index(axis) & 1
    last = count - strip
    first = pl.multiple_of(odd * last, 16)
    second = pl.multiple_of((1 - odd) * last, 16)
    copies = copies_of(
        [
            (tok_hbm.at[pl.ds(first, strip), :], across_ref),
            (tok_hbm.at[pl.ds(second, strip), :], within_ref),
        ],
        sems,
    )
    start_all(copies)
    wait_all(copies)


def edge_kernel(rows, cols, axes, tok_ref, across_ref, within_ref, after_ref, across_out, within_out):
    height = rows + 2 * RADIUS
    strip = RADIUS * cols
    padded = across_out.shape[0]
    odd, odd_col = lax.axis_index(axes[0]) & 1, lax.axis_index(axes[1]) & 1
    block = jnp.concatenate([tok_ref[...], across_ref[...], within_ref[...]], 0)
    out = lax.broadcasted_iota(jnp.int32, (padded, 1), 0)
    src = lax.broadcasted_iota(jnp.int32, (padded, block.shape[0]), 1)
    row = ((out * 21846) >> 16) - RADIUS
    col = out - 3 * (row + RADIUS)
    above = rows * cols + strip * odd + RADIUS * cols
    below = rows * cols + strip * (1 - odd) - rows * cols
    first = row * cols + col + jnp.where(row < 0, above, jnp.where(row >= rows, below, 0))
    first = jnp.where(out < height * RADIUS, first, -2 * cols)
    far = cols - RADIUS
    pick = jnp.where(src == first + far * odd_col, 1.0, 0.0).astype(BF)
    across_out[...] = dot(pick, block).astype(BF)
    pick = jnp.where(src == first + far * (1 - odd_col), 1.0, 0.0).astype(BF)
    within_out[...] = dot(pick, block).astype(BF)


def merge_kernel(
    after_ref, up_ref, gain_ref, scale_ref, head_ref, qkv_hbm,
    merged_ref, scale_out, weight_ref, scaled_ref, total_ref, sems,
):
    size = head_ref.shape[0]
    blocks = sems.shape[0]

    def span_of(block):
        return pl.ds(pl.multiple_of(block * size, size), size)

    def copy(block):
        return pltpu.make_async_copy(
            qkv_hbm.at[span_of(block + 1), :], weight_ref.at[span_of(block), :], sems.at[block]
        )

    for block in range(blocks):
        copy(block).start()
    lane = over(lax.broadcasted_iota(jnp.int32, scale_out.shape, 1), HD)
    scales = jnp.zeros(scale_out.shape, F32)
    for head in range(scale_ref.shape[1]):
        scales = jnp.where(lane == head, scale_ref[0:1, head : head + 1], scales)
    scale_out[...] = scales * (1.0 / HD)
    scaled_ref[...] = (up_ref[...].astype(F32) * gain_ref[...]).astype(BF)
    wide = 4 * size
    rows = scaled_ref[:, :size]

    def begin(part, carry):
        span = pl.ds(pl.multiple_of(part * wide, wide), wide)
        total_ref[:, span] = dot(rows, head_ref[:, span])
        return carry

    lax.fori_loop(0, merged_ref.shape[1] // wide, begin, 0)

    def step(block, carry):
        copy(block).wait()
        rows = scaled_ref[:, span_of(block + 1)]
        depth = span_of(block)
        for at in range(0, merged_ref.shape[1], size):
            span = slice(at, at + size)
            total = total_ref[:, span] + dot(rows, weight_ref[depth, span])
            total_ref[:, span] = total
            merged_ref[:, span] = total.astype(BF)
        return carry

    lax.fori_loop(0, blocks, step, 0)


def half_lanes():
    return lax.broadcasted_iota(jnp.int32, (1, 2 * HD), 1) < HD


def mask_columns(rows, cols):
    place = lax.broadcasted_iota(jnp.int32, (1, 2 * HD), 1) & (HD - 1)
    return place, place < rows, (place >= rows) & (place < rows + cols)


def query_columns(rows, cols):
    place, is_row, is_col = mask_columns(rows, cols)
    spot = lax.broadcasted_iota(jnp.int32, (rows * cols, 1), 0)
    hot = (is_row & (over(spot, cols) == place)) | (is_col & ((spot & (cols - 1)) == place - rows))
    return jnp.where(hot, 1.0, 0.0).astype(BF)


def key_columns(rows, cols, krow, kcol):
    place, is_row, is_col = mask_columns(rows, cols)
    far_row = jnp.abs(krow - place) > RADIUS
    far_col = jnp.abs(kcol - (place - rows)) > RADIUS
    return jnp.where((is_row & far_row) | (is_col & far_col), -BIG, 0.0).astype(BF)


def halo_columns(rows, cols, side, axes):
    strip = RADIUS * cols
    row_axis, col_axis = axes
    place_row, place_col = lax.axis_index(row_axis), lax.axis_index(col_axis)
    row0, col0 = place_row * rows, place_col * cols
    grid_rows = lax.axis_size(row_axis) * rows
    grid_cols = lax.axis_size(col_axis) * cols
    odd, odd_col = place_row & 1, place_col & 1
    row_at = (odd * (rows + RADIUS) - RADIUS, (1 - odd) * (rows + RADIUS) - RADIUS)
    col_at = (odd_col * (cols + RADIUS) - RADIUS, (1 - odd_col) * (cols + RADIUS) - RADIUS)
    spot = lax.broadcasted_iota(jnp.int32, (2 * strip + 2 * side, 1), 0)
    past_first = spot - strip
    past_strips = past_first - strip
    past_third = past_strips - side
    strip_at = jnp.where(past_first >= 0, past_first, spot)
    side_at = jnp.where(past_third >= 0, past_third, past_strips)
    side_row = (side_at * 21846) >> 16
    in_strip = past_strips < 0
    krow = jnp.where(
        in_strip,
        over(strip_at, cols) + jnp.where(past_first >= 0, row_at[1], row_at[0]),
        side_row - RADIUS,
    )
    kcol = jnp.where(
        in_strip,
        strip_at & (cols - 1),
        side_at - 3 * side_row + jnp.where(past_third >= 0, col_at[1], col_at[0]),
    )
    real = in_strip | (side_at < (rows + 2 * RADIUS) * RADIUS)
    real = real & (krow + row0 >= 0) & (krow + row0 < grid_rows)
    real = real & (kcol + col0 >= 0) & (kcol + col0 < grid_cols)
    return key_columns(rows, cols, jnp.where(real, krow, -1000), kcol)


def half_of(head):
    low = half_lanes()
    lanes = 2 * HD
    return (low if head % 2 == 0 else ~low), slice(head // 2 * lanes, (head // 2 + 1) * lanes)


def attend(head, query, key, value, key_mask, factor):
    mine, span = half_of(head)
    k = jnp.where(mine, key[:, span], key_mask)
    v = jnp.where(mine, value[:, span], jnp.ones((1, 2 * HD), BF))
    weights = jnp.exp2(dot_nt(query, k) * (factor * (LOG2E / HD))).astype(BF)
    return dot(weights, v)


def own_kernel(rows, cols, heads, side, axes, *refs):
    count = (len(refs) - 7) // 2
    ins, qkv_c_hbm, outs = refs[:count], refs[count], refs[count + 1 : 2 * count + 1]
    head_ref, query_ref, acc_ref, ones_ref, mask_ref, sems = refs[2 * count + 1 :]
    tok_ref, qkv_ref, gain_ref, scale_ref = outs[:4]
    head = (qkv_c_hbm.at[pl.ds(0, head_ref.shape[0]), :], head_ref)
    copies = copies_of(list(zip(ins, outs)) + [head], sems)
    start_all(copies)

    @after_starts(axes[0])
    def _():
        width = heads * HD
        ones = same_head(width)
        ones_ref[...] = ones
        mask_ref[...] = halo_columns(rows, cols, side, axes)
        query_mask = query_columns(rows, cols)
        spot = lax.broadcasted_iota(jnp.int32, (rows * cols, 1), 0)
        key_mask = key_columns(rows, cols, over(spot, cols), spot & (cols - 1))
        wait_all(copies[:4])
        normed = rms_norm(tok_ref[...].astype(F32), gain_ref[...]).astype(BF)
        query = head_norm(dot(normed, qkv_ref[:, :width]), ones).astype(BF)
        key = head_norm(dot(normed, qkv_ref[:, width : 2 * width]), ones).astype(BF)
        value = dot(normed, qkv_ref[:, 2 * width :]).astype(BF)
        for head in range(heads):
            factor = scale_ref[0:1, head : head + 1]
            mine, span = half_of(head)
            masked = jnp.where(mine, query[:, span], query_mask)
            query_ref[head] = masked
            acc_ref[head] = attend(head, masked, key, value, key_mask, factor)

    wait_all(copies[4:])


def fine_kernel(
    heads, axis,
    tok_ref, halo_refs, query_ref, acc_ref, ones_ref, mask_ref, gain_attn_ref, qkv_ref, scale_ref,
    out_ref, gain_ffn_ref, ffn_in_ref, ffn_out_ref, after_ref, out_c_hbm,
    fine_ref, pooled_ref, out_c_ref, sems,
):
    copies = copies_of([(out_c_hbm, out_c_ref)], sems)
    start_all(copies)

    @after_starts(axis)
    def _():
        width = heads * HD
        halo = jnp.concatenate([ref[...] for ref in halo_refs], 0)
        halo = halo.astype(F32)
        scaled = (halo * gain_attn_ref[...]).astype(BF)
        halo_rms = rms_factor(halo)
        ones = ones_ref[...]
        key = dot(scaled, qkv_ref[:, width : 2 * width])
        key = (key * head_factor(dot((key * key).astype(BF), ones), halo_rms)).astype(BF)
        value = (dot(scaled, qkv_ref[:, 2 * width :]) * halo_rms).astype(BF)

        key_mask = mask_ref[...]
        low = half_lanes()
        parts = []
        for pair in range(heads // 2):
            sums = []
            for head in (2 * pair, 2 * pair + 1):
                factor = scale_ref[0:1, head : head + 1]
                sums.append(acc_ref[head] + attend(head, query_ref[head], key, value, key_mask, factor))
            top = jnp.where(low, sums[0], sums[1])
            bottom = pltpu.roll(jnp.where(low, sums[1], sums[0]), HD, 1)
            parts.append((top / bottom).astype(BF))
        attn = jnp.concatenate(parts, 1)

        h1 = (tok_ref[...].astype(F32) + dot(attn, out_ref[...])).astype(BF)
        h1_wide = h1.astype(F32)
        scaled = (h1_wide * gain_ffn_ref[...]).astype(BF)
        h1_rms = rms_factor(h1_wide)
        hidden = ffn_out_ref.shape[0]
        gate = dot(scaled, ffn_in_ref[:, :hidden]) * h1_rms
        up = dot(scaled, ffn_in_ref[:, hidden:]) * (0.5 * h1_rms)
        inner = gate * (GELU + (GELU * 0.044715) * (gate * gate))
        gated = (gate * up * (1.0 + jnp.tanh(inner))).astype(BF)
        fine = (h1_wide + dot(gated, ffn_out_ref[...])).astype(BF)
        fine_ref[...] = fine
        pooled = jnp.mean(fine.astype(F32), 0, keepdims=True).astype(BF).astype(F32)
        for part in range(pooled_ref.shape[1]):
            pooled_ref[:, part, :] = jnp.broadcast_to(
                pooled[:, part * 128 : (part + 1) * 128], (pooled_ref.shape[0], 128)
            )

    wait_all(copies)


def coarse_kernel(
    axes, pooled_ref, up_ref, merged_ref, scale_ref, out_ref, fine_ref, ones_ref,
    coarse_out_ref, fine_hbm,
    coarse_ref, sems,
):
    copies = copies_of([(fine_ref, fine_hbm)], sems)
    start_all(copies)
    width = out_ref.shape[0]
    row_axis, col_axis = axes
    mine = lax.axis_index(row_axis) * lax.axis_size(col_axis) + lax.axis_index(col_axis)
    pooled = jnp.concatenate([pooled_ref[:, part, :] for part in range(pooled_ref.shape[1])], 1).astype(BF)
    coarse = dot(pooled, up_ref[...]).astype(BF).astype(F32)
    coarse_ref[...] = coarse
    mine_row = [pooled_ref[pl.ds(mine, 1), part, :] for part in range(pooled_ref.shape[1])]
    query = dot(jnp.concatenate(mine_row, 1).astype(BF), merged_ref[:, :width])
    key = dot(pooled, merged_ref[:, width : 2 * width])
    value = dot(pooled, merged_ref[:, 2 * width :])
    own = coarse_ref[pl.ds(mine, 1), :]
    rms = rms_factor(coarse)
    group = 4 * HD
    spans = [slice(at, at + group) for at in range(0, width, group)]
    tall = jnp.concatenate([key[:, span] for span in spans], 0)
    queries = [query[:, span] for span in spans]
    cross = jnp.concatenate([key[:, span] * q for span, q in zip(spans, queries)], 0)
    ones = ones_ref[...]
    query_squares = jnp.concatenate([q * q for q in queries], 0).astype(BF)
    query_norm = head_factor(dot(query_squares, ones), rms_factor(own))
    key_norm = head_factor(dot((tall * tall).astype(BF), ones), jnp.concatenate([rms] * len(spans), 0))
    scores = dot_split(cross, ones) * key_norm
    count = key.shape[0]
    parts = []
    for at, span in enumerate(spans):
        factor = query_norm[at : at + 1] * scale_ref[:, span]
        expo = jnp.exp(scores[at * count : (at + 1) * count] * factor)
        total = jnp.sum(expo, 0, keepdims=True)
        parts.append(jnp.sum(expo * rms * value[:, span], 0, keepdims=True) / total)
    cattn = jnp.concatenate(parts, 1).astype(BF)
    coarse_out_ref[...] = (own + dot(cattn, out_ref[...])).astype(BF)
    wait_all(copies)


def vmem(count):
    return [pl.BlockSpec(memory_space=pltpu.VMEM)] * count


def anywhere(count):
    return [pl.BlockSpec(memory_space=pl.ANY)] * count


def in_vmem(arrays):
    return [pltpu.with_memory_space_constraint(array, pltpu.VMEM) for array in arrays]


def in_hbm(arrays):
    return [pltpu.with_memory_space_constraint(array, pltpu.HBM) for array in arrays]


def shards(
    tokens, gain_attn, qkv_fine, scale_fine, out_fine, gain_ffn, ffn_in, ffn_out,
    up_proj, gain_coarse, qkv_coarse, scale_coarse, out_coarse,
):
    rows, cols, width = tokens.shape
    count = rows * cols
    strip = RADIUS * cols
    side = rounded_up((rows + 2 * RADIUS) * RADIUS, 16)
    heads = width // HD
    width_c = out_coarse.shape[0]
    devices = lax.axis_size("ha") * lax.axis_size("wa")
    axes = ("ha", "wa")
    params = pltpu.CompilerParams(vmem_limit_bytes=16 * MIB)

    def swapped(array, axis, first):
        pairs = [(i, i + 1) for i in range(first, lax.axis_size(axis) - 1, 2)]
        return lax.ppermute(array, axis, pairs + [(j, i) for i, j in pairs])

    flat = tokens.reshape(count, width)
    across, within = pl.pallas_call(
        functools.partial(strip_kernel, rows, cols, "ha"),
        out_shape=[pltpu.VMEM((strip, width), BF)] * 2,
        in_specs=anywhere(1),
        out_specs=vmem(2),
        scratch_shapes=[pltpu.SemaphoreType.DMA((2,))],
        compiler_params=params,
        name="strips",
    )(*in_hbm([flat]))
    across = swapped(across, "ha", 1)
    within = swapped(within, "ha", 0)

    block = 256
    weights = [
        flat, qkv_fine, gain_attn.reshape(1, -1), scale_fine.reshape(1, -1),
        up_proj, gain_coarse.reshape(1, -1), scale_coarse.reshape(1, -1),
        out_fine, gain_ffn.reshape(1, -1), ffn_in, ffn_out,
    ]
    *weights, head, query, acc, ones, mask = pl.pallas_call(
        functools.partial(own_kernel, rows, cols, heads, side, axes),
        out_shape=[pltpu.VMEM(array.shape, array.dtype) for array in weights]
        + [
            pltpu.VMEM((block, 3 * width_c), BF),
            pltpu.VMEM((heads, count, 2 * HD), BF),
            pltpu.VMEM((heads, count, 2 * HD), F32),
            pltpu.VMEM((4 * HD, 4 * HD), BF),
            pltpu.VMEM((2 * strip + 2 * side, 2 * HD), BF),
        ],
        in_specs=anywhere(len(weights) + 1),
        out_specs=vmem(len(weights) + 5),
        scratch_shapes=[pltpu.SemaphoreType.DMA((len(weights) + 1,))],
        compiler_params=params,
        cost_estimate=pl.CostEstimate(
            flops=2 * count * width * (3 * width + 2 * count), bytes_accessed=4 * MIB, transcendentals=0
        ),
        name="own",
    )(*in_hbm(weights + [qkv_coarse]))
    tok_v, qkv_v, gain_attn_v, scale_v, up_v, gain_c_v, scale_c_v = weights[:7]
    out_v, gain_ffn_v, ffn_in_v, ffn_out_v = weights[7:]

    across_edge, within_edge = pl.pallas_call(
        functools.partial(edge_kernel, rows, cols, axes),
        out_shape=[pltpu.VMEM((side, width), BF)] * 2,
        in_specs=vmem(4),
        out_specs=vmem(2),
        compiler_params=params,
        name="edges",
    )(*in_vmem([tok_v, across, within, query]))
    across_side = swapped(across_edge, "wa", 1)
    within_side = swapped(within_edge, "wa", 0)

    merged, scale_lanes = pl.pallas_call(
        merge_kernel,
        out_shape=[pltpu.VMEM((width, 3 * width_c), BF), pltpu.VMEM((1, width_c), F32)],
        in_specs=vmem(5) + anywhere(1),
        out_specs=vmem(2),
        scratch_shapes=[
            pltpu.VMEM((width_c - block, 3 * width_c), BF),
            pltpu.VMEM(up_proj.shape, BF),
            pltpu.VMEM((width, 3 * width_c), F32),
            pltpu.SemaphoreType.DMA((width_c // block - 1,)),
        ],
        compiler_params=params,
        cost_estimate=pl.CostEstimate(
            flops=6 * width * width_c * width_c, bytes_accessed=8 * MIB, transcendentals=0
        ),
        name="merge",
    )(*in_vmem([within_edge, up_v, gain_c_v, scale_c_v, head]), *in_hbm([qkv_coarse]))

    def fine_body(tok_ref, *refs):
        fine_kernel(heads, axes[0], tok_ref, refs[:4], *refs[4:])

    fine, pooled, out_c_v = pl.pallas_call(
        fine_body,
        out_shape=[
            pltpu.VMEM((count, width), BF),
            pltpu.VMEM((devices, width // 128, 128), F32),
            pltpu.VMEM(out_coarse.shape, BF),
        ],
        in_specs=vmem(17) + anywhere(1),
        out_specs=vmem(3),
        scratch_shapes=[pltpu.SemaphoreType.DMA((1,))],
        compiler_params=params,
        name="fine",
    )(
        *in_vmem(
            [tok_v, across, within, across_side, within_side, query, acc, ones, mask, gain_attn_v, qkv_v, scale_v]
            + [out_v, gain_ffn_v, ffn_in_v, ffn_out_v, merged]
        ),
        *in_hbm([out_coarse]),
    )

    every = lax.all_to_all(pooled, axes, split_axis=0, concat_axis=0, tiled=True)
    coarse_out, fine = pl.pallas_call(
        functools.partial(coarse_kernel, axes),
        out_shape=[
            jax.ShapeDtypeStruct((1, width_c), BF),
            jax.ShapeDtypeStruct((count, width), BF),
        ],
        in_specs=vmem(7),
        out_specs=vmem(1) + anywhere(1),
        scratch_shapes=[pltpu.VMEM((devices, width_c), F32), pltpu.SemaphoreType.DMA((1,))],
        compiler_params=params,
        name="coarse",
    )(*in_vmem([every, up_v, merged, scale_lanes, out_c_v, fine, ones]))
    return fine.reshape(rows, cols, width), coarse_out.reshape(1, 1, width_c)


def solution(mesh):
    return jax.shard_map(
        shards,
        mesh=mesh,
        in_specs=(P("ha", "wa", None), P(), P(), P(), P(), P(), P(), P(), P(), P(), P(), P(), P()),
        out_specs=(P("ha", "wa", None), P("ha", "wa", None)),
        check_vma=False,
    )
```

```python
import functools

import jax
import jax.numpy as jnp
from jax import lax
from jax.experimental import pallas as pl
from jax.experimental.pallas import tpu as pltpu
from jax.sharding import PartitionSpec as P

HD = 64
RADIUS = 3
LOG2E = 1.4426950408889634
BIG = 2.0**30
GELU = 0.7978845608028654
BF = jnp.bfloat16
F32 = jnp.float32
MIB = 1 << 20


def rounded_up(value, step):
    return -(-value // step) * step


def over(values, size):
    assert size & (size - 1) == 0
    return values >> (size.bit_length() - 1)


def dot(a, b):
    return jnp.dot(a, b, preferred_element_type=F32)


def dot_nt(a, b):
    return lax.dot_general(a, b, (((1,), (1,)), ((), ())), preferred_element_type=F32)


def dot_split(values, ones):
    high = values.astype(BF)
    low = (values - high.astype(F32)).astype(BF)
    return dot(high, ones) + dot(low, ones)


def same_head(size):
    left = over(lax.broadcasted_iota(jnp.int32, (size, 1), 0), HD)
    right = over(lax.broadcasted_iota(jnp.int32, (1, size), 1), HD)
    return jnp.where(left == right, 1.0, 0.0).astype(BF)


def head_norm(values, ones):
    return values * lax.rsqrt(dot((values * values).astype(BF), ones) * (1.0 / HD) + 1e-06)


def rms_factor(values):
    return lax.rsqrt(jnp.mean(values * values, -1, keepdims=True) + 1e-06)


def rms_norm(values, gain):
    return values * rms_factor(values) * gain


def head_factor(squares, factor):
    return factor * lax.rsqrt(squares * (factor * factor * (1.0 / HD)) + 1e-06)


def copies_of(pairs, sems):
    return [pltpu.make_async_copy(src, dst, sems.at[i]) for i, (src, dst) in enumerate(pairs)]


def start_all(copies):
    for copy in copies:
        copy.start()


def wait_all(copies):
    for copy in copies:
        copy.wait()


def after_starts(axis):
    return pl.when(lax.axis_index(axis) >= 0)


def strip_kernel(rows, cols, axis, tok_hbm, across_ref, within_ref, sems):
    count, strip = rows * cols, RADIUS * cols
    odd = lax.axis_index(axis) & 1
    last = count - strip
    first = pl.multiple_of(odd * last, 16)
    second = pl.multiple_of((1 - odd) * last, 16)
    copies = copies_of(
        [
            (tok_hbm.at[pl.ds(first, strip), :], across_ref),
            (tok_hbm.at[pl.ds(second, strip), :], within_ref),
        ],
        sems,
    )
    start_all(copies)
    wait_all(copies)


def edge_kernel(rows, cols, axes, tok_ref, across_ref, within_ref, after_ref, across_out, within_out):
    height = rows + 2 * RADIUS
    strip = RADIUS * cols
    padded = across_out.shape[0]
    odd, odd_col = lax.axis_index(axes[0]) & 1, lax.axis_index(axes[1]) & 1
    block = jnp.concatenate([tok_ref[...], across_ref[...], within_ref[...]], 0)
    out = lax.broadcasted_iota(jnp.int32, (padded, 1), 0)
    src = lax.broadcasted_iota(jnp.int32, (padded, block.shape[0]), 1)
    row = ((out * 21846) >> 16) - RADIUS
    col = out - 3 * (row + RADIUS)
    above = rows * cols + strip * odd + RADIUS * cols
    below = rows * cols + strip * (1 - odd) - rows * cols
    first = row * cols + col + jnp.where(row < 0, above, jnp.where(row >= rows, below, 0))
    first = jnp.where(out < height * RADIUS, first, -2 * cols)
    far = cols - RADIUS
    pick = jnp.where(src == first + far * odd_col, 1.0, 0.0).astype(BF)
    across_out[...] = dot(pick, block).astype(BF)
    pick = jnp.where(src == first + far * (1 - odd_col), 1.0, 0.0).astype(BF)
    within_out[...] = dot(pick, block).astype(BF)


def merge_kernel(
    after_ref, up_ref, gain_ref, scale_ref, head_ref, qkv_hbm,
    merged_ref, scale_out, weight_ref, scaled_ref, total_ref, sems,
):
    size = head_ref.shape[0]
    blocks = sems.shape[0]

    def span_of(block):
        return pl.ds(pl.multiple_of(block * size, size), size)

    def copy(block):
        return pltpu.make_async_copy(
            qkv_hbm.at[span_of(block + 1), :], weight_ref.at[span_of(block), :], sems.at[block]
        )

    for block in range(blocks):
        copy(block).start()
    lane = over(lax.broadcasted_iota(jnp.int32, scale_out.shape, 1), HD)
    scales = jnp.zeros(scale_out.shape, F32)
    for head in range(scale_ref.shape[1]):
        scales = jnp.where(lane == head, scale_ref[0:1, head : head + 1], scales)
    scale_out[...] = scales * (1.0 / HD)
    scaled_ref[...] = (up_ref[...].astype(F32) * gain_ref[...]).astype(BF)
    wide = 4 * size
    rows = scaled_ref[:, :size]

    def begin(part, carry):
        span = pl.ds(pl.multiple_of(part * wide, wide), wide)
        total_ref[:, span] = dot(rows, head_ref[:, span])
        return carry

    lax.fori_loop(0, merged_ref.shape[1] // wide, begin, 0)

    def step(block, carry):
        copy(block).wait()
        rows = scaled_ref[:, span_of(block + 1)]
        depth = span_of(block)
        for at in range(0, merged_ref.shape[1], size):
            span = slice(at, at + size)
            total = total_ref[:, span] + dot(rows, weight_ref[depth, span])
            total_ref[:, span] = total
            merged_ref[:, span] = total.astype(BF)
        return carry

    lax.fori_loop(0, blocks, step, 0)


def half_lanes():
    return lax.broadcasted_iota(jnp.int32, (1, 2 * HD), 1) < HD


def mask_columns(rows, cols):
    place = lax.broadcasted_iota(jnp.int32, (1, 2 * HD), 1) & (HD - 1)
    return place, place < rows, (place >= rows) & (place < rows + cols)


def query_columns(rows, cols):
    place, is_row, is_col = mask_columns(rows, cols)
    spot = lax.broadcasted_iota(jnp.int32, (rows * cols, 1), 0)
    hot = (is_row & (over(spot, cols) == place)) | (is_col & ((spot & (cols - 1)) == place - rows))
    return jnp.where(hot, 1.0, 0.0).astype(BF)


def key_columns(rows, cols, krow, kcol):
    place, is_row, is_col = mask_columns(rows, cols)
    far_row = jnp.abs(krow - place) > RADIUS
    far_col = jnp.abs(kcol - (place - rows)) > RADIUS
    return jnp.where((is_row & far_row) | (is_col & far_col), -BIG, 0.0).astype(BF)


def halo_columns(rows, cols, side, axes):
    strip = RADIUS * cols
    row_axis, col_axis = axes
    place_row, place_col = lax.axis_index(row_axis), lax.axis_index(col_axis)
    row0, col0 = place_row * rows, place_col * cols
    grid_rows = lax.axis_size(row_axis) * rows
    grid_cols = lax.axis_size(col_axis) * cols
    odd, odd_col = place_row & 1, place_col & 1
    row_at = (odd * (rows + RADIUS) - RADIUS, (1 - odd) * (rows + RADIUS) - RADIUS)
    col_at = (odd_col * (cols + RADIUS) - RADIUS, (1 - odd_col) * (cols + RADIUS) - RADIUS)
    spot = lax.broadcasted_iota(jnp.int32, (2 * strip + 2 * side, 1), 0)
    past_first = spot - strip
    past_strips = past_first - strip
    past_third = past_strips - side
    strip_at = jnp.where(past_first >= 0, past_first, spot)
    side_at = jnp.where(past_third >= 0, past_third, past_strips)
    side_row = (side_at * 21846) >> 16
    in_strip = past_strips < 0
    krow = jnp.where(
        in_strip,
        over(strip_at, cols) + jnp.where(past_first >= 0, row_at[1], row_at[0]),
        side_row - RADIUS,
    )
    kcol = jnp.where(
        in_strip,
        strip_at & (cols - 1),
        side_at - 3 * side_row + jnp.where(past_third >= 0, col_at[1], col_at[0]),
    )
    real = in_strip | (side_at < (rows + 2 * RADIUS) * RADIUS)
    real = real & (krow + row0 >= 0) & (krow + row0 < grid_rows)
    real = real & (kcol + col0 >= 0) & (kcol + col0 < grid_cols)
    return key_columns(rows, cols, jnp.where(real, krow, -1000), kcol)


def half_of(head):
    low = half_lanes()
    lanes = 2 * HD
    return (low if head % 2 == 0 else ~low), slice(head // 2 * lanes, (head // 2 + 1) * lanes)


def attend(head, query, key, value, key_mask, factor):
    mine, span = half_of(head)
    k = jnp.where(mine, key[:, span], key_mask)
    v = jnp.where(mine, value[:, span], jnp.ones((1, 2 * HD), BF))
    weights = jnp.exp2(dot_nt(query, k) * (factor * (LOG2E / HD))).astype(BF)
    return dot(weights, v)


def own_kernel(rows, cols, heads, side, axes, *refs):
    count = (len(refs) - 7) // 2
    ins, qkv_c_hbm, outs = refs[:count], refs[count], refs[count + 1 : 2 * count + 1]
    head_ref, query_ref, acc_ref, ones_ref, mask_ref, sems = refs[2 * count + 1 :]
    tok_ref, qkv_ref, gain_ref, scale_ref = outs[:4]
    head = (qkv_c_hbm.at[pl.ds(0, head_ref.shape[0]), :], head_ref)
    copies = copies_of(list(zip(ins, outs)) + [head], sems)
    start_all(copies)

    @after_starts(axes[0])
    def _():
        width = heads * HD
        ones = same_head(width)
        ones_ref[...] = ones
        mask_ref[...] = halo_columns(rows, cols, side, axes)
        query_mask = query_columns(rows, cols)
        spot = lax.broadcasted_iota(jnp.int32, (rows * cols, 1), 0)
        key_mask = key_columns(rows, cols, over(spot, cols), spot & (cols - 1))
        wait_all(copies[:4])
        normed = rms_norm(tok_ref[...].astype(F32), gain_ref[...]).astype(BF)
        query = head_norm(dot(normed, qkv_ref[:, :width]), ones).astype(BF)
        key = head_norm(dot(normed, qkv_ref[:, width : 2 * width]), ones).astype(BF)
        value = dot(normed, qkv_ref[:, 2 * width :]).astype(BF)
        for head in range(heads):
            factor = scale_ref[0:1, head : head + 1]
            mine, span = half_of(head)
            masked = jnp.where(mine, query[:, span], query_mask)
            query_ref[head] = masked
            acc_ref[head] = attend(head, masked, key, value, key_mask, factor)

    wait_all(copies[4:])


def fine_kernel(
    heads, axis,
    tok_ref, halo_refs, query_ref, acc_ref, ones_ref, mask_ref, gain_attn_ref, qkv_ref, scale_ref,
    out_ref, gain_ffn_ref, ffn_in_ref, ffn_out_ref, after_ref, out_c_hbm,
    fine_ref, pooled_ref, out_c_ref, sems,
):
    copies = copies_of([(out_c_hbm, out_c_ref)], sems)
    start_all(copies)

    @after_starts(axis)
    def _():
        width = heads * HD
        halo = jnp.concatenate([ref[...] for ref in halo_refs], 0)
        halo = halo.astype(F32)
        scaled = (halo * gain_attn_ref[...]).astype(BF)
        halo_rms = rms_factor(halo)
        ones = ones_ref[...]
        key = dot(scaled, qkv_ref[:, width : 2 * width])
        key = (key * head_factor(dot((key * key).astype(BF), ones), halo_rms)).astype(BF)
        value = (dot(scaled, qkv_ref[:, 2 * width :]) * halo_rms).astype(BF)

        key_mask = mask_ref[...]
        low = half_lanes()
        parts = []
        for pair in range(heads // 2):
            sums = []
            for head in (2 * pair, 2 * pair + 1):
                factor = scale_ref[0:1, head : head + 1]
                sums.append(acc_ref[head] + attend(head, query_ref[head], key, value, key_mask, factor))
            top = jnp.where(low, sums[0], sums[1])
            bottom = pltpu.roll(jnp.where(low, sums[1], sums[0]), HD, 1)
            parts.append((top / bottom).astype(BF))
        attn = jnp.concatenate(parts, 1)

        h1 = (tok_ref[...].astype(F32) + dot(attn, out_ref[...])).astype(BF)
        h1_wide = h1.astype(F32)
        scaled = (h1_wide * gain_ffn_ref[...]).astype(BF)
        h1_rms = rms_factor(h1_wide)
        hidden = ffn_out_ref.shape[0]
        gate = dot(scaled, ffn_in_ref[:, :hidden]) * h1_rms
        up = dot(scaled, ffn_in_ref[:, hidden:]) * (0.5 * h1_rms)
        inner = gate * (GELU + (GELU * 0.044715) * (gate * gate))
        gated = (gate * up * (1.0 + jnp.tanh(inner))).astype(BF)
        fine = (h1_wide + dot(gated, ffn_out_ref[...])).astype(BF)
        fine_ref[...] = fine
        pooled = jnp.mean(fine.astype(F32), 0, keepdims=True).astype(BF).astype(F32)
        for part in range(pooled_ref.shape[1]):
            pooled_ref[:, part, :] = jnp.broadcast_to(
                pooled[:, part * 128 : (part + 1) * 128], (pooled_ref.shape[0], 128)
            )

    wait_all(copies)


def coarse_kernel(
    axes, pooled_ref, up_ref, merged_ref, scale_ref, out_ref, fine_ref, ones_ref,
    coarse_out_ref, fine_hbm,
    coarse_ref, sems,
):
    copies = copies_of([(fine_ref, fine_hbm)], sems)
    start_all(copies)
    width = out_ref.shape[0]
    row_axis, col_axis = axes
    mine = lax.axis_index(row_axis) * lax.axis_size(col_axis) + lax.axis_index(col_axis)
    pooled = jnp.concatenate([pooled_ref[:, part, :] for part in range(pooled_ref.shape[1])], 1).astype(BF)
    coarse = dot(pooled, up_ref[...]).astype(BF).astype(F32)
    coarse_ref[...] = coarse
    mine_row = [pooled_ref[pl.ds(mine, 1), part, :] for part in range(pooled_ref.shape[1])]
    query = dot(jnp.concatenate(mine_row, 1).astype(BF), merged_ref[:, :width])
    key = dot(pooled, merged_ref[:, width : 2 * width])
    value = dot(pooled, merged_ref[:, 2 * width :])
    own = coarse_ref[pl.ds(mine, 1), :]
    rms = rms_factor(coarse)
    group = 4 * HD
    spans = [slice(at, at + group) for at in range(0, width, group)]
    tall = jnp.concatenate([key[:, span] for span in spans], 0)
    queries = [query[:, span] for span in spans]
    cross = jnp.concatenate([key[:, span] * q for span, q in zip(spans, queries)], 0)
    ones = ones_ref[...]
    squares = jnp.concatenate([q * q for q in queries], 0)
    sums = dot(jnp.concatenate([tall * tall, cross, squares], 0).astype(BF), ones)
    count = key.shape[0]
    total = count * len(spans)
    key_norm = head_factor(sums[:total], jnp.concatenate([rms] * len(spans), 0))
    scores = sums[total : 2 * total] * key_norm
    query_norm = head_factor(sums[2 * total :], rms_factor(own))
    parts = []
    for at, span in enumerate(spans):
        factor = query_norm[at : at + 1] * scale_ref[:, span]
        expo = jnp.exp(scores[at * count : (at + 1) * count] * factor)
        total = jnp.sum(expo, 0, keepdims=True)
        parts.append(jnp.sum(expo * rms * value[:, span], 0, keepdims=True) / total)
    cattn = jnp.concatenate(parts, 1).astype(BF)
    coarse_out_ref[...] = (own + dot(cattn, out_ref[...])).astype(BF)
    wait_all(copies)


def vmem(count):
    return [pl.BlockSpec(memory_space=pltpu.VMEM)] * count


def anywhere(count):
    return [pl.BlockSpec(memory_space=pl.ANY)] * count


def in_vmem(arrays):
    return [pltpu.with_memory_space_constraint(array, pltpu.VMEM) for array in arrays]


def in_hbm(arrays):
    return [pltpu.with_memory_space_constraint(array, pltpu.HBM) for array in arrays]


def shards(
    tokens, gain_attn, qkv_fine, scale_fine, out_fine, gain_ffn, ffn_in, ffn_out,
    up_proj, gain_coarse, qkv_coarse, scale_coarse, out_coarse,
):
    rows, cols, width = tokens.shape
    count = rows * cols
    strip = RADIUS * cols
    side = rounded_up((rows + 2 * RADIUS) * RADIUS, 16)
    heads = width // HD
    width_c = out_coarse.shape[0]
    devices = lax.axis_size("ha") * lax.axis_size("wa")
    axes = ("ha", "wa")
    params = pltpu.CompilerParams(vmem_limit_bytes=16 * MIB)

    def swapped(array, axis, first):
        pairs = [(i, i + 1) for i in range(first, lax.axis_size(axis) - 1, 2)]
        return lax.ppermute(array, axis, pairs + [(j, i) for i, j in pairs])

    flat = tokens.reshape(count, width)
    across, within = pl.pallas_call(
        functools.partial(strip_kernel, rows, cols, "ha"),
        out_shape=[pltpu.VMEM((strip, width), BF)] * 2,
        in_specs=anywhere(1),
        out_specs=vmem(2),
        scratch_shapes=[pltpu.SemaphoreType.DMA((2,))],
        compiler_params=params,
        name="strips",
    )(*in_hbm([flat]))
    across = swapped(across, "ha", 1)
    within = swapped(within, "ha", 0)

    block = 256
    weights = [
        flat, qkv_fine, gain_attn.reshape(1, -1), scale_fine.reshape(1, -1),
        up_proj, gain_coarse.reshape(1, -1), scale_coarse.reshape(1, -1),
        out_fine, gain_ffn.reshape(1, -1), ffn_in, ffn_out,
    ]
    *weights, head, query, acc, ones, mask = pl.pallas_call(
        functools.partial(own_kernel, rows, cols, heads, side, axes),
        out_shape=[pltpu.VMEM(array.shape, array.dtype) for array in weights]
        + [
            pltpu.VMEM((block, 3 * width_c), BF),
            pltpu.VMEM((heads, count, 2 * HD), BF),
            pltpu.VMEM((heads, count, 2 * HD), F32),
            pltpu.VMEM((4 * HD, 4 * HD), BF),
            pltpu.VMEM((2 * strip + 2 * side, 2 * HD), BF),
        ],
        in_specs=anywhere(len(weights) + 1),
        out_specs=vmem(len(weights) + 5),
        scratch_shapes=[pltpu.SemaphoreType.DMA((len(weights) + 1,))],
        compiler_params=params,
        cost_estimate=pl.CostEstimate(
            flops=2 * count * width * (3 * width + 2 * count), bytes_accessed=4 * MIB, transcendentals=0
        ),
        name="own",
    )(*in_hbm(weights + [qkv_coarse]))
    tok_v, qkv_v, gain_attn_v, scale_v, up_v, gain_c_v, scale_c_v = weights[:7]
    out_v, gain_ffn_v, ffn_in_v, ffn_out_v = weights[7:]

    across_edge, within_edge = pl.pallas_call(
        functools.partial(edge_kernel, rows, cols, axes),
        out_shape=[pltpu.VMEM((side, width), BF)] * 2,
        in_specs=vmem(4),
        out_specs=vmem(2),
        compiler_params=params,
        name="edges",
    )(*in_vmem([tok_v, across, within, query]))
    across_side = swapped(across_edge, "wa", 1)
    within_side = swapped(within_edge, "wa", 0)

    merged, scale_lanes = pl.pallas_call(
        merge_kernel,
        out_shape=[pltpu.VMEM((width, 3 * width_c), BF), pltpu.VMEM((1, width_c), F32)],
        in_specs=vmem(5) + anywhere(1),
        out_specs=vmem(2),
        scratch_shapes=[
            pltpu.VMEM((width_c - block, 3 * width_c), BF),
            pltpu.VMEM(up_proj.shape, BF),
            pltpu.VMEM((width, 3 * width_c), F32),
            pltpu.SemaphoreType.DMA((width_c // block - 1,)),
        ],
        compiler_params=params,
        cost_estimate=pl.CostEstimate(
            flops=6 * width * width_c * width_c, bytes_accessed=8 * MIB, transcendentals=0
        ),
        name="merge",
    )(*in_vmem([within_edge, up_v, gain_c_v, scale_c_v, head]), *in_hbm([qkv_coarse]))

    def fine_body(tok_ref, *refs):
        fine_kernel(heads, axes[0], tok_ref, refs[:4], *refs[4:])

    fine, pooled, out_c_v = pl.pallas_call(
        fine_body,
        out_shape=[
            pltpu.VMEM((count, width), BF),
            pltpu.VMEM((devices, width // 128, 128), F32),
            pltpu.VMEM(out_coarse.shape, BF),
        ],
        in_specs=vmem(17) + anywhere(1),
        out_specs=vmem(3),
        scratch_shapes=[pltpu.SemaphoreType.DMA((1,))],
        compiler_params=params,
        name="fine",
    )(
        *in_vmem(
            [tok_v, across, within, across_side, within_side, query, acc, ones, mask, gain_attn_v, qkv_v, scale_v]
            + [out_v, gain_ffn_v, ffn_in_v, ffn_out_v, merged]
        ),
        *in_hbm([out_coarse]),
    )

    every = lax.all_to_all(pooled, axes, split_axis=0, concat_axis=0, tiled=True)
    coarse_out, fine = pl.pallas_call(
        functools.partial(coarse_kernel, axes),
        out_shape=[
            jax.ShapeDtypeStruct((1, width_c), BF),
            jax.ShapeDtypeStruct((count, width), BF),
        ],
        in_specs=vmem(7),
        out_specs=vmem(1) + anywhere(1),
        scratch_shapes=[pltpu.VMEM((devices, width_c), F32), pltpu.SemaphoreType.DMA((1,))],
        compiler_params=params,
        name="coarse",
    )(*in_vmem([every, up_v, merged, scale_lanes, out_c_v, fine, ones]))
    return fine.reshape(rows, cols, width), coarse_out.reshape(1, 1, width_c)


def solution(mesh):
    return jax.shard_map(
        shards,
        mesh=mesh,
        in_specs=(P("ha", "wa", None), P(), P(), P(), P(), P(), P(), P(), P(), P(), P(), P(), P()),
        out_specs=(P("ha", "wa", None), P("ha", "wa", None)),
        check_vma=False,
    )
```
